32 devices in a mesh: grp: 2 (over y), row: 4 (over x, core), col: 4 (over z).
Axes of the slice: x: 2, y: 2, z: 4, core: 2. Of those that a mesh axis runs over, the one named last changes fastest.
Arguments:
- homolog_tensor: bfloat16 [16, 160, 256], P(('grp', 'row')), parts along dimension 0, may hold values from -6 to 6
- couple_tensor: bfloat16 [320, 160, 128], P(('grp', 'row'), 'col'), parts along dimension 0, may hold values from -6 to 6
- polymer_identity: int32 [320], P('grp'), parts along dimension 0, may hold values from 0 to 3, never falling along the last dimension, each value on 1 to 80 neighbouring positions
- couple_validity: int32 [320, 160], P(('grp', 'row'), 'col'), parts along dimension 0, may hold values 0 or 1
- intra_inter_bias: float32 [2, 128], replicated, may hold values from -6 to 6
- homolog_factor_kernels: bfloat16 [256, 64], replicated, may hold values from -0.375 to 0.375
- tensor_average_kernel: bfloat16 [1024, 128], replicated, may hold values from -1 to 1
- trilateral_input_kernels: bfloat16 [128, 512], replicated, may hold values from -0.5 to 0.5
- sigmoid_filter_kernel: bfloat16 [128, 128], replicated, may hold values from -0.5 to 0.5
- trilateral_final_kernel: bfloat16 [128, 128], replicated, may hold values from -0.5 to 0.5
Outputs:
- updated_pair: bfloat16 [320, 160, 128], P(('grp', 'row'), 'col'), parts along dimension 0
The draws below stay inside these ranges and needn't reach their ends.
There are 2 independent parts, one for each index of `grp`. The reference program is written for one: setup_inputs(seed, part) draws one part's arguments, and reference() takes and returns one part's arrays. A program takes and returns all parts, laid end to end along the dimension named above; an argument that names none is the same for every part. Nothing has to cross between parts.
Inputs may be any that keep to these rules, and one draw needn't show every extreme that they name: `polymer_identity`: chain ids never fall along the residues; every chain holds 1 to 80 residues, one exactly that many.
All inputs are finite; a program needn't handle non-finite values. No bound on the sum of `couple_validity` on one device may be relied on, other than what follows from the above.
Results may differ from the reference program's by a relative error of at most 0.0075.
Values may be sent and summed in bfloat16 or wider, within the bound.
No kernel may reach another device: no remote copies, remote signals or barrier semaphores. Data moves between devices by JAX's collectives and lax.ppermute only.
A program may use at most 128 MiB of HBM per device.

```python
import math
import jax
import jax.numpy as jnp
import numpy as np
from jax import lax

HOMOLOG_DEPTH = 256
CZ = 128
TENSOR_FACTORS = 32
CTRI = 128
RESIDUES_PER_ROW = 40
CHAINS = 4
AMINO_NUMBER = 160
HOMOLOG_NUMBER = 8


def plant(values, stream_key, least, largest):
    extent = values.shape
    place = [jax.random.randint(jax.random.fold_in(stream_key, axis), (), 0, extent[axis]) for axis in range(len(extent))]
    values = values.at[tuple(place)].set(least)
    longest = extent.index(max(extent))
    place[longest] = (place[longest] + 1) % extent[longest]
    return values.at[tuple(place)].set(largest)


def shard_levels(rng, dims, split, least, high):
    gain = 1.0
    for position, blocks in split:
        steps = jax.random.uniform(jax.random.fold_in(jax.random.fold_in(rng, 6), position), (blocks,), jnp.float32, least / len(split), high / len(split))
        gain = gain * jnp.repeat(jnp.exp(steps), dims[position] // blocks).reshape((-1,) + (1,) * (len(dims) - 1 - position))
    return gain


def length_profile(count, total, bound, lean):
    weights = [(1 << 20) // math.isqrt(grade ** lean) + 1 for grade in range(2, count + 1)]
    surplus, counts = total - bound - (count - 1), [1] * (count - 1)
    while surplus > 0:
        free = [i for i in range(count - 1) if counts[i] < bound]
        mass, left = sum([weights[i] for i in free]), surplus
        for i in free:
            addition = min(bound - counts[i], max(1, left * weights[i] // mass), surplus)
            counts[i] = counts[i] + addition
            surplus = surplus - addition
    return np.array([bound] + counts)


def ragged_sizes(key, number_of, total, limit, slope):
    if number_of == 2:
        one = jax.random.randint(key, (), max(1, total - limit), min(limit, total - 1) + 1)
        return jnp.stack([one, total - one])
    lengths = jnp.asarray(length_profile(number_of, total, limit, slope), jnp.int32)
    couples = (number_of - 1) // 2
    source_of, sink = lengths[1:1 + 2 * couples:2], lengths[2:2 + 2 * couples:2]
    room = jnp.minimum(source_of - 1, limit - sink)
    moved = jax.random.randint(jax.random.fold_in(key, 1), (couples,), 0, 1 << 20) % (room + 1)
    lengths = lengths.at[1:1 + 2 * couples:2].set(source_of - moved).at[2:2 + 2 * couples:2].set(sink + moved)
    return lengths[jax.random.permutation(jax.random.fold_in(key, 2), number_of)]


def normal_values(stream_key, extent, width, most, cuts=(), held_as=jnp.bfloat16):
    loudness = shard_levels(stream_key, extent, cuts, -0.22, 0.18) if cuts else 1.0
    array = jax.random.normal(stream_key, extent, jnp.float32) * width * loudness
    return jnp.minimum(jnp.maximum(array, -most), most).astype(held_as)


def setup_inputs(seed: int = 0, part: int = 0) -> dict:
    seeds = jax.random.split(jax.random.key(seed), 11)
    own_keys = jax.random.split(jax.random.fold_in(seeds[10], part), 11)
    return {
        "homolog_tensor": normal_values(own_keys[0], (HOMOLOG_NUMBER, AMINO_NUMBER, HOMOLOG_DEPTH), 1.0, 6.0, ((0, 4),)),
        "couple_tensor": normal_values(own_keys[1], (AMINO_NUMBER, AMINO_NUMBER, CZ), 1.0, 6.0, ((0, 4), (1, 4))),
        "polymer_identity": jnp.searchsorted(jnp.cumsum(ragged_sizes(own_keys[2], CHAINS, AMINO_NUMBER, AMINO_NUMBER // 2, 0)), jnp.arange(AMINO_NUMBER), side="right").astype(jnp.int32),
        "couple_validity": plant((jax.random.randint(own_keys[3], (AMINO_NUMBER, AMINO_NUMBER), 0, 8) < 7).astype(jnp.int32), jax.random.fold_in(own_keys[3], 1), 0, 1),
        "intra_inter_bias": normal_values(seeds[4], (2, CZ), 1.0, 6.0, (), jnp.float32),
        "homolog_factor_kernels": normal_values(seeds[5], (HOMOLOG_DEPTH, 2 * TENSOR_FACTORS), HOMOLOG_DEPTH ** -0.5, 0.375),
        "tensor_average_kernel": normal_values(seeds[6], (TENSOR_FACTORS * TENSOR_FACTORS, CZ), TENSOR_FACTORS ** -0.5, 1.0),
        "trilateral_input_kernels": normal_values(seeds[7], (CZ, 4 * CTRI), CZ ** -0.5, 0.5),
        "sigmoid_filter_kernel": normal_values(seeds[8], (CZ, CZ), CZ ** -0.5, 0.5),
        "trilateral_final_kernel": normal_values(seeds[9], (CTRI, CZ), CTRI ** -0.5, 0.5),
    }


eps = 1e-05

def standardize_activations(values, mesh_axis):
    centre = values - lax.optimization_barrier(jnp.mean(values, axis=mesh_axis, keepdims=True))
    spread = lax.optimization_barrier(jnp.mean(centre * centre, axis=mesh_axis, keepdims=True))
    return centre * lax.rsqrt(spread + eps)

def reference(homolog_tensor, couple_tensor, polymer_identity, couple_validity, intra_inter_bias, homolog_factor_kernels, tensor_average_kernel, trilateral_input_kernels, sigmoid_filter_kernel, trilateral_final_kernel):
    homolog_standardized = standardize_activations(homolog_tensor.astype(jnp.float32), -1).astype(jnp.bfloat16)
    homolog_twofold = jnp.dot(homolog_standardized.reshape(HOMOLOG_NUMBER * AMINO_NUMBER, HOMOLOG_DEPTH), homolog_factor_kernels, preferred_element_type=jnp.float32)
    homolog_twofold = homolog_twofold.reshape(HOMOLOG_NUMBER, AMINO_NUMBER, 2 * TENSOR_FACTORS)
    alignment_left = homolog_twofold[:, :, :TENSOR_FACTORS].astype(jnp.bfloat16)
    alignment_right = homolog_twofold[:, :, TENSOR_FACTORS:].astype(jnp.bfloat16)
    left_block_list = jnp.transpose(alignment_left.reshape(HOMOLOG_NUMBER, AMINO_NUMBER // RESIDUES_PER_ROW, RESIDUES_PER_ROW, TENSOR_FACTORS), (1, 0, 2, 3))
    right_broadened = alignment_right.astype(jnp.float32)

    def outer_rows(residue_slice):
        outer = jnp.einsum('ogy,owe->gwye', residue_slice.astype(jnp.float32), right_broadened) / HOMOLOG_NUMBER
        outer = outer.astype(jnp.bfloat16).reshape(RESIDUES_PER_ROW * AMINO_NUMBER, TENSOR_FACTORS * TENSOR_FACTORS)
        return jnp.dot(outer, tensor_average_kernel, preferred_element_type=jnp.float32).reshape(RESIDUES_PER_ROW, AMINO_NUMBER, CZ)
    opm = lax.map(outer_rows, left_block_list).reshape(AMINO_NUMBER, AMINO_NUMBER, CZ)
    same_chain = (polymer_identity[:, None] == polymer_identity[None, :])[:, :, None]
    base = couple_tensor.astype(jnp.float32) + jnp.where(same_chain, intra_inter_bias[0], intra_inter_bias[1])
    pair_sum = (base + opm).astype(jnp.bfloat16)
    pair_norm = standardize_activations(pair_sum.astype(jnp.float32), -1).astype(jnp.bfloat16)
    flat = pair_norm.reshape(AMINO_NUMBER * AMINO_NUMBER, CZ)
    projected = jnp.dot(flat, trilateral_input_kernels, preferred_element_type=jnp.float32).reshape(AMINO_NUMBER, AMINO_NUMBER, 4 * CTRI)
    mask_wide = couple_validity.astype(jnp.float32)[:, :, None]
    left = (mask_wide * jax.nn.sigmoid(projected[:, :, :CTRI]) * projected[:, :, CTRI:2 * CTRI]).astype(jnp.bfloat16)
    right = (mask_wide * jax.nn.sigmoid(projected[:, :, 2 * CTRI:3 * CTRI]) * projected[:, :, 3 * CTRI:]).astype(jnp.bfloat16)
    left_first = jnp.transpose(left, (2, 0, 1)).astype(jnp.float32)
    right_first = jnp.transpose(right, (2, 1, 0)).astype(jnp.float32)
    mixed = jnp.transpose(jnp.matmul(left_first, right_first), (1, 2, 0))
    mixed_norm = standardize_activations(mixed, -1).astype(jnp.bfloat16)
    update = jnp.dot(mixed_norm.reshape(AMINO_NUMBER * AMINO_NUMBER, CTRI), trilateral_final_kernel, preferred_element_type=jnp.float32)
    gate = jax.nn.sigmoid(jnp.dot(flat, sigmoid_filter_kernel, preferred_element_type=jnp.float32))
    result = pair_sum.astype(jnp.float32) + (gate * update).reshape(AMINO_NUMBER, AMINO_NUMBER, CZ)
    return result.astype(jnp.bfloat16)
```

```python
import functools

import jax
import jax.numpy as jnp
from jax import lax
from jax.experimental import pallas as pl
from jax.experimental.pallas import tpu as pltpu
from jax.sharding import PartitionSpec as P

eps = 1e-05
f32 = jnp.float32
bf16 = jnp.bfloat16
VMEM = pl.BlockSpec(memory_space=pltpu.VMEM)
SMEM = pl.BlockSpec(memory_space=pltpu.SMEM)
PARAMS = pltpu.CompilerParams(vmem_limit_bytes=56 * 1024 * 1024)


def round_up(n, m):
    return (n + m - 1) // m * m


def standardize(values):
    centre = values - jnp.mean(values, axis=-1, keepdims=True)
    spread = jnp.mean(centre * centre, axis=-1, keepdims=True)
    return centre * lax.rsqrt(spread + eps)


def sigmoid(v):
    return 0.5 * jnp.tanh(0.5 * v) + 0.5


def align_body(own_i, own_j, x_ref, w_ref, out_ref, y_ref):
    seqs, residues, depth = x_ref.shape
    width = w_ref.shape[1] // 2
    blocks, _, lanes = out_ref.shape
    at = round_up(own_i, 16)
    z = lax.axis_index("col")
    x = x_ref[...].astype(f32).reshape(seqs * residues, depth)
    normed = standardize(x).astype(bf16)
    y_ref[...] = jnp.dot(normed, w_ref[...], preferred_element_type=f32)
    start = pl.multiple_of(z * own_j, 8)
    right = [y_ref[pl.ds(s * residues + start, own_j), width:] for s in range(seqs)]
    pad = [jnp.zeros((own_j, lanes - seqs * width), f32)] if lanes > seqs * width else []
    right = jnp.concatenate(right + pad, axis=1).astype(bf16)
    for r in range(blocks):
        left = [y_ref[pl.ds(s * residues + r * own_i, own_i), :width] for s in range(seqs)]
        pad = [jnp.zeros((own_i, lanes - seqs * width), f32)] if lanes > seqs * width else []
        out_ref[r, pl.ds(0, own_i), :] = jnp.concatenate(left + pad, axis=1).astype(bf16)
        out_ref[r, pl.ds(at, own_j), :] = right


def pair_body(
    seqs,
    width,
    msg_ref,
    couple_ref,
    ids_ref,
    valid_ref,
    bias_ref,
    avg_ref,
    win_ref,
    wgate_ref,
    left_ref,
    right_ref,
    psum_ref,
    gate_ref,
    xl_ref,
    t_ref,
    wf_ref,
    idc_ref,
):
    own_i, own_j, chans = couple_ref.shape
    blocks, _, lanes = msg_ref.shape
    total = seqs * blocks
    at = round_up(own_i, 16)
    x0 = lax.axis_index("row") * own_i
    z0 = lax.axis_index("col") * own_j
    tri = win_ref.shape[1] // 4

    for r in range(blocks):
        m = msg_ref[r, pl.ds(0, own_i), :].astype(f32)
        for s in range(seqs):
            turned = m if s == 0 else pltpu.roll(m, lanes - s * width, 1)
            xl_ref[pl.ds(r * seqs + s, own_i, stride=total), :] = turned[:, :128]
    lhs = xl_ref[:, :width].astype(bf16)

    row = lax.broadcasted_iota(jnp.int32, (lanes, width * total), 0)
    col = lax.broadcasted_iota(jnp.int32, (lanes, width * total), 1)
    place = (row % width) * total + row // width
    rmat = jnp.zeros((own_j, width * total), f32)
    for r in range(blocks):
        pick = (col == place + r * seqs) & (row < seqs * width)
        pick = jnp.where(pick, 1.0, 0.0).astype(bf16)
        rmat += jnp.dot(msg_ref[r, pl.ds(at, own_j), :], pick, preferred_element_type=f32)
    rmat = rmat.astype(bf16)

    wf_ref[...] = avg_ref[...].astype(f32)

    def expand(h, carry):
        q = h * 2
        both = [wf_ref[pl.ds(q + d, width, stride=width), :] for d in range(2)]
        rhs = jnp.concatenate(both, axis=1).astype(bf16)
        out = jnp.dot(lhs, rhs, preferred_element_type=f32)
        parts = [out[:, d * chans : (d + 1) * chans].reshape(own_i, total, chans) for d in range(2)]
        block = jnp.concatenate(parts, axis=1).astype(bf16)
        t_ref[:, pl.ds(pl.multiple_of(q * total, 16), 2 * total), :] = block
        return carry

    lax.fori_loop(0, width // 2, expand, 0)

    for j in range(own_j):
        idc_ref[pl.ds(j, 1), :] = jnp.full((1, chans), ids_ref[z0 + j], jnp.int32)
    idc = idc_ref[...]
    valid_t = valid_ref[...].astype(f32).T
    lane = lax.broadcasted_iota(jnp.int32, valid_t.shape, 1)
    same_bias = bias_ref[0:1, :]
    cross_bias = bias_ref[1:2, :]
    group = 8 if own_i % 8 == 0 else 1

    def rows(b, carry):
        i0 = b * group
        normed = []
        masks = []
        for g in range(group):
            i = i0 + g
            opm = jnp.dot(rmat, t_ref[i], preferred_element_type=f32) * (1.0 / total)
            base = couple_ref[i].astype(f32) + jnp.where(idc == ids_ref[x0 + i], same_bias, cross_bias)
            psum = (base + opm).astype(bf16)
            psum_ref[i] = psum
            normed.append(standardize(psum.astype(f32)))
            masks.append(jnp.sum(jnp.where(lane == i, valid_t, 0.0), axis=1, keepdims=True))
        flat = jnp.concatenate(normed, axis=0).astype(bf16)
        mask = jnp.concatenate(masks, axis=0)
        proj = jnp.dot(flat, win_ref[...], preferred_element_type=f32)
        left = mask * sigmoid(proj[:, :tri]) * proj[:, tri : 2 * tri]
        right = mask * sigmoid(proj[:, 2 * tri : 3 * tri]) * proj[:, 3 * tri :]
        gate = sigmoid(jnp.dot(flat, wgate_ref[...], preferred_element_type=f32))
        left_ref[pl.ds(i0, group)] = left.reshape(group, own_j, tri).astype(bf16)
        right_ref[pl.ds(i0, group)] = right.reshape(group, own_j, tri).astype(bf16)
        gate_ref[pl.ds(i0, group)] = gate.reshape(group, own_j, chans)
        return carry

    lax.fori_loop(0, own_i // group, rows, 0)


def contract(lf_ref, rk_ref, i0, group, depth, init):
    step = 8

    def add(kb, acc):
        k0 = pl.multiple_of(kb * step, step)
        lefts = [lf_ref[i0 + t, pl.ds(k0, step), :] for t in range(group)]
        acc = list(acc)
        for d in range(step):
            right = rk_ref[k0 + d]
            for t in range(group):
                acc[t] = acc[t] + lefts[t][d : d + 1, :] * right
        return tuple(acc)

    return lax.fori_loop(0, depth // step, add, tuple(init))


def spread_right(r_ref, flat_ref, rk_ref):
    extent, depth, _ = r_ref.shape

    def widen(j, carry):
        flat_ref[pl.ds(pl.multiple_of(j * depth, 8), depth), :] = r_ref[j].astype(f32)
        return carry

    lax.fori_loop(0, extent, widen, 0, unroll=4)

    def turn(k, carry):
        rk_ref[k] = flat_ref[pl.ds(k, extent, stride=depth), :]
        return carry

    lax.fori_loop(0, depth, turn, 0, unroll=4)


def triangle_body(l_ref, r_ref, o_ref, lf_ref, flat_ref, rk_ref):
    own_i, depth, chans = l_ref.shape
    extent = r_ref.shape[0]
    group = 8 if own_i % 8 == 0 else 1

    @pl.when(pl.program_id(0) == 0)
    def _():
        lf_ref[...] = l_ref[...].astype(f32)

    spread_right(r_ref, flat_ref, rk_ref)

    def rows(b, carry):
        i0 = b * group
        zero = [jnp.zeros((extent, chans), f32) for _ in range(group)]
        acc = contract(lf_ref, rk_ref, i0, group, depth, zero)
        for t in range(group):
            o_ref[0, i0 + t] = acc[t].astype(bf16)
        return carry

    lax.fori_loop(0, own_i // group, rows, 0)


def finish_body(sum_ref, psum_ref, gate_ref, w_ref, out_ref):
    parts, own_i, extent, chans = sum_ref.shape
    group = 8 if own_i % 8 == 0 else 1

    def rows(b, carry):
        i0 = b * group
        for part in range(parts):
            cut = pl.ds(part * extent, extent)
            mixed = sum_ref[part, pl.ds(i0, group)].astype(f32)
            normed = standardize(mixed).reshape(group * extent, chans).astype(bf16)
            update = jnp.dot(normed, w_ref[...], preferred_element_type=f32).reshape(group, extent, -1)
            base = psum_ref[pl.ds(i0, group), cut, :].astype(f32)
            gate = gate_ref[pl.ds(i0, group), cut, :]
            out_ref[pl.ds(i0, group), cut, :] = (base + gate * update).astype(bf16)
        return carry

    lax.fori_loop(0, own_i // group, rows, 0)


def shards(homolog, couple, ids, valid, bias, factors, average, w_in, w_gate, w_final):
    rows, cols = lax.axis_size("row"), lax.axis_size("col")
    own_seqs, residues, depth = homolog.shape
    own_i, own_j, chans = couple.shape
    width = factors.shape[1] // 2
    tri = w_final.shape[0]
    total = own_seqs * rows
    lanes = round_up(own_seqs * width, 128)
    height = round_up(own_i, 16) + round_up(own_j, 16)

    msg = pl.pallas_call(
        functools.partial(align_body, own_i, own_j),
        out_shape=jax.ShapeDtypeStruct((rows, height, lanes), bf16),
        in_specs=[VMEM] * 2,
        out_specs=VMEM,
        scratch_shapes=[pltpu.VMEM((own_seqs * residues, 2 * width), f32)],
        compiler_params=PARAMS,
        name="align",
    )(homolog, factors)
    msg = lax.all_to_all(msg, "row", split_axis=0, concat_axis=0, tiled=True)

    block = jax.ShapeDtypeStruct((own_i, own_j, tri), bf16)
    left, right, psum, gate = pl.pallas_call(
        functools.partial(pair_body, own_seqs, width),
        out_shape=[block, block, jax.ShapeDtypeStruct((own_i, own_j, chans), bf16),
                   jax.ShapeDtypeStruct((own_i, own_j, chans), f32)],
        in_specs=[VMEM, VMEM, SMEM, VMEM, VMEM, VMEM, VMEM, VMEM],
        out_specs=[VMEM] * 4,
        scratch_shapes=[
            pltpu.VMEM((own_i * total, 128), f32),
            pltpu.VMEM((own_i, width * total, chans), bf16),
            pltpu.VMEM((width * width, chans), f32),
            pltpu.VMEM((own_j, chans), jnp.int32),
        ],
        compiler_params=PARAMS,
        name="pair",
    )(msg, couple, ids, valid, bias, average, w_in, w_gate)

    right_all = lax.all_gather(right, "row", axis=0, tiled=True)
    partial = pl.pallas_call(
        triangle_body,
        grid=(rows,),
        out_shape=jax.ShapeDtypeStruct((rows, own_i, own_i, tri), bf16),
        in_specs=[
            pl.BlockSpec((own_i, own_j, tri), lambda r: (0, 0, 0)),
            pl.BlockSpec((own_i, own_j, tri), lambda r: (r, 0, 0)),
        ],
        out_specs=pl.BlockSpec((1, own_i, own_i, tri), lambda r: (r, 0, 0, 0)),
        scratch_shapes=[
            pltpu.VMEM((own_i, own_j, tri), f32),
            pltpu.VMEM((own_i * own_j, tri), f32),
            pltpu.VMEM((own_j, own_i, tri), f32),
        ],
        compiler_params=PARAMS,
        name="triangle",
    )(left, right_all)
    summed = lax.psum_scatter(partial, "col", scatter_dimension=0, tiled=True)
    return pl.pallas_call(
        finish_body,
        out_shape=jax.ShapeDtypeStruct((own_i, own_j, chans), bf16),
        in_specs=[VMEM] * 4,
        out_specs=VMEM,
        compiler_params=PARAMS,
        name="finish",
    )(summed, psum, gate, w_final)


def solution(mesh):
    placed = (
        P(("grp", "row"), None, None),
        P(("grp", "row"), "col", None),
        P("grp"),
        P(("grp", "row"), "col"),
        P(),
        P(),
        P(),
        P(),
        P(),
        P(),
    )
    return jax.shard_map(
        shards,
        mesh=mesh,
        in_specs=placed,
        out_specs=P(("grp", "row"), "col", None),
        check_vma=False,
    )
```

```python
import functools

import jax
import jax.numpy as jnp
from jax import lax
from jax.experimental import pallas as pl
from jax.experimental.pallas import tpu as pltpu
from jax.sharding import PartitionSpec as P

eps = 1e-05
f32 = jnp.float32
bf16 = jnp.bfloat16
VMEM = pl.BlockSpec(memory_space=pltpu.VMEM)
SMEM = pl.BlockSpec(memory_space=pltpu.SMEM)
ANY = pl.BlockSpec(memory_space=pl.ANY)


def limit(mib, scale=1):
    return pltpu.CompilerParams(vmem_limit_bytes=min(56, mib * scale) * 1024 * 1024)


def round_up(n, m):
    return (n + m - 1) // m * m


def standardize(values):
    centre = values - jnp.mean(values, axis=-1, keepdims=True)
    spread = jnp.mean(centre * centre, axis=-1, keepdims=True)
    return centre * lax.rsqrt(spread + eps)


def sigmoid(v):
    return 0.5 * jnp.tanh(0.5 * v) + 0.5


def align_body(own_i, own_j, x_ref, w_ref, *refs):
    outs, y_ref = refs[:-1], refs[-1]
    seqs, residues, depth = x_ref.shape
    width = w_ref.shape[0] // 2
    height, lanes = outs[0].shape
    me = lax.axis_index("row")
    z = lax.axis_index("col")
    x = x_ref[...].astype(f32).reshape(seqs * residues, depth)
    normed = standardize(x).astype(bf16)
    y_ref[...] = lax.dot_general(
        normed, w_ref[...], (((1,), (1,)), ((), ())), preferred_element_type=f32
    )
    start = pl.multiple_of(z * own_j, 8)
    extent = max(own_i, own_j)

    def tall(v):
        gap = extent - v.shape[0]
        return jnp.concatenate([v, jnp.zeros((gap, v.shape[1]), f32)], axis=0) if gap else v

    right = [tall(y_ref[pl.ds(s * residues + start, own_j), width:]) for s in range(seqs)]
    gap = lanes - 2 * seqs * width
    right += [jnp.zeros((extent, gap), f32)] if gap else []
    for d, out in enumerate(outs):
        first = pl.multiple_of((me ^ d) * own_i, 8)
        left = [tall(y_ref[pl.ds(s * residues + first, own_i), :width]) for s in range(seqs)]
        out[pl.ds(0, extent), :] = jnp.concatenate(left + right, axis=1).astype(bf16)


def prepare_body(couple_ref, ids_ref, valid_ref, bias_ref, avg_ref, base_ref, mask_ref, wq_ref, wf_ref, idc_ref):
    own_i, own_j, chans = couple_ref.shape
    pairs, width, _ = wq_ref.shape
    x0 = lax.axis_index("row") * own_i
    z0 = lax.axis_index("col") * own_j
    wf_ref[...] = avg_ref[...].astype(f32)
    for h in range(pairs):
        both = [wf_ref[pl.ds(2 * h + d, width, stride=width), :] for d in range(2)]
        wq_ref[h] = jnp.concatenate(both, axis=1).astype(bf16)
    for j in range(own_j):
        idc_ref[pl.ds(j, 1), :] = jnp.full((1, chans), ids_ref[z0 + j], jnp.int32)
    idc = idc_ref[...]
    valid_t = valid_ref[...].astype(f32).T
    lane = lax.broadcasted_iota(jnp.int32, valid_t.shape, 1)
    same_bias = bias_ref[0:1, :]
    cross_bias = bias_ref[1:2, :]

    def row(i, carry):
        bias = jnp.where(idc == ids_ref[x0 + i], same_bias, cross_bias)
        base_ref[i] = couple_ref[i].astype(f32) + bias
        column = jnp.sum(jnp.where(lane == i, valid_t, 0.0), axis=1, keepdims=True)
        mask_ref[i] = jnp.broadcast_to(column, (own_j, mask_ref.shape[2])).astype(bf16)
        return carry

    lax.fori_loop(0, own_i, row, 0, unroll=4)


def pair_body(seqs, width, turned, *refs):
    blocks = len(refs) - 10
    msgs = refs[:blocks]
    base_ref, mask_ref, wq_ref, win_ref = refs[blocks : blocks + 4]
    psum_ref, norm_ref, right_ref = refs[blocks + 4 : blocks + 7]
    xl_ref, t_ref, flat_ref = refs[blocks + 7 :]
    own_i, own_j, chans = base_ref.shape
    height, lanes = msgs[0].shape
    total = seqs * blocks
    tri = win_ref.shape[1] // 4

    for r in range(blocks):
        m = msgs[r][pl.ds(0, own_i), :].astype(f32)
        for s in range(seqs):
            moved = m if s == 0 else pltpu.roll(m, lanes - s * width, 1)
            xl_ref[pl.ds(r * seqs + s, own_i, stride=total), :] = moved[:, :128]
    lhs = xl_ref[:, :width].astype(bf16)

    row = lax.broadcasted_iota(jnp.int32, (lanes, width * total), 0)
    col = lax.broadcasted_iota(jnp.int32, (lanes, width * total), 1)
    unit = row - seqs * width
    place = (unit % width) * total + unit // width
    inside = (unit >= 0) & (unit < seqs * width)
    rmat = jnp.zeros((own_j, width * total), f32)
    for r in range(blocks):
        pick = jnp.where((col == place + r * seqs) & inside, 1.0, 0.0).astype(bf16)
        rmat += jnp.dot(msgs[r][pl.ds(0, own_j), :], pick, preferred_element_type=f32)
    rmat = rmat.astype(bf16)

    def expand(h, carry):
        out = jnp.dot(lhs, wq_ref[h], preferred_element_type=f32)
        parts = [out[:, d * chans : (d + 1) * chans].reshape(own_i, total, chans) for d in range(2)]
        block = jnp.concatenate(parts, axis=1).astype(bf16)
        t_ref[:, pl.ds(pl.multiple_of(h * 2 * total, 16), 2 * total), :] = block
        return carry

    lax.fori_loop(0, width // 2, expand, 0, unroll=2)

    group = 8 if own_i % 8 == 0 else 1

    def rows(b, carry):
        i0 = b * group
        normed = []
        for g in range(group):
            i = i0 + g
            opm = jnp.dot(rmat, t_ref[i], preferred_element_type=f32) * (1.0 / total)
            psum = (base_ref[i] + opm).astype(bf16)
            psum_ref[i] = psum
            normed.append(standardize(psum.astype(f32)))
        flat = jnp.concatenate(normed, axis=0).astype(bf16)
        norm_ref[pl.ds(pl.multiple_of(i0 * own_j, 16), group * own_j), :] = flat
        mask = mask_ref[pl.ds(i0, group)].astype(f32).reshape(group * own_j, tri)
        proj = jnp.dot(flat, win_ref[:, 2 * tri :], preferred_element_type=f32)
        right = mask * sigmoid(proj[:, :tri]) * proj[:, tri:]
        if turned:
            flat_ref[pl.ds(pl.multiple_of(i0 * own_j, 8), group * own_j), :] = right
        else:
            right_ref[pl.ds(i0, group)] = right.reshape(group, own_j, tri).astype(bf16)
        return carry

    lax.fori_loop(0, own_i // group, rows, 0)

    def turn(k, carry):
        right_ref[k] = flat_ref[pl.ds(k, own_i, stride=own_j), :].astype(bf16)
        return carry

    if turned:
        lax.fori_loop(0, own_j, turn, 0, unroll=8)


def left_body(norm_ref, mask_ref, win_ref, *outs):
    own_i, own_j, tri = mask_ref.shape
    group = 8 if own_i % 8 == 0 else 1
    at = 0
    for out in outs:
        first = at

        def rows(b, carry):
            i0 = first + b * group
            flat = norm_ref[pl.ds(pl.multiple_of(i0 * own_j, 16), group * own_j), :]
            mask = mask_ref[pl.ds(i0, group)].astype(f32).reshape(group * own_j, tri)
            proj = jnp.dot(flat, win_ref[:, : 2 * tri], preferred_element_type=f32)
            left = mask * sigmoid(proj[:, :tri]) * proj[:, tri:]
            out[pl.ds(b * group, group)] = left.reshape(group, own_j, tri).astype(bf16)
            return carry

        lax.fori_loop(0, out.shape[0] // group, rows, 0)
        at += out.shape[0]


def contract(lf_ref, rk_ref, i0, group, depth):
    step = 8

    def add(kb, acc):
        k0 = pl.multiple_of(kb * step, step)
        acc = list(acc)
        for d in range(step):
            right = rk_ref[k0 + d].astype(f32)
            for t in range(group):
                acc[t] = acc[t] + lf_ref[i0 + t, pl.ds(k0 + d, 1), :] * right
        return tuple(acc)

    zero = jnp.zeros(rk_ref.shape[1:], f32)
    return lax.fori_loop(0, depth // step, add, (zero,) * group)


def pick_right(own_pair, refs, rk_ref, sem):
    own, p_own, got, p_got, late, p_late = refs
    r, z = lax.axis_index("row"), lax.axis_index("col")
    keeper = (r % 2) == (z % 2)
    near = ((r // 2) == (z // 2)) == own_pair
    depth = own.shape[0]
    table = [
        (near & keeper, own, p_got),
        (near & ~keeper, p_own, got),
        (~near & keeper, got, p_late),
        (~near & ~keeper, p_got, late),
    ]
    for cond, a, b in table:

        @pl.when(cond)
        def _():
            for h, src in enumerate((a, b)):
                pltpu.make_async_copy(src, rk_ref.at[pl.ds(h * depth, depth)], sem.at[h]).start()

    def wait():
        for h in range(2):
            pltpu.make_async_copy(own, rk_ref.at[pl.ds(h * depth, depth)], sem.at[h]).wait()

    return wait


def send_body(*refs):
    rights, (l_ref, m_ref, o_ref, lf_ref, rk_ref, sem) = refs[:6], refs[6:]
    own_i, depth, chans = l_ref.shape
    wait = pick_right(False, rights, rk_ref, sem)
    lf_ref[:, pl.ds(0, depth), :] = l_ref[...].astype(f32)
    lf_ref[:, pl.ds(depth, depth), :] = m_ref[...].astype(f32)
    wait()
    group = 8

    def rows(b, carry):
        acc = contract(lf_ref, rk_ref, b * group, group, 2 * depth)
        for t in range(group):
            o_ref[b * group + t] = acc[t].astype(bf16)
        return carry

    lax.fori_loop(0, own_i // group, rows, 0)


def keep_body(cuts, *refs):
    rights, refs = refs[:6], refs[6:]
    lefts, mets = refs[:cuts], refs[cuts : 2 * cuts]
    norm_ref, wgate_ref, o_ref, gate_ref, lf_ref, rk_ref, sem = refs[2 * cuts :]
    own_i, depth, chans = o_ref.shape
    wait = pick_right(True, rights, rk_ref, sem)
    at = 0
    for l_ref, m_ref in zip(lefts, mets):
        n = l_ref.shape[0]
        lf_ref[pl.ds(at, n), pl.ds(0, depth), :] = l_ref[...].astype(f32)
        lf_ref[pl.ds(at, n), pl.ds(depth, depth), :] = m_ref[...].astype(f32)
        at += n
    group = 8

    def gates(b, carry):
        flat = norm_ref[pl.ds(pl.multiple_of(b * group * depth, 16), group * depth), :]
        gate = sigmoid(jnp.dot(flat, wgate_ref[...], preferred_element_type=f32))
        gate_ref[pl.ds(b * group, group)] = gate.reshape(group, depth, -1)
        return carry

    lax.fori_loop(0, own_i // group, gates, 0)
    wait()

    def rows(b, carry):
        acc = contract(lf_ref, rk_ref, b * group, group, 2 * depth)
        for t in range(group):
            o_ref[b * group + t] = acc[t]
        return carry

    lax.fori_loop(0, own_i // group, rows, 0)


def join_body(cuts, *refs):
    sums, (own_ref, psum_ref, gate_ref, w_ref, out_ref) = refs[:cuts], refs[cuts:]
    own_i, extent, chans = out_ref.shape
    group = 8
    at = 0
    for part in sums:
        first = at

        def rows(b, carry):
            rows_ = pl.ds(first + b * group, group)
            mixed = own_ref[rows_] + part[pl.ds(b * group, group)].astype(f32)
            normed = standardize(mixed).reshape(group * extent, -1).astype(bf16)
            update = jnp.dot(normed, w_ref[...], preferred_element_type=f32).reshape(group, extent, -1)
            out_ref[rows_] = (psum_ref[rows_].astype(f32) + gate_ref[rows_] * update).astype(bf16)
            return carry

        lax.fori_loop(0, part.shape[0] // group, rows, 0)
        at += part.shape[0]


def triangle_body(l_ref, r_ref, o_ref, lf_ref, flat_ref, rk_ref):
    own_i, depth, chans = l_ref.shape
    extent = r_ref.shape[0]
    group = 8 if own_i % 8 == 0 else 1

    @pl.when(pl.program_id(0) == 0)
    def _():
        lf_ref[...] = l_ref[...].astype(f32)

    def widen(j, carry):
        flat_ref[pl.ds(pl.multiple_of(j * depth, 8), depth), :] = r_ref[j].astype(f32)
        return carry

    lax.fori_loop(0, extent, widen, 0)

    def turn(k, carry):
        rk_ref[k] = flat_ref[pl.ds(k, extent, stride=depth), :]
        return carry

    lax.fori_loop(0, depth, turn, 0)

    def rows(b, carry):
        i0 = b * group
        acc = contract(lf_ref, rk_ref, i0, group, depth)
        for t in range(group):
            o_ref[0, i0 + t] = acc[t].astype(bf16)
        return carry

    lax.fori_loop(0, own_i // group, rows, 0)


def finish_body(sum_ref, psum_ref, norm_ref, wgate_ref, w_ref, out_ref):
    parts, own_i, extent, chans = sum_ref.shape
    own_j = psum_ref.shape[1]

    def row(i, carry):
        flat = norm_ref[pl.ds(pl.multiple_of(i * own_j, 16), own_j), :]
        gate = sigmoid(jnp.dot(flat, wgate_ref[...], preferred_element_type=f32))
        normed = [standardize(sum_ref[part, i].astype(f32)) for part in range(parts)]
        normed = jnp.concatenate(normed, axis=0).astype(bf16)
        update = jnp.dot(normed, w_ref[...], preferred_element_type=f32)
        out_ref[i] = (psum_ref[i].astype(f32) + gate * update).astype(bf16)
        return carry

    lax.fori_loop(0, own_i, row, 0)


def gathered_plan(left, right, psum, norm, w_gate, w_final):
    own_i, own_j, chans = psum.shape
    rows = lax.axis_size("row")
    tri = w_final.shape[0]
    right_all = lax.all_gather(right, "row", axis=0, tiled=True)
    partial = pl.pallas_call(
        triangle_body,
        grid=(rows,),
        out_shape=jax.ShapeDtypeStruct((rows, own_i, own_i, tri), bf16),
        in_specs=[
            pl.BlockSpec((own_i, own_j, tri), lambda r: (0, 0, 0)),
            pl.BlockSpec((own_i, own_j, tri), lambda r: (r, 0, 0)),
        ],
        out_specs=pl.BlockSpec((1, own_i, own_i, tri), lambda r: (r, 0, 0, 0)),
        scratch_shapes=[
            pltpu.VMEM((own_i, own_j, tri), f32),
            pltpu.VMEM((own_i * own_j, tri), f32),
            pltpu.VMEM((own_j, own_i, tri), f32),
        ],
        compiler_params=limit(56),
        name="triangle",
    )(left, right_all)
    summed = lax.psum_scatter(partial, "col", scatter_dimension=0, tiled=True)
    return pl.pallas_call(
        finish_body,
        out_shape=jax.ShapeDtypeStruct((own_i, own_j, chans), bf16),
        in_specs=[VMEM] * 5,
        out_specs=VMEM,
        compiler_params=limit(56),
        name="finish",
    )(summed, psum, norm, w_gate, w_final)


def paired_plan(lefts, right, psum, norm, w_gate, w_final):
    own_i, own_j, chans = psum.shape
    tri = w_final.shape[0]
    cuts = len(lefts)
    cells = [(r, z) for r in range(4) for z in range(4)]

    def move(value, where, step):
        pairs = [(r * 4 + z, step(r, z)) for r, z in cells if where(r, z)]
        pairs = [(src, r * 4 + z) for src, (r, z) in pairs]
        return lax.ppermute(value, ("row", "col"), pairs)

    every = lambda r, z: True
    keeper = lambda r, z: r % 2 == z % 2
    other = lambda r, z: r % 2 != z % 2
    got = move(right, every, lambda r, z: (r ^ 2, z) if r % 2 == z % 2 else (r ^ 1, z ^ 1))
    mets = [move(left, every, lambda r, z: (r, z ^ 1)) for left in lefts]
    late = move(got, other, lambda r, z: (r ^ 2, z))
    p_own = move(right, keeper, lambda r, z: (r ^ 1, z))
    p_got = move(got, every, lambda r, z: (r ^ 1, z))
    p_late = move(late, other, lambda r, z: (r ^ 1, z))
    rights = (right, p_own, got, p_got, late, p_late)

    sums = []
    for left, met in zip(lefts, mets):
        n = left.shape[0]
        part = pl.pallas_call(
            send_body,
            out_shape=jax.ShapeDtypeStruct((n, own_j, tri), bf16),
            in_specs=[ANY] * 6 + [VMEM] * 2,
            out_specs=VMEM,
            scratch_shapes=[
                pltpu.VMEM((n, 2 * own_j, tri), f32),
                pltpu.VMEM((2 * own_j, own_i, tri), bf16),
                pltpu.SemaphoreType.DMA((2,)),
            ],
            compiler_params=limit(12),
            name="send_sums",
        )(*rights, left, met)
        sums.append(move(part, every, lambda r, z: (r, z ^ 2)))

    own, gate = pl.pallas_call(
        functools.partial(keep_body, cuts),
        out_shape=[jax.ShapeDtypeStruct((own_i, own_j, tri), f32),
                   jax.ShapeDtypeStruct((own_i, own_j, chans), f32)],
        in_specs=[ANY] * 6 + [VMEM] * (2 * cuts + 2),
        out_specs=[VMEM] * 2,
        scratch_shapes=[
            pltpu.VMEM((own_i, 2 * own_j, tri), f32),
            pltpu.VMEM((2 * own_j, own_i, tri), bf16),
            pltpu.SemaphoreType.DMA((2,)),
        ],
        compiler_params=limit(16),
        name="keep_sums",
    )(*rights, *lefts, *mets, norm, w_gate)
    return pl.pallas_call(
        functools.partial(join_body, cuts),
        out_shape=jax.ShapeDtypeStruct((own_i, own_j, chans), bf16),
        in_specs=[VMEM] * (cuts + 4),
        out_specs=VMEM,
        compiler_params=limit(12),
        name="join",
    )(*sums, own, psum, gate, w_final)


def shards(homolog, couple, ids, valid, bias, factors, average, w_in, w_gate, w_final):
    rows, cols = lax.axis_size("row"), lax.axis_size("col")
    own_seqs, residues, depth = homolog.shape
    own_i, own_j, chans = couple.shape
    width = factors.shape[1] // 2
    tri = w_final.shape[0]
    total = own_seqs * rows
    lanes = round_up(2 * own_seqs * width, 128)
    height = round_up(max(own_i, own_j), 16)
    paired = rows == 4 and cols == 4 and own_i == own_j and own_i % 8 == 0
    scale = 1 if paired else 8

    msgs = pl.pallas_call(
        functools.partial(align_body, own_i, own_j),
        out_shape=[jax.ShapeDtypeStruct((height, lanes), bf16)] * rows,
        in_specs=[VMEM] * 2,
        out_specs=[VMEM] * rows,
        scratch_shapes=[pltpu.VMEM((own_seqs * residues, 2 * width), f32)],
        compiler_params=limit(8, scale),
        name="align",
    )(homolog, factors.T)
    msgs = [msgs[0]] + [
        lax.ppermute(msg, "row", [(r, r ^ d) for r in range(rows)])
        for d, msg in enumerate(msgs) if d
    ]

    base, mask, wq = pl.pallas_call(
        prepare_body,
        out_shape=[jax.ShapeDtypeStruct((own_i, own_j, chans), f32),
                   jax.ShapeDtypeStruct((own_i, own_j, tri), bf16),
                   jax.ShapeDtypeStruct((width // 2, width, 2 * chans), bf16)],
        in_specs=[VMEM, SMEM, VMEM, VMEM, VMEM],
        out_specs=[VMEM] * 3,
        scratch_shapes=[
            pltpu.VMEM((width * width, chans), f32),
            pltpu.VMEM((own_j, chans), jnp.int32),
        ],
        compiler_params=limit(8, scale),
        name="prepare",
    )(couple, ids, valid, bias, average)

    extents = (own_j, own_i) if paired else (own_i, own_j)
    psum, norm, right = pl.pallas_call(
        functools.partial(pair_body, own_seqs, width, paired),
        out_shape=[jax.ShapeDtypeStruct((own_i, own_j, chans), bf16),
                   jax.ShapeDtypeStruct((own_i * own_j, chans), bf16),
                   jax.ShapeDtypeStruct(extents + (tri,), bf16)],
        in_specs=[VMEM] * (rows + 4),
        out_specs=[VMEM] * 3,
        scratch_shapes=[
            pltpu.VMEM((own_i * total, 128), f32),
            pltpu.VMEM((own_i, width * total, chans), bf16),
            pltpu.VMEM((own_i * own_j, tri), f32),
        ],
        compiler_params=limit(16, scale),
        name="pair",
    )(*msgs, base, mask, wq, w_in)

    cuts = [16, own_i - 16] if paired else [own_i]
    lefts = pl.pallas_call(
        left_body,
        out_shape=[jax.ShapeDtypeStruct((n, own_j, tri), bf16) for n in cuts],
        in_specs=[VMEM] * 3,
        out_specs=[VMEM] * len(cuts),
        compiler_params=limit(8, scale),
        name="left",
    )(norm, mask, w_in)
    if paired:
        return paired_plan(lefts, right, psum, norm, w_gate, w_final)
    return gathered_plan(lefts[0], right, psum, norm, w_gate, w_final)


def solution(mesh):
    placed = (
        P(("grp", "row"), None, None),
        P(("grp", "row"), "col", None),
        P("grp"),
        P(("grp", "row"), "col"),
        P(),
        P(),
        P(),
        P(),
        P(),
        P(),
    )
    return jax.shard_map(
        shards,
        mesh=mesh,
        in_specs=placed,
        out_specs=P(("grp", "row"), "col", None),
        check_vma=False,
    )
```

```python
import functools

import jax
import jax.numpy as jnp
from jax import lax
from jax.experimental import pallas as pl
from jax.experimental.pallas import tpu as pltpu
from jax.sharding import PartitionSpec as P

eps = 1e-05
f32 = jnp.float32
bf16 = jnp.bfloat16
VMEM = pl.BlockSpec(memory_space=pltpu.VMEM)
SMEM = pl.BlockSpec(memory_space=pltpu.SMEM)
HBM = pl.BlockSpec(memory_space=pltpu.HBM)


def limit(mib, scale=1):
    return pltpu.CompilerParams(vmem_limit_bytes=min(56, mib * scale) * 1024 * 1024)


def round_up(n, m):
    return (n + m - 1) // m * m


def cost(us):
    return pl.CostEstimate(flops=0, bytes_accessed=int(us * 3.69e6), transcendentals=0)


def hold(x):
    return pltpu.with_memory_space_constraint(x, pltpu.HBM)


def fetch(pairs, sem):
    copies = [pltpu.make_async_copy(src, dst, sem.at[n]) for n, (src, dst) in enumerate(pairs)]
    for copy in copies:
        copy.start()
    return copies


def standardize(values):
    centre = values - jnp.mean(values, axis=-1, keepdims=True)
    spread = jnp.mean(centre * centre, axis=-1, keepdims=True)
    return centre * lax.rsqrt(spread + eps)


def sigmoid(v):
    return 0.5 * jnp.tanh(0.5 * v) + 0.5


def align_body(own_i, own_j, count, x_hbm, w_hbm, *refs):
    outs, (x_ref, w_ref, y_ref, sem) = refs[:count], refs[count:]
    copies = fetch([(x_hbm, x_ref), (w_hbm, w_ref)], sem)
    seqs, residues, depth = x_ref.shape
    width = w_ref.shape[0] // 2
    height, lanes = outs[0].shape
    me = lax.axis_index("row")
    z = lax.axis_index("col")
    copies[0].wait()
    x = x_ref[...].astype(f32).reshape(seqs * residues, depth)
    normed = standardize(x).astype(bf16)
    copies[1].wait()
    y_ref[...] = lax.dot_general(
        normed, w_ref[...], (((1,), (1,)), ((), ())), preferred_element_type=f32
    )
    start = pl.multiple_of(z * own_j, 8)
    extent = max(own_i, own_j)

    def tall(v):
        gap = extent - v.shape[0]
        return jnp.concatenate([v, jnp.zeros((gap, v.shape[1]), f32)], axis=0) if gap else v

    right = [tall(y_ref[pl.ds(s * residues + start, own_j), width:]) for s in range(seqs)]
    gap = lanes - 2 * seqs * width
    right += [jnp.zeros((extent, gap), f32)] if gap else []
    for d, out in enumerate(outs):
        first = pl.multiple_of((me ^ d) * own_i, 8)
        left = [tall(y_ref[pl.ds(s * residues + first, own_i), :width]) for s in range(seqs)]
        out[pl.ds(0, extent), :] = jnp.concatenate(left + right, axis=1).astype(bf16)


def prepare_body(seqs, couple_hbm, ids_ref, valid_hbm, bias_hbm, avg_hbm, base_ref, mask_ref, wq_ref, pick_ref,
                 couple_ref, valid_ref, bias_ref, avg_ref, wf_ref, idc_ref, sem):
    sources = (avg_hbm, valid_hbm, bias_hbm, couple_hbm)
    copies = fetch(list(zip(sources, (avg_ref, valid_ref, bias_ref, couple_ref))), sem)
    own_i, own_j, chans = couple_ref.shape
    pairs, width, _ = wq_ref.shape
    blocks, lanes, _ = pick_ref.shape
    total = blocks * seqs
    x0 = lax.axis_index("row") * own_i
    z0 = lax.axis_index("col") * own_j

    row = lax.broadcasted_iota(jnp.int32, pick_ref.shape[1:], 0)
    col = lax.broadcasted_iota(jnp.int32, pick_ref.shape[1:], 1)
    unit = row - seqs * width
    place = lax.rem(unit, width) * total + lax.div(unit, width)
    place = jnp.where((unit >= 0) & (unit < seqs * width), col - place, -1)

    def pick(r, carry):
        pick_ref[r] = jnp.where(place == r * seqs, 1.0, 0.0).astype(bf16)
        return carry

    lax.fori_loop(0, blocks, pick, 0)
    for j in range(own_j):
        idc_ref[pl.ds(j, 1), :] = jnp.full((1, chans), ids_ref[z0 + j], jnp.int32)
    copies[0].wait()
    wf_ref[...] = avg_ref[...].astype(f32)
    for h in range(pairs):
        both = [wf_ref[pl.ds(2 * h + d, width, stride=width), :] for d in range(2)]
        wq_ref[h] = jnp.concatenate(both, axis=1).astype(bf16)
    for copy in copies[1:]:
        copy.wait()
    idc = idc_ref[...]
    valid_t = valid_ref[...].astype(f32).T
    lane = lax.broadcasted_iota(jnp.int32, valid_t.shape, 1)
    same_bias = bias_ref[0:1, :]
    cross_bias = bias_ref[1:2, :]

    def rows(i, carry):
        bias = jnp.where(idc == ids_ref[x0 + i], same_bias, cross_bias)
        base_ref[i] = couple_ref[i].astype(f32) + bias
        column = jnp.sum(jnp.where(lane == i, valid_t, 0.0), axis=1, keepdims=True)
        mask_ref[i] = jnp.broadcast_to(column, (own_j, mask_ref.shape[2])).astype(bf16)
        return carry

    lax.fori_loop(0, own_i, rows, 0, unroll=8)


def pair_body(seqs, width, blocks, turned, *refs):
    msgs = refs[:blocks]
    base_ref, mask_ref, wq_ref, pick_ref, win_ref = refs[blocks : blocks + 5]
    psum_ref, norm_ref, right_ref = refs[blocks + 5 : blocks + 8]
    xl_ref, t_ref, flat_ref = refs[blocks + 8 :]
    own_i, own_j, chans = base_ref.shape
    height, lanes = msgs[0].shape
    total = seqs * blocks
    tri = win_ref.shape[1] // 4
    half = own_i // 2

    for r in range(blocks):
        m = msgs[r][pl.ds(0, own_i), :].astype(f32)
        for s in range(seqs):
            moved = m if s == 0 else pltpu.roll(m, lanes - s * width, 1)
            xl_ref[pl.ds(r * seqs + s, own_i, stride=total), :] = moved[:, :128]
    lhs = xl_ref[:, :width].astype(bf16)

    rmat = jnp.zeros((own_j, width * total), f32)
    for r in range(blocks):
        rmat += jnp.dot(msgs[r][pl.ds(0, own_j), :], pick_ref[r], preferred_element_type=f32)
    rmat = rmat.astype(bf16)

    def expand(h, carry):
        out = jnp.dot(lhs, wq_ref[h], preferred_element_type=f32)
        parts = [out[:, d * chans : (d + 1) * chans].reshape(own_i, total, chans) for d in range(2)]
        block = jnp.concatenate(parts, axis=1).astype(bf16)
        where = pl.ds(pl.multiple_of(h * 2 * total, 16), 2 * total)
        t_ref[:, where, :chans] = block[:half]
        t_ref[:, where, chans:] = block[half:]
        return carry

    lax.fori_loop(0, width // 2, expand, 0, unroll=4)

    step = 4 if half % 4 == 0 else 1

    def rows(b, carry):
        normed = [[], []]
        for g in range(step):
            i = b * step + g
            both = jnp.dot(rmat, t_ref[i], preferred_element_type=f32) * (1.0 / total)
            for side in range(2):
                at = i + side * half
                psum = (base_ref[at] + both[:, side * chans : (side + 1) * chans]).astype(bf16)
                psum_ref[at] = psum
                normed[side].append(standardize(psum.astype(f32)))
        flat = jnp.concatenate(normed[0] + normed[1], axis=0).astype(bf16)
        proj = jnp.dot(flat, win_ref[:, 2 * tri :], preferred_element_type=f32)
        count = step * own_j
        for side in range(2):
            cut = slice(side * count, (side + 1) * count)
            i0 = b * step + side * half
            norm_ref[pl.ds(pl.multiple_of(i0 * own_j, 16), count), :] = flat[cut]
            mask = mask_ref[pl.ds(i0, step)].astype(f32).reshape(count, tri)
            right = mask * sigmoid(proj[cut, :tri]) * proj[cut, tri:]
            if turned:
                flat_ref[pl.ds(pl.multiple_of(i0 * own_j, 8), count), :] = right
            else:
                right_ref[pl.ds(i0, step)] = right.reshape(step, own_j, tri).astype(bf16)
        return carry

    lax.fori_loop(0, half // step, rows, 0, unroll=True)

    def turn(k, carry):
        right_ref[k] = flat_ref[pl.ds(k, own_i, stride=own_j), :].astype(bf16)
        return carry

    if turned:
        lax.fori_loop(0, own_j, turn, 0, unroll=8)


def left_body(norm_ref, mask_ref, win_ref, *outs):
    own_i, own_j, tri = mask_ref.shape
    group = 8 if own_i % 8 == 0 else 1
    at = 0
    for out in outs:
        first = at

        def rows(b, carry):
            i0 = first + b * group
            flat = norm_ref[pl.ds(pl.multiple_of(i0 * own_j, 16), group * own_j), :]
            mask = mask_ref[pl.ds(i0, group)].astype(f32).reshape(group * own_j, tri)
            proj = jnp.dot(flat, win_ref[:, : 2 * tri], preferred_element_type=f32)
            left = mask * sigmoid(proj[:, :tri]) * proj[:, tri:]
            out[pl.ds(b * group, group)] = left.reshape(group, own_j, tri).astype(bf16)
            return carry

        lax.fori_loop(0, out.shape[0] // group, rows, 0, unroll=True)
        at += out.shape[0]


def contract(lf_ref, halves, i0, group):
    step = 8
    acc = (jnp.zeros(halves[0].shape[1:], f32),) * group
    for h, r_ref in enumerate(halves):
        depth = r_ref.shape[0]

        def add(kb, acc):
            k0 = kb * step
            acc = list(acc)
            for d in range(step):
                right = r_ref[k0 + d].astype(f32)
                for t in range(group):
                    acc[t] = acc[t] + lf_ref[i0 + t, pl.ds(h * depth + k0 + d, 1), :] * right
            return tuple(acc)

        acc = lax.fori_loop(0, depth // step, add, acc)
    return acc


def with_right(own_pair, refs, use):
    own, p_own, got, p_got, late, p_late = refs
    r, z = lax.axis_index("row"), lax.axis_index("col")
    keeper = (r % 2) == (z % 2)
    near = ((r // 2) == (z // 2)) == own_pair
    table = [
        (near & keeper, own, p_got),
        (near & ~keeper, p_own, got),
        (~near & keeper, got, p_late),
        (~near & ~keeper, p_got, late),
    ]
    for cond, a, b in table:
        pl.when(cond)(functools.partial(use, (a, b)))


def send_body(first, *refs):
    rights, (l_ref, m_ref, o_ref, lf_ref) = refs[:6], refs[6:]
    count, depth = o_ref.shape[0], l_ref.shape[1]
    group = 8
    lf_ref[:, pl.ds(0, depth), :] = l_ref[pl.ds(first, count)].astype(f32)
    lf_ref[:, pl.ds(depth, depth), :] = m_ref[pl.ds(first, count)].astype(f32)

    def use(halves):
        def rows(b, carry):
            acc = contract(lf_ref, halves, b * group, group)
            for t in range(group):
                o_ref[b * group + t] = acc[t].astype(bf16)
            return carry

        lax.fori_loop(0, count // group, rows, 0)

    with_right(False, rights, use)


def keep_body(cuts, *refs):
    rights, refs = refs[:6], refs[6:]
    lefts, mets = refs[:cuts], refs[cuts : 2 * cuts]
    norm_ref, wgate_ref, o_ref, gate_ref, lf_ref = refs[2 * cuts :]
    own_i, depth, chans = o_ref.shape
    at = 0
    for l_ref, m_ref in zip(lefts, mets):
        n = l_ref.shape[0]
        lf_ref[pl.ds(at, n), pl.ds(0, depth), :] = l_ref[...].astype(f32)
        lf_ref[pl.ds(at, n), pl.ds(depth, depth), :] = m_ref[...].astype(f32)
        at += n
    group = 8

    def gates(b, carry):
        flat = norm_ref[pl.ds(pl.multiple_of(b * group * depth, 16), group * depth), :]
        gate = sigmoid(jnp.dot(flat, wgate_ref[...], preferred_element_type=f32))
        gate_ref[pl.ds(b * group, group)] = gate.reshape(group, depth, -1)
        return carry

    lax.fori_loop(0, own_i // group, gates, 0, unroll=True)

    def use(halves):
        def rows(b, carry):
            acc = contract(lf_ref, halves, b * group, group)
            for t in range(group):
                o_ref[b * group + t] = acc[t]
            return carry

        lax.fori_loop(0, own_i // group, rows, 0)

    with_right(True, rights, use)


def join_body(cuts, *refs):
    sums, (own_ref, psum_ref, gate_ref, w_ref, out_ref) = refs[:cuts], refs[cuts:]
    own_i, extent, chans = out_ref.shape
    group = 8
    at = 0
    for part in sums:
        first = at

        def rows(b, carry):
            rows_ = pl.ds(first + b * group, group)
            mixed = own_ref[rows_] + part[pl.ds(b * group, group)].astype(f32)
            normed = standardize(mixed).reshape(group * extent, -1).astype(bf16)
            update = jnp.dot(normed, w_ref[...], preferred_element_type=f32).reshape(group, extent, -1)
            out_ref[rows_] = (psum_ref[rows_].astype(f32) + gate_ref[rows_] * update).astype(bf16)
            return carry

        lax.fori_loop(0, part.shape[0] // group, rows, 0)
        at += part.shape[0]


def triangle_body(l_ref, r_ref, o_ref, lf_ref, flat_ref, rk_ref):
    own_i, depth, chans = l_ref.shape
    extent = r_ref.shape[0]
    group = 8 if own_i % 8 == 0 else 1

    @pl.when(pl.program_id(0) == 0)
    def _():
        lf_ref[...] = l_ref[...].astype(f32)

    def widen(j, carry):
        flat_ref[pl.ds(pl.multiple_of(j * depth, 8), depth), :] = r_ref[j].astype(f32)
        return carry

    lax.fori_loop(0, extent, widen, 0)

    def turn(k, carry):
        rk_ref[k] = flat_ref[pl.ds(k, extent, stride=depth), :]
        return carry

    lax.fori_loop(0, depth, turn, 0)

    def rows(b, carry):
        i0 = b * group
        acc = contract(lf_ref, [rk_ref], i0, group)
        for t in range(group):
            o_ref[0, i0 + t] = acc[t].astype(bf16)
        return carry

    lax.fori_loop(0, own_i // group, rows, 0)


def finish_body(sum_ref, psum_ref, norm_ref, wgate_ref, w_ref, out_ref):
    parts, own_i, extent, chans = sum_ref.shape
    own_j = psum_ref.shape[1]

    def row(i, carry):
        flat = norm_ref[pl.ds(pl.multiple_of(i * own_j, 16), own_j), :]
        gate = sigmoid(jnp.dot(flat, wgate_ref[...], preferred_element_type=f32))
        normed = [standardize(sum_ref[part, i].astype(f32)) for part in range(parts)]
        normed = jnp.concatenate(normed, axis=0).astype(bf16)
        update = jnp.dot(normed, w_ref[...], preferred_element_type=f32)
        out_ref[i] = (psum_ref[i].astype(f32) + gate * update).astype(bf16)
        return carry

    lax.fori_loop(0, own_i, row, 0)


def gathered_plan(left, right, psum, norm, w_gate, w_final):
    own_i, own_j, chans = psum.shape
    rows = lax.axis_size("row")
    tri = w_final.shape[0]
    right_all = lax.all_gather(right, "row", axis=0, tiled=True)
    partial = pl.pallas_call(
        triangle_body,
        grid=(rows,),
        out_shape=jax.ShapeDtypeStruct((rows, own_i, own_i, tri), bf16),
        in_specs=[
            pl.BlockSpec((own_i, own_j, tri), lambda r: (0, 0, 0)),
            pl.BlockSpec((own_i, own_j, tri), lambda r: (r, 0, 0)),
        ],
        out_specs=pl.BlockSpec((1, own_i, own_i, tri), lambda r: (r, 0, 0, 0)),
        scratch_shapes=[
            pltpu.VMEM((own_i, own_j, tri), f32),
            pltpu.VMEM((own_i * own_j, tri), f32),
            pltpu.VMEM((own_j, own_i, tri), f32),
        ],
        compiler_params=limit(56),
        name="triangle",
    )(left, right_all)
    summed = lax.psum_scatter(partial, "col", scatter_dimension=0, tiled=True)
    return pl.pallas_call(
        finish_body,
        out_shape=jax.ShapeDtypeStruct((own_i, own_j, chans), bf16),
        in_specs=[VMEM] * 5,
        out_specs=VMEM,
        compiler_params=limit(56),
        name="finish",
    )(summed, psum, norm, w_gate, w_final)


def paired_plan(lefts, right, psum, norm, w_gate, w_final):
    own_i, own_j, chans = psum.shape
    tri = w_final.shape[0]
    cuts = len(lefts)
    cells = [(r, z) for r in range(4) for z in range(4)]

    def move(value, where, step):
        pairs = [(r * 4 + z, step(r, z)) for r, z in cells if where(r, z)]
        pairs = [(src, r * 4 + z) for src, (r, z) in pairs]
        return lax.ppermute(value, ("row", "col"), pairs)

    every = lambda r, z: True
    keeper = lambda r, z: r % 2 == z % 2
    other = lambda r, z: r % 2 != z % 2
    got = move(right, every, lambda r, z: (r ^ 2, z) if r % 2 == z % 2 else (r ^ 1, z ^ 1))
    p_own = move(right, keeper, lambda r, z: (r ^ 1, z))
    mets = [move(left, every, lambda r, z: (r, z ^ 1)) for left in lefts]
    got, *_ = lax.optimization_barrier((got, *lefts))
    late = move(got, other, lambda r, z: (r ^ 2, z))
    p_got = move(got, every, lambda r, z: (r ^ 1, z))
    late, *mets = lax.optimization_barrier((late, *mets))
    p_late = move(late, other, lambda r, z: (r ^ 1, z))
    rights = (right, p_own, got, p_got, late, p_late)

    sums = []
    for at, first, n in ((0, 0, 8), (0, 8, 16), (0, 24, own_i - 24)):
        part = pl.pallas_call(
            functools.partial(send_body, first),
            out_shape=jax.ShapeDtypeStruct((n, own_j, tri), bf16),
            in_specs=[VMEM] * 8,
            out_specs=VMEM,
            scratch_shapes=[pltpu.VMEM((n, 2 * own_j, tri), f32)],
            compiler_params=limit(8),
            cost_estimate=cost(0.12 * n + 0.4),
            name="send_sums",
        )(*rights, lefts[at], mets[at])
        sums.append(move(part, every, lambda r, z: (r, z ^ 2)))

    own, gate = pl.pallas_call(
        functools.partial(keep_body, cuts),
        out_shape=[jax.ShapeDtypeStruct((own_i, own_j, tri), f32),
                   jax.ShapeDtypeStruct((own_i, own_j, chans), f32)],
        in_specs=[VMEM] * (6 + 2 * cuts + 2),
        out_specs=[VMEM] * 2,
        scratch_shapes=[pltpu.VMEM((own_i, 2 * own_j, tri), f32)],
        compiler_params=limit(12),
        cost_estimate=cost(6),
        name="keep_sums",
    )(*rights, *lefts, *mets, norm, w_gate)
    return pl.pallas_call(
        functools.partial(join_body, len(sums)),
        out_shape=jax.ShapeDtypeStruct((own_i, own_j, chans), bf16),
        in_specs=[VMEM] * (len(sums) + 4),
        out_specs=VMEM,
        compiler_params=limit(12),
        cost_estimate=cost(2.4),
        name="join",
    )(*sums, own, psum, gate, w_final)


def shards(homolog, couple, ids, valid, bias, factors, average, w_in, w_gate, w_final):
    rows, cols = lax.axis_size("row"), lax.axis_size("col")
    own_seqs, residues, depth = homolog.shape
    own_i, own_j, chans = couple.shape
    width = factors.shape[1] // 2
    tri = w_final.shape[0]
    total = own_seqs * rows
    lanes = round_up(2 * own_seqs * width, 128)
    height = round_up(max(own_i, own_j), 16)
    paired = rows == 4 and cols == 4 and own_i == own_j and own_i % 8 == 0 and own_i > 24
    scale = 1 if paired else 8

    msgs = pl.pallas_call(
        functools.partial(align_body, own_i, own_j, rows),
        out_shape=[jax.ShapeDtypeStruct((height, lanes), bf16)] * rows,
        in_specs=[HBM] * 2,
        out_specs=[VMEM] * rows,
        scratch_shapes=[
            pltpu.VMEM(homolog.shape, bf16),
            pltpu.VMEM((2 * width, depth), bf16),
            pltpu.VMEM((own_seqs * residues, 2 * width), f32),
            pltpu.SemaphoreType.DMA((2,)),
        ],
        compiler_params=limit(8, scale),
        cost_estimate=cost(1.5),
        name="align",
    )(hold(homolog), hold(factors.T))
    msgs = [msgs[0]] + [
        lax.ppermute(msg, "row", [(r, r ^ d) for r in range(rows)])
        for d, msg in enumerate(msgs) if d
    ]

    base, mask, wq, pick = pl.pallas_call(
        functools.partial(prepare_body, own_seqs),
        out_shape=[jax.ShapeDtypeStruct((own_i, own_j, chans), f32),
                   jax.ShapeDtypeStruct((own_i, own_j, tri), bf16),
                   jax.ShapeDtypeStruct((width // 2, width, 2 * chans), bf16),
                   jax.ShapeDtypeStruct((rows, lanes, width * total), bf16)],
        in_specs=[HBM, SMEM, HBM, HBM, HBM],
        out_specs=[VMEM] * 4,
        scratch_shapes=[
            pltpu.VMEM(couple.shape, bf16),
            pltpu.VMEM(valid.shape, jnp.int32),
            pltpu.VMEM(bias.shape, f32),
            pltpu.VMEM(average.shape, bf16),
            pltpu.VMEM(average.shape, f32),
            pltpu.VMEM((own_j, chans), jnp.int32),
            pltpu.SemaphoreType.DMA((4,)),
        ],
        compiler_params=limit(8, scale),
        cost_estimate=cost(2.5),
        name="prepare",
    )(hold(couple), ids, hold(valid), hold(bias), hold(average))

    extents = (own_j, own_i) if paired else (own_i, own_j)
    psum, norm, right = pl.pallas_call(
        functools.partial(pair_body, own_seqs, width, rows, paired),
        out_shape=[jax.ShapeDtypeStruct((own_i, own_j, chans), bf16),
                   jax.ShapeDtypeStruct((own_i * own_j, chans), bf16),
                   jax.ShapeDtypeStruct(extents + (tri,), bf16)],
        in_specs=[VMEM] * (rows + 5),
        out_specs=[VMEM] * 3,
        scratch_shapes=[
            pltpu.VMEM((own_i * total, 128), f32),
            pltpu.VMEM((own_i // 2, width * total, 2 * chans), bf16),
            pltpu.VMEM((own_i * own_j, tri), f32),
        ],
        compiler_params=limit(16, scale),
        cost_estimate=cost(4.5),
        name="pair",
    )(*msgs, base, mask, wq, pick, w_in)

    cuts = [own_i]
    lefts = pl.pallas_call(
        left_body,
        out_shape=[jax.ShapeDtypeStruct((n, own_j, tri), bf16) for n in cuts],
        in_specs=[VMEM] * 3,
        out_specs=[VMEM] * len(cuts),
        compiler_params=limit(8, scale),
        cost_estimate=cost(1),
        name="left",
    )(norm, mask, w_in)
    if paired:
        return paired_plan(lefts, right, psum, norm, w_gate, w_final)
    return gathered_plan(lefts[0], right, psum, norm, w_gate, w_final)


def solution(mesh):
    placed = (
        P(("grp", "row"), None, None),
        P(("grp", "row"), "col", None),
        P("grp"),
        P(("grp", "row"), "col"),
        P(),
        P(),
        P(),
        P(),
        P(),
        P(),
    )
    return jax.shard_map(
        shards,
        mesh=mesh,
        in_specs=placed,
        out_specs=P(("grp", "row"), "col", None),
        check_vma=False,
    )
```

```python
import functools

import jax
import jax.numpy as jnp
from jax import lax
from jax.experimental import pallas as pl
from jax.experimental.pallas import tpu as pltpu
from jax.sharding import PartitionSpec as P

eps = 1e-05
f32 = jnp.float32
bf16 = jnp.bfloat16
VMEM = pl.BlockSpec(memory_space=pltpu.VMEM)
SMEM = pl.BlockSpec(memory_space=pltpu.SMEM)
HBM = pl.BlockSpec(memory_space=pltpu.HBM)


def limit(mib, scale=1):
    return pltpu.CompilerParams(vmem_limit_bytes=min(56, mib * scale) * 1024 * 1024)


def round_up(n, m):
    return (n + m - 1) // m * m


def cost(us):
    return pl.CostEstimate(flops=0, bytes_accessed=int(us * 3.69e6), transcendentals=0)


def hold(x):
    return pltpu.with_memory_space_constraint(x, pltpu.HBM)


def fetch(pairs, sem):
    copies = [pltpu.make_async_copy(src, dst, sem.at[n]) for n, (src, dst) in enumerate(pairs)]
    for copy in copies:
        copy.start()
    return copies


def standardize(values):
    centre = values - jnp.mean(values, axis=-1, keepdims=True)
    spread = jnp.mean(centre * centre, axis=-1, keepdims=True)
    return centre * lax.rsqrt(spread + eps)


def sigmoid(v):
    return 0.5 * jnp.tanh(0.5 * v) + 0.5


def align_body(own_i, own_j, count, x_hbm, w_hbm, *refs):
    outs, (x_ref, w_ref, y_ref, sem) = refs[:count], refs[count:]
    copies = fetch([(x_hbm, x_ref), (w_hbm, w_ref)], sem)
    seqs, residues, depth = x_ref.shape
    width = w_ref.shape[0] // 2
    height, lanes = outs[0].shape
    me = lax.axis_index("row")
    z = lax.axis_index("col")
    copies[0].wait()
    x = x_ref[...].astype(f32).reshape(seqs * residues, depth)
    normed = standardize(x).astype(bf16)
    copies[1].wait()
    y_ref[...] = lax.dot_general(
        normed, w_ref[...], (((1,), (1,)), ((), ())), preferred_element_type=f32
    )
    start = pl.multiple_of(z * own_j, 8)
    extent = max(own_i, own_j)

    def tall(v):
        gap = extent - v.shape[0]
        return jnp.concatenate([v, jnp.zeros((gap, v.shape[1]), f32)], axis=0) if gap else v

    right = [tall(y_ref[pl.ds(s * residues + start, own_j), width:]) for s in range(seqs)]
    gap = lanes - 2 * seqs * width
    right += [jnp.zeros((extent, gap), f32)] if gap else []
    for d, out in enumerate(outs):
        first = pl.multiple_of((me ^ d) * own_i, 8)
        left = [tall(y_ref[pl.ds(s * residues + first, own_i), :width]) for s in range(seqs)]
        out[pl.ds(0, extent), :] = jnp.concatenate(left + right, axis=1).astype(bf16)


def prepare_body(seqs, couple_hbm, ids_ref, valid_hbm, bias_hbm, avg_hbm, base_ref, mask_ref, wq_ref, pick_ref,
                 couple_ref, valid_ref, bias_ref, avg_ref, wf_ref, idc_ref, sem):
    sources = (avg_hbm, valid_hbm, bias_hbm, couple_hbm)
    copies = fetch(list(zip(sources, (avg_ref, valid_ref, bias_ref, couple_ref))), sem)
    own_i, own_j, chans = couple_ref.shape
    pairs, width, _ = wq_ref.shape
    blocks, lanes, _ = pick_ref.shape
    total = blocks * seqs
    x0 = lax.axis_index("row") * own_i
    z0 = lax.axis_index("col") * own_j

    row = lax.broadcasted_iota(jnp.int32, pick_ref.shape[1:], 0)
    col = lax.broadcasted_iota(jnp.int32, pick_ref.shape[1:], 1)
    unit = row - seqs * width
    place = lax.rem(unit, width) * total + lax.div(unit, width)
    place = jnp.where((unit >= 0) & (unit < seqs * width), col - place, -1)

    def pick(r, carry):
        pick_ref[r] = jnp.where(place == r * seqs, 1.0, 0.0).astype(bf16)
        return carry

    lax.fori_loop(0, blocks, pick, 0)
    for j in range(own_j):
        idc_ref[pl.ds(j, 1), :] = jnp.full((1, chans), ids_ref[z0 + j], jnp.int32)
    copies[0].wait()
    wf_ref[...] = avg_ref[...].astype(f32)
    for h in range(pairs):
        both = [wf_ref[pl.ds(2 * h + d, width, stride=width), :] for d in range(2)]
        wq_ref[h] = jnp.concatenate(both, axis=1).astype(bf16)
    for copy in copies[1:]:
        copy.wait()
    idc = idc_ref[...]
    valid_t = valid_ref[...].astype(f32).T
    lane = lax.broadcasted_iota(jnp.int32, valid_t.shape, 1)
    same_bias = bias_ref[0:1, :]
    cross_bias = bias_ref[1:2, :]

    def rows(i, carry):
        bias = jnp.where(idc == ids_ref[x0 + i], same_bias, cross_bias)
        base_ref[i] = couple_ref[i].astype(f32) + bias
        column = jnp.sum(jnp.where(lane == i, valid_t, 0.0), axis=1, keepdims=True)
        mask_ref[i] = jnp.broadcast_to(column, (own_j, mask_ref.shape[2])).astype(bf16)
        return carry

    lax.fori_loop(0, own_i, rows, 0, unroll=8)


def pair_body(seqs, width, blocks, turned, *refs):
    msgs = refs[:blocks]
    base_ref, mask_ref, wq_ref, pick_ref, win_ref = refs[blocks : blocks + 5]
    psum_ref, norm_ref, right_ref = refs[blocks + 5 : blocks + 8]
    xl_ref, t_ref, flat_ref = refs[blocks + 8 :]
    own_i, own_j, chans = base_ref.shape
    height, lanes = msgs[0].shape
    total = seqs * blocks
    tri = win_ref.shape[1] // 4
    half = own_i // 2

    for r in range(blocks):
        m = msgs[r][pl.ds(0, own_i), :].astype(f32)
        for s in range(seqs):
            moved = m if s == 0 else pltpu.roll(m, lanes - s * width, 1)
            xl_ref[pl.ds(r * seqs + s, own_i, stride=total), :] = moved[:, :128]
    lhs = xl_ref[:, :width].astype(bf16)

    rmat = jnp.zeros((own_j, width * total), f32)
    for r in range(blocks):
        rmat += jnp.dot(msgs[r][pl.ds(0, own_j), :], pick_ref[r], preferred_element_type=f32)
    rmat = rmat.astype(bf16)

    def expand(h, carry):
        out = jnp.dot(lhs, wq_ref[h], preferred_element_type=f32)
        parts = [out[:, d * chans : (d + 1) * chans].reshape(own_i, total, chans) for d in range(2)]
        block = jnp.concatenate(parts, axis=1).astype(bf16)
        where = pl.ds(pl.multiple_of(h * 2 * total, 16), 2 * total)
        t_ref[:, where, :chans] = block[:half]
        t_ref[:, where, chans:] = block[half:]
        return carry

    lax.fori_loop(0, width // 2, expand, 0, unroll=4)

    step = 4 if half % 4 == 0 else 1

    def rows(b, carry):
        normed = [[], []]
        for g in range(step):
            i = b * step + g
            both = jnp.dot(rmat, t_ref[i], preferred_element_type=f32) * (1.0 / total)
            for side in range(2):
                at = i + side * half
                psum = (base_ref[at] + both[:, side * chans : (side + 1) * chans]).astype(bf16)
                psum_ref[at] = psum
                normed[side].append(standardize(psum.astype(f32)))
        flat = jnp.concatenate(normed[0] + normed[1], axis=0).astype(bf16)
        proj = jnp.dot(flat, win_ref[:, 2 * tri :], preferred_element_type=f32)
        count = step * own_j
        for side in range(2):
            cut = slice(side * count, (side + 1) * count)
            i0 = b * step + side * half
            norm_ref[pl.ds(pl.multiple_of(i0 * own_j, 16), count), :] = flat[cut]
            mask = mask_ref[pl.ds(i0, step)].astype(f32).reshape(count, tri)
            right = mask * sigmoid(proj[cut, :tri]) * proj[cut, tri:]
            if turned:
                flat_ref[pl.ds(pl.multiple_of(i0 * own_j, 8), count), :] = right
            else:
                right_ref[pl.ds(i0, step)] = right.reshape(step, own_j, tri).astype(bf16)
        return carry

    lax.fori_loop(0, half // step, rows, 0, unroll=True)

    def turn(k, carry):
        right_ref[k] = flat_ref[pl.ds(k, own_i, stride=own_j), :].astype(bf16)
        return carry

    if turned:
        lax.fori_loop(0, own_j, turn, 0, unroll=8)


def left_body(norm_ref, mask_ref, win_ref, *outs):
    own_i, own_j, tri = mask_ref.shape
    group = 8 if own_i % 8 == 0 else 1
    at = 0
    for out in outs:
        first = at

        def rows(b, carry):
            i0 = first + b * group
            flat = norm_ref[pl.ds(pl.multiple_of(i0 * own_j, 16), group * own_j), :]
            mask = mask_ref[pl.ds(i0, group)].astype(f32).reshape(group * own_j, tri)
            proj = jnp.dot(flat, win_ref[:, : 2 * tri], preferred_element_type=f32)
            left = mask * sigmoid(proj[:, :tri]) * proj[:, tri:]
            out[pl.ds(b * group, group)] = left.reshape(group, own_j, tri).astype(bf16)
            return carry

        lax.fori_loop(0, out.shape[0] // group, rows, 0, unroll=True)
        at += out.shape[0]


def contract(lf_ref, halves, i0, group):
    step = 8
    acc = (jnp.zeros(halves[0].shape[1:], f32),) * group
    for h, r_ref in enumerate(halves):
        depth = r_ref.shape[0]

        def add(kb, acc):
            k0 = kb * step
            acc = list(acc)
            for d in range(step):
                right = r_ref[k0 + d].astype(f32)
                for t in range(group):
                    acc[t] = acc[t] + lf_ref[i0 + t, pl.ds(h * depth + k0 + d, 1), :] * right
            return tuple(acc)

        acc = lax.fori_loop(0, depth // step, add, acc)
    return acc


def with_right(own_pair, refs, use):
    own, p_own, got, p_got, late, p_late = refs
    r, z = lax.axis_index("row"), lax.axis_index("col")
    keeper = (r % 2) == (z % 2)
    near = ((r // 2) == (z // 2)) == own_pair
    table = [
        (near & keeper, own, p_got),
        (near & ~keeper, p_own, got),
        (~near & keeper, got, p_late),
        (~near & ~keeper, p_got, late),
    ]
    for cond, a, b in table:
        pl.when(cond)(functools.partial(use, (a, b)))


def send_body(first, *refs):
    rights, (l_ref, m_ref, o_ref, lf_ref) = refs[:6], refs[6:]
    count, depth = o_ref.shape[0], l_ref.shape[1]
    group = 8
    lf_ref[:, pl.ds(0, depth), :] = l_ref[pl.ds(first, count)].astype(f32)
    lf_ref[:, pl.ds(depth, depth), :] = m_ref[pl.ds(first, count)].astype(f32)

    def use(halves):
        def rows(b, carry):
            acc = contract(lf_ref, halves, b * group, group)
            for t in range(group):
                o_ref[b * group + t] = acc[t].astype(bf16)
            return carry

        lax.fori_loop(0, count // group, rows, 0)

    with_right(False, rights, use)


def keep_body(cuts, *refs):
    rights, refs = refs[:6], refs[6:]
    lefts, mets = refs[:cuts], refs[cuts : 2 * cuts]
    norm_ref, wgate_ref, o_ref, gate_ref, lf_ref = refs[2 * cuts :]
    own_i, depth, chans = o_ref.shape
    at = 0
    for l_ref, m_ref in zip(lefts, mets):
        n = l_ref.shape[0]
        lf_ref[pl.ds(at, n), pl.ds(0, depth), :] = l_ref[...].astype(f32)
        lf_ref[pl.ds(at, n), pl.ds(depth, depth), :] = m_ref[...].astype(f32)
        at += n
    group = 8

    def gates(b, carry):
        flat = norm_ref[pl.ds(pl.multiple_of(b * group * depth, 16), group * depth), :]
        gate = sigmoid(jnp.dot(flat, wgate_ref[...], preferred_element_type=f32))
        gate_ref[pl.ds(b * group, group)] = gate.reshape(group, depth, -1)
        return carry

    lax.fori_loop(0, own_i // group, gates, 0, unroll=True)

    def use(halves):
        def rows(b, carry):
            acc = contract(lf_ref, halves, b * group, group)
            for t in range(group):
                o_ref[b * group + t] = acc[t]
            return carry

        lax.fori_loop(0, own_i // group, rows, 0)

    with_right(True, rights, use)


def join_body(first, sum_ref, own_ref, psum_ref, gate_ref, w_ref, *refs):
    out_hbm, done_ref, sem = refs[-3:]
    count, extent, chans = done_ref.shape
    group = 8

    def rows(b, carry):
        some = pl.ds(b * group, group)
        all_ = pl.ds(first + b * group, group)
        mixed = own_ref[all_] + sum_ref[some].astype(f32)
        normed = standardize(mixed).reshape(group * extent, -1).astype(bf16)
        update = jnp.dot(normed, w_ref[...], preferred_element_type=f32).reshape(group, extent, -1)
        done_ref[some] = (psum_ref[all_].astype(f32) + gate_ref[all_] * update).astype(bf16)
        return carry

    lax.fori_loop(0, count // group, rows, 0, unroll=True)
    copy = pltpu.make_async_copy(done_ref, out_hbm.at[pl.ds(first, count)], sem)
    copy.start()
    copy.wait()


def triangle_body(l_ref, r_ref, o_ref, lf_ref, flat_ref, rk_ref):
    own_i, depth, chans = l_ref.shape
    extent = r_ref.shape[0]
    group = 8 if own_i % 8 == 0 else 1

    @pl.when(pl.program_id(0) == 0)
    def _():
        lf_ref[...] = l_ref[...].astype(f32)

    def widen(j, carry):
        flat_ref[pl.ds(pl.multiple_of(j * depth, 8), depth), :] = r_ref[j].astype(f32)
        return carry

    lax.fori_loop(0, extent, widen, 0)

    def turn(k, carry):
        rk_ref[k] = flat_ref[pl.ds(k, extent, stride=depth), :]
        return carry

    lax.fori_loop(0, depth, turn, 0)

    def rows(b, carry):
        i0 = b * group
        acc = contract(lf_ref, [rk_ref], i0, group)
        for t in range(group):
            o_ref[0, i0 + t] = acc[t].astype(bf16)
        return carry

    lax.fori_loop(0, own_i // group, rows, 0)


def finish_body(sum_ref, psum_ref, norm_ref, wgate_ref, w_ref, out_ref):
    parts, own_i, extent, chans = sum_ref.shape
    own_j = psum_ref.shape[1]

    def row(i, carry):
        flat = norm_ref[pl.ds(pl.multiple_of(i * own_j, 16), own_j), :]
        gate = sigmoid(jnp.dot(flat, wgate_ref[...], preferred_element_type=f32))
        normed = [standardize(sum_ref[part, i].astype(f32)) for part in range(parts)]
        normed = jnp.concatenate(normed, axis=0).astype(bf16)
        update = jnp.dot(normed, w_ref[...], preferred_element_type=f32)
        out_ref[i] = (psum_ref[i].astype(f32) + gate * update).astype(bf16)
        return carry

    lax.fori_loop(0, own_i, row, 0)


def gathered_plan(left, right, psum, norm, w_gate, w_final):
    own_i, own_j, chans = psum.shape
    rows = lax.axis_size("row")
    tri = w_final.shape[0]
    right_all = lax.all_gather(right, "row", axis=0, tiled=True)
    partial = pl.pallas_call(
        triangle_body,
        grid=(rows,),
        out_shape=jax.ShapeDtypeStruct((rows, own_i, own_i, tri), bf16),
        in_specs=[
            pl.BlockSpec((own_i, own_j, tri), lambda r: (0, 0, 0)),
            pl.BlockSpec((own_i, own_j, tri), lambda r: (r, 0, 0)),
        ],
        out_specs=pl.BlockSpec((1, own_i, own_i, tri), lambda r: (r, 0, 0, 0)),
        scratch_shapes=[
            pltpu.VMEM((own_i, own_j, tri), f32),
            pltpu.VMEM((own_i * own_j, tri), f32),
            pltpu.VMEM((own_j, own_i, tri), f32),
        ],
        compiler_params=limit(56),
        name="triangle",
    )(left, right_all)
    summed = lax.psum_scatter(partial, "col", scatter_dimension=0, tiled=True)
    return pl.pallas_call(
        finish_body,
        out_shape=jax.ShapeDtypeStruct((own_i, own_j, chans), bf16),
        in_specs=[VMEM] * 5,
        out_specs=VMEM,
        compiler_params=limit(56),
        name="finish",
    )(summed, psum, norm, w_gate, w_final)


def paired_plan(lefts, right, psum, norm, w_gate, w_final):
    own_i, own_j, chans = psum.shape
    tri = w_final.shape[0]
    cuts = len(lefts)
    cells = [(r, z) for r in range(4) for z in range(4)]

    def move(value, where, step):
        pairs = [(r * 4 + z, step(r, z)) for r, z in cells if where(r, z)]
        pairs = [(src, r * 4 + z) for src, (r, z) in pairs]
        return lax.ppermute(value, ("row", "col"), pairs)

    every = lambda r, z: True
    keeper = lambda r, z: r % 2 == z % 2
    got = move(right, every, lambda r, z: (r ^ 2, z) if keeper(r, z) else (r ^ 1, z ^ 1))
    p_own = move(right, every, lambda r, z: (r ^ 1, z))
    got, p_own, *lefts = lax.optimization_barrier((got, p_own, *lefts))
    late = move(got, every, lambda r, z: (r, z) if keeper(r, z) else (r ^ 2, z))
    p_got = move(got, every, lambda r, z: (r ^ 1, z))
    mets = [move(left, every, lambda r, z: (r, z ^ 1)) for left in lefts]
    late, mets[0] = lax.optimization_barrier((late, mets[0]))
    p_late = move(late, every, lambda r, z: (r ^ 1, z))
    rights = (right, p_own, got, p_got, late, p_late)

    sums = []
    chunks = ((0, 0, 0, 16), (1, 0, 24, own_i - 24), (0, 16, 16, 8))
    for at, first, _, n in chunks:
        part = pl.pallas_call(
            functools.partial(send_body, first),
            out_shape=jax.ShapeDtypeStruct((n, own_j, tri), bf16),
            in_specs=[VMEM] * 8,
            out_specs=VMEM,
            scratch_shapes=[pltpu.VMEM((n, 2 * own_j, tri), f32)],
            compiler_params=limit(8),
            cost_estimate=cost(0.12 * n + 0.4),
            name="send_sums",
        )(*rights, lefts[at], mets[at])
        sums.append(move(part, every, lambda r, z: (r, z ^ 2)))

    own, gate = pl.pallas_call(
        functools.partial(keep_body, cuts),
        out_shape=[jax.ShapeDtypeStruct((own_i, own_j, tri), f32),
                   jax.ShapeDtypeStruct((own_i, own_j, chans), f32)],
        in_specs=[VMEM] * (6 + 2 * cuts + 2),
        out_specs=[VMEM] * 2,
        scratch_shapes=[pltpu.VMEM((own_i, 2 * own_j, tri), f32)],
        compiler_params=limit(12),
        cost_estimate=cost(6),
        name="keep_sums",
    )(*rights, *lefts, *mets, norm, w_gate)
    out = []
    for part, (_, _, first, n) in zip(sums, chunks):
        out = [pl.pallas_call(
            functools.partial(join_body, first),
            out_shape=jax.ShapeDtypeStruct((own_i, own_j, chans), bf16),
            in_specs=[VMEM] * 5 + [HBM] * len(out),
            out_specs=HBM,
            scratch_shapes=[pltpu.VMEM((n, own_j, chans), bf16), pltpu.SemaphoreType.DMA],
            input_output_aliases={5: 0} if out else {},
            compiler_params=limit(8),
            cost_estimate=cost(0.06 * n),
            name="join",
        )(part, own, psum, gate, w_final, *out)]
    return out[0]


def shards(homolog, couple, ids, valid, bias, factors, average, w_in, w_gate, w_final):
    rows, cols = lax.axis_size("row"), lax.axis_size("col")
    own_seqs, residues, depth = homolog.shape
    own_i, own_j, chans = couple.shape
    width = factors.shape[1] // 2
    tri = w_final.shape[0]
    total = own_seqs * rows
    lanes = round_up(2 * own_seqs * width, 128)
    height = round_up(max(own_i, own_j), 16)
    paired = rows == 4 and cols == 4 and own_i == own_j and own_i % 8 == 0 and own_i > 24
    scale = 1 if paired else 8

    msgs = pl.pallas_call(
        functools.partial(align_body, own_i, own_j, rows),
        out_shape=[jax.ShapeDtypeStruct((height, lanes), bf16)] * rows,
        in_specs=[HBM] * 2,
        out_specs=[VMEM] * rows,
        scratch_shapes=[
            pltpu.VMEM(homolog.shape, bf16),
            pltpu.VMEM((2 * width, depth), bf16),
            pltpu.VMEM((own_seqs * residues, 2 * width), f32),
            pltpu.SemaphoreType.DMA((2,)),
        ],
        compiler_params=limit(8, scale),
        cost_estimate=cost(1.5),
        name="align",
    )(hold(homolog), hold(factors.T))
    msgs = [msgs[0]] + [
        lax.ppermute(msg, "row", [(r, r ^ d) for r in range(rows)])
        for d, msg in enumerate(msgs) if d
    ]

    base, mask, wq, pick = pl.pallas_call(
        functools.partial(prepare_body, own_seqs),
        out_shape=[jax.ShapeDtypeStruct((own_i, own_j, chans), f32),
                   jax.ShapeDtypeStruct((own_i, own_j, tri), bf16),
                   jax.ShapeDtypeStruct((width // 2, width, 2 * chans), bf16),
                   jax.ShapeDtypeStruct((rows, lanes, width * total), bf16)],
        in_specs=[HBM, SMEM, HBM, HBM, HBM],
        out_specs=[VMEM] * 4,
        scratch_shapes=[
            pltpu.VMEM(couple.shape, bf16),
            pltpu.VMEM(valid.shape, jnp.int32),
            pltpu.VMEM(bias.shape, f32),
            pltpu.VMEM(average.shape, bf16),
            pltpu.VMEM(average.shape, f32),
            pltpu.VMEM((own_j, chans), jnp.int32),
            pltpu.SemaphoreType.DMA((4,)),
        ],
        compiler_params=limit(8, scale),
        cost_estimate=cost(2.5),
        name="prepare",
    )(hold(couple), ids, hold(valid), hold(bias), hold(average))

    extents = (own_j, own_i) if paired else (own_i, own_j)
    psum, norm, right = pl.pallas_call(
        functools.partial(pair_body, own_seqs, width, rows, paired),
        out_shape=[jax.ShapeDtypeStruct((own_i, own_j, chans), bf16),
                   jax.ShapeDtypeStruct((own_i * own_j, chans), bf16),
                   jax.ShapeDtypeStruct(extents + (tri,), bf16)],
        in_specs=[VMEM] * (rows + 5),
        out_specs=[VMEM] * 3,
        scratch_shapes=[
            pltpu.VMEM((own_i * total, 128), f32),
            pltpu.VMEM((own_i // 2, width * total, 2 * chans), bf16),
            pltpu.VMEM((own_i * own_j, tri), f32),
        ],
        compiler_params=limit(16, scale),
        cost_estimate=cost(4.5),
        name="pair",
    )(*msgs, base, mask, wq, pick, w_in)

    cuts = [24, own_i - 24] if paired else [own_i]
    lefts = pl.pallas_call(
        left_body,
        out_shape=[jax.ShapeDtypeStruct((n, own_j, tri), bf16) for n in cuts],
        in_specs=[VMEM] * 3,
        out_specs=[VMEM] * len(cuts),
        compiler_params=limit(8, scale),
        cost_estimate=cost(1),
        name="left",
    )(norm, mask, w_in)
    if paired:
        return paired_plan(lefts, right, psum, norm, w_gate, w_final)
    return gathered_plan(lefts[0], right, psum, norm, w_gate, w_final)


def solution(mesh):
    placed = (
        P(("grp", "row"), None, None),
        P(("grp", "row"), "col", None),
        P("grp"),
        P(("grp", "row"), "col"),
        P(),
        P(),
        P(),
        P(),
        P(),
        P(),
    )
    return jax.shard_map(
        shards,
        mesh=mesh,
        in_specs=placed,
        out_specs=P(("grp", "row"), "col", None),
        check_vma=False,
    )
```

```python
import functools

import jax
import jax.numpy as jnp
from jax import lax
from jax.experimental import pallas as pl
from jax.experimental.pallas import tpu as pltpu
from jax.sharding import PartitionSpec as P

eps = 1e-05
f32 = jnp.float32
bf16 = jnp.bfloat16
VMEM = pl.BlockSpec(memory_space=pltpu.VMEM)
SMEM = pl.BlockSpec(memory_space=pltpu.SMEM)
HBM = pl.BlockSpec(memory_space=pltpu.HBM)


def limit(mib, scale=1):
    return pltpu.CompilerParams(vmem_limit_bytes=min(56, mib * scale) * 1024 * 1024)


def round_up(n, m):
    return (n + m - 1) // m * m


def cost(us):
    return pl.CostEstimate(flops=0, bytes_accessed=int(us * 3.69e6), transcendentals=0)


def hold(x):
    return pltpu.with_memory_space_constraint(x, pltpu.HBM)


def fetch(pairs, sem):
    copies = [pltpu.make_async_copy(src, dst, sem.at[n]) for n, (src, dst) in enumerate(pairs)]
    for copy in copies:
        copy.start()
    return copies


def standardize(values):
    centre = values - jnp.mean(values, axis=-1, keepdims=True)
    spread = jnp.mean(centre * centre, axis=-1, keepdims=True)
    return centre * lax.rsqrt(spread + eps)


def sigmoid(v):
    return 0.5 * jnp.tanh(0.5 * v) + 0.5


def align_body(own_i, own_j, count, x_hbm, w_hbm, *refs):
    outs, (x_ref, w_ref, y_ref, sem) = refs[:count], refs[count:]
    copies = fetch([(x_hbm, x_ref), (w_hbm, w_ref)], sem)
    seqs, residues, depth = x_ref.shape
    width = w_ref.shape[0] // 2
    height, lanes = outs[0].shape
    me = lax.axis_index("row")
    z = lax.axis_index("col")
    copies[0].wait()
    x = x_ref[...].astype(f32).reshape(seqs * residues, depth)
    normed = standardize(x).astype(bf16)
    copies[1].wait()
    y_ref[...] = lax.dot_general(
        normed, w_ref[...], (((1,), (1,)), ((), ())), preferred_element_type=f32
    )
    start = pl.multiple_of(z * own_j, 8)
    extent = max(own_i, own_j)

    def tall(v):
        gap = extent - v.shape[0]
        return jnp.concatenate([v, jnp.zeros((gap, v.shape[1]), f32)], axis=0) if gap else v

    right = [tall(y_ref[pl.ds(s * residues + start, own_j), width:]) for s in range(seqs)]
    gap = lanes - 2 * seqs * width
    right += [jnp.zeros((extent, gap), f32)] if gap else []
    for d, out in enumerate(outs):
        first = pl.multiple_of((me ^ d) * own_i, 8)
        left = [tall(y_ref[pl.ds(s * residues + first, own_i), :width]) for s in range(seqs)]
        out[pl.ds(0, extent), :] = jnp.concatenate(left + right, axis=1).astype(bf16)


def prepare_body(seqs, couple_hbm, ids_ref, valid_hbm, bias_hbm, avg_hbm, base_ref, mask_ref, wq_ref, pick_ref,
                 couple_ref, valid_ref, bias_ref, avg_ref, wf_ref, idc_ref, sem):
    sources = (avg_hbm, valid_hbm, bias_hbm, couple_hbm)
    copies = fetch(list(zip(sources, (avg_ref, valid_ref, bias_ref, couple_ref))), sem)
    own_i, own_j, chans = couple_ref.shape
    pairs, width, _ = wq_ref.shape
    blocks, lanes, _ = pick_ref.shape
    total = blocks * seqs
    x0 = lax.axis_index("row") * own_i
    z0 = lax.axis_index("col") * own_j

    row = lax.broadcasted_iota(jnp.int32, pick_ref.shape[1:], 0)
    col = lax.broadcasted_iota(jnp.int32, pick_ref.shape[1:], 1)
    unit = row - seqs * width
    place = lax.rem(unit, width) * total + lax.div(unit, width)
    place = jnp.where((unit >= 0) & (unit < seqs * width), col - place, -1)

    def pick(r, carry):
        pick_ref[r] = jnp.where(place == r * seqs, 1.0, 0.0).astype(bf16)
        return carry

    lax.fori_loop(0, blocks, pick, 0)
    for j in range(own_j):
        idc_ref[pl.ds(j, 1), :] = jnp.full((1, chans), ids_ref[z0 + j], jnp.int32)
    copies[0].wait()
    wf_ref[...] = avg_ref[...].astype(f32)
    for h in range(pairs):
        both = [wf_ref[pl.ds(2 * h + d, width, stride=width), :] for d in range(2)]
        wq_ref[h] = jnp.concatenate(both, axis=1).astype(bf16)
    for copy in copies[1:]:
        copy.wait()
    idc = idc_ref[...]
    valid_t = valid_ref[...].astype(f32).T
    lane = lax.broadcasted_iota(jnp.int32, valid_t.shape, 1)
    same_bias = bias_ref[0:1, :]
    cross_bias = bias_ref[1:2, :]

    def rows(i, carry):
        bias = jnp.where(idc == ids_ref[x0 + i], same_bias, cross_bias)
        base_ref[i] = couple_ref[i].astype(f32) + bias
        column = jnp.sum(jnp.where(lane == i, valid_t, 0.0), axis=1, keepdims=True)
        mask_ref[i] = jnp.broadcast_to(column, (own_j, mask_ref.shape[2])).astype(bf16)
        return carry

    lax.fori_loop(0, own_i, rows, 0, unroll=8)


def pair_body(seqs, width, blocks, turned, *refs):
    msgs = refs[:blocks]
    base_ref, mask_ref, wq_ref, pick_ref, win_ref = refs[blocks : blocks + 5]
    psum_ref, norm_ref, right_ref = refs[blocks + 5 : blocks + 8]
    xl_ref, t_ref, flat_ref = refs[blocks + 8 :]
    own_i, own_j, chans = base_ref.shape
    height, lanes = msgs[0].shape
    total = seqs * blocks
    tri = win_ref.shape[1] // 4
    half = own_i // 2

    for r in range(blocks):
        m = msgs[r][pl.ds(0, own_i), :].astype(f32)
        for s in range(seqs):
            moved = m if s == 0 else pltpu.roll(m, lanes - s * width, 1)
            xl_ref[pl.ds(r * seqs + s, own_i, stride=total), :] = moved[:, :128]
    lhs = xl_ref[:, :width].astype(bf16)

    rmat = jnp.zeros((own_j, width * total), f32)
    for r in range(blocks):
        rmat += jnp.dot(msgs[r][pl.ds(0, own_j), :], pick_ref[r], preferred_element_type=f32)
    rmat = rmat.astype(bf16)

    def expand(h, carry):
        out = jnp.dot(lhs, wq_ref[h], preferred_element_type=f32)
        parts = [out[:, d * chans : (d + 1) * chans].reshape(own_i, total, chans) for d in range(2)]
        block = jnp.concatenate(parts, axis=1).astype(bf16)
        where = pl.ds(pl.multiple_of(h * 2 * total, 16), 2 * total)
        t_ref[:, where, :chans] = block[:half]
        t_ref[:, where, chans:] = block[half:]
        return carry

    lax.fori_loop(0, width // 2, expand, 0, unroll=4)

    step = 4 if half % 4 == 0 else 1

    def rows(b, carry):
        normed = [[], []]
        for g in range(step):
            i = b * step + g
            both = jnp.dot(rmat, t_ref[i], preferred_element_type=f32) * (1.0 / total)
            for side in range(2):
                at = i + side * half
                psum = (base_ref[at] + both[:, side * chans : (side + 1) * chans]).astype(bf16)
                psum_ref[at] = psum
                normed[side].append(standardize(psum.astype(f32)))
        flat = jnp.concatenate(normed[0] + normed[1], axis=0).astype(bf16)
        proj = jnp.dot(flat, win_ref[:, 2 * tri :], preferred_element_type=f32)
        count = step * own_j
        for side in range(2):
            cut = slice(side * count, (side + 1) * count)
            i0 = b * step + side * half
            norm_ref[pl.ds(pl.multiple_of(i0 * own_j, 16), count), :] = flat[cut]
            mask = mask_ref[pl.ds(i0, step)].astype(f32).reshape(count, tri)
            right = mask * sigmoid(proj[cut, :tri]) * proj[cut, tri:]
            if turned:
                flat_ref[pl.ds(pl.multiple_of(i0 * own_j, 8), count), :] = right
            else:
                right_ref[pl.ds(i0, step)] = right.reshape(step, own_j, tri).astype(bf16)
        return carry

    lax.fori_loop(0, half // step, rows, 0, unroll=True)

    def turn(k, carry):
        right_ref[k] = flat_ref[pl.ds(k, own_i, stride=own_j), :].astype(bf16)
        return carry

    if turned:
        lax.fori_loop(0, own_j, turn, 0, unroll=8)


def left_body(norm_ref, mask_ref, win_ref, *outs):
    own_i, own_j, tri = mask_ref.shape
    group = 8 if own_i % 8 == 0 else 1
    at = 0
    for out in outs:
        first = at

        def rows(b, carry):
            i0 = first + b * group
            flat = norm_ref[pl.ds(pl.multiple_of(i0 * own_j, 16), group * own_j), :]
            mask = mask_ref[pl.ds(i0, group)].astype(f32).reshape(group * own_j, tri)
            proj = jnp.dot(flat, win_ref[:, : 2 * tri], preferred_element_type=f32)
            left = mask * sigmoid(proj[:, :tri]) * proj[:, tri:]
            out[pl.ds(b * group, group)] = left.reshape(group, own_j, tri).astype(bf16)
            return carry

        lax.fori_loop(0, out.shape[0] // group, rows, 0, unroll=True)
        at += out.shape[0]


def contract(lf_ref, halves, i0, group):
    step = 8
    acc = (jnp.zeros(halves[0].shape[1:], f32),) * group
    for h, r_ref in enumerate(halves):
        depth = r_ref.shape[0]

        def add(kb, acc):
            k0 = kb * step
            acc = list(acc)
            for d in range(step):
                right = r_ref[k0 + d].astype(f32)
                for t in range(group):
                    acc[t] = acc[t] + lf_ref[i0 + t, pl.ds(h * depth + k0 + d, 1), :] * right
            return tuple(acc)

        acc = lax.fori_loop(0, depth // step, add, acc)
    return acc


def with_right(own_pair, refs, use):
    own, got, p_got, far, p_far = refs
    r, z = lax.axis_index("row"), lax.axis_index("col")
    keeper = (r % 2) == (z % 2)
    near = ((r // 2) == (z // 2)) == own_pair
    table = [
        (near & keeper, own, p_got),
        (near & ~keeper, far, got),
        (~near & keeper, got, far),
        (~near & ~keeper, p_got, p_far),
    ]
    for cond, a, b in table:
        pl.when(cond)(functools.partial(use, (a, b)))


def send_body(first, *refs):
    rights, (l_ref, m_ref, o_ref, lf_ref) = refs[:5], refs[5:]
    count, depth = o_ref.shape[0], l_ref.shape[1]
    group = 8
    lf_ref[:, pl.ds(0, depth), :] = l_ref[pl.ds(first, count)].astype(f32)
    lf_ref[:, pl.ds(depth, depth), :] = m_ref[pl.ds(first, count)].astype(f32)

    def use(halves):
        def rows(b, carry):
            acc = contract(lf_ref, halves, b * group, group)
            for t in range(group):
                o_ref[b * group + t] = acc[t].astype(bf16)
            return carry

        lax.fori_loop(0, count // group, rows, 0)

    with_right(False, rights, use)


def keep_body(cuts, *refs):
    rights, refs = refs[:5], refs[5:]
    lefts, mets = refs[:cuts], refs[cuts : 2 * cuts]
    norm_ref, wgate_ref, o_ref, gate_ref, lf_ref = refs[2 * cuts :]
    own_i, depth, chans = o_ref.shape
    at = 0
    for l_ref, m_ref in zip(lefts, mets):
        n = l_ref.shape[0]
        lf_ref[pl.ds(at, n), pl.ds(0, depth), :] = l_ref[...].astype(f32)
        lf_ref[pl.ds(at, n), pl.ds(depth, depth), :] = m_ref[...].astype(f32)
        at += n
    group = 8

    def gates(b, carry):
        flat = norm_ref[pl.ds(pl.multiple_of(b * group * depth, 16), group * depth), :]
        gate = sigmoid(jnp.dot(flat, wgate_ref[...], preferred_element_type=f32))
        gate_ref[pl.ds(b * group, group)] = gate.reshape(group, depth, -1)
        return carry

    lax.fori_loop(0, own_i // group, gates, 0, unroll=True)

    def use(halves):
        def rows(b, carry):
            acc = contract(lf_ref, halves, b * group, group)
            for t in range(group):
                o_ref[b * group + t] = acc[t]
            return carry

        lax.fori_loop(0, own_i // group, rows, 0)

    with_right(True, rights, use)


def join_body(first, sum_ref, own_ref, psum_ref, gate_ref, w_ref, *refs):
    out_hbm, done_ref, sem = refs[-3:]
    count, extent, chans = done_ref.shape
    group = 8

    def rows(b, carry):
        some = pl.ds(b * group, group)
        all_ = pl.ds(first + b * group, group)
        mixed = own_ref[all_] + sum_ref[some].astype(f32)
        normed = standardize(mixed).reshape(group * extent, -1).astype(bf16)
        update = jnp.dot(normed, w_ref[...], preferred_element_type=f32).reshape(group, extent, -1)
        done_ref[some] = (psum_ref[all_].astype(f32) + gate_ref[all_] * update).astype(bf16)
        return carry

    lax.fori_loop(0, count // group, rows, 0, unroll=True)
    copy = pltpu.make_async_copy(done_ref, out_hbm.at[pl.ds(first, count)], sem)
    copy.start()
    copy.wait()


def triangle_body(l_ref, r_ref, o_ref, lf_ref, flat_ref, rk_ref):
    own_i, depth, chans = l_ref.shape
    extent = r_ref.shape[0]
    group = 8 if own_i % 8 == 0 else 1

    @pl.when(pl.program_id(0) == 0)
    def _():
        lf_ref[...] = l_ref[...].astype(f32)

    def widen(j, carry):
        flat_ref[pl.ds(pl.multiple_of(j * depth, 8), depth), :] = r_ref[j].astype(f32)
        return carry

    lax.fori_loop(0, extent, widen, 0)

    def turn(k, carry):
        rk_ref[k] = flat_ref[pl.ds(k, extent, stride=depth), :]
        return carry

    lax.fori_loop(0, depth, turn, 0)

    def rows(b, carry):
        i0 = b * group
        acc = contract(lf_ref, [rk_ref], i0, group)
        for t in range(group):
            o_ref[0, i0 + t] = acc[t].astype(bf16)
        return carry

    lax.fori_loop(0, own_i // group, rows, 0)


def finish_body(sum_ref, psum_ref, norm_ref, wgate_ref, w_ref, out_ref):
    parts, own_i, extent, chans = sum_ref.shape
    own_j = psum_ref.shape[1]

    def row(i, carry):
        flat = norm_ref[pl.ds(pl.multiple_of(i * own_j, 16), own_j), :]
        gate = sigmoid(jnp.dot(flat, wgate_ref[...], preferred_element_type=f32))
        normed = [standardize(sum_ref[part, i].astype(f32)) for part in range(parts)]
        normed = jnp.concatenate(normed, axis=0).astype(bf16)
        update = jnp.dot(normed, w_ref[...], preferred_element_type=f32)
        out_ref[i] = (psum_ref[i].astype(f32) + gate * update).astype(bf16)
        return carry

    lax.fori_loop(0, own_i, row, 0)


def gathered_plan(left, right, psum, norm, w_gate, w_final):
    own_i, own_j, chans = psum.shape
    rows = lax.axis_size("row")
    tri = w_final.shape[0]
    right_all = lax.all_gather(right, "row", axis=0, tiled=True)
    partial = pl.pallas_call(
        triangle_body,
        grid=(rows,),
        out_shape=jax.ShapeDtypeStruct((rows, own_i, own_i, tri), bf16),
        in_specs=[
            pl.BlockSpec((own_i, own_j, tri), lambda r: (0, 0, 0)),
            pl.BlockSpec((own_i, own_j, tri), lambda r: (r, 0, 0)),
        ],
        out_specs=pl.BlockSpec((1, own_i, own_i, tri), lambda r: (r, 0, 0, 0)),
        scratch_shapes=[
            pltpu.VMEM((own_i, own_j, tri), f32),
            pltpu.VMEM((own_i * own_j, tri), f32),
            pltpu.VMEM((own_j, own_i, tri), f32),
        ],
        compiler_params=limit(56),
        name="triangle",
    )(left, right_all)
    summed = lax.psum_scatter(partial, "col", scatter_dimension=0, tiled=True)
    return pl.pallas_call(
        finish_body,
        out_shape=jax.ShapeDtypeStruct((own_i, own_j, chans), bf16),
        in_specs=[VMEM] * 5,
        out_specs=VMEM,
        compiler_params=limit(56),
        name="finish",
    )(summed, psum, norm, w_gate, w_final)


def paired_plan(lefts, right, psum, norm, w_gate, w_final):
    own_i, own_j, chans = psum.shape
    tri = w_final.shape[0]
    cuts = len(lefts)
    cells = [(r, z) for r in range(4) for z in range(4)]

    def move(value, where, step):
        pairs = [(r * 4 + z, step(r, z)) for r, z in cells if where(r, z)]
        pairs = [(src, r * 4 + z) for src, (r, z) in pairs]
        return lax.ppermute(value, ("row", "col"), pairs)

    every = lambda r, z: True
    keeper = lambda r, z: r % 2 == z % 2
    got = move(right, every, lambda r, z: (r ^ 2, z) if keeper(r, z) else (r ^ 1, z ^ 1))
    far = move(right, every, lambda r, z: (r ^ 1, z) if keeper(r, z) else (r ^ 2, z ^ 1))
    mets = [move(left, every, lambda r, z: (r, z ^ 1)) for left in lefts]
    got, far, mets[0] = lax.optimization_barrier((got, far, mets[0]))
    p_got = move(got, every, lambda r, z: (r ^ 1, z))
    p_far = move(far, every, lambda r, z: (r ^ 1, z))
    rights = (right, got, p_got, far, p_far)

    sums = []
    chunks = ((0, 0, 0, 16), (1, 0, 16, 16), (1, 16, 32, own_i - 32))
    for at, first, _, n in chunks:
        part = pl.pallas_call(
            functools.partial(send_body, first),
            out_shape=jax.ShapeDtypeStruct((n, own_j, tri), bf16),
            in_specs=[VMEM] * 7,
            out_specs=VMEM,
            scratch_shapes=[pltpu.VMEM((n, 2 * own_j, tri), f32)],
            compiler_params=limit(8),
            cost_estimate=cost(0.12 * n + 0.4),
            name="send_sums",
        )(*rights, lefts[at], mets[at])
        sums.append(move(part, every, lambda r, z: (r, z ^ 2)))

    own, gate = pl.pallas_call(
        functools.partial(keep_body, cuts),
        out_shape=[jax.ShapeDtypeStruct((own_i, own_j, tri), f32),
                   jax.ShapeDtypeStruct((own_i, own_j, chans), f32)],
        in_specs=[VMEM] * (5 + 2 * cuts + 2),
        out_specs=[VMEM] * 2,
        scratch_shapes=[pltpu.VMEM((own_i, 2 * own_j, tri), f32)],
        compiler_params=limit(12),
        cost_estimate=cost(6),
        name="keep_sums",
    )(*rights, *lefts, *mets, norm, w_gate)
    out = []
    for part, (_, _, first, n) in zip(sums, chunks):
        out = [pl.pallas_call(
            functools.partial(join_body, first),
            out_shape=jax.ShapeDtypeStruct((own_i, own_j, chans), bf16),
            in_specs=[VMEM] * 5 + [HBM] * len(out),
            out_specs=HBM,
            scratch_shapes=[pltpu.VMEM((n, own_j, chans), bf16), pltpu.SemaphoreType.DMA],
            input_output_aliases={5: 0} if out else {},
            compiler_params=limit(8),
            cost_estimate=cost(0.06 * n),
            name="join",
        )(part, own, psum, gate, w_final, *out)]
    return out[0]


def shards(homolog, couple, ids, valid, bias, factors, average, w_in, w_gate, w_final):
    rows, cols = lax.axis_size("row"), lax.axis_size("col")
    own_seqs, residues, depth = homolog.shape
    own_i, own_j, chans = couple.shape
    width = factors.shape[1] // 2
    tri = w_final.shape[0]
    total = own_seqs * rows
    lanes = round_up(2 * own_seqs * width, 128)
    height = round_up(max(own_i, own_j), 16)
    paired = rows == 4 and cols == 4 and own_i == own_j and own_i % 8 == 0 and own_i > 32
    scale = 1 if paired else 8

    msgs = pl.pallas_call(
        functools.partial(align_body, own_i, own_j, rows),
        out_shape=[jax.ShapeDtypeStruct((height, lanes), bf16)] * rows,
        in_specs=[HBM] * 2,
        out_specs=[VMEM] * rows,
        scratch_shapes=[
            pltpu.VMEM(homolog.shape, bf16),
            pltpu.VMEM((2 * width, depth), bf16),
            pltpu.VMEM((own_seqs * residues, 2 * width), f32),
            pltpu.SemaphoreType.DMA((2,)),
        ],
        compiler_params=limit(8, scale),
        cost_estimate=cost(1.5),
        name="align",
    )(hold(homolog), hold(factors.T))
    msgs = [msgs[0]] + [
        lax.ppermute(msg, "row", [(r, r ^ d) for r in range(rows)])
        for d, msg in enumerate(msgs) if d
    ]

    base, mask, wq, pick = pl.pallas_call(
        functools.partial(prepare_body, own_seqs),
        out_shape=[jax.ShapeDtypeStruct((own_i, own_j, chans), f32),
                   jax.ShapeDtypeStruct((own_i, own_j, tri), bf16),
                   jax.ShapeDtypeStruct((width // 2, width, 2 * chans), bf16),
                   jax.ShapeDtypeStruct((rows, lanes, width * total), bf16)],
        in_specs=[HBM, SMEM, HBM, HBM, HBM],
        out_specs=[VMEM] * 4,
        scratch_shapes=[
            pltpu.VMEM(couple.shape, bf16),
            pltpu.VMEM(valid.shape, jnp.int32),
            pltpu.VMEM(bias.shape, f32),
            pltpu.VMEM(average.shape, bf16),
            pltpu.VMEM(average.shape, f32),
            pltpu.VMEM((own_j, chans), jnp.int32),
            pltpu.SemaphoreType.DMA((4,)),
        ],
        compiler_params=limit(8, scale),
        cost_estimate=cost(2.5),
        name="prepare",
    )(hold(couple), ids, hold(valid), hold(bias), hold(average))

    extents = (own_j, own_i) if paired else (own_i, own_j)
    psum, norm, right = pl.pallas_call(
        functools.partial(pair_body, own_seqs, width, rows, paired),
        out_shape=[jax.ShapeDtypeStruct((own_i, own_j, chans), bf16),
                   jax.ShapeDtypeStruct((own_i * own_j, chans), bf16),
                   jax.ShapeDtypeStruct(extents + (tri,), bf16)],
        in_specs=[VMEM] * (rows + 5),
        out_specs=[VMEM] * 3,
        scratch_shapes=[
            pltpu.VMEM((own_i * total, 128), f32),
            pltpu.VMEM((own_i // 2, width * total, 2 * chans), bf16),
            pltpu.VMEM((own_i * own_j, tri), f32),
        ],
        compiler_params=limit(16, scale),
        cost_estimate=cost(4.5),
        name="pair",
    )(*msgs, base, mask, wq, pick, w_in)

    cuts = [16, own_i - 16] if paired else [own_i]
    lefts = pl.pallas_call(
        left_body,
        out_shape=[jax.ShapeDtypeStruct((n, own_j, tri), bf16) for n in cuts],
        in_specs=[VMEM] * 3,
        out_specs=[VMEM] * len(cuts),
        compiler_params=limit(8, scale),
        cost_estimate=cost(1),
        name="left",
    )(norm, mask, w_in)
    if paired:
        return paired_plan(lefts, right, psum, norm, w_gate, w_final)
    return gathered_plan(lefts[0], right, psum, norm, w_gate, w_final)


def solution(mesh):
    placed = (
        P(("grp", "row"), None, None),
        P(("grp", "row"), "col", None),
        P("grp"),
        P(("grp", "row"), "col"),
        P(),
        P(),
        P(),
        P(),
        P(),
        P(),
    )
    return jax.shard_map(
        shards,
        mesh=mesh,
        in_specs=placed,
        out_specs=P(("grp", "row"), "col", None),
        check_vma=False,
    )
```

```python
import functools

import jax
import jax.numpy as jnp
from jax import lax
from jax.experimental import pallas as pl
from jax.experimental.pallas import tpu as pltpu
from jax.sharding import PartitionSpec as P

eps = 1e-05
f32 = jnp.float32
bf16 = jnp.bfloat16
VMEM = pl.BlockSpec(memory_space=pltpu.VMEM)
SMEM = pl.BlockSpec(memory_space=pltpu.SMEM)
HBM = pl.BlockSpec(memory_space=pltpu.HBM)


def limit(mib, scale=1):
    return pltpu.CompilerParams(vmem_limit_bytes=min(56, mib * scale) * 1024 * 1024)


def round_up(n, m):
    return (n + m - 1) // m * m


def cost(us):
    return pl.CostEstimate(flops=0, bytes_accessed=int(us * 3.69e6), transcendentals=0)


def hold(x):
    return pltpu.with_memory_space_constraint(x, pltpu.HBM)


def fetch(pairs, sem):
    copies = [pltpu.make_async_copy(src, dst, sem.at[n]) for n, (src, dst) in enumerate(pairs)]
    for copy in copies:
        copy.start()
    return copies


def standardize(values):
    centre = values - jnp.mean(values, axis=-1, keepdims=True)
    spread = jnp.mean(centre * centre, axis=-1, keepdims=True)
    return centre * lax.rsqrt(spread + eps)


def sigmoid(v):
    return 0.5 * jnp.tanh(0.5 * v) + 0.5


def align_body(own_i, own_j, count, x_hbm, w_hbm, *refs):
    later, outs, refs = refs[:4], refs[4 : 4 + count], refs[4 + count :]
    brought, (x_ref, w_ref, y_ref, sem) = refs[:4], refs[4:]
    copies = fetch([(x_hbm, x_ref), (w_hbm, w_ref), *zip(later, brought)], sem)
    seqs, residues, depth = x_ref.shape
    width = w_ref.shape[0] // 2
    height, lanes = outs[0].shape
    me = lax.axis_index("row")
    z = lax.axis_index("col")
    copies[0].wait()
    x = x_ref[...].astype(f32).reshape(seqs * residues, depth)
    normed = standardize(x).astype(bf16)
    copies[1].wait()
    y_ref[...] = lax.dot_general(
        normed, w_ref[...], (((1,), (1,)), ((), ())), preferred_element_type=f32
    )
    start = pl.multiple_of(z * own_j, 8)

    def tall(v):
        gap = height - v.shape[0]
        return jnp.concatenate([v, jnp.zeros((gap, v.shape[1]), f32)], axis=0) if gap else v

    right = [tall(y_ref[pl.ds(s * residues + start, own_j), width:]) for s in range(seqs)]
    gap = lanes - 2 * seqs * width
    right += [jnp.zeros((height, gap), f32)] if gap else []
    for d, out in enumerate(outs):
        first = pl.multiple_of((me ^ d) * own_i, 8)
        left = [tall(y_ref[pl.ds(s * residues + first, own_i), :width]) for s in range(seqs)]
        out[...] = jnp.concatenate(left + right, axis=1).astype(bf16)
    for copy in copies[2:]:
        copy.wait()


def prepare_body(seqs, couple_ref, ids_hbm, valid_ref, bias_ref, avg_ref, base_ref, mask_ref, wq_ref, pick_ref,
                 wf_ref, idc_ref, ids_ref, sem):
    (copy,) = fetch([(ids_hbm, ids_ref)], sem)
    own_i, own_j, chans = couple_ref.shape
    pairs, width, _ = wq_ref.shape
    blocks, lanes, _ = pick_ref.shape
    total = blocks * seqs
    x0 = lax.axis_index("row") * own_i
    z0 = lax.axis_index("col") * own_j

    row = lax.broadcasted_iota(jnp.int32, pick_ref.shape[1:], 0)
    col = lax.broadcasted_iota(jnp.int32, pick_ref.shape[1:], 1)
    unit = row - seqs * width
    place = lax.rem(unit, width) * total + lax.div(unit, width)
    place = jnp.where((unit >= 0) & (unit < seqs * width), col - place, -1)

    def pick(r, carry):
        pick_ref[r] = jnp.where(place == r * seqs, 1.0, 0.0).astype(bf16)
        return carry

    lax.fori_loop(0, blocks, pick, 0)
    wf_ref[...] = avg_ref[...].astype(f32)
    for h in range(pairs):
        both = [wf_ref[pl.ds(2 * h + d, width, stride=width), :] for d in range(2)]
        wq_ref[h] = jnp.concatenate(both, axis=1).astype(bf16)
    copy.wait()
    for j in range(own_j):
        idc_ref[pl.ds(j, 1), :] = jnp.full((1, chans), ids_ref[z0 + j], jnp.int32)
    idc = idc_ref[...]
    valid_t = valid_ref[...].astype(f32).T
    lane = lax.broadcasted_iota(jnp.int32, valid_t.shape, 1)
    same_bias = bias_ref[0:1, :]
    cross_bias = bias_ref[1:2, :]

    def rows(i, carry):
        bias = jnp.where(idc == ids_ref[x0 + i], same_bias, cross_bias)
        base_ref[i] = couple_ref[i].astype(f32) + bias
        column = jnp.sum(jnp.where(lane == i, valid_t, 0.0), axis=1, keepdims=True)
        mask_ref[i] = jnp.broadcast_to(column, (own_j, mask_ref.shape[2])).astype(bf16)
        return carry

    lax.fori_loop(0, own_i, rows, 0, unroll=8)


def pair_body(seqs, width, blocks, turned, *refs):
    msgs = refs[:blocks]
    base_ref, mask_ref, wq_ref, pick_ref, win_ref = refs[blocks : blocks + 5]
    psum_ref, norm_ref, right_ref = refs[blocks + 5 : blocks + 8]
    xl_ref, t_ref, flat_ref = refs[blocks + 8 :]
    own_i, own_j, chans = base_ref.shape
    height, lanes = msgs[0].shape
    total = seqs * blocks
    tri = win_ref.shape[1] // 4
    half = own_i // 2

    for r in range(blocks):
        m = msgs[r][pl.ds(0, own_i), :].astype(f32)
        for s in range(seqs):
            moved = m if s == 0 else pltpu.roll(m, lanes - s * width, 1)
            xl_ref[pl.ds(r * seqs + s, own_i, stride=total), :] = moved[:, :128]
    lhs = xl_ref[:, :width].astype(bf16)

    joined = jnp.concatenate([msg[...] for msg in msgs], axis=1)
    picks = pick_ref[...].reshape(blocks * lanes, width * total)
    rmat = jnp.dot(joined, picks, preferred_element_type=f32)[:own_j].astype(bf16)

    def expand(h, carry):
        out = jnp.dot(lhs, wq_ref[h], preferred_element_type=f32)
        parts = [out[:, d * chans : (d + 1) * chans].reshape(own_i, total, chans) for d in range(2)]
        block = jnp.concatenate(parts, axis=1).astype(bf16)
        where = pl.ds(pl.multiple_of(h * 2 * total, 16), 2 * total)
        t_ref[:, where, :chans] = block[:half]
        t_ref[:, where, chans:] = block[half:]
        return carry

    lax.fori_loop(0, width // 2, expand, 0, unroll=16 if turned else 4)

    step = 4 if half % 4 == 0 else 1

    def rows(b, carry):
        normed = [[], []]
        for g in range(step):
            i = b * step + g
            both = jnp.dot(rmat, t_ref[i], preferred_element_type=f32) * (1.0 / total)
            for side in range(2):
                at = i + side * half
                psum = (base_ref[at] + both[:, side * chans : (side + 1) * chans]).astype(bf16)
                psum_ref[at] = psum
                normed[side].append(standardize(psum.astype(f32)))
        flat = jnp.concatenate(normed[0] + normed[1], axis=0).astype(bf16)
        proj = jnp.dot(flat, win_ref[:, 2 * tri :], preferred_element_type=f32)
        count = step * own_j
        for side in range(2):
            cut = slice(side * count, (side + 1) * count)
            i0 = b * step + side * half
            norm_ref[pl.ds(pl.multiple_of(i0 * own_j, 16), count), :] = flat[cut]
            mask = mask_ref[pl.ds(i0, step)].astype(f32).reshape(count, tri)
            right = mask * sigmoid(proj[cut, :tri]) * proj[cut, tri:]
            if turned:
                flat_ref[pl.ds(pl.multiple_of(i0 * own_j, 8), count), :] = right
            else:
                right_ref[pl.ds(i0, step)] = right.reshape(step, own_j, tri).astype(bf16)
        return carry

    lax.fori_loop(0, half // step, rows, 0, unroll=True)

    def turn(k, carry):
        right_ref[k] = flat_ref[pl.ds(k, own_i, stride=own_j), :].astype(bf16)
        return carry

    if turned:
        lax.fori_loop(0, own_j, turn, 0, unroll=8)


def left_body(norm_ref, mask_ref, win_ref, *outs):
    own_i, own_j, tri = mask_ref.shape
    group = 8 if own_i % 8 == 0 else 1
    at = 0
    for out in outs:
        first = at

        def rows(b, carry):
            i0 = first + b * group
            flat = norm_ref[pl.ds(pl.multiple_of(i0 * own_j, 16), group * own_j), :]
            mask = mask_ref[pl.ds(i0, group)].astype(f32).reshape(group * own_j, tri)
            proj = jnp.dot(flat, win_ref[:, : 2 * tri], preferred_element_type=f32)
            left = mask * sigmoid(proj[:, :tri]) * proj[:, tri:]
            out[pl.ds(b * group, group)] = left.reshape(group, own_j, tri).astype(bf16)
            return carry

        lax.fori_loop(0, out.shape[0] // group, rows, 0, unroll=True)
        at += out.shape[0]


def contract(lf_ref, halves, i0, group):
    step = 8
    acc = (jnp.zeros(halves[0].shape[1:], f32),) * group
    for h, r_ref in enumerate(halves):
        depth = r_ref.shape[0]

        def add(kb, acc):
            k0 = kb * step
            acc = list(acc)
            for d in range(step):
                right = r_ref[k0 + d].astype(f32)
                for t in range(group):
                    acc[t] = acc[t] + lf_ref[i0 + t, pl.ds(h * depth + k0 + d, 1), :] * right
            return tuple(acc)

        acc = lax.fori_loop(0, depth // step, add, acc)
    return acc


def with_right(own_pair, refs, use):
    own, got, p_got, far, p_far = refs
    r, z = lax.axis_index("row"), lax.axis_index("col")
    keeper = (r % 2) == (z % 2)
    near = ((r // 2) == (z // 2)) == own_pair
    table = [
        (near & keeper, own, p_got),
        (near & ~keeper, far, got),
        (~near & keeper, got, far),
        (~near & ~keeper, p_got, p_far),
    ]
    for cond, a, b in table:
        pl.when(cond)(functools.partial(use, (a, b)))


def send_body(first, *refs):
    rights, (l_ref, m_ref, o_ref, lf_ref) = refs[:5], refs[5:]
    count, depth = o_ref.shape[0], l_ref.shape[1]
    group = 8
    lf_ref[:, pl.ds(0, depth), :] = l_ref[pl.ds(first, count)].astype(f32)
    lf_ref[:, pl.ds(depth, depth), :] = m_ref[pl.ds(first, count)].astype(f32)

    def use(halves):
        def rows(b, carry):
            acc = contract(lf_ref, halves, b * group, group)
            for t in range(group):
                o_ref[b * group + t] = acc[t].astype(bf16)
            return carry

        lax.fori_loop(0, count // group, rows, 0)

    with_right(False, rights, use)


def keep_body(cuts, *refs):
    rights, refs = refs[:5], refs[5:]
    lefts, mets = refs[:cuts], refs[cuts : 2 * cuts]
    norm_ref, wgate_ref, o_ref, gate_ref, lf_ref = refs[2 * cuts :]
    own_i, depth, chans = o_ref.shape
    at = 0
    for l_ref, m_ref in zip(lefts, mets):
        n = l_ref.shape[0]
        lf_ref[pl.ds(at, n), pl.ds(0, depth), :] = l_ref[...].astype(f32)
        lf_ref[pl.ds(at, n), pl.ds(depth, depth), :] = m_ref[...].astype(f32)
        at += n
    group = 8

    def gates(b, carry):
        flat = norm_ref[pl.ds(pl.multiple_of(b * group * depth, 16), group * depth), :]
        gate = sigmoid(jnp.dot(flat, wgate_ref[...], preferred_element_type=f32))
        gate_ref[pl.ds(b * group, group)] = gate.reshape(group, depth, -1)
        return carry

    lax.fori_loop(0, own_i // group, gates, 0, unroll=True)

    def use(halves):
        def rows(b, carry):
            acc = contract(lf_ref, halves, b * group, group)
            for t in range(group):
                o_ref[b * group + t] = acc[t]
            return carry

        lax.fori_loop(0, own_i // group, rows, 0)

    with_right(True, rights, use)


def join_body(first, parts, own_ref, psum_ref, gate_ref, w_ref, *refs):
    sums, (out_hbm, done_ref, sem) = refs[:parts], refs[-3:]
    count, extent, chans = done_ref.shape
    group = 8
    at = 0
    for sum_ref in sums:
        start = at

        def rows(b, carry):
            here = pl.ds(start + b * group, group)
            there = pl.ds(first + start + b * group, group)
            mixed = own_ref[there] + sum_ref[pl.ds(b * group, group)].astype(f32)
            normed = standardize(mixed).reshape(group * extent, -1).astype(bf16)
            update = jnp.dot(normed, w_ref[...], preferred_element_type=f32).reshape(group, extent, -1)
            done_ref[here] = (psum_ref[there].astype(f32) + gate_ref[there] * update).astype(bf16)
            return carry

        lax.fori_loop(0, sum_ref.shape[0] // group, rows, 0, unroll=True)
        at += sum_ref.shape[0]
    copy = pltpu.make_async_copy(done_ref, out_hbm.at[pl.ds(first, count)], sem)
    copy.start()
    copy.wait()


def triangle_body(l_ref, r_ref, o_ref, lf_ref, flat_ref, rk_ref):
    own_i, depth, chans = l_ref.shape
    extent = r_ref.shape[0]
    group = 8 if own_i % 8 == 0 else 1

    @pl.when(pl.program_id(0) == 0)
    def _():
        lf_ref[...] = l_ref[...].astype(f32)

    def widen(j, carry):
        flat_ref[pl.ds(pl.multiple_of(j * depth, 8), depth), :] = r_ref[j].astype(f32)
        return carry

    lax.fori_loop(0, extent, widen, 0)

    def turn(k, carry):
        rk_ref[k] = flat_ref[pl.ds(k, extent, stride=depth), :]
        return carry

    lax.fori_loop(0, depth, turn, 0)

    def rows(b, carry):
        i0 = b * group
        acc = contract(lf_ref, [rk_ref], i0, group)
        for t in range(group):
            o_ref[0, i0 + t] = acc[t].astype(bf16)
        return carry

    lax.fori_loop(0, own_i // group, rows, 0)


def finish_body(sum_ref, psum_ref, norm_ref, wgate_ref, w_ref, out_ref):
    parts, own_i, extent, chans = sum_ref.shape
    own_j = psum_ref.shape[1]

    def row(i, carry):
        flat = norm_ref[pl.ds(pl.multiple_of(i * own_j, 16), own_j), :]
        gate = sigmoid(jnp.dot(flat, wgate_ref[...], preferred_element_type=f32))
        normed = [standardize(sum_ref[part, i].astype(f32)) for part in range(parts)]
        normed = jnp.concatenate(normed, axis=0).astype(bf16)
        update = jnp.dot(normed, w_ref[...], preferred_element_type=f32)
        out_ref[i] = (psum_ref[i].astype(f32) + gate * update).astype(bf16)
        return carry

    lax.fori_loop(0, own_i, row, 0)


def gathered_plan(left, right, psum, norm, w_gate, w_final):
    own_i, own_j, chans = psum.shape
    rows = lax.axis_size("row")
    tri = w_final.shape[0]
    right_all = lax.all_gather(right, "row", axis=0, tiled=True)
    partial = pl.pallas_call(
        triangle_body,
        grid=(rows,),
        out_shape=jax.ShapeDtypeStruct((rows, own_i, own_i, tri), bf16),
        in_specs=[
            pl.BlockSpec((own_i, own_j, tri), lambda r: (0, 0, 0)),
            pl.BlockSpec((own_i, own_j, tri), lambda r: (r, 0, 0)),
        ],
        out_specs=pl.BlockSpec((1, own_i, own_i, tri), lambda r: (r, 0, 0, 0)),
        scratch_shapes=[
            pltpu.VMEM((own_i, own_j, tri), f32),
            pltpu.VMEM((own_i * own_j, tri), f32),
            pltpu.VMEM((own_j, own_i, tri), f32),
        ],
        compiler_params=limit(56),
        name="triangle",
    )(left, right_all)
    summed = lax.psum_scatter(partial, "col", scatter_dimension=0, tiled=True)
    return pl.pallas_call(
        finish_body,
        out_shape=jax.ShapeDtypeStruct((own_i, own_j, chans), bf16),
        in_specs=[VMEM] * 5,
        out_specs=VMEM,
        compiler_params=limit(56),
        name="finish",
    )(summed, psum, norm, w_gate, w_final)


def paired_plan(lefts, right, psum, norm, w_gate, w_final):
    own_i, own_j, chans = psum.shape
    tri = w_final.shape[0]
    cuts = len(lefts)
    cells = [(r, z) for r in range(4) for z in range(4)]

    def move(value, where, step):
        pairs = [(r * 4 + z, step(r, z)) for r, z in cells if where(r, z)]
        pairs = [(src, r * 4 + z) for src, (r, z) in pairs]
        return lax.ppermute(value, ("row", "col"), pairs)

    every = lambda r, z: True
    keeper = lambda r, z: r % 2 == z % 2
    got = move(right, every, lambda r, z: (r ^ 2, z) if keeper(r, z) else (r ^ 1, z ^ 1))
    far = move(right, every, lambda r, z: (r ^ 1, z) if keeper(r, z) else (r ^ 2, z ^ 1))
    mets = [move(left, every, lambda r, z: (r, z ^ 1)) for left in lefts]
    got, far, mets[0] = lax.optimization_barrier((got, far, mets[0]))
    p_got = move(got, every, lambda r, z: (r ^ 1, z))
    p_far = move(far, every, lambda r, z: (r ^ 1, z))
    rights = (right, got, p_got, far, p_far)

    sums = []
    chunks = ((0, 0, 0, 16), (1, 0, 16, 16), (1, 16, 32, own_i - 32))
    for at, first, _, n in chunks:
        part = pl.pallas_call(
            functools.partial(send_body, first),
            out_shape=jax.ShapeDtypeStruct((n, own_j, tri), bf16),
            in_specs=[VMEM] * 7,
            out_specs=VMEM,
            scratch_shapes=[pltpu.VMEM((n, 2 * own_j, tri), f32)],
            compiler_params=limit(8),
            cost_estimate=cost(0.12 * n + 0.4),
            name="send_sums",
        )(*rights, lefts[at], mets[at])
        sums.append(move(part, every, lambda r, z: (r, z ^ 2)))

    own, gate = pl.pallas_call(
        functools.partial(keep_body, cuts),
        out_shape=[jax.ShapeDtypeStruct((own_i, own_j, tri), f32),
                   jax.ShapeDtypeStruct((own_i, own_j, chans), f32)],
        in_specs=[VMEM] * (5 + 2 * cuts + 2),
        out_specs=[VMEM] * 2,
        scratch_shapes=[pltpu.VMEM((own_i, 2 * own_j, tri), f32)],
        compiler_params=limit(12),
        cost_estimate=cost(6),
        name="keep_sums",
    )(*rights, *lefts, *mets, norm, w_gate)
    out = []
    for first, n, parts in ((0, 16, sums[:1]), (16, own_i - 16, sums[1:])):
        out = [pl.pallas_call(
            functools.partial(join_body, first, len(parts)),
            out_shape=jax.ShapeDtypeStruct((own_i, own_j, chans), bf16),
            in_specs=[VMEM] * (4 + len(parts)) + [HBM] * len(out),
            out_specs=HBM,
            scratch_shapes=[pltpu.VMEM((n, own_j, chans), bf16), pltpu.SemaphoreType.DMA],
            input_output_aliases={4 + len(parts): 0} if out else {},
            compiler_params=limit(8),
            cost_estimate=cost(0.06 * n),
            name="join",
        )(own, psum, gate, w_final, *parts, *out)]
    return out[0]


def shards(homolog, couple, ids, valid, bias, factors, average, w_in, w_gate, w_final):
    rows, cols = lax.axis_size("row"), lax.axis_size("col")
    own_seqs, residues, depth = homolog.shape
    own_i, own_j, chans = couple.shape
    width = factors.shape[1] // 2
    tri = w_final.shape[0]
    total = own_seqs * rows
    lanes = round_up(2 * own_seqs * width, 128)
    height = round_up(max(own_i, own_j), 16)
    paired = rows == 4 and cols == 4 and own_i == own_j and own_i % 8 == 0 and own_i > 32
    scale = 1 if paired else 8

    later = (average, valid, bias, couple)
    *msgs, average, valid, bias, couple = pl.pallas_call(
        functools.partial(align_body, own_i, own_j, rows),
        out_shape=[jax.ShapeDtypeStruct((height, lanes), bf16)] * rows
        + [jax.ShapeDtypeStruct(x.shape, x.dtype) for x in later],
        in_specs=[HBM] * 6,
        out_specs=[VMEM] * (rows + 4),
        scratch_shapes=[
            pltpu.VMEM(homolog.shape, bf16),
            pltpu.VMEM((2 * width, depth), bf16),
            pltpu.VMEM((own_seqs * residues, 2 * width), f32),
            pltpu.SemaphoreType.DMA((6,)),
        ],
        compiler_params=limit(8, scale),
        cost_estimate=cost(1.5),
        name="align",
    )(hold(homolog), hold(factors.T), *map(hold, later))
    msgs = [msgs[0]] + [
        lax.ppermute(msg, "row", [(r, r ^ d) for r in range(rows)])
        for d, msg in enumerate(msgs) if d
    ]

    base, mask, wq, pick = pl.pallas_call(
        functools.partial(prepare_body, own_seqs),
        out_shape=[jax.ShapeDtypeStruct((own_i, own_j, chans), f32),
                   jax.ShapeDtypeStruct((own_i, own_j, tri), bf16),
                   jax.ShapeDtypeStruct((width // 2, width, 2 * chans), bf16),
                   jax.ShapeDtypeStruct((rows, lanes, width * total), bf16)],
        in_specs=[VMEM, HBM, VMEM, VMEM, VMEM],
        out_specs=[VMEM] * 4,
        scratch_shapes=[
            pltpu.VMEM(average.shape, f32),
            pltpu.VMEM((own_j, chans), jnp.int32),
            pltpu.SMEM(ids.shape, jnp.int32),
            pltpu.SemaphoreType.DMA((1,)),
        ],
        compiler_params=limit(8, scale),
        cost_estimate=cost(2),
        name="prepare",
    )(couple, hold(ids), valid, bias, average)

    extents = (own_j, own_i) if paired else (own_i, own_j)
    psum, norm, right = pl.pallas_call(
        functools.partial(pair_body, own_seqs, width, rows, paired),
        out_shape=[jax.ShapeDtypeStruct((own_i, own_j, chans), bf16),
                   jax.ShapeDtypeStruct((own_i * own_j, chans), bf16),
                   jax.ShapeDtypeStruct(extents + (tri,), bf16)],
        in_specs=[VMEM] * (rows + 5),
        out_specs=[VMEM] * 3,
        scratch_shapes=[
            pltpu.VMEM((own_i * total, 128), f32),
            pltpu.VMEM((own_i // 2, width * total, 2 * chans), bf16),
            pltpu.VMEM((own_i * own_j, tri), f32),
        ],
        compiler_params=limit(16, scale),
        cost_estimate=cost(4.5),
        name="pair",
    )(*msgs, base, mask, wq, pick, w_in)

    cuts = [16, own_i - 16] if paired else [own_i]
    lefts = pl.pallas_call(
        left_body,
        out_shape=[jax.ShapeDtypeStruct((n, own_j, tri), bf16) for n in cuts],
        in_specs=[VMEM] * 3,
        out_specs=[VMEM] * len(cuts),
        compiler_params=limit(8, scale),
        cost_estimate=cost(1),
        name="left",
    )(norm, mask, w_in)
    if paired:
        return paired_plan(lefts, right, psum, norm, w_gate, w_final)
    return gathered_plan(lefts[0], right, psum, norm, w_gate, w_final)


def solution(mesh):
    placed = (
        P(("grp", "row"), None, None),
        P(("grp", "row"), "col", None),
        P("grp"),
        P(("grp", "row"), "col"),
        P(),
        P(),
        P(),
        P(),
        P(),
        P(),
    )
    return jax.shard_map(
        shards,
        mesh=mesh,
        in_specs=placed,
        out_specs=P(("grp", "row"), "col", None),
        check_vma=False,
    )
```

```python
import functools

import jax
import jax.numpy as jnp
from jax import lax
from jax.experimental import pallas as pl
from jax.experimental.pallas import tpu as pltpu
from jax.sharding import PartitionSpec as P

eps = 1e-05
f32 = jnp.float32
bf16 = jnp.bfloat16
VMEM = pl.BlockSpec(memory_space=pltpu.VMEM)
SMEM = pl.BlockSpec(memory_space=pltpu.SMEM)
HBM = pl.BlockSpec(memory_space=pltpu.HBM)


def limit(mib, scale=1):
    return pltpu.CompilerParams(vmem_limit_bytes=min(56, mib * scale) * 1024 * 1024)


def round_up(n, m):
    return (n + m - 1) // m * m


def cost(us):
    return pl.CostEstimate(flops=0, bytes_accessed=int(us * 3.69e6), transcendentals=0)


def hold(x):
    return pltpu.with_memory_space_constraint(x, pltpu.HBM)


def fetch(pairs, sem):
    copies = [pltpu.make_async_copy(src, dst, sem.at[n]) for n, (src, dst) in enumerate(pairs)]
    for copy in copies:
        copy.start()
    return copies


def standardize(values):
    centre = values - jnp.mean(values, axis=-1, keepdims=True)
    spread = jnp.mean(centre * centre, axis=-1, keepdims=True)
    return centre * lax.rsqrt(spread + eps)


def sigmoid(v):
    return 0.5 * jnp.tanh(0.5 * v) + 0.5


def align_body(own_i, own_j, count, x_hbm, w_hbm, *refs):
    later, outs, refs = refs[:4], refs[4 : 4 + count], refs[4 + count :]
    brought, (x_ref, w_ref, y_ref, sem) = refs[:4], refs[4:]
    copies = fetch([(x_hbm, x_ref), (w_hbm, w_ref), *zip(later, brought)], sem)
    seqs, residues, depth = x_ref.shape
    width = w_ref.shape[0] // 2
    height, lanes = outs[0].shape
    me = lax.axis_index("row")
    z = lax.axis_index("col")
    copies[0].wait()
    x = x_ref[...].astype(f32).reshape(seqs * residues, depth)
    normed = standardize(x).astype(bf16)
    copies[1].wait()
    y_ref[...] = lax.dot_general(
        normed, w_ref[...], (((1,), (1,)), ((), ())), preferred_element_type=f32
    )
    start = pl.multiple_of(z * own_j, 8)

    def tall(v):
        gap = height - v.shape[0]
        return jnp.concatenate([v, jnp.zeros((gap, v.shape[1]), f32)], axis=0) if gap else v

    right = [tall(y_ref[pl.ds(s * residues + start, own_j), width:]) for s in range(seqs)]
    gap = lanes - 2 * seqs * width
    right += [jnp.zeros((height, gap), f32)] if gap else []
    for d, out in enumerate(outs):
        first = pl.multiple_of((me ^ d) * own_i, 8)
        left = [tall(y_ref[pl.ds(s * residues + first, own_i), :width]) for s in range(seqs)]
        out[...] = jnp.concatenate(left + right, axis=1).astype(bf16)
    for copy in copies[2:]:
        copy.wait()


def prepare_body(seqs, couple_ref, ids_hbm, valid_ref, bias_ref, avg_ref, base_ref, mask_ref, wq_ref, pick_ref,
                 wf_ref, idc_ref, ids_ref, sem):
    (copy,) = fetch([(ids_hbm, ids_ref)], sem)
    own_i, own_j, chans = couple_ref.shape
    pairs, width, _ = wq_ref.shape
    blocks, lanes, _ = pick_ref.shape
    total = blocks * seqs
    x0 = lax.axis_index("row") * own_i
    z0 = lax.axis_index("col") * own_j

    row = lax.broadcasted_iota(jnp.int32, pick_ref.shape[1:], 0)
    col = lax.broadcasted_iota(jnp.int32, pick_ref.shape[1:], 1)
    unit = row - seqs * width
    place = lax.rem(unit, width) * total + lax.div(unit, width)
    place = jnp.where((unit >= 0) & (unit < seqs * width), col - place, -1)

    def pick(r, carry):
        pick_ref[r] = jnp.where(place == r * seqs, 1.0, 0.0).astype(bf16)
        return carry

    lax.fori_loop(0, blocks, pick, 0)
    wf_ref[...] = avg_ref[...].astype(f32)
    for h in range(pairs):
        both = [wf_ref[pl.ds(2 * h + d, width, stride=width), :] for d in range(2)]
        wq_ref[h] = jnp.concatenate(both, axis=1).astype(bf16)
    copy.wait()
    for j in range(own_j):
        idc_ref[pl.ds(j, 1), :] = jnp.full((1, chans), ids_ref[z0 + j], jnp.int32)
    idc = idc_ref[...]
    valid_t = valid_ref[...].astype(f32).T
    lane = lax.broadcasted_iota(jnp.int32, valid_t.shape, 1)
    same_bias = bias_ref[0:1, :]
    cross_bias = bias_ref[1:2, :]

    def rows(i, carry):
        bias = jnp.where(idc == ids_ref[x0 + i], same_bias, cross_bias)
        base_ref[i] = couple_ref[i].astype(f32) + bias
        column = jnp.sum(jnp.where(lane == i, valid_t, 0.0), axis=1, keepdims=True)
        mask_ref[i] = jnp.broadcast_to(column, (own_j, mask_ref.shape[2])).astype(bf16)
        return carry

    lax.fori_loop(0, own_i, rows, 0, unroll=8)


def pair_body(seqs, width, blocks, turned, *refs):
    msgs = refs[:blocks]
    base_ref, mask_ref, wq_ref, pick_ref, win_ref = refs[blocks : blocks + 5]
    psum_ref, norm_ref, right_ref = refs[blocks + 5 : blocks + 8]
    xl_ref, t_ref, flat_ref = refs[blocks + 8 :]
    own_i, own_j, chans = base_ref.shape
    height, lanes = msgs[0].shape
    total = seqs * blocks
    tri = win_ref.shape[1] // 4
    half = own_i // 2

    for r in range(blocks):
        m = msgs[r][pl.ds(0, own_i), :].astype(f32)
        for s in range(seqs):
            moved = m if s == 0 else pltpu.roll(m, lanes - s * width, 1)
            xl_ref[pl.ds(r * seqs + s, own_i, stride=total), :] = moved[:, :128]
    lhs = xl_ref[:, :width].astype(bf16)

    joined = jnp.concatenate([msg[...] for msg in msgs], axis=1)
    picks = pick_ref[...].reshape(blocks * lanes, width * total)
    rmat = jnp.dot(joined, picks, preferred_element_type=f32)[:own_j].astype(bf16)

    def expand(h, carry):
        out = jnp.dot(lhs, wq_ref[h], preferred_element_type=f32)
        parts = [out[:, d * chans : (d + 1) * chans].reshape(own_i, total, chans) for d in range(2)]
        block = jnp.concatenate(parts, axis=1).astype(bf16)
        where = pl.ds(pl.multiple_of(h * 2 * total, 16), 2 * total)
        t_ref[:, where, :chans] = block[:half]
        t_ref[:, where, chans:] = block[half:]
        return carry

    lax.fori_loop(0, width // 2, expand, 0, unroll=16 if turned else 4)

    step = 4 if half % 4 == 0 else 1

    def rows(b, carry):
        normed = [[], []]
        for g in range(step):
            i = b * step + g
            both = jnp.dot(rmat, t_ref[i], preferred_element_type=f32) * (1.0 / total)
            for side in range(2):
                at = i + side * half
                psum = (base_ref[at] + both[:, side * chans : (side + 1) * chans]).astype(bf16)
                psum_ref[at] = psum
                normed[side].append(standardize(psum.astype(f32)))
        flat = jnp.concatenate(normed[0] + normed[1], axis=0).astype(bf16)
        proj = jnp.dot(flat, win_ref[:, 2 * tri :], preferred_element_type=f32)
        count = step * own_j
        for side in range(2):
            cut = slice(side * count, (side + 1) * count)
            i0 = b * step + side * half
            norm_ref[pl.ds(pl.multiple_of(i0 * own_j, 16), count), :] = flat[cut]
            mask = mask_ref[pl.ds(i0, step)].astype(f32).reshape(count, tri)
            right = mask * sigmoid(proj[cut, :tri]) * proj[cut, tri:]
            if turned:
                flat_ref[pl.ds(pl.multiple_of(i0 * own_j, 8), count), :] = right
            else:
                right_ref[pl.ds(i0, step)] = right.reshape(step, own_j, tri).astype(bf16)
        return carry

    lax.fori_loop(0, half // step, rows, 0, unroll=True)

    def turn(k, carry):
        right_ref[k] = flat_ref[pl.ds(k, own_i, stride=own_j), :].astype(bf16)
        return carry

    if turned:
        lax.fori_loop(0, own_j, turn, 0, unroll=8)


def left_body(norm_ref, mask_ref, win_ref, *outs):
    own_i, own_j, tri = mask_ref.shape
    group = 8 if own_i % 8 == 0 else 1
    at = 0
    for out in outs:
        first = at

        def rows(b, carry):
            i0 = first + b * group
            flat = norm_ref[pl.ds(pl.multiple_of(i0 * own_j, 16), group * own_j), :]
            mask = mask_ref[pl.ds(i0, group)].astype(f32).reshape(group * own_j, tri)
            proj = jnp.dot(flat, win_ref[:, : 2 * tri], preferred_element_type=f32)
            left = mask * sigmoid(proj[:, :tri]) * proj[:, tri:]
            out[pl.ds(b * group, group)] = left.reshape(group, own_j, tri).astype(bf16)
            return carry

        lax.fori_loop(0, out.shape[0] // group, rows, 0, unroll=True)
        at += out.shape[0]


def contract(lf_ref, halves, i0, group):
    step = 8
    acc = (jnp.zeros(halves[0].shape[1:], f32),) * group
    for h, r_ref in enumerate(halves):
        depth = r_ref.shape[0]

        def add(kb, acc):
            k0 = kb * step
            acc = list(acc)
            for d in range(step):
                right = r_ref[k0 + d].astype(f32)
                for t in range(group):
                    acc[t] = acc[t] + lf_ref[i0 + t, pl.ds(h * depth + k0 + d, 1), :] * right
            return tuple(acc)

        acc = lax.fori_loop(0, depth // step, add, acc)
    return acc


def with_right(own_pair, refs, use):
    own, got, p_got, far, p_far = refs
    r, z = lax.axis_index("row"), lax.axis_index("col")
    keeper = (r % 2) == (z % 2)
    near = ((r // 2) == (z // 2)) == own_pair
    table = [
        (near & keeper, own, p_got),
        (near & ~keeper, far, got),
        (~near & keeper, got, far),
        (~near & ~keeper, p_got, p_far),
    ]
    for cond, a, b in table:
        pl.when(cond)(functools.partial(use, (a, b)))


def send_body(first, *refs):
    rights, (l_ref, m_ref, o_ref, lf_ref) = refs[:5], refs[5:]
    count, depth = o_ref.shape[0], l_ref.shape[1]
    group = 8
    lf_ref[:, pl.ds(0, depth), :] = l_ref[pl.ds(first, count)].astype(f32)
    lf_ref[:, pl.ds(depth, depth), :] = m_ref[pl.ds(first, count)].astype(f32)

    def use(halves):
        def rows(b, carry):
            acc = contract(lf_ref, halves, b * group, group)
            for t in range(group):
                o_ref[b * group + t] = acc[t].astype(bf16)
            return carry

        lax.fori_loop(0, count // group, rows, 0)

    with_right(False, rights, use)


def keep_body(cuts, *refs):
    rights, refs = refs[:5], refs[5:]
    lefts, mets = refs[:cuts], refs[cuts : 2 * cuts]
    norm_ref, wgate_ref, o_ref, gate_ref, lf_ref = refs[2 * cuts :]
    own_i, depth, chans = o_ref.shape
    at = 0
    for l_ref, m_ref in zip(lefts, mets):
        n = l_ref.shape[0]
        lf_ref[pl.ds(at, n), pl.ds(0, depth), :] = l_ref[...].astype(f32)
        lf_ref[pl.ds(at, n), pl.ds(depth, depth), :] = m_ref[...].astype(f32)
        at += n
    group = 8

    def gates(b, carry):
        flat = norm_ref[pl.ds(pl.multiple_of(b * group * depth, 16), group * depth), :]
        gate = sigmoid(jnp.dot(flat, wgate_ref[...], preferred_element_type=f32))
        gate_ref[pl.ds(b * group, group)] = gate.reshape(group, depth, -1)
        return carry

    lax.fori_loop(0, own_i // group, gates, 0, unroll=True)

    def use(halves):
        def rows(b, carry):
            acc = contract(lf_ref, halves, b * group, group)
            for t in range(group):
                o_ref[b * group + t] = acc[t]
            return carry

        lax.fori_loop(0, own_i // group, rows, 0)

    with_right(True, rights, use)


def join_body(first, parts, own_ref, psum_ref, gate_ref, w_ref, *refs):
    sums, (out_hbm, done_ref, sem) = refs[:parts], refs[-3:]
    count, extent, chans = done_ref.shape
    group = 8
    at = 0
    for sum_ref in sums:
        start = at

        def rows(b, carry):
            here = pl.ds(start + b * group, group)
            there = pl.ds(first + start + b * group, group)
            mixed = own_ref[there] + sum_ref[pl.ds(b * group, group)].astype(f32)
            normed = standardize(mixed).reshape(group * extent, -1).astype(bf16)
            update = jnp.dot(normed, w_ref[...], preferred_element_type=f32).reshape(group, extent, -1)
            done_ref[here] = (psum_ref[there].astype(f32) + gate_ref[there] * update).astype(bf16)
            return carry

        lax.fori_loop(0, sum_ref.shape[0] // group, rows, 0, unroll=True)
        at += sum_ref.shape[0]
    copy = pltpu.make_async_copy(done_ref, out_hbm.at[pl.ds(first, count)], sem)
    copy.start()
    copy.wait()


def triangle_body(l_ref, r_ref, o_ref, lf_ref, flat_ref, rk_ref):
    own_i, depth, chans = l_ref.shape
    extent = r_ref.shape[0]
    group = 8 if own_i % 8 == 0 else 1

    @pl.when(pl.program_id(0) == 0)
    def _():
        lf_ref[...] = l_ref[...].astype(f32)

    def widen(j, carry):
        flat_ref[pl.ds(pl.multiple_of(j * depth, 8), depth), :] = r_ref[j].astype(f32)
        return carry

    lax.fori_loop(0, extent, widen, 0)

    def turn(k, carry):
        rk_ref[k] = flat_ref[pl.ds(k, extent, stride=depth), :]
        return carry

    lax.fori_loop(0, depth, turn, 0)

    def rows(b, carry):
        i0 = b * group
        acc = contract(lf_ref, [rk_ref], i0, group)
        for t in range(group):
            o_ref[0, i0 + t] = acc[t].astype(bf16)
        return carry

    lax.fori_loop(0, own_i // group, rows, 0)


def finish_body(sum_ref, psum_ref, norm_ref, wgate_ref, w_ref, out_ref):
    parts, own_i, extent, chans = sum_ref.shape
    own_j = psum_ref.shape[1]

    def row(i, carry):
        flat = norm_ref[pl.ds(pl.multiple_of(i * own_j, 16), own_j), :]
        gate = sigmoid(jnp.dot(flat, wgate_ref[...], preferred_element_type=f32))
        normed = [standardize(sum_ref[part, i].astype(f32)) for part in range(parts)]
        normed = jnp.concatenate(normed, axis=0).astype(bf16)
        update = jnp.dot(normed, w_ref[...], preferred_element_type=f32)
        out_ref[i] = (psum_ref[i].astype(f32) + gate * update).astype(bf16)
        return carry

    lax.fori_loop(0, own_i, row, 0)


def gathered_plan(left, right, psum, norm, w_gate, w_final):
    own_i, own_j, chans = psum.shape
    rows = lax.axis_size("row")
    tri = w_final.shape[0]
    right_all = lax.all_gather(right, "row", axis=0, tiled=True)
    partial = pl.pallas_call(
        triangle_body,
        grid=(rows,),
        out_shape=jax.ShapeDtypeStruct((rows, own_i, own_i, tri), bf16),
        in_specs=[
            pl.BlockSpec((own_i, own_j, tri), lambda r: (0, 0, 0)),
            pl.BlockSpec((own_i, own_j, tri), lambda r: (r, 0, 0)),
        ],
        out_specs=pl.BlockSpec((1, own_i, own_i, tri), lambda r: (r, 0, 0, 0)),
        scratch_shapes=[
            pltpu.VMEM((own_i, own_j, tri), f32),
            pltpu.VMEM((own_i * own_j, tri), f32),
            pltpu.VMEM((own_j, own_i, tri), f32),
        ],
        compiler_params=limit(56),
        name="triangle",
    )(left, right_all)
    summed = lax.psum_scatter(partial, "col", scatter_dimension=0, tiled=True)
    return pl.pallas_call(
        finish_body,
        out_shape=jax.ShapeDtypeStruct((own_i, own_j, chans), bf16),
        in_specs=[VMEM] * 5,
        out_specs=VMEM,
        compiler_params=limit(56),
        name="finish",
    )(summed, psum, norm, w_gate, w_final)


def paired_plan(lefts, right, psum, norm, w_gate, w_final):
    own_i, own_j, chans = psum.shape
    tri = w_final.shape[0]
    cuts = len(lefts)
    cells = [(r, z) for r in range(4) for z in range(4)]

    def move(value, where, step):
        pairs = [(r * 4 + z, step(r, z)) for r, z in cells if where(r, z)]
        pairs = [(src, r * 4 + z) for src, (r, z) in pairs]
        return lax.ppermute(value, ("row", "col"), pairs)

    every = lambda r, z: True
    keeper = lambda r, z: r % 2 == z % 2
    got = move(right, every, lambda r, z: (r ^ 2, z) if keeper(r, z) else (r ^ 1, z ^ 1))
    far = move(right, every, lambda r, z: (r ^ 1, z) if keeper(r, z) else (r ^ 2, z ^ 1))
    mets = [move(left, every, lambda r, z: (r, z ^ 1)) for left in lefts]
    got, far, mets[0] = lax.optimization_barrier((got, far, mets[0]))
    p_got = move(got, every, lambda r, z: (r ^ 1, z))
    p_far = move(far, every, lambda r, z: (r ^ 1, z))
    rights = (right, got, p_got, far, p_far)

    sums = []
    chunks = [(n, m, 0, 8) for n, left in enumerate(lefts) for m in range(0, left.shape[0], 8)]
    for at, first, _, n in chunks:
        part = pl.pallas_call(
            functools.partial(send_body, first),
            out_shape=jax.ShapeDtypeStruct((n, own_j, tri), bf16),
            in_specs=[VMEM] * 7,
            out_specs=VMEM,
            scratch_shapes=[pltpu.VMEM((n, 2 * own_j, tri), f32)],
            compiler_params=limit(8),
            cost_estimate=cost(0.12 * n + 0.4),
            name="send_sums",
        )(*rights, lefts[at], mets[at])
        sums.append(move(part, every, lambda r, z: (r, z ^ 2)))

    own, gate = pl.pallas_call(
        functools.partial(keep_body, cuts),
        out_shape=[jax.ShapeDtypeStruct((own_i, own_j, tri), f32),
                   jax.ShapeDtypeStruct((own_i, own_j, chans), f32)],
        in_specs=[VMEM] * (5 + 2 * cuts + 2),
        out_specs=[VMEM] * 2,
        scratch_shapes=[pltpu.VMEM((own_i, 2 * own_j, tri), f32)],
        compiler_params=limit(12),
        cost_estimate=cost(6),
        name="keep_sums",
    )(*rights, *lefts, *mets, norm, w_gate)
    out = []
    for first, n in ((0, 16), (16, own_i - 16)):
        parts = sums[first // 8 : (first + n) // 8]
        out = [pl.pallas_call(
            functools.partial(join_body, first, len(parts)),
            out_shape=jax.ShapeDtypeStruct((own_i, own_j, chans), bf16),
            in_specs=[VMEM] * (4 + len(parts)) + [HBM] * len(out),
            out_specs=HBM,
            scratch_shapes=[pltpu.VMEM((n, own_j, chans), bf16), pltpu.SemaphoreType.DMA],
            input_output_aliases={4 + len(parts): 0} if out else {},
            compiler_params=limit(8),
            cost_estimate=cost(0.06 * n),
            name="join",
        )(own, psum, gate, w_final, *parts, *out)]
    return out[0]


def shards(homolog, couple, ids, valid, bias, factors, average, w_in, w_gate, w_final):
    rows, cols = lax.axis_size("row"), lax.axis_size("col")
    own_seqs, residues, depth = homolog.shape
    own_i, own_j, chans = couple.shape
    width = factors.shape[1] // 2
    tri = w_final.shape[0]
    total = own_seqs * rows
    lanes = round_up(2 * own_seqs * width, 128)
    height = round_up(max(own_i, own_j), 16)
    paired = rows == 4 and cols == 4 and own_i == own_j and own_i % 8 == 0 and own_i > 32
    scale = 1 if paired else 8

    later = (average, valid, bias, couple)
    *msgs, average, valid, bias, couple = pl.pallas_call(
        functools.partial(align_body, own_i, own_j, rows),
        out_shape=[jax.ShapeDtypeStruct((height, lanes), bf16)] * rows
        + [jax.ShapeDtypeStruct(x.shape, x.dtype) for x in later],
        in_specs=[HBM] * 6,
        out_specs=[VMEM] * (rows + 4),
        scratch_shapes=[
            pltpu.VMEM(homolog.shape, bf16),
            pltpu.VMEM((2 * width, depth), bf16),
            pltpu.VMEM((own_seqs * residues, 2 * width), f32),
            pltpu.SemaphoreType.DMA((6,)),
        ],
        compiler_params=limit(8, scale),
        cost_estimate=cost(1.5),
        name="align",
    )(hold(homolog), hold(factors.T), *map(hold, later))
    for d in reversed(range(1, rows)):
        msgs[d] = lax.ppermute(msgs[d], "row", [(r, r ^ d) for r in range(rows)])

    base, mask, wq, pick = pl.pallas_call(
        functools.partial(prepare_body, own_seqs),
        out_shape=[jax.ShapeDtypeStruct((own_i, own_j, chans), f32),
                   jax.ShapeDtypeStruct((own_i, own_j, tri), bf16),
                   jax.ShapeDtypeStruct((width // 2, width, 2 * chans), bf16),
                   jax.ShapeDtypeStruct((rows, lanes, width * total), bf16)],
        in_specs=[VMEM, HBM, VMEM, VMEM, VMEM],
        out_specs=[VMEM] * 4,
        scratch_shapes=[
            pltpu.VMEM(average.shape, f32),
            pltpu.VMEM((own_j, chans), jnp.int32),
            pltpu.SMEM(ids.shape, jnp.int32),
            pltpu.SemaphoreType.DMA((1,)),
        ],
        compiler_params=limit(8, scale),
        cost_estimate=cost(2),
        name="prepare",
    )(couple, hold(ids), valid, bias, average)

    extents = (own_j, own_i) if paired else (own_i, own_j)
    psum, norm, right = pl.pallas_call(
        functools.partial(pair_body, own_seqs, width, rows, paired),
        out_shape=[jax.ShapeDtypeStruct((own_i, own_j, chans), bf16),
                   jax.ShapeDtypeStruct((own_i * own_j, chans), bf16),
                   jax.ShapeDtypeStruct(extents + (tri,), bf16)],
        in_specs=[VMEM] * (rows + 5),
        out_specs=[VMEM] * 3,
        scratch_shapes=[
            pltpu.VMEM((own_i * total, 128), f32),
            pltpu.VMEM((own_i // 2, width * total, 2 * chans), bf16),
            pltpu.VMEM((own_i * own_j, tri), f32),
        ],
        compiler_params=limit(16, scale),
        cost_estimate=cost(4.5),
        name="pair",
    )(*msgs, base, mask, wq, pick, w_in)

    cuts = [8, 16, own_i - 24] if paired else [own_i]
    lefts = pl.pallas_call(
        left_body,
        out_shape=[jax.ShapeDtypeStruct((n, own_j, tri), bf16) for n in cuts],
        in_specs=[VMEM] * 3,
        out_specs=[VMEM] * len(cuts),
        compiler_params=limit(8, scale),
        cost_estimate=cost(1),
        name="left",
    )(norm, mask, w_in)
    if paired:
        return paired_plan(lefts, right, psum, norm, w_gate, w_final)
    return gathered_plan(lefts[0], right, psum, norm, w_gate, w_final)


def solution(mesh):
    placed = (
        P(("grp", "row"), None, None),
        P(("grp", "row"), "col", None),
        P("grp"),
        P(("grp", "row"), "col"),
        P(),
        P(),
        P(),
        P(),
        P(),
        P(),
    )
    return jax.shard_map(
        shards,
        mesh=mesh,
        in_specs=placed,
        out_specs=P(("grp", "row"), "col", None),
        check_vma=False,
    )
```

```python
import functools

import jax
import jax.numpy as jnp
from jax import lax
from jax.experimental import pallas as pl
from jax.experimental.pallas import tpu as pltpu
from jax.sharding import PartitionSpec as P

eps = 1e-05
f32 = jnp.float32
bf16 = jnp.bfloat16
VMEM = pl.BlockSpec(memory_space=pltpu.VMEM)
SMEM = pl.BlockSpec(memory_space=pltpu.SMEM)
HBM = pl.BlockSpec(memory_space=pltpu.HBM)


def limit(mib, scale=1):
    return pltpu.CompilerParams(vmem_limit_bytes=min(56, mib * scale) * 1024 * 1024)


def round_up(n, m):
    return (n + m - 1) // m * m


def cost(us):
    return pl.CostEstimate(flops=0, bytes_accessed=int(us * 3.69e6), transcendentals=0)


def hold(x):
    return pltpu.with_memory_space_constraint(x, pltpu.HBM)


def fetch(pairs, sem):
    copies = [pltpu.make_async_copy(src, dst, sem.at[n]) for n, (src, dst) in enumerate(pairs)]
    for copy in copies:
        copy.start()
    return copies


def standardize(values):
    centre = values - jnp.mean(values, axis=-1, keepdims=True)
    spread = jnp.mean(centre * centre, axis=-1, keepdims=True)
    return centre * lax.rsqrt(spread + eps)


def sigmoid(v):
    return 0.5 * jnp.tanh(0.5 * v) + 0.5


def align_body(own_i, own_j, count, x_hbm, w_hbm, *refs):
    later, outs, refs = refs[:4], refs[4 : 4 + count], refs[4 + count :]
    brought, (x_ref, w_ref, y_ref, sem) = refs[:4], refs[4:]
    copies = fetch([(x_hbm, x_ref), (w_hbm, w_ref), *zip(later, brought)], sem)
    seqs, residues, depth = x_ref.shape
    width = w_ref.shape[0] // 2
    height, lanes = outs[0].shape
    me = lax.axis_index("row")
    z = lax.axis_index("col")
    copies[0].wait()
    x = x_ref[...].astype(f32).reshape(seqs * residues, depth)
    normed = standardize(x).astype(bf16)
    copies[1].wait()
    y_ref[...] = lax.dot_general(
        normed, w_ref[...], (((1,), (1,)), ((), ())), preferred_element_type=f32
    )
    start = pl.multiple_of(z * own_j, 8)

    def tall(v):
        gap = height - v.shape[0]
        return jnp.concatenate([v, jnp.zeros((gap, v.shape[1]), f32)], axis=0) if gap else v

    right = [tall(y_ref[pl.ds(s * residues + start, own_j), width:]) for s in range(seqs)]
    gap = lanes - 2 * seqs * width
    right += [jnp.zeros((height, gap), f32)] if gap else []
    for d, out in enumerate(outs):
        first = pl.multiple_of((me ^ d) * own_i, 8)
        left = [tall(y_ref[pl.ds(s * residues + first, own_i), :width]) for s in range(seqs)]
        out[...] = jnp.concatenate(left + right, axis=1).astype(bf16)
    for copy in copies[2:]:
        copy.wait()


def prepare_body(seqs, couple_ref, ids_hbm, valid_ref, bias_ref, avg_ref, base_ref, mask_ref, wq_ref, pick_ref,
                 wf_ref, idc_ref, ids_ref, sem):
    (copy,) = fetch([(ids_hbm, ids_ref)], sem)
    own_i, own_j, chans = couple_ref.shape
    pairs, width, _ = wq_ref.shape
    blocks, lanes, _ = pick_ref.shape
    total = blocks * seqs
    x0 = lax.axis_index("row") * own_i
    z0 = lax.axis_index("col") * own_j

    row = lax.broadcasted_iota(jnp.int32, pick_ref.shape[1:], 0)
    col = lax.broadcasted_iota(jnp.int32, pick_ref.shape[1:], 1)
    unit = row - seqs * width
    place = lax.rem(unit, width) * total + lax.div(unit, width)
    place = jnp.where((unit >= 0) & (unit < seqs * width), col - place, -1)

    def pick(r, carry):
        pick_ref[r] = jnp.where(place == r * seqs, 1.0, 0.0).astype(bf16)
        return carry

    lax.fori_loop(0, blocks, pick, 0)
    wf_ref[...] = avg_ref[...].astype(f32)
    for h in range(pairs):
        both = [wf_ref[pl.ds(2 * h + d, width, stride=width), :] for d in range(2)]
        wq_ref[h] = jnp.concatenate(both, axis=1).astype(bf16)
    copy.wait()
    for j in range(own_j):
        idc_ref[pl.ds(j, 1), :] = jnp.full((1, chans), ids_ref[z0 + j], jnp.int32)
    idc = idc_ref[...]
    valid_t = valid_ref[...].astype(f32).T
    lane = lax.broadcasted_iota(jnp.int32, valid_t.shape, 1)
    same_bias = bias_ref[0:1, :]
    cross_bias = bias_ref[1:2, :]

    def rows(i, carry):
        bias = jnp.where(idc == ids_ref[x0 + i], same_bias, cross_bias)
        base_ref[i] = couple_ref[i].astype(f32) + bias
        column = jnp.sum(jnp.where(lane == i, valid_t, 0.0), axis=1, keepdims=True)
        mask_ref[i] = jnp.broadcast_to(column, (own_j, mask_ref.shape[2])).astype(bf16)
        return carry

    lax.fori_loop(0, own_i, rows, 0, unroll=8)


def pair_body(seqs, width, blocks, turned, *refs):
    msgs = refs[:blocks]
    base_ref, mask_ref, wq_ref, pick_ref, win_ref = refs[blocks : blocks + 5]
    psum_ref, norm_ref, right_ref = refs[blocks + 5 : blocks + 8]
    xl_ref, t_ref, flat_ref = refs[blocks + 8 :]
    own_i, own_j, chans = base_ref.shape
    height, lanes = msgs[0].shape
    total = seqs * blocks
    tri = win_ref.shape[1] // 4
    half = own_i // 2

    for r in range(blocks):
        m = msgs[r][pl.ds(0, own_i), :].astype(f32)
        for s in range(seqs):
            moved = m if s == 0 else pltpu.roll(m, lanes - s * width, 1)
            xl_ref[pl.ds(r * seqs + s, own_i, stride=total), :] = moved[:, :128]
    lhs = xl_ref[:, :width].astype(bf16)

    joined = jnp.concatenate([msg[...] for msg in msgs], axis=1)
    picks = pick_ref[...].reshape(blocks * lanes, width * total)
    rmat = jnp.dot(joined, picks, preferred_element_type=f32)[:own_j].astype(bf16)

    def expand(h, carry):
        out = jnp.dot(lhs, wq_ref[h], preferred_element_type=f32)
        parts = [out[:, d * chans : (d + 1) * chans].reshape(own_i, total, chans) for d in range(2)]
        block = jnp.concatenate(parts, axis=1).astype(bf16)
        where = pl.ds(pl.multiple_of(h * 2 * total, 16), 2 * total)
        t_ref[:, where, :chans] = block[:half]
        t_ref[:, where, chans:] = block[half:]
        return carry

    lax.fori_loop(0, width // 2, expand, 0, unroll=16 if turned else 4)

    step = 4 if half % 4 == 0 else 1

    def rows(b, carry):
        normed = [[], []]
        for g in range(step):
            i = b * step + g
            both = jnp.dot(rmat, t_ref[i], preferred_element_type=f32) * (1.0 / total)
            for side in range(2):
                at = i + side * half
                psum = (base_ref[at] + both[:, side * chans : (side + 1) * chans]).astype(bf16)
                psum_ref[at] = psum
                normed[side].append(standardize(psum.astype(f32)))
        flat = jnp.concatenate(normed[0] + normed[1], axis=0).astype(bf16)
        proj = jnp.dot(flat, win_ref[:, 2 * tri :], preferred_element_type=f32)
        count = step * own_j
        for side in range(2):
            cut = slice(side * count, (side + 1) * count)
            i0 = b * step + side * half
            norm_ref[pl.ds(pl.multiple_of(i0 * own_j, 16), count), :] = flat[cut]
            mask = mask_ref[pl.ds(i0, step)].astype(f32).reshape(count, tri)
            right = mask * sigmoid(proj[cut, :tri]) * proj[cut, tri:]
            if turned:
                flat_ref[pl.ds(pl.multiple_of(i0 * own_j, 8), count), :] = right
            else:
                right_ref[pl.ds(i0, step)] = right.reshape(step, own_j, tri).astype(bf16)
        return carry

    lax.fori_loop(0, half // step, rows, 0, unroll=True)

    def turn(k, carry):
        right_ref[k] = flat_ref[pl.ds(k, own_i, stride=own_j), :].astype(bf16)
        return carry

    if turned:
        lax.fori_loop(0, own_j, turn, 0, unroll=8)


def left_body(norm_ref, mask_ref, win_ref, *outs):
    own_i, own_j, tri = mask_ref.shape
    group = 8 if own_i % 8 == 0 else 1
    at = 0
    for out in outs:
        first = at

        def rows(b, carry):
            i0 = first + b * group
            flat = norm_ref[pl.ds(pl.multiple_of(i0 * own_j, 16), group * own_j), :]
            mask = mask_ref[pl.ds(i0, group)].astype(f32).reshape(group * own_j, tri)
            proj = jnp.dot(flat, win_ref[:, : 2 * tri], preferred_element_type=f32)
            left = mask * sigmoid(proj[:, :tri]) * proj[:, tri:]
            out[pl.ds(b * group, group)] = left.reshape(group, own_j, tri).astype(bf16)
            return carry

        lax.fori_loop(0, out.shape[0] // group, rows, 0, unroll=True)
        at += out.shape[0]


def contract(lf_ref, halves, i0, group):
    step = 8
    acc = (jnp.zeros(halves[0].shape[1:], f32),) * group
    for h, r_ref in enumerate(halves):
        depth = r_ref.shape[0]

        def add(kb, acc):
            k0 = kb * step
            acc = list(acc)
            for d in range(step):
                right = r_ref[k0 + d].astype(f32)
                for t in range(group):
                    acc[t] = acc[t] + lf_ref[i0 + t, pl.ds(h * depth + k0 + d, 1), :] * right
            return tuple(acc)

        acc = lax.fori_loop(0, depth // step, add, acc)
    return acc


def with_right(own_pair, refs, use):
    own, got, p_got, far, p_far = refs
    r, z = lax.axis_index("row"), lax.axis_index("col")
    keeper = (r % 2) == (z % 2)
    near = ((r // 2) == (z // 2)) == own_pair
    table = [
        (near & keeper, own, p_got),
        (near & ~keeper, far, got),
        (~near & keeper, got, far),
        (~near & ~keeper, p_got, p_far),
    ]
    for cond, a, b in table:
        pl.when(cond)(functools.partial(use, (a, b)))


def send_body(first, *refs):
    rights, (l_ref, m_ref, o_ref, lf_ref) = refs[:5], refs[5:]
    count, depth = o_ref.shape[0], l_ref.shape[1]
    group = 8
    lf_ref[:, pl.ds(0, depth), :] = l_ref[pl.ds(first, count)].astype(f32)
    lf_ref[:, pl.ds(depth, depth), :] = m_ref[pl.ds(first, count)].astype(f32)

    def use(halves):
        def rows(b, carry):
            acc = contract(lf_ref, halves, b * group, group)
            for t in range(group):
                o_ref[b * group + t] = acc[t].astype(bf16)
            return carry

        lax.fori_loop(0, count // group, rows, 0)

    with_right(False, rights, use)


def keep_body(first, *refs):
    rights, (l_ref, m_ref, norm_ref, wgate_ref, o_ref, gate_ref, lf_ref) = refs[:5], refs[5:]
    count, depth, chans = o_ref.shape
    group = 8
    lf_ref[:, pl.ds(0, depth), :] = l_ref[...].astype(f32)
    lf_ref[:, pl.ds(depth, depth), :] = m_ref[...].astype(f32)

    def gates(b, carry):
        at = pl.multiple_of((first + b * group) * depth, 16)
        flat = norm_ref[pl.ds(at, group * depth), :]
        gate = sigmoid(jnp.dot(flat, wgate_ref[...], preferred_element_type=f32))
        gate_ref[pl.ds(b * group, group)] = gate.reshape(group, depth, -1)
        return carry

    lax.fori_loop(0, count // group, gates, 0, unroll=True)

    def use(halves):
        def rows(b, carry):
            acc = contract(lf_ref, halves, b * group, group)
            for t in range(group):
                o_ref[b * group + t] = acc[t]
            return carry

        lax.fori_loop(0, count // group, rows, 0)

    with_right(True, rights, use)


def join_body(first, parts, own_ref, psum_ref, gate_ref, w_ref, *refs):
    sums, (out_hbm, done_ref, sem) = refs[:parts], refs[-3:]
    count, extent, chans = done_ref.shape
    group = 8
    at = 0
    for sum_ref in sums:
        start = at

        def rows(b, carry):
            here = pl.ds(start + b * group, group)
            there = pl.ds(first + start + b * group, group)
            mixed = own_ref[here] + sum_ref[pl.ds(b * group, group)].astype(f32)
            normed = standardize(mixed).reshape(group * extent, -1).astype(bf16)
            update = jnp.dot(normed, w_ref[...], preferred_element_type=f32).reshape(group, extent, -1)
            done_ref[here] = (psum_ref[there].astype(f32) + gate_ref[here] * update).astype(bf16)
            return carry

        lax.fori_loop(0, sum_ref.shape[0] // group, rows, 0, unroll=True)
        at += sum_ref.shape[0]
    copy = pltpu.make_async_copy(done_ref, out_hbm.at[pl.ds(first, count)], sem)
    copy.start()
    copy.wait()


def triangle_body(l_ref, r_ref, o_ref, lf_ref, flat_ref, rk_ref):
    own_i, depth, chans = l_ref.shape
    extent = r_ref.shape[0]
    group = 8 if own_i % 8 == 0 else 1

    @pl.when(pl.program_id(0) == 0)
    def _():
        lf_ref[...] = l_ref[...].astype(f32)

    def widen(j, carry):
        flat_ref[pl.ds(pl.multiple_of(j * depth, 8), depth), :] = r_ref[j].astype(f32)
        return carry

    lax.fori_loop(0, extent, widen, 0)

    def turn(k, carry):
        rk_ref[k] = flat_ref[pl.ds(k, extent, stride=depth), :]
        return carry

    lax.fori_loop(0, depth, turn, 0)

    def rows(b, carry):
        i0 = b * group
        acc = contract(lf_ref, [rk_ref], i0, group)
        for t in range(group):
            o_ref[0, i0 + t] = acc[t].astype(bf16)
        return carry

    lax.fori_loop(0, own_i // group, rows, 0)


def finish_body(sum_ref, psum_ref, norm_ref, wgate_ref, w_ref, out_ref):
    parts, own_i, extent, chans = sum_ref.shape
    own_j = psum_ref.shape[1]

    def row(i, carry):
        flat = norm_ref[pl.ds(pl.multiple_of(i * own_j, 16), own_j), :]
        gate = sigmoid(jnp.dot(flat, wgate_ref[...], preferred_element_type=f32))
        normed = [standardize(sum_ref[part, i].astype(f32)) for part in range(parts)]
        normed = jnp.concatenate(normed, axis=0).astype(bf16)
        update = jnp.dot(normed, w_ref[...], preferred_element_type=f32)
        out_ref[i] = (psum_ref[i].astype(f32) + gate * update).astype(bf16)
        return carry

    lax.fori_loop(0, own_i, row, 0)


def gathered_plan(left, right, psum, norm, w_gate, w_final):
    own_i, own_j, chans = psum.shape
    rows = lax.axis_size("row")
    tri = w_final.shape[0]
    right_all = lax.all_gather(right, "row", axis=0, tiled=True)
    partial = pl.pallas_call(
        triangle_body,
        grid=(rows,),
        out_shape=jax.ShapeDtypeStruct((rows, own_i, own_i, tri), bf16),
        in_specs=[
            pl.BlockSpec((own_i, own_j, tri), lambda r: (0, 0, 0)),
            pl.BlockSpec((own_i, own_j, tri), lambda r: (r, 0, 0)),
        ],
        out_specs=pl.BlockSpec((1, own_i, own_i, tri), lambda r: (r, 0, 0, 0)),
        scratch_shapes=[
            pltpu.VMEM((own_i, own_j, tri), f32),
            pltpu.VMEM((own_i * own_j, tri), f32),
            pltpu.VMEM((own_j, own_i, tri), f32),
        ],
        compiler_params=limit(56),
        name="triangle",
    )(left, right_all)
    summed = lax.psum_scatter(partial, "col", scatter_dimension=0, tiled=True)
    return pl.pallas_call(
        finish_body,
        out_shape=jax.ShapeDtypeStruct((own_i, own_j, chans), bf16),
        in_specs=[VMEM] * 5,
        out_specs=VMEM,
        compiler_params=limit(56),
        name="finish",
    )(summed, psum, norm, w_gate, w_final)


def paired_plan(lefts, right, psum, norm, w_gate, w_final):
    own_i, own_j, chans = psum.shape
    tri = w_final.shape[0]
    cuts = len(lefts)
    cells = [(r, z) for r in range(4) for z in range(4)]

    def move(value, where, step):
        pairs = [(r * 4 + z, step(r, z)) for r, z in cells if where(r, z)]
        pairs = [(src, r * 4 + z) for src, (r, z) in pairs]
        return lax.ppermute(value, ("row", "col"), pairs)

    every = lambda r, z: True
    keeper = lambda r, z: r % 2 == z % 2
    got = move(right, every, lambda r, z: (r ^ 2, z) if keeper(r, z) else (r ^ 1, z ^ 1))
    far = move(right, every, lambda r, z: (r ^ 1, z) if keeper(r, z) else (r ^ 2, z ^ 1))
    mets = [move(left, every, lambda r, z: (r, z ^ 1)) for left in lefts[:2]]
    got, far, mets[0] = lax.optimization_barrier((got, far, mets[0]))
    p_got = move(got, every, lambda r, z: (r ^ 1, z))
    p_far = move(far, every, lambda r, z: (r ^ 1, z))
    rights = (right, got, p_got, far, p_far)

    def send(left, met, first):
        part = pl.pallas_call(
            functools.partial(send_body, first),
            out_shape=jax.ShapeDtypeStruct((8, own_j, tri), bf16),
            in_specs=[VMEM] * 7,
            out_specs=VMEM,
            scratch_shapes=[pltpu.VMEM((8, 2 * own_j, tri), f32)],
            compiler_params=limit(8),
            cost_estimate=cost(1),
            name="send_sums",
        )(*rights, left, met)
        return part, move(part, every, lambda r, z: (r, z ^ 2))

    def keep(left, met, first):
        n = left.shape[0]
        return pl.pallas_call(
            functools.partial(keep_body, first),
            out_shape=[jax.ShapeDtypeStruct((n, own_j, tri), f32),
                       jax.ShapeDtypeStruct((n, own_j, chans), f32)],
            in_specs=[VMEM] * 9,
            out_specs=[VMEM] * 2,
            scratch_shapes=[pltpu.VMEM((n, 2 * own_j, tri), f32)],
            compiler_params=limit(12),
            cost_estimate=cost(0.13 * n),
            name="keep_sums",
        )(*rights, left, met, norm, w_gate)

    sums, kept = [], []
    at = 0
    for n, left in enumerate(lefts):
        met = mets[n]
        if kept:
            met, _ = lax.optimization_barrier((met, kept[-1][0]))
        parts = [send(left, met, m) for m in range(0, left.shape[0], 8)]
        sums.append([there for _, there in parts])
        if len(mets) < cuts:
            later, _ = lax.optimization_barrier((lefts[n + 2], parts[0][0]))
            mets.append(move(later, every, lambda r, z: (r, z ^ 1)))
        kept.append(keep(left, met, at))
        at += left.shape[0]

    out = []
    at = 0
    for (own, gate), parts in zip(kept, sums):
        n = own.shape[0]
        out = [pl.pallas_call(
            functools.partial(join_body, at, len(parts)),
            out_shape=jax.ShapeDtypeStruct((own_i, own_j, chans), bf16),
            in_specs=[VMEM] * (4 + len(parts)) + [HBM] * len(out),
            out_specs=HBM,
            scratch_shapes=[pltpu.VMEM((n, own_j, chans), bf16), pltpu.SemaphoreType.DMA],
            input_output_aliases={4 + len(parts): 0} if out else {},
            compiler_params=limit(8),
            cost_estimate=cost(0.06 * n),
            name="join",
        )(own, psum, gate, w_final, *parts, *out)]
        at += n
    return out[0]


def shards(homolog, couple, ids, valid, bias, factors, average, w_in, w_gate, w_final):
    rows, cols = lax.axis_size("row"), lax.axis_size("col")
    own_seqs, residues, depth = homolog.shape
    own_i, own_j, chans = couple.shape
    width = factors.shape[1] // 2
    tri = w_final.shape[0]
    total = own_seqs * rows
    lanes = round_up(2 * own_seqs * width, 128)
    height = round_up(max(own_i, own_j), 16)
    paired = rows == 4 and cols == 4 and own_i == own_j and own_i % 8 == 0 and own_i > 32
    scale = 1 if paired else 8

    later = (average, valid, bias, couple)
    *msgs, average, valid, bias, couple = pl.pallas_call(
        functools.partial(align_body, own_i, own_j, rows),
        out_shape=[jax.ShapeDtypeStruct((height, lanes), bf16)] * rows
        + [jax.ShapeDtypeStruct(x.shape, x.dtype) for x in later],
        in_specs=[HBM] * 6,
        out_specs=[VMEM] * (rows + 4),
        scratch_shapes=[
            pltpu.VMEM(homolog.shape, bf16),
            pltpu.VMEM((2 * width, depth), bf16),
            pltpu.VMEM((own_seqs * residues, 2 * width), f32),
            pltpu.SemaphoreType.DMA((6,)),
        ],
        compiler_params=limit(8, scale),
        cost_estimate=cost(1.5),
        name="align",
    )(hold(homolog), hold(factors.T), *map(hold, later))
    msgs = [msgs[0]] + [
        lax.ppermute(msgs[d], "row", [(r, r ^ d) for r in range(rows)])
        for d in reversed(range(1, rows))
    ]

    base, mask, wq, pick = pl.pallas_call(
        functools.partial(prepare_body, own_seqs),
        out_shape=[jax.ShapeDtypeStruct((own_i, own_j, chans), f32),
                   jax.ShapeDtypeStruct((own_i, own_j, tri), bf16),
                   jax.ShapeDtypeStruct((width // 2, width, 2 * chans), bf16),
                   jax.ShapeDtypeStruct((rows, lanes, width * total), bf16)],
        in_specs=[VMEM, HBM, VMEM, VMEM, VMEM],
        out_specs=[VMEM] * 4,
        scratch_shapes=[
            pltpu.VMEM(average.shape, f32),
            pltpu.VMEM((own_j, chans), jnp.int32),
            pltpu.SMEM(ids.shape, jnp.int32),
            pltpu.SemaphoreType.DMA((1,)),
        ],
        compiler_params=limit(8, scale),
        cost_estimate=cost(2),
        name="prepare",
    )(couple, hold(ids), valid, bias, average)

    extents = (own_j, own_i) if paired else (own_i, own_j)
    psum, norm, right = pl.pallas_call(
        functools.partial(pair_body, own_seqs, width, rows, paired),
        out_shape=[jax.ShapeDtypeStruct((own_i, own_j, chans), bf16),
                   jax.ShapeDtypeStruct((own_i * own_j, chans), bf16),
                   jax.ShapeDtypeStruct(extents + (tri,), bf16)],
        in_specs=[VMEM] * (rows + 5),
        out_specs=[VMEM] * 3,
        scratch_shapes=[
            pltpu.VMEM((own_i * total, 128), f32),
            pltpu.VMEM((own_i // 2, width * total, 2 * chans), bf16),
            pltpu.VMEM((own_i * own_j, tri), f32),
        ],
        compiler_params=limit(16, scale),
        cost_estimate=cost(4.5),
        name="pair",
    )(*msgs, base, mask, wq, pick, w_in)

    cuts = [8, 16, own_i - 24] if paired else [own_i]
    lefts = pl.pallas_call(
        left_body,
        out_shape=[jax.ShapeDtypeStruct((n, own_j, tri), bf16) for n in cuts],
        in_specs=[VMEM] * 3,
        out_specs=[VMEM] * len(cuts),
        compiler_params=limit(8, scale),
        cost_estimate=cost(1),
        name="left",
    )(norm, mask, w_in)
    if paired:
        return paired_plan(lefts, right, psum, norm, w_gate, w_final)
    return gathered_plan(lefts[0], right, psum, norm, w_gate, w_final)


def solution(mesh):
    placed = (
        P(("grp", "row"), None, None),
        P(("grp", "row"), "col", None),
        P("grp"),
        P(("grp", "row"), "col"),
        P(),
        P(),
        P(),
        P(),
        P(),
        P(),
    )
    return jax.shard_map(
        shards,
        mesh=mesh,
        in_specs=placed,
        out_specs=P(("grp", "row"), "col", None),
        check_vma=False,
    )
```

```python
import functools

import jax
import jax.numpy as jnp
from jax import lax
from jax.experimental import pallas as pl
from jax.experimental.pallas import tpu as pltpu
from jax.sharding import PartitionSpec as P

eps = 1e-05
f32 = jnp.float32
bf16 = jnp.bfloat16
VMEM = pl.BlockSpec(memory_space=pltpu.VMEM)
SMEM = pl.BlockSpec(memory_space=pltpu.SMEM)
HBM = pl.BlockSpec(memory_space=pltpu.HBM)


def limit(mib, scale=1):
    return pltpu.CompilerParams(vmem_limit_bytes=min(56, mib * scale) * 1024 * 1024)


def round_up(n, m):
    return (n + m - 1) // m * m


def cost(us):
    return pl.CostEstimate(flops=0, bytes_accessed=int(us * 3.69e6), transcendentals=0)


def hold(x):
    return pltpu.with_memory_space_constraint(x, pltpu.HBM)


def fetch(pairs, sem):
    copies = [pltpu.make_async_copy(src, dst, sem.at[n]) for n, (src, dst) in enumerate(pairs)]
    for copy in copies:
        copy.start()
    return copies


def standardize(values):
    centre = values - jnp.mean(values, axis=-1, keepdims=True)
    spread = jnp.mean(centre * centre, axis=-1, keepdims=True)
    return centre * lax.rsqrt(spread + eps)


def sigmoid(v):
    return 0.5 * jnp.tanh(0.5 * v) + 0.5


def align_body(own_i, own_j, count, x_hbm, w_hbm, *refs):
    later, outs, refs = refs[:4], refs[4 : 4 + count], refs[4 + count :]
    brought, (x_ref, w_ref, y_ref, sem) = refs[:4], refs[4:]
    copies = fetch([(x_hbm, x_ref), (w_hbm, w_ref), *zip(later, brought)], sem)
    seqs, residues, depth = x_ref.shape
    width = w_ref.shape[0] // 2
    height, lanes = outs[0].shape
    me = lax.axis_index("row")
    z = lax.axis_index("col")
    copies[0].wait()
    x = x_ref[...].astype(f32).reshape(seqs * residues, depth)
    normed = standardize(x).astype(bf16)
    copies[1].wait()
    y_ref[...] = lax.dot_general(
        normed, w_ref[...], (((1,), (1,)), ((), ())), preferred_element_type=f32
    )
    start = pl.multiple_of(z * own_j, 8)

    def tall(v):
        gap = height - v.shape[0]
        return jnp.concatenate([v, jnp.zeros((gap, v.shape[1]), f32)], axis=0) if gap else v

    right = [tall(y_ref[pl.ds(s * residues + start, own_j), width:]) for s in range(seqs)]
    gap = lanes - 2 * seqs * width
    right += [jnp.zeros((height, gap), f32)] if gap else []
    for d, out in enumerate(outs):
        first = pl.multiple_of((me ^ d) * own_i, 8)
        left = [tall(y_ref[pl.ds(s * residues + first, own_i), :width]) for s in range(seqs)]
        out[...] = jnp.concatenate(left + right, axis=1).astype(bf16)
    for copy in copies[2:]:
        copy.wait()


def prepare_body(seqs, couple_ref, ids_hbm, valid_ref, bias_ref, avg_ref, base_ref, mask_ref, wq_ref, pick_ref,
                 wf_ref, idc_ref, ids_ref, sem):
    (copy,) = fetch([(ids_hbm, ids_ref)], sem)
    own_i, own_j, chans = couple_ref.shape
    pairs, width, _ = wq_ref.shape
    blocks, lanes, _ = pick_ref.shape
    total = blocks * seqs
    x0 = lax.axis_index("row") * own_i
    z0 = lax.axis_index("col") * own_j

    row = lax.broadcasted_iota(jnp.int32, pick_ref.shape[1:], 0)
    col = lax.broadcasted_iota(jnp.int32, pick_ref.shape[1:], 1)
    unit = row - seqs * width
    place = lax.rem(unit, width) * total + lax.div(unit, width)
    place = jnp.where((unit >= 0) & (unit < seqs * width), col - place, -1)

    def pick(r, carry):
        pick_ref[r] = jnp.where(place == r * seqs, 1.0, 0.0).astype(bf16)
        return carry

    lax.fori_loop(0, blocks, pick, 0)
    wf_ref[...] = avg_ref[...].astype(f32)
    for h in range(pairs):
        both = [wf_ref[pl.ds(2 * h + d, width, stride=width), :] for d in range(2)]
        wq_ref[h] = jnp.concatenate(both, axis=1).astype(bf16)
    copy.wait()
    for j in range(own_j):
        idc_ref[pl.ds(j, 1), :] = jnp.full((1, chans), ids_ref[z0 + j], jnp.int32)
    idc = idc_ref[...]
    valid_t = valid_ref[...].astype(f32).T
    lane = lax.broadcasted_iota(jnp.int32, valid_t.shape, 1)
    same_bias = bias_ref[0:1, :]
    cross_bias = bias_ref[1:2, :]

    def rows(i, carry):
        bias = jnp.where(idc == ids_ref[x0 + i], same_bias, cross_bias)
        base_ref[i] = couple_ref[i].astype(f32) + bias
        column = jnp.sum(jnp.where(lane == i, valid_t, 0.0), axis=1, keepdims=True)
        mask_ref[i] = jnp.broadcast_to(column, (own_j, mask_ref.shape[2])).astype(bf16)
        return carry

    lax.fori_loop(0, own_i, rows, 0, unroll=8)


def pair_body(seqs, width, blocks, turned, *refs):
    msgs = refs[:blocks]
    base_ref, mask_ref, wq_ref, pick_ref, win_ref = refs[blocks : blocks + 5]
    psum_ref, norm_ref, right_ref = refs[blocks + 5 : blocks + 8]
    xl_ref, t_ref, flat_ref = refs[blocks + 8 :]
    own_i, own_j, chans = base_ref.shape
    height, lanes = msgs[0].shape
    total = seqs * blocks
    tri = win_ref.shape[1] // 4
    half = own_i // 2

    for r in range(blocks):
        m = msgs[r][pl.ds(0, own_i), :].astype(f32)
        for s in range(seqs):
            moved = m if s == 0 else pltpu.roll(m, lanes - s * width, 1)
            xl_ref[pl.ds(r * seqs + s, own_i, stride=total), :] = moved[:, :128]
    lhs = xl_ref[:, :width].astype(bf16)

    joined = jnp.concatenate([msg[...] for msg in msgs], axis=1)
    picks = pick_ref[...].reshape(blocks * lanes, width * total)
    rmat = jnp.dot(joined, picks, preferred_element_type=f32)[:own_j].astype(bf16)

    def expand(h, carry):
        out = jnp.dot(lhs, wq_ref[h], preferred_element_type=f32)
        parts = [out[:, d * chans : (d + 1) * chans].reshape(own_i, total, chans) for d in range(2)]
        block = jnp.concatenate(parts, axis=1).astype(bf16)
        where = pl.ds(pl.multiple_of(h * 2 * total, 16), 2 * total)
        t_ref[:, where, :chans] = block[:half]
        t_ref[:, where, chans:] = block[half:]
        return carry

    lax.fori_loop(0, width // 2, expand, 0, unroll=16 if turned else 4)

    step = 4 if half % 4 == 0 else 1

    def rows(b, carry):
        normed = [[], []]
        for g in range(step):
            i = b * step + g
            both = jnp.dot(rmat, t_ref[i], preferred_element_type=f32) * (1.0 / total)
            for side in range(2):
                at = i + side * half
                psum = (base_ref[at] + both[:, side * chans : (side + 1) * chans]).astype(bf16)
                psum_ref[at] = psum
                normed[side].append(standardize(psum.astype(f32)))
        flat = jnp.concatenate(normed[0] + normed[1], axis=0).astype(bf16)
        proj = jnp.dot(flat, win_ref[:, 2 * tri :], preferred_element_type=f32)
        count = step * own_j
        for side in range(2):
            cut = slice(side * count, (side + 1) * count)
            i0 = b * step + side * half
            norm_ref[pl.ds(pl.multiple_of(i0 * own_j, 16), count), :] = flat[cut]
            mask = mask_ref[pl.ds(i0, step)].astype(f32).reshape(count, tri)
            right = mask * sigmoid(proj[cut, :tri]) * proj[cut, tri:]
            if turned:
                flat_ref[pl.ds(pl.multiple_of(i0 * own_j, 8), count), :] = right
            else:
                right_ref[pl.ds(i0, step)] = right.reshape(step, own_j, tri).astype(bf16)
        return carry

    lax.fori_loop(0, half // step, rows, 0, unroll=True)

    def turn(k, carry):
        right_ref[k] = flat_ref[pl.ds(k, own_i, stride=own_j), :].astype(bf16)
        return carry

    if turned:
        lax.fori_loop(0, own_j, turn, 0, unroll=8)


def left_body(norm_ref, mask_ref, win_ref, *outs):
    own_i, own_j, tri = mask_ref.shape
    group = 8 if own_i % 8 == 0 else 1
    at = 0
    for out in outs:
        first = at

        def rows(b, carry):
            i0 = first + b * group
            flat = norm_ref[pl.ds(pl.multiple_of(i0 * own_j, 16), group * own_j), :]
            mask = mask_ref[pl.ds(i0, group)].astype(f32).reshape(group * own_j, tri)
            proj = jnp.dot(flat, win_ref[:, : 2 * tri], preferred_element_type=f32)
            left = mask * sigmoid(proj[:, :tri]) * proj[:, tri:]
            out[pl.ds(b * group, group)] = left.reshape(group, own_j, tri).astype(bf16)
            return carry

        lax.fori_loop(0, out.shape[0] // group, rows, 0, unroll=True)
        at += out.shape[0]


def contract(lf_ref, halves, i0, group):
    step = 8
    acc = (jnp.zeros(halves[0].shape[1:], f32),) * group
    for h, r_ref in enumerate(halves):
        depth = r_ref.shape[0]

        def add(kb, acc):
            k0 = kb * step
            acc = list(acc)
            for d in range(step):
                right = r_ref[k0 + d].astype(f32)
                for t in range(group):
                    acc[t] = acc[t] + lf_ref[i0 + t, pl.ds(h * depth + k0 + d, 1), :] * right
            return tuple(acc)

        acc = lax.fori_loop(0, depth // step, add, acc)
    return acc


def with_right(own_pair, refs, use):
    own, got, p_got, far, p_far = refs
    r, z = lax.axis_index("row"), lax.axis_index("col")
    keeper = (r % 2) == (z % 2)
    near = ((r // 2) == (z // 2)) == own_pair
    table = [
        (near & keeper, own, p_got),
        (near & ~keeper, far, got),
        (~near & keeper, got, far),
        (~near & ~keeper, p_got, p_far),
    ]
    for cond, a, b in table:
        pl.when(cond)(functools.partial(use, (a, b)))


def send_body(first, *refs):
    rights, (l_ref, m_ref, o_ref, lf_ref) = refs[:5], refs[5:]
    count, depth = o_ref.shape[0], l_ref.shape[1]
    group = 8
    lf_ref[:, pl.ds(0, depth), :] = l_ref[pl.ds(first, count)].astype(f32)
    lf_ref[:, pl.ds(depth, depth), :] = m_ref[pl.ds(first, count)].astype(f32)

    def use(halves):
        def rows(b, carry):
            acc = contract(lf_ref, halves, b * group, group)
            for t in range(group):
                o_ref[b * group + t] = acc[t].astype(bf16)
            return carry

        lax.fori_loop(0, count // group, rows, 0)

    with_right(False, rights, use)


def keep_body(cuts, *refs):
    rights, refs = refs[:5], refs[5:]
    lefts, mets = refs[:cuts], refs[cuts : 2 * cuts]
    norm_ref, wgate_ref, o_ref, gate_ref, lf_ref = refs[2 * cuts :]
    own_i, depth, chans = o_ref.shape
    at = 0
    for l_ref, m_ref in zip(lefts, mets):
        n = l_ref.shape[0]
        lf_ref[pl.ds(at, n), pl.ds(0, depth), :] = l_ref[...].astype(f32)
        lf_ref[pl.ds(at, n), pl.ds(depth, depth), :] = m_ref[...].astype(f32)
        at += n
    group = 8

    def gates(b, carry):
        flat = norm_ref[pl.ds(pl.multiple_of(b * group * depth, 16), group * depth), :]
        gate = sigmoid(jnp.dot(flat, wgate_ref[...], preferred_element_type=f32))
        gate_ref[pl.ds(b * group, group)] = gate.reshape(group, depth, -1)
        return carry

    lax.fori_loop(0, own_i // group, gates, 0, unroll=True)

    def use(halves):
        def rows(b, carry):
            acc = contract(lf_ref, halves, b * group, group)
            for t in range(group):
                o_ref[b * group + t] = acc[t]
            return carry

        lax.fori_loop(0, own_i // group, rows, 0)

    with_right(True, rights, use)


def join_body(first, parts, own_ref, psum_ref, gate_ref, w_ref, *refs):
    sums, (out_hbm, done_ref, sem) = refs[:parts], refs[-3:]
    count, extent, chans = done_ref.shape
    group = 8
    at = 0
    for sum_ref in sums:
        start = at

        def rows(b, carry):
            here = pl.ds(start + b * group, group)
            there = pl.ds(first + start + b * group, group)
            mixed = own_ref[there] + sum_ref[pl.ds(b * group, group)].astype(f32)
            normed = standardize(mixed).reshape(group * extent, -1).astype(bf16)
            update = jnp.dot(normed, w_ref[...], preferred_element_type=f32).reshape(group, extent, -1)
            done_ref[here] = (psum_ref[there].astype(f32) + gate_ref[there] * update).astype(bf16)
            return carry

        lax.fori_loop(0, sum_ref.shape[0] // group, rows, 0, unroll=True)
        at += sum_ref.shape[0]
    copy = pltpu.make_async_copy(done_ref, out_hbm.at[pl.ds(first, count)], sem)
    copy.start()
    copy.wait()


def triangle_body(l_ref, r_ref, o_ref, lf_ref, flat_ref, rk_ref):
    own_i, depth, chans = l_ref.shape
    extent = r_ref.shape[0]
    group = 8 if own_i % 8 == 0 else 1

    @pl.when(pl.program_id(0) == 0)
    def _():
        lf_ref[...] = l_ref[...].astype(f32)

    def widen(j, carry):
        flat_ref[pl.ds(pl.multiple_of(j * depth, 8), depth), :] = r_ref[j].astype(f32)
        return carry

    lax.fori_loop(0, extent, widen, 0)

    def turn(k, carry):
        rk_ref[k] = flat_ref[pl.ds(k, extent, stride=depth), :]
        return carry

    lax.fori_loop(0, depth, turn, 0)

    def rows(b, carry):
        i0 = b * group
        acc = contract(lf_ref, [rk_ref], i0, group)
        for t in range(group):
            o_ref[0, i0 + t] = acc[t].astype(bf16)
        return carry

    lax.fori_loop(0, own_i // group, rows, 0)


def finish_body(sum_ref, psum_ref, norm_ref, wgate_ref, w_ref, out_ref):
    parts, own_i, extent, chans = sum_ref.shape
    own_j = psum_ref.shape[1]

    def row(i, carry):
        flat = norm_ref[pl.ds(pl.multiple_of(i * own_j, 16), own_j), :]
        gate = sigmoid(jnp.dot(flat, wgate_ref[...], preferred_element_type=f32))
        normed = [standardize(sum_ref[part, i].astype(f32)) for part in range(parts)]
        normed = jnp.concatenate(normed, axis=0).astype(bf16)
        update = jnp.dot(normed, w_ref[...], preferred_element_type=f32)
        out_ref[i] = (psum_ref[i].astype(f32) + gate * update).astype(bf16)
        return carry

    lax.fori_loop(0, own_i, row, 0)


def gathered_plan(left, right, psum, norm, w_gate, w_final):
    own_i, own_j, chans = psum.shape
    rows = lax.axis_size("row")
    tri = w_final.shape[0]
    right_all = lax.all_gather(right, "row", axis=0, tiled=True)
    partial = pl.pallas_call(
        triangle_body,
        grid=(rows,),
        out_shape=jax.ShapeDtypeStruct((rows, own_i, own_i, tri), bf16),
        in_specs=[
            pl.BlockSpec((own_i, own_j, tri), lambda r: (0, 0, 0)),
            pl.BlockSpec((own_i, own_j, tri), lambda r: (r, 0, 0)),
        ],
        out_specs=pl.BlockSpec((1, own_i, own_i, tri), lambda r: (r, 0, 0, 0)),
        scratch_shapes=[
            pltpu.VMEM((own_i, own_j, tri), f32),
            pltpu.VMEM((own_i * own_j, tri), f32),
            pltpu.VMEM((own_j, own_i, tri), f32),
        ],
        compiler_params=limit(56),
        name="triangle",
    )(left, right_all)
    summed = lax.psum_scatter(partial, "col", scatter_dimension=0, tiled=True)
    return pl.pallas_call(
        finish_body,
        out_shape=jax.ShapeDtypeStruct((own_i, own_j, chans), bf16),
        in_specs=[VMEM] * 5,
        out_specs=VMEM,
        compiler_params=limit(56),
        name="finish",
    )(summed, psum, norm, w_gate, w_final)


def paired_plan(lefts, right, psum, norm, w_gate, w_final):
    own_i, own_j, chans = psum.shape
    tri = w_final.shape[0]
    cuts = len(lefts)
    cells = [(r, z) for r in range(4) for z in range(4)]

    def move(value, where, step):
        pairs = [(r * 4 + z, step(r, z)) for r, z in cells if where(r, z)]
        pairs = [(src, r * 4 + z) for src, (r, z) in pairs]
        return lax.ppermute(value, ("row", "col"), pairs)

    every = lambda r, z: True
    keeper = lambda r, z: r % 2 == z % 2
    got = move(right, every, lambda r, z: (r ^ 2, z) if keeper(r, z) else (r ^ 1, z ^ 1))
    far = move(right, every, lambda r, z: (r ^ 1, z) if keeper(r, z) else (r ^ 2, z ^ 1))
    mets = [move(left, every, lambda r, z: (r, z ^ 1)) for left in lefts[:2]]
    got, far, mets[0] = lax.optimization_barrier((got, far, mets[0]))
    p_got = move(got, every, lambda r, z: (r ^ 1, z))
    p_far = move(far, every, lambda r, z: (r ^ 1, z))
    rights = (right, got, p_got, far, p_far)

    sums = []
    chunks = [(n, m, 0, 8) for n, left in enumerate(lefts) for m in range(0, left.shape[0], 8)]
    for at, first, _, n in chunks:
        part = pl.pallas_call(
            functools.partial(send_body, first),
            out_shape=jax.ShapeDtypeStruct((n, own_j, tri), bf16),
            in_specs=[VMEM] * 7,
            out_specs=VMEM,
            scratch_shapes=[pltpu.VMEM((n, 2 * own_j, tri), f32)],
            compiler_params=limit(8),
            cost_estimate=cost(0.12 * n + 0.4),
            name="send_sums",
        )(*rights, lefts[at], mets[at])
        sums.append(move(part, every, lambda r, z: (r, z ^ 2)))
        if len(mets) < cuts:
            left, _ = lax.optimization_barrier((lefts[len(mets)], part))
            mets.append(move(left, every, lambda r, z: (r, z ^ 1)))

    own, gate = pl.pallas_call(
        functools.partial(keep_body, cuts),
        out_shape=[jax.ShapeDtypeStruct((own_i, own_j, tri), f32),
                   jax.ShapeDtypeStruct((own_i, own_j, chans), f32)],
        in_specs=[VMEM] * (5 + 2 * cuts + 2),
        out_specs=[VMEM] * 2,
        scratch_shapes=[pltpu.VMEM((own_i, 2 * own_j, tri), f32)],
        compiler_params=limit(12),
        cost_estimate=cost(6),
        name="keep_sums",
    )(*rights, *lefts, *mets, norm, w_gate)
    out = []
    for first, n in ((0, 16), (16, own_i - 16)):
        parts = sums[first // 8 : (first + n) // 8]
        out = [pl.pallas_call(
            functools.partial(join_body, first, len(parts)),
            out_shape=jax.ShapeDtypeStruct((own_i, own_j, chans), bf16),
            in_specs=[VMEM] * (4 + len(parts)) + [HBM] * len(out),
            out_specs=HBM,
            scratch_shapes=[pltpu.VMEM((n, own_j, chans), bf16), pltpu.SemaphoreType.DMA],
            input_output_aliases={4 + len(parts): 0} if out else {},
            compiler_params=limit(8),
            cost_estimate=cost(0.06 * n),
            name="join",
        )(own, psum, gate, w_final, *parts, *out)]
    return out[0]


def shards(homolog, couple, ids, valid, bias, factors, average, w_in, w_gate, w_final):
    rows, cols = lax.axis_size("row"), lax.axis_size("col")
    own_seqs, residues, depth = homolog.shape
    own_i, own_j, chans = couple.shape
    width = factors.shape[1] // 2
    tri = w_final.shape[0]
    total = own_seqs * rows
    lanes = round_up(2 * own_seqs * width, 128)
    height = round_up(max(own_i, own_j), 16)
    paired = rows == 4 and cols == 4 and own_i == own_j and own_i % 8 == 0 and own_i > 32
    scale = 1 if paired else 8

    later = (average, valid, bias, couple)
    *msgs, average, valid, bias, couple = pl.pallas_call(
        functools.partial(align_body, own_i, own_j, rows),
        out_shape=[jax.ShapeDtypeStruct((height, lanes), bf16)] * rows
        + [jax.ShapeDtypeStruct(x.shape, x.dtype) for x in later],
        in_specs=[HBM] * 6,
        out_specs=[VMEM] * (rows + 4),
        scratch_shapes=[
            pltpu.VMEM(homolog.shape, bf16),
            pltpu.VMEM((2 * width, depth), bf16),
            pltpu.VMEM((own_seqs * residues, 2 * width), f32),
            pltpu.SemaphoreType.DMA((6,)),
        ],
        compiler_params=limit(8, scale),
        cost_estimate=cost(1.5),
        name="align",
    )(hold(homolog), hold(factors.T), *map(hold, later))
    msgs = [msgs[0]] + [
        lax.ppermute(msgs[d], "row", [(r, r ^ d) for r in range(rows)])
        for d in reversed(range(1, rows))
    ]

    base, mask, wq, pick = pl.pallas_call(
        functools.partial(prepare_body, own_seqs),
        out_shape=[jax.ShapeDtypeStruct((own_i, own_j, chans), f32),
                   jax.ShapeDtypeStruct((own_i, own_j, tri), bf16),
                   jax.ShapeDtypeStruct((width // 2, width, 2 * chans), bf16),
                   jax.ShapeDtypeStruct((rows, lanes, width * total), bf16)],
        in_specs=[VMEM, HBM, VMEM, VMEM, VMEM],
        out_specs=[VMEM] * 4,
        scratch_shapes=[
            pltpu.VMEM(average.shape, f32),
            pltpu.VMEM((own_j, chans), jnp.int32),
            pltpu.SMEM(ids.shape, jnp.int32),
            pltpu.SemaphoreType.DMA((1,)),
        ],
        compiler_params=limit(8, scale),
        cost_estimate=cost(2),
        name="prepare",
    )(couple, hold(ids), valid, bias, average)

    extents = (own_j, own_i) if paired else (own_i, own_j)
    psum, norm, right = pl.pallas_call(
        functools.partial(pair_body, own_seqs, width, rows, paired),
        out_shape=[jax.ShapeDtypeStruct((own_i, own_j, chans), bf16),
                   jax.ShapeDtypeStruct((own_i * own_j, chans), bf16),
                   jax.ShapeDtypeStruct(extents + (tri,), bf16)],
        in_specs=[VMEM] * (rows + 5),
        out_specs=[VMEM] * 3,
        scratch_shapes=[
            pltpu.VMEM((own_i * total, 128), f32),
            pltpu.VMEM((own_i // 2, width * total, 2 * chans), bf16),
            pltpu.VMEM((own_i * own_j, tri), f32),
        ],
        compiler_params=limit(16, scale),
        cost_estimate=cost(4.5),
        name="pair",
    )(*msgs, base, mask, wq, pick, w_in)

    cuts = [8, 16, own_i - 24] if paired else [own_i]
    lefts = pl.pallas_call(
        left_body,
        out_shape=[jax.ShapeDtypeStruct((n, own_j, tri), bf16) for n in cuts],
        in_specs=[VMEM] * 3,
        out_specs=[VMEM] * len(cuts),
        compiler_params=limit(8, scale),
        cost_estimate=cost(1),
        name="left",
    )(norm, mask, w_in)
    if paired:
        return paired_plan(lefts, right, psum, norm, w_gate, w_final)
    return gathered_plan(lefts[0], right, psum, norm, w_gate, w_final)


def solution(mesh):
    placed = (
        P(("grp", "row"), None, None),
        P(("grp", "row"), "col", None),
        P("grp"),
        P(("grp", "row"), "col"),
        P(),
        P(),
        P(),
        P(),
        P(),
        P(),
    )
    return jax.shard_map(
        shards,
        mesh=mesh,
        in_specs=placed,
        out_specs=P(("grp", "row"), "col", None),
        check_vma=False,
    )
```

```python
import functools

import jax
import jax.numpy as jnp
from jax import lax
from jax.experimental import pallas as pl
from jax.experimental.pallas import tpu as pltpu
from jax.sharding import PartitionSpec as P

eps = 1e-05
f32 = jnp.float32
bf16 = jnp.bfloat16
VMEM = pl.BlockSpec(memory_space=pltpu.VMEM)
SMEM = pl.BlockSpec(memory_space=pltpu.SMEM)
HBM = pl.BlockSpec(memory_space=pltpu.HBM)


def limit(mib, scale=1):
    return pltpu.CompilerParams(vmem_limit_bytes=min(56, mib * scale) * 1024 * 1024)


def aligned(n, m):
    return n if isinstance(n, int) else pl.multiple_of(n, m)


def round_up(n, m):
    return (n + m - 1) // m * m


def cost(us):
    return pl.CostEstimate(flops=0, bytes_accessed=int(us * 3.69e6), transcendentals=0)


def hold(x):
    return pltpu.with_memory_space_constraint(x, pltpu.HBM)


def fetch(pairs, sem):
    copies = [pltpu.make_async_copy(src, dst, sem.at[n]) for n, (src, dst) in enumerate(pairs)]
    for copy in copies:
        copy.start()
    return copies


def standardize(values):
    centre = values - jnp.mean(values, axis=-1, keepdims=True)
    spread = jnp.mean(centre * centre, axis=-1, keepdims=True)
    return centre * lax.rsqrt(spread + eps)


def sigmoid(v):
    return 0.5 * jnp.tanh(0.5 * v) + 0.5


def align_body(own_i, own_j, count, x_hbm, w_hbm, *refs):
    later, outs, refs = refs[:4], refs[4 : 4 + count], refs[4 + count :]
    brought, (x_ref, w_ref, y_ref, sem) = refs[:4], refs[4:]
    copies = fetch([(x_hbm, x_ref), (w_hbm, w_ref), *zip(later, brought)], sem)
    seqs, residues, depth = x_ref.shape
    width = w_ref.shape[0] // 2
    height, lanes = outs[0].shape
    me = lax.axis_index("row")
    z = lax.axis_index("col")
    copies[0].wait()
    x = x_ref[...].astype(f32).reshape(seqs * residues, depth)
    normed = standardize(x).astype(bf16)
    copies[1].wait()
    y_ref[...] = lax.dot_general(
        normed, w_ref[...], (((1,), (1,)), ((), ())), preferred_element_type=f32
    )
    start = pl.multiple_of(z * own_j, 8)

    def tall(v):
        gap = height - v.shape[0]
        return jnp.concatenate([v, jnp.zeros((gap, v.shape[1]), f32)], axis=0) if gap else v

    right = [tall(y_ref[pl.ds(s * residues + start, own_j), width:]) for s in range(seqs)]
    gap = lanes - 2 * seqs * width
    right += [jnp.zeros((height, gap), f32)] if gap else []
    for d, out in enumerate(outs):
        first = pl.multiple_of((me ^ d) * own_i, 8)
        left = [tall(y_ref[pl.ds(s * residues + first, own_i), :width]) for s in range(seqs)]
        out[...] = jnp.concatenate(left + right, axis=1).astype(bf16)
    for copy in copies[2:]:
        copy.wait()


def prepare_body(seqs, couple_ref, ids_hbm, valid_ref, bias_ref, avg_ref, base_ref, mask_ref, wq_ref, pick_ref,
                 wf_ref, idc_ref, ids_ref, sem):
    (copy,) = fetch([(ids_hbm, ids_ref)], sem)
    own_i, own_j, chans = couple_ref.shape
    pairs, width, _ = wq_ref.shape
    blocks, lanes, _ = pick_ref.shape
    total = blocks * seqs
    x0 = lax.axis_index("row") * own_i
    z0 = lax.axis_index("col") * own_j

    row = lax.broadcasted_iota(jnp.int32, pick_ref.shape[1:], 0)
    col = lax.broadcasted_iota(jnp.int32, pick_ref.shape[1:], 1)
    unit = row - seqs * width
    place = lax.rem(unit, width) * total + lax.div(unit, width)
    place = jnp.where((unit >= 0) & (unit < seqs * width), col - place, -1)

    def pick(r, carry):
        pick_ref[r] = jnp.where(place == r * seqs, 1.0, 0.0).astype(bf16)
        return carry

    lax.fori_loop(0, blocks, pick, 0)
    wf_ref[...] = avg_ref[...].astype(f32)
    for h in range(pairs):
        both = [wf_ref[pl.ds(2 * h + d, width, stride=width), :] for d in range(2)]
        wq_ref[h] = jnp.concatenate(both, axis=1).astype(bf16)
    copy.wait()
    for j in range(own_j):
        idc_ref[pl.ds(j, 1), :] = jnp.full((1, chans), ids_ref[z0 + j], jnp.int32)
    idc = idc_ref[...]
    valid_t = valid_ref[...].astype(f32).T
    lane = lax.broadcasted_iota(jnp.int32, valid_t.shape, 1)
    same_bias = bias_ref[0:1, :]
    cross_bias = bias_ref[1:2, :]

    def rows(i, carry):
        bias = jnp.where(idc == ids_ref[x0 + i], same_bias, cross_bias)
        base_ref[i] = couple_ref[i].astype(f32) + bias
        column = jnp.sum(jnp.where(lane == i, valid_t, 0.0), axis=1, keepdims=True)
        mask_ref[i] = jnp.broadcast_to(column, (own_j, mask_ref.shape[2])).astype(bf16)
        return carry

    lax.fori_loop(0, own_i, rows, 0, unroll=8)


def pair_body(seqs, width, blocks, turned, *refs):
    msgs = refs[:blocks]
    base_ref, mask_ref, wq_ref, pick_ref, win_ref = refs[blocks : blocks + 5]
    psum_ref, norm_ref, right_ref = refs[blocks + 5 : blocks + 8]
    xl_ref, t_ref, flat_ref = refs[blocks + 8 :]
    own_i, own_j, chans = base_ref.shape
    height, lanes = msgs[0].shape
    total = seqs * blocks
    tri = win_ref.shape[1] // 4
    half = own_i // 2

    for r in range(blocks):
        m = msgs[r][pl.ds(0, own_i), :].astype(f32)
        for s in range(seqs):
            moved = m if s == 0 else pltpu.roll(m, lanes - s * width, 1)
            xl_ref[pl.ds(r * seqs + s, own_i, stride=total), :] = moved[:, :128]
    lhs = xl_ref[:, :width].astype(bf16)

    joined = jnp.concatenate([msg[...] for msg in msgs], axis=1)
    picks = pick_ref[...].reshape(blocks * lanes, width * total)
    rmat = jnp.dot(joined, picks, preferred_element_type=f32)[:own_j].astype(bf16)

    def expand(h, carry):
        out = jnp.dot(lhs, wq_ref[h], preferred_element_type=f32)
        parts = [out[:, d * chans : (d + 1) * chans].reshape(own_i, total, chans) for d in range(2)]
        block = jnp.concatenate(parts, axis=1).astype(bf16)
        where = pl.ds(aligned(h * 2 * total, 16), 2 * total)
        t_ref[:, where, :chans] = block[:half]
        t_ref[:, where, chans:] = block[half:]
        return carry

    repeat(width // 2, expand, turned)

    step = 4 if half % 4 == 0 else 1

    def rows(b, carry):
        normed = [[], []]
        for g in range(step):
            i = b * step + g
            both = jnp.dot(rmat, t_ref[i], preferred_element_type=f32) * (1.0 / total)
            for side in range(2):
                at = i + side * half
                psum = (base_ref[at] + both[:, side * chans : (side + 1) * chans]).astype(bf16)
                psum_ref[at] = psum
                normed[side].append(standardize(psum.astype(f32)))
        flat = jnp.concatenate(normed[0] + normed[1], axis=0).astype(bf16)
        proj = jnp.dot(flat, win_ref[:, 2 * tri :], preferred_element_type=f32)
        count = step * own_j
        for side in range(2):
            cut = slice(side * count, (side + 1) * count)
            i0 = b * step + side * half
            norm_ref[pl.ds(aligned(i0 * own_j, 16), count), :] = flat[cut]
            mask = mask_ref[pl.ds(i0, step)].astype(f32).reshape(count, tri)
            right = mask * sigmoid(proj[cut, :tri]) * proj[cut, tri:]
            if turned:
                flat_ref[pl.ds(aligned(i0 * own_j, 8), count), :] = right
            else:
                right_ref[pl.ds(i0, step)] = right.reshape(step, own_j, tri).astype(bf16)
        return carry

    repeat(half // step, rows, turned)

    def turn(k, carry):
        right_ref[k] = flat_ref[pl.ds(k, own_i, stride=own_j), :].astype(bf16)
        return carry

    if turned:
        repeat(own_j, turn, True)


def repeat(count, body, static):
    if static:
        for n in range(count):
            body(n, 0)
    else:
        lax.fori_loop(0, count, body, 0)


def left_body(norm_ref, mask_ref, win_ref, *outs):
    own_i, own_j, tri = mask_ref.shape
    group = 8 if own_i % 8 == 0 else 1
    at = 0
    for out in outs:
        first = at

        def rows(b, carry):
            i0 = first + b * group
            flat = norm_ref[pl.ds(pl.multiple_of(i0 * own_j, 16), group * own_j), :]
            mask = mask_ref[pl.ds(i0, group)].astype(f32).reshape(group * own_j, tri)
            proj = jnp.dot(flat, win_ref[:, : 2 * tri], preferred_element_type=f32)
            left = mask * sigmoid(proj[:, :tri]) * proj[:, tri:]
            out[pl.ds(b * group, group)] = left.reshape(group, own_j, tri).astype(bf16)
            return carry

        lax.fori_loop(0, out.shape[0] // group, rows, 0, unroll=True)
        at += out.shape[0]


def gate_body(norm_ref, wgate_ref, gate_ref):
    own_i, depth, chans = gate_ref.shape
    group = 8

    def gates(b, carry):
        flat = norm_ref[pl.ds(pl.multiple_of(b * group * depth, 16), group * depth), :]
        gate = sigmoid(jnp.dot(flat, wgate_ref[...], preferred_element_type=f32))
        gate_ref[pl.ds(b * group, group)] = gate.reshape(group, depth, -1)
        return carry

    lax.fori_loop(0, own_i // group, gates, 0, unroll=True)


def contract(lf_ref, halves, i0, group):
    step = 8
    acc = (jnp.zeros(halves[0].shape[1:], f32),) * group
    for h, r_ref in enumerate(halves):
        depth = r_ref.shape[0]

        def add(kb, acc):
            k0 = kb * step
            acc = list(acc)
            for d in range(step):
                right = r_ref[k0 + d].astype(f32)
                for t in range(group):
                    acc[t] = acc[t] + lf_ref[i0 + t, pl.ds(h * depth + k0 + d, 1), :] * right
            return tuple(acc)

        acc = lax.fori_loop(0, depth // step, add, acc)
    return acc


def with_right(own_pair, refs, use):
    own, got, p_got, far, p_far = refs
    r, z = lax.axis_index("row"), lax.axis_index("col")
    keeper = (r % 2) == (z % 2)
    near = ((r // 2) == (z // 2)) == own_pair
    table = [
        (near & keeper, own, p_got),
        (near & ~keeper, far, got),
        (~near & keeper, got, far),
        (~near & ~keeper, p_got, p_far),
    ]
    for cond, a, b in table:
        pl.when(cond)(functools.partial(use, (a, b)))


def send_body(first, *refs):
    rights, (l_ref, m_ref, o_ref, lf_ref) = refs[:5], refs[5:]
    count, depth = o_ref.shape[0], l_ref.shape[1]
    group = 8
    lf_ref[:, pl.ds(0, depth), :] = l_ref[pl.ds(first, count)].astype(f32)
    lf_ref[:, pl.ds(depth, depth), :] = m_ref[pl.ds(first, count)].astype(f32)

    def use(halves):
        def rows(b, carry):
            acc = contract(lf_ref, halves, b * group, group)
            for t in range(group):
                o_ref[b * group + t] = acc[t].astype(bf16)
            return carry

        lax.fori_loop(0, count // group, rows, 0)

    with_right(False, rights, use)


def keep_body(cuts, *refs):
    rights, refs = refs[:5], refs[5:]
    lefts, mets = refs[:cuts], refs[cuts : 2 * cuts]
    o_ref, lf_ref = refs[2 * cuts :]
    own_i, depth, chans = o_ref.shape
    at = 0
    for l_ref, m_ref in zip(lefts, mets):
        n = l_ref.shape[0]
        lf_ref[pl.ds(at, n), pl.ds(0, depth), :] = l_ref[...].astype(f32)
        lf_ref[pl.ds(at, n), pl.ds(depth, depth), :] = m_ref[...].astype(f32)
        at += n
    group = 8

    def use(halves):
        def rows(b, carry):
            acc = contract(lf_ref, halves, b * group, group)
            for t in range(group):
                o_ref[b * group + t] = acc[t]
            return carry

        lax.fori_loop(0, own_i // group, rows, 0)

    with_right(True, rights, use)


def join_body(first, parts, own_ref, psum_ref, gate_ref, w_ref, *refs):
    sums, (out_hbm, done_ref, sem) = refs[:parts], refs[-3:]
    count, extent, chans = done_ref.shape
    group = 8
    at = 0
    for sum_ref in sums:
        start = at

        def rows(b, carry):
            here = pl.ds(start + b * group, group)
            there = pl.ds(first + start + b * group, group)
            mixed = own_ref[there] + sum_ref[pl.ds(b * group, group)].astype(f32)
            normed = standardize(mixed).reshape(group * extent, -1).astype(bf16)
            update = jnp.dot(normed, w_ref[...], preferred_element_type=f32).reshape(group, extent, -1)
            done_ref[here] = (psum_ref[there].astype(f32) + gate_ref[there] * update).astype(bf16)
            return carry

        lax.fori_loop(0, sum_ref.shape[0] // group, rows, 0, unroll=True)
        at += sum_ref.shape[0]
    copy = pltpu.make_async_copy(done_ref, out_hbm.at[pl.ds(first, count)], sem)
    copy.start()
    copy.wait()


def triangle_body(l_ref, r_ref, o_ref, lf_ref, flat_ref, rk_ref):
    own_i, depth, chans = l_ref.shape
    extent = r_ref.shape[0]
    group = 8 if own_i % 8 == 0 else 1

    @pl.when(pl.program_id(0) == 0)
    def _():
        lf_ref[...] = l_ref[...].astype(f32)

    def widen(j, carry):
        flat_ref[pl.ds(pl.multiple_of(j * depth, 8), depth), :] = r_ref[j].astype(f32)
        return carry

    lax.fori_loop(0, extent, widen, 0)

    def turn(k, carry):
        rk_ref[k] = flat_ref[pl.ds(k, extent, stride=depth), :]
        return carry

    lax.fori_loop(0, depth, turn, 0)

    def rows(b, carry):
        i0 = b * group
        acc = contract(lf_ref, [rk_ref], i0, group)
        for t in range(group):
            o_ref[0, i0 + t] = acc[t].astype(bf16)
        return carry

    lax.fori_loop(0, own_i // group, rows, 0)


def finish_body(sum_ref, psum_ref, norm_ref, wgate_ref, w_ref, out_ref):
    parts, own_i, extent, chans = sum_ref.shape
    own_j = psum_ref.shape[1]

    def row(i, carry):
        flat = norm_ref[pl.ds(pl.multiple_of(i * own_j, 16), own_j), :]
        gate = sigmoid(jnp.dot(flat, wgate_ref[...], preferred_element_type=f32))
        normed = [standardize(sum_ref[part, i].astype(f32)) for part in range(parts)]
        normed = jnp.concatenate(normed, axis=0).astype(bf16)
        update = jnp.dot(normed, w_ref[...], preferred_element_type=f32)
        out_ref[i] = (psum_ref[i].astype(f32) + gate * update).astype(bf16)
        return carry

    lax.fori_loop(0, own_i, row, 0)


def gathered_plan(left, right, psum, norm, w_gate, w_final):
    own_i, own_j, chans = psum.shape
    rows = lax.axis_size("row")
    tri = w_final.shape[0]
    right_all = lax.all_gather(right, "row", axis=0, tiled=True)
    partial = pl.pallas_call(
        triangle_body,
        grid=(rows,),
        out_shape=jax.ShapeDtypeStruct((rows, own_i, own_i, tri), bf16),
        in_specs=[
            pl.BlockSpec((own_i, own_j, tri), lambda r: (0, 0, 0)),
            pl.BlockSpec((own_i, own_j, tri), lambda r: (r, 0, 0)),
        ],
        out_specs=pl.BlockSpec((1, own_i, own_i, tri), lambda r: (r, 0, 0, 0)),
        scratch_shapes=[
            pltpu.VMEM((own_i, own_j, tri), f32),
            pltpu.VMEM((own_i * own_j, tri), f32),
            pltpu.VMEM((own_j, own_i, tri), f32),
        ],
        compiler_params=limit(56),
        name="triangle",
    )(left, right_all)
    summed = lax.psum_scatter(partial, "col", scatter_dimension=0, tiled=True)
    return pl.pallas_call(
        finish_body,
        out_shape=jax.ShapeDtypeStruct((own_i, own_j, chans), bf16),
        in_specs=[VMEM] * 5,
        out_specs=VMEM,
        compiler_params=limit(56),
        name="finish",
    )(summed, psum, norm, w_gate, w_final)


def paired_plan(lefts, right, psum, norm, w_gate, w_final):
    own_i, own_j, chans = psum.shape
    tri = w_final.shape[0]
    cuts = len(lefts)
    cells = [(r, z) for r in range(4) for z in range(4)]

    def move(value, where, step):
        pairs = [(r * 4 + z, step(r, z)) for r, z in cells if where(r, z)]
        pairs = [(src, r * 4 + z) for src, (r, z) in pairs]
        return lax.ppermute(value, ("row", "col"), pairs)

    every = lambda r, z: True
    keeper = lambda r, z: r % 2 == z % 2
    got = move(right, every, lambda r, z: (r ^ 2, z) if keeper(r, z) else (r ^ 1, z ^ 1))
    far = move(right, every, lambda r, z: (r ^ 1, z) if keeper(r, z) else (r ^ 2, z ^ 1))
    mets = [move(left, every, lambda r, z: (r, z ^ 1)) for left in lefts[:2]]
    gate = pl.pallas_call(
        gate_body,
        out_shape=jax.ShapeDtypeStruct((own_i, own_j, chans), f32),
        in_specs=[VMEM] * 2,
        out_specs=VMEM,
        compiler_params=limit(8),
        cost_estimate=cost(1),
        name="gate",
    )(norm, w_gate)
    got, far, mets[0], gate = lax.optimization_barrier((got, far, mets[0], gate))
    p_got = move(got, every, lambda r, z: (r ^ 1, z))
    p_far = move(far, every, lambda r, z: (r ^ 1, z))
    rights = (right, got, p_got, far, p_far)

    sums = []
    chunks = [(n, m, 0, 8) for n, left in enumerate(lefts) for m in range(0, left.shape[0], 8)]
    for at, first, _, n in chunks:
        part = pl.pallas_call(
            functools.partial(send_body, first),
            out_shape=jax.ShapeDtypeStruct((n, own_j, tri), bf16),
            in_specs=[VMEM] * 7,
            out_specs=VMEM,
            scratch_shapes=[pltpu.VMEM((n, 2 * own_j, tri), f32)],
            compiler_params=limit(8),
            cost_estimate=cost(0.12 * n + 0.4),
            name="send_sums",
        )(*rights, lefts[at], mets[at])
        sums.append(move(part, every, lambda r, z: (r, z ^ 2)))
        if len(mets) < cuts:
            left, _ = lax.optimization_barrier((lefts[len(mets)], part))
            mets.append(move(left, every, lambda r, z: (r, z ^ 1)))

    own = pl.pallas_call(
        functools.partial(keep_body, cuts),
        out_shape=jax.ShapeDtypeStruct((own_i, own_j, tri), f32),
        in_specs=[VMEM] * (5 + 2 * cuts),
        out_specs=VMEM,
        scratch_shapes=[pltpu.VMEM((own_i, 2 * own_j, tri), f32)],
        compiler_params=limit(12),
        cost_estimate=cost(6),
        name="keep_sums",
    )(*rights, *lefts, *mets)
    out = []
    for first, n in ((0, 16), (16, own_i - 16)):
        parts = sums[first // 8 : (first + n) // 8]
        out = [pl.pallas_call(
            functools.partial(join_body, first, len(parts)),
            out_shape=jax.ShapeDtypeStruct((own_i, own_j, chans), bf16),
            in_specs=[VMEM] * (4 + len(parts)) + [HBM] * len(out),
            out_specs=HBM,
            scratch_shapes=[pltpu.VMEM((n, own_j, chans), bf16), pltpu.SemaphoreType.DMA],
            input_output_aliases={4 + len(parts): 0} if out else {},
            compiler_params=limit(8),
            cost_estimate=cost(0.06 * n),
            name="join",
        )(own, psum, gate, w_final, *parts, *out)]
    return out[0]


def shards(homolog, couple, ids, valid, bias, factors, average, w_in, w_gate, w_final):
    rows, cols = lax.axis_size("row"), lax.axis_size("col")
    own_seqs, residues, depth = homolog.shape
    own_i, own_j, chans = couple.shape
    width = factors.shape[1] // 2
    tri = w_final.shape[0]
    total = own_seqs * rows
    lanes = round_up(2 * own_seqs * width, 128)
    height = round_up(max(own_i, own_j), 16)
    paired = rows == 4 and cols == 4 and own_i == own_j and own_i % 8 == 0 and own_i > 32
    scale = 1 if paired else 8

    later = (average, valid, bias, couple)
    *msgs, average, valid, bias, couple = pl.pallas_call(
        functools.partial(align_body, own_i, own_j, rows),
        out_shape=[jax.ShapeDtypeStruct((height, lanes), bf16)] * rows
        + [jax.ShapeDtypeStruct(x.shape, x.dtype) for x in later],
        in_specs=[HBM] * 6,
        out_specs=[VMEM] * (rows + 4),
        scratch_shapes=[
            pltpu.VMEM(homolog.shape, bf16),
            pltpu.VMEM((2 * width, depth), bf16),
            pltpu.VMEM((own_seqs * residues, 2 * width), f32),
            pltpu.SemaphoreType.DMA((6,)),
        ],
        compiler_params=limit(8, scale),
        cost_estimate=cost(1.5),
        name="align",
    )(hold(homolog), hold(factors.T), *map(hold, later))
    msgs = [msgs[0]] + [
        lax.ppermute(msgs[d], "row", [(r, r ^ d) for r in range(rows)])
        for d in reversed(range(1, rows))
    ]

    base, mask, wq, pick = pl.pallas_call(
        functools.partial(prepare_body, own_seqs),
        out_shape=[jax.ShapeDtypeStruct((own_i, own_j, chans), f32),
                   jax.ShapeDtypeStruct((own_i, own_j, tri), bf16),
                   jax.ShapeDtypeStruct((width // 2, width, 2 * chans), bf16),
                   jax.ShapeDtypeStruct((rows, lanes, width * total), bf16)],
        in_specs=[VMEM, HBM, VMEM, VMEM, VMEM],
        out_specs=[VMEM] * 4,
        scratch_shapes=[
            pltpu.VMEM(average.shape, f32),
            pltpu.VMEM((own_j, chans), jnp.int32),
            pltpu.SMEM(ids.shape, jnp.int32),
            pltpu.SemaphoreType.DMA((1,)),
        ],
        compiler_params=limit(8, scale),
        cost_estimate=cost(2),
        name="prepare",
    )(couple, hold(ids), valid, bias, average)

    extents = (own_j, own_i) if paired else (own_i, own_j)
    psum, norm, right = pl.pallas_call(
        functools.partial(pair_body, own_seqs, width, rows, paired),
        out_shape=[jax.ShapeDtypeStruct((own_i, own_j, chans), bf16),
                   jax.ShapeDtypeStruct((own_i * own_j, chans), bf16),
                   jax.ShapeDtypeStruct(extents + (tri,), bf16)],
        in_specs=[VMEM] * (rows + 5),
        out_specs=[VMEM] * 3,
        scratch_shapes=[
            pltpu.VMEM((own_i * total, 128), f32),
            pltpu.VMEM((own_i // 2, width * total, 2 * chans), bf16),
            pltpu.VMEM((own_i * own_j, tri), f32),
        ],
        compiler_params=limit(16, scale),
        cost_estimate=cost(4.5),
        name="pair",
    )(*msgs, base, mask, wq, pick, w_in)

    cuts = [8, 16, own_i - 24] if paired else [own_i]
    lefts = pl.pallas_call(
        left_body,
        out_shape=[jax.ShapeDtypeStruct((n, own_j, tri), bf16) for n in cuts],
        in_specs=[VMEM] * 3,
        out_specs=[VMEM] * len(cuts),
        compiler_params=limit(8, scale),
        cost_estimate=cost(1),
        name="left",
    )(norm, mask, w_in)
    if paired:
        return paired_plan(lefts, right, psum, norm, w_gate, w_final)
    return gathered_plan(lefts[0], right, psum, norm, w_gate, w_final)


def solution(mesh):
    placed = (
        P(("grp", "row"), None, None),
        P(("grp", "row"), "col", None),
        P("grp"),
        P(("grp", "row"), "col"),
        P(),
        P(),
        P(),
        P(),
        P(),
        P(),
    )
    return jax.shard_map(
        shards,
        mesh=mesh,
        in_specs=placed,
        out_specs=P(("grp", "row"), "col", None),
        check_vma=False,
    )
```

```python
import functools

import jax
import jax.numpy as jnp
from jax import lax
from jax.experimental import pallas as pl
from jax.experimental.pallas import tpu as pltpu
from jax.sharding import PartitionSpec as P

eps = 1e-05
f32 = jnp.float32
bf16 = jnp.bfloat16
VMEM = pl.BlockSpec(memory_space=pltpu.VMEM)
SMEM = pl.BlockSpec(memory_space=pltpu.SMEM)
HBM = pl.BlockSpec(memory_space=pltpu.HBM)


def limit(mib, scale=1):
    return pltpu.CompilerParams(vmem_limit_bytes=min(56, mib * scale) * 1024 * 1024)


def round_up(n, m):
    return (n + m - 1) // m * m


def cost(us):
    return pl.CostEstimate(flops=0, bytes_accessed=int(us * 3.69e6), transcendentals=0)


def hold(x):
    return pltpu.with_memory_space_constraint(x, pltpu.HBM)


def fetch(pairs, sem):
    copies = [pltpu.make_async_copy(src, dst, sem.at[n]) for n, (src, dst) in enumerate(pairs)]
    for copy in copies:
        copy.start()
    return copies


def standardize(values):
    centre = values - jnp.mean(values, axis=-1, keepdims=True)
    spread = jnp.mean(centre * centre, axis=-1, keepdims=True)
    return centre * lax.rsqrt(spread + eps)


def sigmoid(v):
    return 0.5 * jnp.tanh(0.5 * v) + 0.5


def align_body(own_i, own_j, count, x_hbm, w_hbm, *refs):
    later, outs, refs = refs[:4], refs[4 : 4 + count], refs[4 + count :]
    brought, (x_ref, w_ref, y_ref, sem) = refs[:4], refs[4:]
    copies = fetch([(x_hbm, x_ref), (w_hbm, w_ref), *zip(later, brought)], sem)
    seqs, residues, depth = x_ref.shape
    width = w_ref.shape[0] // 2
    height, lanes = outs[0].shape
    me = lax.axis_index("row")
    z = lax.axis_index("col")
    copies[0].wait()
    x = x_ref[...].astype(f32).reshape(seqs * residues, depth)
    normed = standardize(x).astype(bf16)
    copies[1].wait()
    y_ref[...] = lax.dot_general(
        normed, w_ref[...], (((1,), (1,)), ((), ())), preferred_element_type=f32
    )
    start = pl.multiple_of(z * own_j, 8)

    def tall(v):
        gap = height - v.shape[0]
        return jnp.concatenate([v, jnp.zeros((gap, v.shape[1]), f32)], axis=0) if gap else v

    right = [tall(y_ref[pl.ds(s * residues + start, own_j), width:]) for s in range(seqs)]
    gap = lanes - 2 * seqs * width
    right += [jnp.zeros((height, gap), f32)] if gap else []
    for d, out in enumerate(outs):
        first = pl.multiple_of((me ^ d) * own_i, 8)
        left = [tall(y_ref[pl.ds(s * residues + first, own_i), :width]) for s in range(seqs)]
        out[...] = jnp.concatenate(left + right, axis=1).astype(bf16)
    for copy in copies[2:]:
        copy.wait()


def prepare_body(seqs, couple_ref, ids_hbm, valid_ref, bias_ref, avg_ref, base_ref, mask_ref, wq_ref, pick_ref,
                 wf_ref, idc_ref, ids_ref, sem):
    (copy,) = fetch([(ids_hbm, ids_ref)], sem)
    own_i, own_j, chans = couple_ref.shape
    pairs, width, _ = wq_ref.shape
    blocks, lanes, _ = pick_ref.shape
    total = blocks * seqs
    x0 = lax.axis_index("row") * own_i
    z0 = lax.axis_index("col") * own_j

    row = lax.broadcasted_iota(jnp.int32, pick_ref.shape[1:], 0)
    col = lax.broadcasted_iota(jnp.int32, pick_ref.shape[1:], 1)
    unit = row - seqs * width
    place = lax.rem(unit, width) * total + lax.div(unit, width)
    place = jnp.where((unit >= 0) & (unit < seqs * width), col - place, -1)

    def pick(r, carry):
        pick_ref[r] = jnp.where(place == r * seqs, 1.0, 0.0).astype(bf16)
        return carry

    lax.fori_loop(0, blocks, pick, 0)
    wf_ref[...] = avg_ref[...].astype(f32)
    for h in range(pairs):
        both = [wf_ref[pl.ds(2 * h + d, width, stride=width), :] for d in range(2)]
        wq_ref[h] = jnp.concatenate(both, axis=1).astype(bf16)
    copy.wait()
    for j in range(own_j):
        idc_ref[pl.ds(j, 1), :] = jnp.full((1, chans), ids_ref[z0 + j], jnp.int32)
    idc = idc_ref[...]
    valid_t = valid_ref[...].astype(f32).T
    lane = lax.broadcasted_iota(jnp.int32, valid_t.shape, 1)
    same_bias = bias_ref[0:1, :]
    cross_bias = bias_ref[1:2, :]

    def rows(i, carry):
        bias = jnp.where(idc == ids_ref[x0 + i], same_bias, cross_bias)
        base_ref[i] = couple_ref[i].astype(f32) + bias
        column = jnp.sum(jnp.where(lane == i, valid_t, 0.0), axis=1, keepdims=True)
        mask_ref[i] = jnp.broadcast_to(column, (own_j, mask_ref.shape[2])).astype(bf16)
        return carry

    lax.fori_loop(0, own_i, rows, 0, unroll=8)


def pair_body(seqs, width, blocks, *refs):
    msgs = refs[:blocks]
    base_ref, mask_ref, wq_ref, pick_ref, win_ref = refs[blocks : blocks + 5]
    psum_ref, norm_ref, right_ref = refs[blocks + 5 : blocks + 8]
    xl_ref, t_ref = refs[blocks + 8 :]
    own_i, own_j, chans = base_ref.shape
    height, lanes = msgs[0].shape
    total = seqs * blocks
    tri = win_ref.shape[1] // 4
    half = own_i // 2

    for r in range(blocks):
        m = msgs[r][pl.ds(0, own_i), :].astype(f32)
        for s in range(seqs):
            moved = m if s == 0 else pltpu.roll(m, lanes - s * width, 1)
            xl_ref[pl.ds(r * seqs + s, own_i, stride=total), :] = moved[:, :128]
    lhs = xl_ref[:, :width].astype(bf16)

    joined = jnp.concatenate([msg[...] for msg in msgs], axis=1)
    picks = pick_ref[...].reshape(blocks * lanes, width * total)
    rmat = jnp.dot(joined, picks, preferred_element_type=f32)[:own_j].astype(bf16)

    def expand(h, carry):
        out = jnp.dot(lhs, wq_ref[h], preferred_element_type=f32)
        parts = [out[:, d * chans : (d + 1) * chans].reshape(own_i, total, chans) for d in range(2)]
        block = jnp.concatenate(parts, axis=1).astype(bf16)
        where = pl.ds(pl.multiple_of(h * 2 * total, 16), 2 * total)
        t_ref[:, where, :chans] = block[:half]
        t_ref[:, where, chans:] = block[half:]
        return carry

    lax.fori_loop(0, width // 2, expand, 0)

    step = 4 if half % 4 == 0 else 1

    def rows(b, carry):
        normed = [[], []]
        for g in range(step):
            i = b * step + g
            both = jnp.dot(rmat, t_ref[i], preferred_element_type=f32) * (1.0 / total)
            for side in range(2):
                at = i + side * half
                psum = (base_ref[at] + both[:, side * chans : (side + 1) * chans]).astype(bf16)
                psum_ref[at] = psum
                normed[side].append(standardize(psum.astype(f32)))
        flat = jnp.concatenate(normed[0] + normed[1], axis=0).astype(bf16)
        proj = jnp.dot(flat, win_ref[:, 2 * tri :], preferred_element_type=f32)
        count = step * own_j
        for side in range(2):
            cut = slice(side * count, (side + 1) * count)
            i0 = b * step + side * half
            norm_ref[pl.ds(pl.multiple_of(i0 * own_j, 16), count), :] = flat[cut]
            mask = mask_ref[pl.ds(i0, step)].astype(f32).reshape(count, tri)
            right = mask * sigmoid(proj[cut, :tri]) * proj[cut, tri:]
            right_ref[pl.ds(i0, step)] = right.reshape(step, own_j, tri).astype(bf16)
        return carry

    lax.fori_loop(0, half // step, rows, 0)


def left_body(norm_ref, mask_ref, win_ref, *outs):
    own_i, own_j, tri = mask_ref.shape
    group = 8 if own_i % 8 == 0 else 1
    at = 0
    for out in outs:
        first = at

        def rows(b, carry):
            i0 = first + b * group
            flat = norm_ref[pl.ds(pl.multiple_of(i0 * own_j, 16), group * own_j), :]
            mask = mask_ref[pl.ds(i0, group)].astype(f32).reshape(group * own_j, tri)
            proj = jnp.dot(flat, win_ref[:, : 2 * tri], preferred_element_type=f32)
            left = mask * sigmoid(proj[:, :tri]) * proj[:, tri:]
            out[pl.ds(b * group, group)] = left.reshape(group, own_j, tri).astype(bf16)
            return carry

        lax.fori_loop(0, out.shape[0] // group, rows, 0, unroll=True)
        at += out.shape[0]


def contract(lf_ref, halves, i0, group):
    step = 8
    acc = (jnp.zeros(halves[0].shape[1:], f32),) * group
    for h, r_ref in enumerate(halves):
        depth = r_ref.shape[0]

        def add(kb, acc):
            k0 = kb * step
            acc = list(acc)
            for d in range(step):
                right = r_ref[k0 + d].astype(f32)
                for t in range(group):
                    acc[t] = acc[t] + lf_ref[i0 + t, pl.ds(h * depth + k0 + d, 1), :] * right
            return tuple(acc)

        acc = lax.fori_loop(0, depth // step, add, acc)
    return acc


def sums_body(first, right0_ref, right1_ref, l_ref, m_ref, o_ref, lf_ref):
    count, depth = o_ref.shape[0], l_ref.shape[1]
    group = 8
    lf_ref[:, pl.ds(0, depth), :] = l_ref[pl.ds(first, count)].astype(f32)
    lf_ref[:, pl.ds(depth, depth), :] = m_ref[pl.ds(first, count)].astype(f32)

    def rows(b, carry):
        acc = contract(lf_ref, (right0_ref, right1_ref), b * group, group)
        for t in range(group):
            o_ref[b * group + t] = acc[t].astype(o_ref.dtype)
        return carry

    lax.fori_loop(0, count // group, rows, 0)


def open_body(x_hbm, w_hbm, valid_hbm, couple_hbm, *refs):
    later, outs, brought = refs[:5], refs[5:9], refs[9:14]
    block_ref, longer_ref, x_ref, w_ref, valid_ref, y_ref, sem = refs[14:]
    own_i, own_j, chans = couple_hbm.shape
    copies = fetch([(x_hbm, x_ref), (w_hbm, w_ref), (valid_hbm, valid_ref),
                    (couple_hbm, block_ref.at[pl.ds(0, own_i)]),
                    (couple_hbm, longer_ref.at[pl.ds(0, own_i)]), *zip(later, brought)], sem)
    seqs, residues, depth = x_ref.shape
    width = w_ref.shape[0] // 2
    height, lanes = outs[0].shape
    me = lax.axis_index("row")
    z = lax.axis_index("col")
    copies[0].wait()
    x = x_ref[...].astype(f32).reshape(seqs * residues, depth)
    normed = standardize(x).astype(bf16)
    copies[1].wait()
    y_ref[...] = lax.dot_general(
        normed, w_ref[...], (((1,), (1,)), ((), ())), preferred_element_type=f32
    )

    def cut(start, lane):
        start = pl.multiple_of(start * own_i, 8)
        return [y_ref[pl.ds(s * residues + start, own_i), lane : lane + width] for s in range(seqs)]

    empty = jnp.zeros((own_i, seqs * width), f32)
    shared = cut(z, 0) + cut(z ^ 2, 0) + [empty] + cut(z, width) + cut(z ^ 1, width)
    below = jnp.zeros((height - own_i, lanes), f32)
    for d, out in enumerate(outs):
        rows = jnp.concatenate(cut(me ^ d, 0) + shared, axis=1)
        out[...] = jnp.concatenate([rows, below], axis=0).astype(bf16)
    copies[2].wait()
    mask = valid_ref[...].astype(f32).T
    mask = jnp.concatenate([mask, jnp.zeros((own_j, chans - own_i), f32)], axis=1)
    block_ref[own_i] = mask.astype(bf16)
    for n in range(own_i, longer_ref.shape[0]):
        longer_ref[n] = mask.astype(bf16)
    for copy in copies[3:]:
        copy.wait()


def ready_body(seqs, avg_ref, ids_hbm, wq_ref, pick_ref, idt_ref, wf_ref, ids_ref, sem):
    (copy,) = fetch([(ids_hbm, ids_ref)], sem)
    pairs, width, _ = wq_ref.shape
    kinds, blocks, lanes, _ = pick_ref.shape
    total = blocks * seqs
    row = lax.broadcasted_iota(jnp.int32, pick_ref.shape[2:], 0)
    col = lax.broadcasted_iota(jnp.int32, pick_ref.shape[2:], 1)
    for n in range(kinds):
        unit = row - n * seqs * width
        place = lax.rem(unit, width) * total + lax.div(unit, width)
        place = jnp.where((unit >= 0) & (unit < seqs * width), col - place, -1)
        for r in range(blocks):
            pick_ref[n, r] = jnp.where(place == r * seqs, 1.0, 0.0).astype(bf16)
    wf_ref[...] = avg_ref[...].astype(f32)
    for h in range(pairs):
        both = [wf_ref[pl.ds(2 * h + d, width, stride=width), :] for d in range(2)]
        wq_ref[h] = jnp.concatenate(both, axis=1).astype(bf16)
    copy.wait()

    def spread(n, carry):
        idt_ref[pl.ds(n, 1), :] = jnp.full((1, idt_ref.shape[1]), ids_ref[n], jnp.int32)
        return carry

    lax.fori_loop(0, idt_ref.shape[0], spread, 0, unroll=8)


def mix_body(seqs, width, own_i, sets, blocks, *refs):
    msgs, (wq_ref, pick_ref), outs, xl_ref = refs[:blocks], refs[blocks : blocks + 2], refs[blocks + 2 : -1], refs[-1]
    total = seqs * blocks
    half = own_i // 2
    chans = wq_ref.shape[2] // 2
    for t_ref, n in zip(outs, sets):
        group = n // 2 * 128
        for r in range(blocks):
            m = msgs[r][pl.ds(0, own_i), group : group + 128].astype(f32)
            for s in range(seqs):
                lane = (n % 2) * seqs * width + s * width
                moved = pltpu.roll(m, 128 - lane, 1) if lane else m
                xl_ref[pl.ds(r * seqs + s, own_i, stride=total), :] = moved
        lhs = xl_ref[:, :width].astype(bf16)
        for h in range(width // 2):
            out = jnp.dot(lhs, wq_ref[h], preferred_element_type=f32)
            parts = [out[:, d * chans : (d + 1) * chans].reshape(own_i, total, chans) for d in range(2)]
            block = jnp.concatenate(parts, axis=1).astype(bf16)
            where = pl.ds(h * 2 * total, 2 * total)
            t_ref[:, where, :chans] = block[:half]
            t_ref[:, where, chans:] = block[half:]
    if len(outs) > len(sets):
        joined = jnp.concatenate([msg[:, 256:384] for msg in msgs], axis=1)
        for n in range(pick_ref.shape[0]):
            picks = pick_ref[n].reshape(blocks * 128, width * total)
            right = jnp.dot(joined, picks, preferred_element_type=f32)[:own_i]
            outs[-1][n] = (right * (1.0 / total)).astype(bf16)


def block_norms(block_ref, t_ref, right, row0, col0, idt_ref, bias_ref, use):
    half, terms, _ = t_ref.shape
    own_i, own_j, chans = 2 * half, right.shape[0], bias_ref.shape[1]
    idc = idt_ref[pl.ds(pl.multiple_of(col0, 8), own_j), :]
    step = 4
    for b in range(half // step):
        rows, psums = [[], []], [[], []]
        for i in range(b * step, b * step + step):
            both = jnp.dot(right, t_ref[i], preferred_element_type=f32)
            for side in range(2):
                at = i + side * half
                same = idc == idt_ref[pl.ds(row0 + at, 1), :]
                base = block_ref[at].astype(f32) + jnp.where(same, bias_ref[0:1, :], bias_ref[1:2, :])
                rows[side].append(at)
                psums[side].append((base + both[:, side * chans : (side + 1) * chans]).astype(bf16))
        rows, psums = rows[0] + rows[1], psums[0] + psums[1]
        flat = jnp.concatenate([standardize(p.astype(f32)) for p in psums], axis=0).astype(bf16)
        use(rows, psums, flat)


def gated(block_ref, rows, flat, w_ref):
    own_j = block_ref.shape[1]
    tri = w_ref.shape[1] // 2
    mask = block_ref[block_ref.shape[0] - 1].astype(f32)
    proj = jnp.dot(flat, w_ref[...], preferred_element_type=f32)
    both = sigmoid(proj[:, :tri]) * proj[:, tri:]
    return [mask[:, at : at + 1] * both[n * own_j : (n + 1) * own_j] for n, at in enumerate(rows)]


def own_body(block_ref, t_ref, right_ref, idt_ref, bias_ref, win_ref, wgate_ref, psum_ref, gate_ref, left_ref):
    own_i, own_j, chans = psum_ref.shape
    r, z = lax.axis_index("row"), lax.axis_index("col")
    w_left = win_ref.at[:, pl.ds(0, win_ref.shape[1] // 2)]

    def use(rows, psums, flat):
        lefts = gated(block_ref, rows, flat, w_left)
        gate = sigmoid(jnp.dot(flat, wgate_ref[...], preferred_element_type=f32))
        for n, at in enumerate(rows):
            psum_ref[at] = psums[n]
            gate_ref[at] = gate[n * own_j : (n + 1) * own_j]
            left_ref[at] = lefts[n].astype(bf16)

    block_norms(block_ref, t_ref, right_ref[0], r * own_i, z * own_j, idt_ref, bias_ref, use)


def met_body(block_ref, t_ref, right_ref, idt_ref, bias_ref, win_ref, left_ref):
    own_i, own_j, _ = left_ref.shape
    r, z = lax.axis_index("row"), lax.axis_index("col")
    w_left = win_ref.at[:, pl.ds(0, win_ref.shape[1] // 2)]

    def use(rows, psums, flat):
        for at, left in zip(rows, gated(block_ref, rows, flat, w_left)):
            left_ref[at] = left.astype(bf16)

    block_norms(block_ref, t_ref, right_ref[1], r * own_i, (z ^ 1) * own_j, idt_ref, bias_ref, use)


def right_body(own_pair, h, a_ref, b_ref, c_ref, d_ref, t_ref, right_ref, idt_ref, bias_ref, win_ref, out_ref,
               block_ref, flat_ref, sem):
    own_j, own_i, tri = out_ref.shape
    r, z = lax.axis_index("row"), lax.axis_index("col")
    keeper = (r % 2) == (z % 2)
    near = ((r // 2) == (z // 2)) == own_pair
    table = [(near & keeper, a_ref), (near & ~keeper, b_ref), (~near & keeper, c_ref), (~near & ~keeper, d_ref)]
    for cond, src in table:

        @pl.when(cond)
        def _():
            pltpu.make_async_copy(src.at[pl.ds(0, block_ref.shape[0])], block_ref, sem).start()

    pltpu.make_async_copy(a_ref.at[pl.ds(0, block_ref.shape[0])], block_ref, sem).wait()
    side = win_ref.shape[1] // 2
    w_right = win_ref.at[:, pl.ds(side, side)]

    def use(rows, psums, flat):
        for at, right in zip(rows, gated(block_ref, rows, flat, w_right)):
            flat_ref[pl.ds(at * own_j, own_j), :] = right

    row0 = (z if own_pair else z ^ 2) * own_i
    col0 = (z ^ h) * own_j
    block_norms(block_ref, t_ref, right_ref[h], row0, col0, idt_ref, bias_ref, use)
    for k in range(own_j):
        out_ref[k] = flat_ref[pl.ds(k, own_i, stride=own_j), :].astype(bf16)


def join_body(first, parts, own_ref, psum_ref, gate_ref, w_ref, *refs):
    sums, (out_hbm, done_ref, sem) = refs[:parts], refs[-3:]
    count, extent, chans = done_ref.shape
    group = 8
    at = 0
    for sum_ref in sums:
        start = at

        def rows(b, carry):
            here = pl.ds(start + b * group, group)
            there = pl.ds(first + start + b * group, group)
            mixed = own_ref[there] + sum_ref[pl.ds(b * group, group)].astype(f32)
            normed = standardize(mixed).reshape(group * extent, -1).astype(bf16)
            update = jnp.dot(normed, w_ref[...], preferred_element_type=f32).reshape(group, extent, -1)
            done_ref[here] = (psum_ref[there].astype(f32) + gate_ref[there] * update).astype(bf16)
            return carry

        lax.fori_loop(0, sum_ref.shape[0] // group, rows, 0, unroll=True)
        at += sum_ref.shape[0]
    copy = pltpu.make_async_copy(done_ref, out_hbm.at[pl.ds(first, count)], sem)
    copy.start()
    copy.wait()


def triangle_body(l_ref, r_ref, o_ref, lf_ref, flat_ref, rk_ref):
    own_i, depth, chans = l_ref.shape
    extent = r_ref.shape[0]
    group = 8 if own_i % 8 == 0 else 1

    @pl.when(pl.program_id(0) == 0)
    def _():
        lf_ref[...] = l_ref[...].astype(f32)

    def widen(j, carry):
        flat_ref[pl.ds(pl.multiple_of(j * depth, 8), depth), :] = r_ref[j].astype(f32)
        return carry

    lax.fori_loop(0, extent, widen, 0)

    def turn(k, carry):
        rk_ref[k] = flat_ref[pl.ds(k, extent, stride=depth), :]
        return carry

    lax.fori_loop(0, depth, turn, 0)

    def rows(b, carry):
        i0 = b * group
        acc = contract(lf_ref, [rk_ref], i0, group)
        for t in range(group):
            o_ref[0, i0 + t] = acc[t].astype(bf16)
        return carry

    lax.fori_loop(0, own_i // group, rows, 0)


def finish_body(sum_ref, psum_ref, norm_ref, wgate_ref, w_ref, out_ref):
    parts, own_i, extent, chans = sum_ref.shape
    own_j = psum_ref.shape[1]

    def row(i, carry):
        flat = norm_ref[pl.ds(pl.multiple_of(i * own_j, 16), own_j), :]
        gate = sigmoid(jnp.dot(flat, wgate_ref[...], preferred_element_type=f32))
        normed = [standardize(sum_ref[part, i].astype(f32)) for part in range(parts)]
        normed = jnp.concatenate(normed, axis=0).astype(bf16)
        update = jnp.dot(normed, w_ref[...], preferred_element_type=f32)
        out_ref[i] = (psum_ref[i].astype(f32) + gate * update).astype(bf16)
        return carry

    lax.fori_loop(0, own_i, row, 0)


def gathered_plan(left, right, psum, norm, w_gate, w_final):
    own_i, own_j, chans = psum.shape
    rows = lax.axis_size("row")
    tri = w_final.shape[0]
    right_all = lax.all_gather(right, "row", axis=0, tiled=True)
    partial = pl.pallas_call(
        triangle_body,
        grid=(rows,),
        out_shape=jax.ShapeDtypeStruct((rows, own_i, own_i, tri), bf16),
        in_specs=[
            pl.BlockSpec((own_i, own_j, tri), lambda r: (0, 0, 0)),
            pl.BlockSpec((own_i, own_j, tri), lambda r: (r, 0, 0)),
        ],
        out_specs=pl.BlockSpec((1, own_i, own_i, tri), lambda r: (r, 0, 0, 0)),
        scratch_shapes=[
            pltpu.VMEM((own_i, own_j, tri), f32),
            pltpu.VMEM((own_i * own_j, tri), f32),
            pltpu.VMEM((own_j, own_i, tri), f32),
        ],
        compiler_params=limit(56),
        name="triangle",
    )(left, right_all)
    summed = lax.psum_scatter(partial, "col", scatter_dimension=0, tiled=True)
    return pl.pallas_call(
        finish_body,
        out_shape=jax.ShapeDtypeStruct((own_i, own_j, chans), bf16),
        in_specs=[VMEM] * 5,
        out_specs=VMEM,
        compiler_params=limit(56),
        name="finish",
    )(summed, psum, norm, w_gate, w_final)


def paired_plan(homolog, couple, ids, valid, bias, factors, average, w_in, w_gate, w_final):
    seqs, residues, depth = homolog.shape
    own_i, own_j, chans = couple.shape
    width = factors.shape[1] // 2
    tri = w_final.shape[0]
    total = seqs * 4
    cells = [(r, z) for r in range(4) for z in range(4)]
    struct = jax.ShapeDtypeStruct

    def move(value, step):
        pairs = [(r * 4 + z, step(r, z)) for r, z in cells]
        pairs = [(src, r * 4 + z) for src, (r, z) in pairs]
        return lax.ppermute(value, ("row", "col"), pairs)

    def call(body, us, out_shape, scratch, *args, mib=12):
        return pl.pallas_call(
            body,
            out_shape=out_shape,
            in_specs=[VMEM] * len(args),
            out_specs=[VMEM] * len(out_shape) if isinstance(out_shape, list) else VMEM,
            scratch_shapes=scratch,
            compiler_params=limit(mib),
            cost_estimate=cost(us),
            name=getattr(body, "func", body).__name__.removesuffix("_body"),
        )(*args)

    keeper = lambda r, z: r % 2 == z % 2
    beside = lambda r, z: (r ^ 1, z)
    height, lanes = round_up(own_i, 16), 384
    block = struct((own_i + 1, own_j, chans), bf16)
    longer = struct((own_i + 2, own_j, chans), bf16)
    later = (average, bias, w_in, w_gate, w_final)
    *msgs, average, bias, w_in, w_gate, w_final, own, own_z = pl.pallas_call(
        open_body,
        out_shape=[struct((height, lanes), bf16)] * 4 + [struct(x.shape, x.dtype) for x in later] + [block, longer],
        in_specs=[HBM] * 9,
        out_specs=[VMEM] * 11,
        scratch_shapes=[
            pltpu.VMEM(homolog.shape, bf16),
            pltpu.VMEM((2 * width, depth), bf16),
            pltpu.VMEM(valid.shape, jnp.int32),
            pltpu.VMEM((seqs * residues, 2 * width), f32),
            pltpu.SemaphoreType.DMA((10,)),
        ],
        compiler_params=limit(8),
        cost_estimate=cost(1.5),
        name="open",
    )(*map(hold, (homolog, factors.T, valid, couple) + later))
    msgs = [msgs[0]] + [
        lax.ppermute(msgs[d], "row", [(r, r ^ d) for r in range(4)]) for d in (1, 2, 3)
    ]
    far = move(own, lambda r, z: (r ^ 2, z) if keeper(r, z) else (r ^ 3, z ^ 1))
    met = move(own_z, lambda r, z: (r, z ^ 1))

    wq, pick, idt = pl.pallas_call(
        functools.partial(ready_body, seqs),
        out_shape=[struct((width // 2, width, 2 * chans), bf16),
                   struct((2, 4, 128, width * total), bf16),
                   struct((residues, 128), jnp.int32)],
        in_specs=[VMEM, HBM],
        out_specs=[VMEM] * 3,
        scratch_shapes=[
            pltpu.VMEM(average.shape, f32),
            pltpu.SMEM(ids.shape, jnp.int32),
            pltpu.SemaphoreType.DMA((1,)),
        ],
        compiler_params=limit(8),
        cost_estimate=cost(1.5),
        name="ready",
    )(average, hold(ids))

    raw, _ = lax.optimization_barrier((own, idt))
    p_own = move(raw, beside)
    t_shape = struct((own_i // 2, width * total, 2 * chans), bf16)
    xl = [pltpu.VMEM((own_i * total, 128), f32)]
    t_own, t_send, right = call(
        functools.partial(mix_body, seqs, width, own_i, (0, 2), 4), 2.4,
        [t_shape, t_shape, struct((2, own_j, width * total), bf16)], xl, *msgs, wq, pick,
    )
    left_shape = struct((own_i, own_j, tri), bf16)
    psum, gate, left = call(
        own_body, 2.4,
        [struct(couple.shape, bf16), struct(couple.shape, f32), left_shape], [],
        own, t_own, right, idt, bias, w_in, w_gate,
    )

    def make_right(own_pair, h, t, blocks):
        return call(
            functools.partial(right_body, own_pair, h), 1.8,
            struct((own_j, own_i, tri), bf16),
            [pltpu.VMEM(block.shape, bf16), pltpu.VMEM((own_i * own_j, tri), f32), pltpu.SemaphoreType.DMA],
            *blocks, t, right, idt, bias, w_in,
        )

    far, *_ = lax.optimization_barrier((far, psum))
    p_far = move(far, beside)
    here = (own, p_own, far, p_far)
    send0 = make_right(False, 0, t_send, here)
    met, *_ = lax.optimization_barrier((met, send0))
    p_met = move(met, beside)
    there = (met, p_met, p_far, far)
    met_left = call(met_body, 1.8, left_shape, [], met, t_own, right, idt, bias, w_in)
    send1 = make_right(False, 1, t_send, there)

    def sums(rights, first, n, dtype):
        return call(
            functools.partial(sums_body, first), 0.13 * n, struct((n, own_j, tri), dtype),
            [pltpu.VMEM((n, 2 * own_j, tri), f32)], *rights, left, met_left,
        )

    chunks = [(0, 16), (16, 16), (32, own_i - 32)]
    leaving = [sums((send0, send1), first, n, bf16) for first, n in chunks]
    came = [move(part, lambda r, z: (r, z ^ 2)) for part in leaving]

    msgs, _ = lax.optimization_barrier((msgs, leaving[-1]))
    t_keep = call(functools.partial(mix_body, seqs, width, own_i, (1,), 4), 1.2, [t_shape], xl, *msgs, wq, pick)[0]
    rights = make_right(True, 0, t_keep, here), make_right(True, 1, t_keep, there)
    kept = sums(rights, 0, own_i, f32)

    out = []
    for first, n, parts in ((0, 16, came[:1]), (16, own_i - 16, came[1:])):
        out = [pl.pallas_call(
            functools.partial(join_body, first, len(parts)),
            out_shape=struct(couple.shape, bf16),
            in_specs=[VMEM] * (4 + len(parts)) + [HBM] * len(out),
            out_specs=HBM,
            scratch_shapes=[pltpu.VMEM((n, own_j, chans), bf16), pltpu.SemaphoreType.DMA],
            input_output_aliases={4 + len(parts): 0} if out else {},
            compiler_params=limit(8),
            cost_estimate=cost(0.06 * n),
            name="join",
        )(kept, psum, gate, w_final, *parts, *out)]
    return out[0]


def shards(homolog, couple, ids, valid, bias, factors, average, w_in, w_gate, w_final):
    rows, cols = lax.axis_size("row"), lax.axis_size("col")
    own_seqs, residues, depth = homolog.shape
    own_i, own_j, chans = couple.shape
    width = factors.shape[1] // 2
    tri = w_final.shape[0]
    total = own_seqs * rows
    lanes = round_up(2 * own_seqs * width, 128)
    height = round_up(max(own_i, own_j), 16)
    paired = (rows, cols, own_seqs * width, chans, tri) == (4, 4, 64, 128, 128)
    if paired and own_i == own_j == 40:
        return paired_plan(homolog, couple, ids, valid, bias, factors, average, w_in, w_gate, w_final)
    scale = 8

    later = (average, valid, bias, couple)
    *msgs, average, valid, bias, couple = pl.pallas_call(
        functools.partial(align_body, own_i, own_j, rows),
        out_shape=[jax.ShapeDtypeStruct((height, lanes), bf16)] * rows
        + [jax.ShapeDtypeStruct(x.shape, x.dtype) for x in later],
        in_specs=[HBM] * 6,
        out_specs=[VMEM] * (rows + 4),
        scratch_shapes=[
            pltpu.VMEM(homolog.shape, bf16),
            pltpu.VMEM((2 * width, depth), bf16),
            pltpu.VMEM((own_seqs * residues, 2 * width), f32),
            pltpu.SemaphoreType.DMA((6,)),
        ],
        compiler_params=limit(8, scale),
        cost_estimate=cost(1.5),
        name="align",
    )(hold(homolog), hold(factors.T), *map(hold, later))
    msgs = [msgs[0]] + [
        lax.ppermute(msgs[d], "row", [(r, r ^ d) for r in range(rows)])
        for d in reversed(range(1, rows))
    ]

    base, mask, wq, pick = pl.pallas_call(
        functools.partial(prepare_body, own_seqs),
        out_shape=[jax.ShapeDtypeStruct((own_i, own_j, chans), f32),
                   jax.ShapeDtypeStruct((own_i, own_j, tri), bf16),
                   jax.ShapeDtypeStruct((width // 2, width, 2 * chans), bf16),
                   jax.ShapeDtypeStruct((rows, lanes, width * total), bf16)],
        in_specs=[VMEM, HBM, VMEM, VMEM, VMEM],
        out_specs=[VMEM] * 4,
        scratch_shapes=[
            pltpu.VMEM(average.shape, f32),
            pltpu.VMEM((own_j, chans), jnp.int32),
            pltpu.SMEM(ids.shape, jnp.int32),
            pltpu.SemaphoreType.DMA((1,)),
        ],
        compiler_params=limit(8, scale),
        cost_estimate=cost(2),
        name="prepare",
    )(couple, hold(ids), valid, bias, average)

    extents = (own_i, own_j)
    psum, norm, right = pl.pallas_call(
        functools.partial(pair_body, own_seqs, width, rows),
        out_shape=[jax.ShapeDtypeStruct((own_i, own_j, chans), bf16),
                   jax.ShapeDtypeStruct((own_i * own_j, chans), bf16),
                   jax.ShapeDtypeStruct(extents + (tri,), bf16)],
        in_specs=[VMEM] * (rows + 5),
        out_specs=[VMEM] * 3,
        scratch_shapes=[
            pltpu.VMEM((own_i * total, 128), f32),
            pltpu.VMEM((own_i // 2, width * total, 2 * chans), bf16),
        ],
        compiler_params=limit(16, scale),
        cost_estimate=cost(4.5),
        name="pair",
    )(*msgs, base, mask, wq, pick, w_in)

    cuts = [own_i]
    lefts = pl.pallas_call(
        left_body,
        out_shape=[jax.ShapeDtypeStruct((n, own_j, tri), bf16) for n in cuts],
        in_specs=[VMEM] * 3,
        out_specs=[VMEM] * len(cuts),
        compiler_params=limit(8, scale),
        cost_estimate=cost(1),
        name="left",
    )(norm, mask, w_in)
    return gathered_plan(lefts[0], right, psum, norm, w_gate, w_final)


def solution(mesh):
    placed = (
        P(("grp", "row"), None, None),
        P(("grp", "row"), "col", None),
        P("grp"),
        P(("grp", "row"), "col"),
        P(),
        P(),
        P(),
        P(),
        P(),
        P(),
    )
    return jax.shard_map(
        shards,
        mesh=mesh,
        in_specs=placed,
        out_specs=P(("grp", "row"), "col", None),
        check_vma=False,
    )
```

```python
import functools

import jax
import jax.numpy as jnp
from jax import lax
from jax.experimental import pallas as pl
from jax.experimental.pallas import tpu as pltpu
from jax.sharding import PartitionSpec as P

eps = 1e-05
f32 = jnp.float32
bf16 = jnp.bfloat16
VMEM = pl.BlockSpec(memory_space=pltpu.VMEM)
SMEM = pl.BlockSpec(memory_space=pltpu.SMEM)
HBM = pl.BlockSpec(memory_space=pltpu.HBM)


def limit(mib, scale=1):
    return pltpu.CompilerParams(vmem_limit_bytes=min(56, mib * scale) * 1024 * 1024)


def round_up(n, m):
    return (n + m - 1) // m * m


def cost(us):
    return pl.CostEstimate(flops=0, bytes_accessed=int(us * 3.69e6), transcendentals=0)


def hold(x):
    return pltpu.with_memory_space_constraint(x, pltpu.HBM)


def fetch(pairs, sem):
    copies = [pltpu.make_async_copy(src, dst, sem.at[n]) for n, (src, dst) in enumerate(pairs)]
    for copy in copies:
        copy.start()
    return copies


def standardize(values):
    centre = values - jnp.mean(values, axis=-1, keepdims=True)
    spread = jnp.mean(centre * centre, axis=-1, keepdims=True)
    return centre * lax.rsqrt(spread + eps)


def sigmoid(v):
    return 0.5 * jnp.tanh(0.5 * v) + 0.5


def align_body(own_i, own_j, count, x_hbm, w_hbm, *refs):
    later, outs, refs = refs[:4], refs[4 : 4 + count], refs[4 + count :]
    brought, (x_ref, w_ref, y_ref, sem) = refs[:4], refs[4:]
    copies = fetch([(x_hbm, x_ref), (w_hbm, w_ref), *zip(later, brought)], sem)
    seqs, residues, depth = x_ref.shape
    width = w_ref.shape[0] // 2
    height, lanes = outs[0].shape
    me = lax.axis_index("row")
    z = lax.axis_index("col")
    copies[0].wait()
    x = x_ref[...].astype(f32).reshape(seqs * residues, depth)
    normed = standardize(x).astype(bf16)
    copies[1].wait()
    y_ref[...] = lax.dot_general(
        normed, w_ref[...], (((1,), (1,)), ((), ())), preferred_element_type=f32
    )
    start = pl.multiple_of(z * own_j, 8)

    def tall(v):
        gap = height - v.shape[0]
        return jnp.concatenate([v, jnp.zeros((gap, v.shape[1]), f32)], axis=0) if gap else v

    right = [tall(y_ref[pl.ds(s * residues + start, own_j), width:]) for s in range(seqs)]
    gap = lanes - 2 * seqs * width
    right += [jnp.zeros((height, gap), f32)] if gap else []
    for d, out in enumerate(outs):
        first = pl.multiple_of((me ^ d) * own_i, 8)
        left = [tall(y_ref[pl.ds(s * residues + first, own_i), :width]) for s in range(seqs)]
        out[...] = jnp.concatenate(left + right, axis=1).astype(bf16)
    for copy in copies[2:]:
        copy.wait()


def prepare_body(seqs, couple_ref, ids_hbm, valid_ref, bias_ref, avg_ref, base_ref, mask_ref, wq_ref, pick_ref,
                 wf_ref, idc_ref, ids_ref, sem):
    (copy,) = fetch([(ids_hbm, ids_ref)], sem)
    own_i, own_j, chans = couple_ref.shape
    pairs, width, _ = wq_ref.shape
    blocks, lanes, _ = pick_ref.shape
    total = blocks * seqs
    x0 = lax.axis_index("row") * own_i
    z0 = lax.axis_index("col") * own_j

    row = lax.broadcasted_iota(jnp.int32, pick_ref.shape[1:], 0)
    col = lax.broadcasted_iota(jnp.int32, pick_ref.shape[1:], 1)
    unit = row - seqs * width
    place = lax.rem(unit, width) * total + lax.div(unit, width)
    place = jnp.where((unit >= 0) & (unit < seqs * width), col - place, -1)

    def pick(r, carry):
        pick_ref[r] = jnp.where(place == r * seqs, 1.0, 0.0).astype(bf16)
        return carry

    lax.fori_loop(0, blocks, pick, 0)
    wf_ref[...] = avg_ref[...].astype(f32)
    for h in range(pairs):
        both = [wf_ref[pl.ds(2 * h + d, width, stride=width), :] for d in range(2)]
        wq_ref[h] = jnp.concatenate(both, axis=1).astype(bf16)
    copy.wait()
    for j in range(own_j):
        idc_ref[pl.ds(j, 1), :] = jnp.full((1, chans), ids_ref[z0 + j], jnp.int32)
    idc = idc_ref[...]
    valid_t = valid_ref[...].astype(f32).T
    lane = lax.broadcasted_iota(jnp.int32, valid_t.shape, 1)
    same_bias = bias_ref[0:1, :]
    cross_bias = bias_ref[1:2, :]

    def rows(i, carry):
        bias = jnp.where(idc == ids_ref[x0 + i], same_bias, cross_bias)
        base_ref[i] = couple_ref[i].astype(f32) + bias
        column = jnp.sum(jnp.where(lane == i, valid_t, 0.0), axis=1, keepdims=True)
        mask_ref[i] = jnp.broadcast_to(column, (own_j, mask_ref.shape[2])).astype(bf16)
        return carry

    lax.fori_loop(0, own_i, rows, 0, unroll=8)


def pair_body(seqs, width, blocks, *refs):
    msgs = refs[:blocks]
    base_ref, mask_ref, wq_ref, pick_ref, win_ref = refs[blocks : blocks + 5]
    psum_ref, norm_ref, right_ref = refs[blocks + 5 : blocks + 8]
    xl_ref, t_ref = refs[blocks + 8 :]
    own_i, own_j, chans = base_ref.shape
    height, lanes = msgs[0].shape
    total = seqs * blocks
    tri = win_ref.shape[1] // 4
    half = own_i // 2

    for r in range(blocks):
        m = msgs[r][pl.ds(0, own_i), :].astype(f32)
        for s in range(seqs):
            moved = m if s == 0 else pltpu.roll(m, lanes - s * width, 1)
            xl_ref[pl.ds(r * seqs + s, own_i, stride=total), :] = moved[:, :128]
    lhs = xl_ref[:, :width].astype(bf16)

    joined = jnp.concatenate([msg[...] for msg in msgs], axis=1)
    picks = pick_ref[...].reshape(blocks * lanes, width * total)
    rmat = jnp.dot(joined, picks, preferred_element_type=f32)[:own_j].astype(bf16)

    def expand(h, carry):
        out = jnp.dot(lhs, wq_ref[h], preferred_element_type=f32)
        parts = [out[:, d * chans : (d + 1) * chans].reshape(own_i, total, chans) for d in range(2)]
        block = jnp.concatenate(parts, axis=1).astype(bf16)
        where = pl.ds(pl.multiple_of(h * 2 * total, 16), 2 * total)
        t_ref[:, where, :chans] = block[:half]
        t_ref[:, where, chans:] = block[half:]
        return carry

    lax.fori_loop(0, width // 2, expand, 0)

    step = 4 if half % 4 == 0 else 1

    def rows(b, carry):
        normed = [[], []]
        for g in range(step):
            i = b * step + g
            both = jnp.dot(rmat, t_ref[i], preferred_element_type=f32) * (1.0 / total)
            for side in range(2):
                at = i + side * half
                psum = (base_ref[at] + both[:, side * chans : (side + 1) * chans]).astype(bf16)
                psum_ref[at] = psum
                normed[side].append(standardize(psum.astype(f32)))
        flat = jnp.concatenate(normed[0] + normed[1], axis=0).astype(bf16)
        proj = jnp.dot(flat, win_ref[:, 2 * tri :], preferred_element_type=f32)
        count = step * own_j
        for side in range(2):
            cut = slice(side * count, (side + 1) * count)
            i0 = b * step + side * half
            norm_ref[pl.ds(pl.multiple_of(i0 * own_j, 16), count), :] = flat[cut]
            mask = mask_ref[pl.ds(i0, step)].astype(f32).reshape(count, tri)
            right = mask * sigmoid(proj[cut, :tri]) * proj[cut, tri:]
            right_ref[pl.ds(i0, step)] = right.reshape(step, own_j, tri).astype(bf16)
        return carry

    lax.fori_loop(0, half // step, rows, 0)


def left_body(norm_ref, mask_ref, win_ref, *outs):
    own_i, own_j, tri = mask_ref.shape
    group = 8 if own_i % 8 == 0 else 1
    at = 0
    for out in outs:
        first = at

        def rows(b, carry):
            i0 = first + b * group
            flat = norm_ref[pl.ds(pl.multiple_of(i0 * own_j, 16), group * own_j), :]
            mask = mask_ref[pl.ds(i0, group)].astype(f32).reshape(group * own_j, tri)
            proj = jnp.dot(flat, win_ref[:, : 2 * tri], preferred_element_type=f32)
            left = mask * sigmoid(proj[:, :tri]) * proj[:, tri:]
            out[pl.ds(b * group, group)] = left.reshape(group, own_j, tri).astype(bf16)
            return carry

        lax.fori_loop(0, out.shape[0] // group, rows, 0, unroll=True)
        at += out.shape[0]


def contract(lf_ref, halves, i0, group):
    step = 8
    acc = (jnp.zeros(halves[0].shape[1:], f32),) * group
    for h, r_ref in enumerate(halves):
        depth = r_ref.shape[0]

        def add(kb, acc):
            k0 = kb * step
            acc = list(acc)
            for d in range(step):
                right = r_ref[k0 + d].astype(f32)
                for t in range(group):
                    acc[t] = acc[t] + lf_ref[i0 + t, pl.ds(h * depth + k0 + d, 1), :] * right
            return tuple(acc)

        acc = lax.fori_loop(0, depth // step, add, acc)
    return acc


def sums_body(own_pair, first, own_ref, p_own, met_ref, p_met, far_ref, p_far, l_ref, m_ref, o_ref, lf_ref):
    count, depth = o_ref.shape[0], l_ref.shape[1]
    group = 8
    lf_ref[:, pl.ds(0, depth), :] = l_ref[pl.ds(first, count)].astype(f32)
    lf_ref[:, pl.ds(depth, depth), :] = m_ref[pl.ds(first, count)].astype(f32)

    def use(halves):
        def rows(b, carry):
            acc = contract(lf_ref, halves, b * group, group)
            for t in range(group):
                o_ref[b * group + t] = acc[t].astype(o_ref.dtype)
            return carry

        lax.fori_loop(0, count // group, rows, 0)

    r, z = lax.axis_index("row"), lax.axis_index("col")
    keeper = (r % 2) == (z % 2)
    near = ((r // 2) == (z // 2)) == own_pair
    table = [
        (near & keeper, own_ref, met_ref),
        (near & ~keeper, p_own, p_met),
        (~near & keeper, far_ref, p_far),
        (~near & ~keeper, p_far, far_ref),
    ]
    for cond, a, b in table:
        pl.when(cond)(functools.partial(use, (a, b)))


def open_body(x_hbm, w_hbm, valid_hbm, couple_hbm, *refs):
    later, outs, brought = refs[:5], refs[5:9], refs[9:14]
    block_ref, x_ref, w_ref, valid_ref, y_ref, sem = refs[14:]
    own_i, own_j, chans = couple_hbm.shape
    copies = fetch([(x_hbm, x_ref), (w_hbm, w_ref), (valid_hbm, valid_ref),
                    (couple_hbm, block_ref.at[pl.ds(0, own_i)]),
                    *zip(later, brought)], sem)
    seqs, residues, depth = x_ref.shape
    width = w_ref.shape[0] // 2
    height, lanes = outs[0].shape
    me = lax.axis_index("row")
    z = lax.axis_index("col")
    copies[0].wait()
    x = x_ref[...].astype(f32).reshape(seqs * residues, depth)
    normed = standardize(x).astype(bf16)
    copies[1].wait()
    y_ref[...] = lax.dot_general(
        normed, w_ref[...], (((1,), (1,)), ((), ())), preferred_element_type=f32
    )

    def cut(start, lane):
        start = pl.multiple_of(start * own_i, 8)
        return [y_ref[pl.ds(s * residues + start, own_i), lane : lane + width] for s in range(seqs)]

    empty = jnp.zeros((own_i, seqs * width), f32)
    shared = [empty] + cut(z, width) + cut(z ^ 1, width)
    below = jnp.zeros((height - own_i, lanes), f32)
    for d, out in enumerate(outs):
        rows = jnp.concatenate(cut(me ^ d, 0) + shared, axis=1)
        out[...] = jnp.concatenate([rows, below], axis=0).astype(bf16)
    copies[2].wait()
    mask = valid_ref[...].astype(f32).T
    mask = jnp.concatenate([mask, jnp.zeros((own_j, chans - own_i), f32)], axis=1)
    for n in range(own_i, block_ref.shape[0]):
        block_ref[n] = mask.astype(bf16)
    for copy in copies[3:]:
        copy.wait()


def ready_body(seqs, avg_ref, ids_hbm, wq_ref, pick_ref, idt_ref, wf_ref, ids_ref, sem):
    (copy,) = fetch([(ids_hbm, ids_ref)], sem)
    pairs, width, _ = wq_ref.shape
    kinds, blocks, lanes, _ = pick_ref.shape
    total = blocks * seqs
    row = lax.broadcasted_iota(jnp.int32, pick_ref.shape[2:], 0)
    col = lax.broadcasted_iota(jnp.int32, pick_ref.shape[2:], 1)
    for n in range(kinds):
        unit = row - n * seqs * width
        place = lax.rem(unit, width) * total + lax.div(unit, width)
        place = jnp.where((unit >= 0) & (unit < seqs * width), col - place, -1)
        for r in range(blocks):
            pick_ref[n, r] = jnp.where(place == r * seqs, 1.0, 0.0).astype(bf16)
    wf_ref[...] = avg_ref[...].astype(f32)
    for h in range(pairs):
        both = [wf_ref[pl.ds(2 * h + d, width, stride=width), :] for d in range(2)]
        wq_ref[h] = jnp.concatenate(both, axis=1).astype(bf16)
    copy.wait()

    def spread(n, carry):
        idt_ref[pl.ds(n, 1), :] = jnp.full((1, idt_ref.shape[1]), ids_ref[n], jnp.int32)
        return carry

    lax.fori_loop(0, idt_ref.shape[0], spread, 0, unroll=8)


def mix_body(seqs, width, *refs):
    msgs, (wq_ref, pick_ref, t_ref, right_ref, xl_ref) = refs[:4], refs[4:]
    half, terms, both = t_ref.shape
    chans, own_i, total = both // 2, 2 * half, seqs * 4
    for r in range(4):
        m = msgs[r][pl.ds(0, own_i), :128].astype(f32)
        for s in range(seqs):
            moved = pltpu.roll(m, 128 - s * width, 1) if s else m
            xl_ref[pl.ds(r * seqs + s, own_i, stride=total), :] = moved
    lhs = xl_ref[:, :width].astype(bf16)
    joined = jnp.concatenate([msg[:, 128:] for msg in msgs], axis=1)
    for n in range(2):
        right = jnp.dot(joined, pick_ref[n].reshape(512, terms), preferred_element_type=f32)[:own_i]
        right_ref[n] = (right * (1.0 / total)).astype(bf16)
    for h in range(width // 2):
        out = jnp.dot(lhs, wq_ref[h], preferred_element_type=f32)
        parts = [out[:, d * chans : (d + 1) * chans].reshape(own_i, total, chans) for d in range(2)]
        block = jnp.concatenate(parts, axis=1).astype(bf16)
        where = pl.ds(h * 2 * total, 2 * total)
        t_ref[:, where, :chans] = block[:half]
        t_ref[:, where, chans:] = block[half:]


def block_norms(block_ref, t_ref, right, row0, col0, idt_ref, bias_ref, use):
    half, terms, _ = t_ref.shape
    own_i, own_j, chans = 2 * half, right.shape[0], bias_ref.shape[1]
    idc = idt_ref[pl.ds(pl.multiple_of(col0, 8), own_j), :]
    step = 4
    for b in range(half // step):
        rows, psums = [[], []], [[], []]
        for i in range(b * step, b * step + step):
            both = jnp.dot(right, t_ref[i], preferred_element_type=f32)
            for side in range(2):
                at = i + side * half
                same = idc == idt_ref[pl.ds(row0 + at, 1), :]
                base = block_ref[at].astype(f32) + jnp.where(same, bias_ref[0:1, :], bias_ref[1:2, :])
                rows[side].append(at)
                psums[side].append((base + both[:, side * chans : (side + 1) * chans]).astype(bf16))
        rows, psums = rows[0] + rows[1], psums[0] + psums[1]
        flat = jnp.concatenate([standardize(p.astype(f32)) for p in psums], axis=0).astype(bf16)
        use(rows, psums, flat)


def gated(block_ref, rows, flat, w_ref):
    own_j = block_ref.shape[1]
    tri = w_ref.shape[1] // 2
    mask = block_ref[block_ref.shape[0] - 1].astype(f32)
    proj = jnp.dot(flat, w_ref[...], preferred_element_type=f32)
    both = sigmoid(proj[:, :tri]) * proj[:, tri:]
    return [mask[:, at : at + 1] * both[n * own_j : (n + 1) * own_j] for n, at in enumerate(rows)]


def own_body(block_ref, t_ref, right_ref, idt_ref, bias_ref, win_ref, psum_ref, norm_ref, out_ref, flat_ref):
    own_i, own_j, chans = psum_ref.shape
    r, z = lax.axis_index("row"), lax.axis_index("col")
    side = win_ref.shape[1] // 2
    w_right = win_ref.at[:, pl.ds(side, side)]

    def use(rows, psums, flat):
        rights = gated(block_ref, rows, flat, w_right)
        for n, at in enumerate(rows):
            psum_ref[at] = psums[n]
            norm_ref[pl.ds(at * own_j, own_j), :] = flat[n * own_j : (n + 1) * own_j]
            flat_ref[pl.ds(at * own_j, own_j), :] = rights[n]

    block_norms(block_ref, t_ref, right_ref[0], r * own_i, z * own_j, idt_ref, bias_ref, use)
    for k in range(own_j):
        out_ref[k] = flat_ref[pl.ds(k, own_i, stride=own_j), :].astype(bf16)


def rest_body(block_ref, norm_ref, win_ref, wgate_ref, left_ref, gate_ref):
    own_i, own_j, _ = left_ref.shape
    w_left = win_ref.at[:, pl.ds(0, win_ref.shape[1] // 2)]
    group = 8
    for i in range(0, own_i, group):
        flat = norm_ref[pl.ds(i * own_j, group * own_j), :]
        rows = list(range(i, i + group))
        gate = sigmoid(jnp.dot(flat, wgate_ref[...], preferred_element_type=f32))
        for n, left in enumerate(gated(block_ref, rows, flat, w_left)):
            left_ref[i + n] = left.astype(bf16)
            gate_ref[i + n] = gate[n * own_j : (n + 1) * own_j]


def met_body(block_ref, t_ref, right_ref, idt_ref, bias_ref, win_ref, left_ref, out_ref, flat_ref):
    own_i, own_j, _ = left_ref.shape
    r, z = lax.axis_index("row"), lax.axis_index("col")
    side = win_ref.shape[1] // 2
    w_left, w_right = win_ref.at[:, pl.ds(0, side)], win_ref.at[:, pl.ds(side, side)]

    def use(rows, psums, flat):
        lefts = gated(block_ref, rows, flat, w_left)
        rights = gated(block_ref, rows, flat, w_right)
        for n, at in enumerate(rows):
            left_ref[at] = lefts[n].astype(bf16)
            flat_ref[pl.ds(at * own_j, own_j), :] = rights[n]

    block_norms(block_ref, t_ref, right_ref[1], r * own_i, (z ^ 1) * own_j, idt_ref, bias_ref, use)
    for k in range(own_j):
        out_ref[k] = flat_ref[pl.ds(k, own_i, stride=own_j), :].astype(bf16)


def join_body(first, parts, own_ref, psum_ref, gate_ref, w_ref, *refs):
    sums, (out_hbm, done_ref, sem) = refs[:parts], refs[-3:]
    count, extent, chans = done_ref.shape
    group = 8
    at = 0
    for sum_ref in sums:
        start = at

        def rows(b, carry):
            here = pl.ds(start + b * group, group)
            there = pl.ds(first + start + b * group, group)
            mixed = own_ref[there] + sum_ref[pl.ds(b * group, group)].astype(f32)
            normed = standardize(mixed).reshape(group * extent, -1).astype(bf16)
            update = jnp.dot(normed, w_ref[...], preferred_element_type=f32).reshape(group, extent, -1)
            done_ref[here] = (psum_ref[there].astype(f32) + gate_ref[there] * update).astype(bf16)
            return carry

        lax.fori_loop(0, sum_ref.shape[0] // group, rows, 0, unroll=True)
        at += sum_ref.shape[0]
    copy = pltpu.make_async_copy(done_ref, out_hbm.at[pl.ds(first, count)], sem)
    copy.start()
    copy.wait()


def triangle_body(l_ref, r_ref, o_ref, lf_ref, flat_ref, rk_ref):
    own_i, depth, chans = l_ref.shape
    extent = r_ref.shape[0]
    group = 8 if own_i % 8 == 0 else 1

    @pl.when(pl.program_id(0) == 0)
    def _():
        lf_ref[...] = l_ref[...].astype(f32)

    def widen(j, carry):
        flat_ref[pl.ds(pl.multiple_of(j * depth, 8), depth), :] = r_ref[j].astype(f32)
        return carry

    lax.fori_loop(0, extent, widen, 0)

    def turn(k, carry):
        rk_ref[k] = flat_ref[pl.ds(k, extent, stride=depth), :]
        return carry

    lax.fori_loop(0, depth, turn, 0)

    def rows(b, carry):
        i0 = b * group
        acc = contract(lf_ref, [rk_ref], i0, group)
        for t in range(group):
            o_ref[0, i0 + t] = acc[t].astype(bf16)
        return carry

    lax.fori_loop(0, own_i // group, rows, 0)


def finish_body(sum_ref, psum_ref, norm_ref, wgate_ref, w_ref, out_ref):
    parts, own_i, extent, chans = sum_ref.shape
    own_j = psum_ref.shape[1]

    def row(i, carry):
        flat = norm_ref[pl.ds(pl.multiple_of(i * own_j, 16), own_j), :]
        gate = sigmoid(jnp.dot(flat, wgate_ref[...], preferred_element_type=f32))
        normed = [standardize(sum_ref[part, i].astype(f32)) for part in range(parts)]
        normed = jnp.concatenate(normed, axis=0).astype(bf16)
        update = jnp.dot(normed, w_ref[...], preferred_element_type=f32)
        out_ref[i] = (psum_ref[i].astype(f32) + gate * update).astype(bf16)
        return carry

    lax.fori_loop(0, own_i, row, 0)


def gathered_plan(left, right, psum, norm, w_gate, w_final):
    own_i, own_j, chans = psum.shape
    rows = lax.axis_size("row")
    tri = w_final.shape[0]
    right_all = lax.all_gather(right, "row", axis=0, tiled=True)
    partial = pl.pallas_call(
        triangle_body,
        grid=(rows,),
        out_shape=jax.ShapeDtypeStruct((rows, own_i, own_i, tri), bf16),
        in_specs=[
            pl.BlockSpec((own_i, own_j, tri), lambda r: (0, 0, 0)),
            pl.BlockSpec((own_i, own_j, tri), lambda r: (r, 0, 0)),
        ],
        out_specs=pl.BlockSpec((1, own_i, own_i, tri), lambda r: (r, 0, 0, 0)),
        scratch_shapes=[
            pltpu.VMEM((own_i, own_j, tri), f32),
            pltpu.VMEM((own_i * own_j, tri), f32),
            pltpu.VMEM((own_j, own_i, tri), f32),
        ],
        compiler_params=limit(56),
        name="triangle",
    )(left, right_all)
    summed = lax.psum_scatter(partial, "col", scatter_dimension=0, tiled=True)
    return pl.pallas_call(
        finish_body,
        out_shape=jax.ShapeDtypeStruct((own_i, own_j, chans), bf16),
        in_specs=[VMEM] * 5,
        out_specs=VMEM,
        compiler_params=limit(56),
        name="finish",
    )(summed, psum, norm, w_gate, w_final)


def paired_plan(homolog, couple, ids, valid, bias, factors, average, w_in, w_gate, w_final):
    seqs, residues, depth = homolog.shape
    own_i, own_j, chans = couple.shape
    width = factors.shape[1] // 2
    tri = w_final.shape[0]
    total = seqs * 4
    cells = [(r, z) for r in range(4) for z in range(4)]
    struct = jax.ShapeDtypeStruct

    def move(value, step):
        pairs = [(r * 4 + z, step(r, z)) for r, z in cells]
        pairs = [(src, r * 4 + z) for src, (r, z) in pairs]
        return lax.ppermute(value, ("row", "col"), pairs)

    def call(body, us, out_shape, scratch, *args, mib=12):
        return pl.pallas_call(
            body,
            out_shape=out_shape,
            in_specs=[VMEM] * len(args),
            out_specs=[VMEM] * len(out_shape) if isinstance(out_shape, list) else VMEM,
            scratch_shapes=scratch,
            compiler_params=limit(mib),
            cost_estimate=cost(us),
            name=getattr(body, "func", body).__name__.removesuffix("_body"),
        )(*args)

    keeper = lambda r, z: r % 2 == z % 2
    beside = lambda r, z: (r ^ 1, z)
    height, lanes = round_up(own_i, 16), 256
    block = struct((own_i + 1, own_j, chans), bf16)
    later = (average, bias, w_in, w_gate, w_final)
    *msgs, average, bias, w_in, w_gate, w_final, raw = pl.pallas_call(
        open_body,
        out_shape=[struct((height, lanes), bf16)] * 4 + [struct(x.shape, x.dtype) for x in later] + [block],
        in_specs=[HBM] * 9,
        out_specs=[VMEM] * 10,
        scratch_shapes=[
            pltpu.VMEM(homolog.shape, bf16),
            pltpu.VMEM((2 * width, depth), bf16),
            pltpu.VMEM(valid.shape, jnp.int32),
            pltpu.VMEM((seqs * residues, 2 * width), f32),
            pltpu.SemaphoreType.DMA((9,)),
        ],
        compiler_params=limit(8),
        cost_estimate=cost(1.5),
        name="open",
    )(*map(hold, (homolog, factors.T, valid, couple) + later))
    msgs = [msgs[0]] + [
        lax.ppermute(msgs[d], "row", [(r, r ^ d) for r in range(4)]) for d in (1, 2, 3)
    ]
    met = move(raw, lambda r, z: (r, z ^ 1))

    wq, pick, idt = pl.pallas_call(
        functools.partial(ready_body, seqs),
        out_shape=[struct((width // 2, width, 2 * chans), bf16),
                   struct((2, 4, 128, width * total), bf16),
                   struct((residues, 128), jnp.int32)],
        in_specs=[VMEM, HBM],
        out_specs=[VMEM] * 3,
        scratch_shapes=[
            pltpu.VMEM(average.shape, f32),
            pltpu.SMEM(ids.shape, jnp.int32),
            pltpu.SemaphoreType.DMA((1,)),
        ],
        compiler_params=limit(8),
        cost_estimate=cost(1.5),
        name="ready",
    )(average, hold(ids))

    t, mixed = call(
        functools.partial(mix_body, seqs, width), 1,
        [struct((own_i // 2, width * total, 2 * chans), bf16), struct((2, own_j, width * total), bf16)],
        [pltpu.VMEM((own_i * total, 128), f32)], *msgs, wq, pick,
    )
    square = struct((own_i, own_j, tri), bf16)
    flat = [pltpu.VMEM((own_i * own_j, tri), f32)]
    psum, norm, right = call(
        own_body, 2.4, [square, struct((own_i * own_j, chans), bf16), square], flat,
        raw, t, mixed, idt, bias, w_in,
    )
    far = move(right, lambda r, z: (r ^ 2, z) if keeper(r, z) else (r ^ 3, z ^ 1))
    p_own = move(right, beside)
    left, gate = call(rest_body, 0.6, [square, struct(couple.shape, f32)], [], raw, norm, w_in, w_gate)
    met, *_ = lax.optimization_barrier((met, left))
    met_left, met_right = call(met_body, 3, [square, square], flat, met, t, mixed, idt, bias, w_in)
    p_met = move(met_right, beside)
    far, *_ = lax.optimization_barrier((far, met_left))
    p_far = move(far, beside)

    def sums(own_pair, first, n, dtype):
        return call(
            functools.partial(sums_body, own_pair, first), 0.13 * n, struct((n, own_j, tri), dtype),
            [pltpu.VMEM((n, 2 * own_j, tri), f32)],
            right, p_own, met_right, p_met, far, p_far, left, met_left,
        )

    came = [move(sums(False, first, 8, bf16), lambda r, z: (r, z ^ 2)) for first in range(0, own_i, 8)]
    kept = sums(True, 0, own_i, f32)

    out = []
    for first, n in ((0, 16), (16, own_i - 16)):
        parts = came[first // 8 : (first + n) // 8]
        out = [pl.pallas_call(
            functools.partial(join_body, first, len(parts)),
            out_shape=struct(couple.shape, bf16),
            in_specs=[VMEM] * (4 + len(parts)) + [HBM] * len(out),
            out_specs=HBM,
            scratch_shapes=[pltpu.VMEM((n, own_j, chans), bf16), pltpu.SemaphoreType.DMA],
            input_output_aliases={4 + len(parts): 0} if out else {},
            compiler_params=limit(8),
            cost_estimate=cost(0.06 * n),
            name="join",
        )(kept, psum, gate, w_final, *parts, *out)]
    return out[0]


def shards(homolog, couple, ids, valid, bias, factors, average, w_in, w_gate, w_final):
    rows, cols = lax.axis_size("row"), lax.axis_size("col")
    own_seqs, residues, depth = homolog.shape
    own_i, own_j, chans = couple.shape
    width = factors.shape[1] // 2
    tri = w_final.shape[0]
    total = own_seqs * rows
    lanes = round_up(2 * own_seqs * width, 128)
    height = round_up(max(own_i, own_j), 16)
    paired = (rows, cols, own_seqs * width, chans, tri) == (4, 4, 64, 128, 128)
    if paired and own_i == own_j == 40:
        return paired_plan(homolog, couple, ids, valid, bias, factors, average, w_in, w_gate, w_final)
    scale = 8

    later = (average, valid, bias, couple)
    *msgs, average, valid, bias, couple = pl.pallas_call(
        functools.partial(align_body, own_i, own_j, rows),
        out_shape=[jax.ShapeDtypeStruct((height, lanes), bf16)] * rows
        + [jax.ShapeDtypeStruct(x.shape, x.dtype) for x in later],
        in_specs=[HBM] * 6,
        out_specs=[VMEM] * (rows + 4),
        scratch_shapes=[
            pltpu.VMEM(homolog.shape, bf16),
            pltpu.VMEM((2 * width, depth), bf16),
            pltpu.VMEM((own_seqs * residues, 2 * width), f32),
            pltpu.SemaphoreType.DMA((6,)),
        ],
        compiler_params=limit(8, scale),
        cost_estimate=cost(1.5),
        name="align",
    )(hold(homolog), hold(factors.T), *map(hold, later))
    msgs = [msgs[0]] + [
        lax.ppermute(msgs[d], "row", [(r, r ^ d) for r in range(rows)])
        for d in reversed(range(1, rows))
    ]

    base, mask, wq, pick = pl.pallas_call(
        functools.partial(prepare_body, own_seqs),
        out_shape=[jax.ShapeDtypeStruct((own_i, own_j, chans), f32),
                   jax.ShapeDtypeStruct((own_i, own_j, tri), bf16),
                   jax.ShapeDtypeStruct((width // 2, width, 2 * chans), bf16),
                   jax.ShapeDtypeStruct((rows, lanes, width * total), bf16)],
        in_specs=[VMEM, HBM, VMEM, VMEM, VMEM],
        out_specs=[VMEM] * 4,
        scratch_shapes=[
            pltpu.VMEM(average.shape, f32),
            pltpu.VMEM((own_j, chans), jnp.int32),
            pltpu.SMEM(ids.shape, jnp.int32),
            pltpu.SemaphoreType.DMA((1,)),
        ],
        compiler_params=limit(8, scale),
        cost_estimate=cost(2),
        name="prepare",
    )(couple, hold(ids), valid, bias, average)

    extents = (own_i, own_j)
    psum, norm, right = pl.pallas_call(
        functools.partial(pair_body, own_seqs, width, rows),
        out_shape=[jax.ShapeDtypeStruct((own_i, own_j, chans), bf16),
                   jax.ShapeDtypeStruct((own_i * own_j, chans), bf16),
                   jax.ShapeDtypeStruct(extents + (tri,), bf16)],
        in_specs=[VMEM] * (rows + 5),
        out_specs=[VMEM] * 3,
        scratch_shapes=[
            pltpu.VMEM((own_i * total, 128), f32),
            pltpu.VMEM((own_i // 2, width * total, 2 * chans), bf16),
        ],
        compiler_params=limit(16, scale),
        cost_estimate=cost(4.5),
        name="pair",
    )(*msgs, base, mask, wq, pick, w_in)

    cuts = [own_i]
    lefts = pl.pallas_call(
        left_body,
        out_shape=[jax.ShapeDtypeStruct((n, own_j, tri), bf16) for n in cuts],
        in_specs=[VMEM] * 3,
        out_specs=[VMEM] * len(cuts),
        compiler_params=limit(8, scale),
        cost_estimate=cost(1),
        name="left",
    )(norm, mask, w_in)
    return gathered_plan(lefts[0], right, psum, norm, w_gate, w_final)


def solution(mesh):
    placed = (
        P(("grp", "row"), None, None),
        P(("grp", "row"), "col", None),
        P("grp"),
        P(("grp", "row"), "col"),
        P(),
        P(),
        P(),
        P(),
        P(),
        P(),
    )
    return jax.shard_map(
        shards,
        mesh=mesh,
        in_specs=placed,
        out_specs=P(("grp", "row"), "col", None),
        check_vma=False,
    )
```

```python
import functools

import jax
import jax.numpy as jnp
from jax import lax
from jax.experimental import pallas as pl
from jax.experimental.pallas import tpu as pltpu
from jax.sharding import PartitionSpec as P

eps = 1e-05
f32 = jnp.float32
bf16 = jnp.bfloat16
VMEM = pl.BlockSpec(memory_space=pltpu.VMEM)
SMEM = pl.BlockSpec(memory_space=pltpu.SMEM)
HBM = pl.BlockSpec(memory_space=pltpu.HBM)


def limit(mib, scale=1):
    return pltpu.CompilerParams(vmem_limit_bytes=min(56, mib * scale) * 1024 * 1024)


def round_up(n, m):
    return (n + m - 1) // m * m


def cost(us):
    return pl.CostEstimate(flops=0, bytes_accessed=int(us * 3.69e6), transcendentals=0)


def hold(x):
    return pltpu.with_memory_space_constraint(x, pltpu.HBM)


def fetch(pairs, sem):
    copies = [pltpu.make_async_copy(src, dst, sem.at[n]) for n, (src, dst) in enumerate(pairs)]
    for copy in copies:
        copy.start()
    return copies


def standardize(values):
    centre = values - jnp.mean(values, axis=-1, keepdims=True)
    spread = jnp.mean(centre * centre, axis=-1, keepdims=True)
    return centre * lax.rsqrt(spread + eps)


def sigmoid(v):
    return 0.5 * jnp.tanh(0.5 * v) + 0.5


def align_body(own_i, own_j, count, x_hbm, w_hbm, *refs):
    later, outs, refs = refs[:4], refs[4 : 4 + count], refs[4 + count :]
    brought, (x_ref, w_ref, y_ref, sem) = refs[:4], refs[4:]
    copies = fetch([(x_hbm, x_ref), (w_hbm, w_ref), *zip(later, brought)], sem)
    seqs, residues, depth = x_ref.shape
    width = w_ref.shape[0] // 2
    height, lanes = outs[0].shape
    me = lax.axis_index("row")
    z = lax.axis_index("col")
    copies[0].wait()
    x = x_ref[...].astype(f32).reshape(seqs * residues, depth)
    normed = standardize(x).astype(bf16)
    copies[1].wait()
    y_ref[...] = lax.dot_general(
        normed, w_ref[...], (((1,), (1,)), ((), ())), preferred_element_type=f32
    )
    start = pl.multiple_of(z * own_j, 8)

    def tall(v):
        gap = height - v.shape[0]
        return jnp.concatenate([v, jnp.zeros((gap, v.shape[1]), f32)], axis=0) if gap else v

    right = [tall(y_ref[pl.ds(s * residues + start, own_j), width:]) for s in range(seqs)]
    gap = lanes - 2 * seqs * width
    right += [jnp.zeros((height, gap), f32)] if gap else []
    for d, out in enumerate(outs):
        first = pl.multiple_of((me ^ d) * own_i, 8)
        left = [tall(y_ref[pl.ds(s * residues + first, own_i), :width]) for s in range(seqs)]
        out[...] = jnp.concatenate(left + right, axis=1).astype(bf16)
    for copy in copies[2:]:
        copy.wait()


def prepare_body(seqs, couple_ref, ids_hbm, valid_ref, bias_ref, avg_ref, base_ref, mask_ref, wq_ref, pick_ref,
                 wf_ref, idc_ref, ids_ref, sem):
    (copy,) = fetch([(ids_hbm, ids_ref)], sem)
    own_i, own_j, chans = couple_ref.shape
    pairs, width, _ = wq_ref.shape
    blocks, lanes, _ = pick_ref.shape
    total = blocks * seqs
    x0 = lax.axis_index("row") * own_i
    z0 = lax.axis_index("col") * own_j

    row = lax.broadcasted_iota(jnp.int32, pick_ref.shape[1:], 0)
    col = lax.broadcasted_iota(jnp.int32, pick_ref.shape[1:], 1)
    unit = row - seqs * width
    place = lax.rem(unit, width) * total + lax.div(unit, width)
    place = jnp.where((unit >= 0) & (unit < seqs * width), col - place, -1)

    def pick(r, carry):
        pick_ref[r] = jnp.where(place == r * seqs, 1.0, 0.0).astype(bf16)
        return carry

    lax.fori_loop(0, blocks, pick, 0)
    wf_ref[...] = avg_ref[...].astype(f32)
    for h in range(pairs):
        both = [wf_ref[pl.ds(2 * h + d, width, stride=width), :] for d in range(2)]
        wq_ref[h] = jnp.concatenate(both, axis=1).astype(bf16)
    copy.wait()
    for j in range(own_j):
        idc_ref[pl.ds(j, 1), :] = jnp.full((1, chans), ids_ref[z0 + j], jnp.int32)
    idc = idc_ref[...]
    valid_t = valid_ref[...].astype(f32).T
    lane = lax.broadcasted_iota(jnp.int32, valid_t.shape, 1)
    same_bias = bias_ref[0:1, :]
    cross_bias = bias_ref[1:2, :]

    def rows(i, carry):
        bias = jnp.where(idc == ids_ref[x0 + i], same_bias, cross_bias)
        base_ref[i] = couple_ref[i].astype(f32) + bias
        column = jnp.sum(jnp.where(lane == i, valid_t, 0.0), axis=1, keepdims=True)
        mask_ref[i] = jnp.broadcast_to(column, (own_j, mask_ref.shape[2])).astype(bf16)
        return carry

    lax.fori_loop(0, own_i, rows, 0, unroll=8)


def pair_body(seqs, width, blocks, *refs):
    msgs = refs[:blocks]
    base_ref, mask_ref, wq_ref, pick_ref, win_ref = refs[blocks : blocks + 5]
    psum_ref, norm_ref, right_ref = refs[blocks + 5 : blocks + 8]
    xl_ref, t_ref = refs[blocks + 8 :]
    own_i, own_j, chans = base_ref.shape
    height, lanes = msgs[0].shape
    total = seqs * blocks
    tri = win_ref.shape[1] // 4
    half = own_i // 2

    for r in range(blocks):
        m = msgs[r][pl.ds(0, own_i), :].astype(f32)
        for s in range(seqs):
            moved = m if s == 0 else pltpu.roll(m, lanes - s * width, 1)
            xl_ref[pl.ds(r * seqs + s, own_i, stride=total), :] = moved[:, :128]
    lhs = xl_ref[:, :width].astype(bf16)

    joined = jnp.concatenate([msg[...] for msg in msgs], axis=1)
    picks = pick_ref[...].reshape(blocks * lanes, width * total)
    rmat = jnp.dot(joined, picks, preferred_element_type=f32)[:own_j].astype(bf16)

    def expand(h, carry):
        out = jnp.dot(lhs, wq_ref[h], preferred_element_type=f32)
        parts = [out[:, d * chans : (d + 1) * chans].reshape(own_i, total, chans) for d in range(2)]
        block = jnp.concatenate(parts, axis=1).astype(bf16)
        where = pl.ds(pl.multiple_of(h * 2 * total, 16), 2 * total)
        t_ref[:, where, :chans] = block[:half]
        t_ref[:, where, chans:] = block[half:]
        return carry

    lax.fori_loop(0, width // 2, expand, 0)

    step = 4 if half % 4 == 0 else 1

    def rows(b, carry):
        normed = [[], []]
        for g in range(step):
            i = b * step + g
            both = jnp.dot(rmat, t_ref[i], preferred_element_type=f32) * (1.0 / total)
            for side in range(2):
                at = i + side * half
                psum = (base_ref[at] + both[:, side * chans : (side + 1) * chans]).astype(bf16)
                psum_ref[at] = psum
                normed[side].append(standardize(psum.astype(f32)))
        flat = jnp.concatenate(normed[0] + normed[1], axis=0).astype(bf16)
        proj = jnp.dot(flat, win_ref[:, 2 * tri :], preferred_element_type=f32)
        count = step * own_j
        for side in range(2):
            cut = slice(side * count, (side + 1) * count)
            i0 = b * step + side * half
            norm_ref[pl.ds(pl.multiple_of(i0 * own_j, 16), count), :] = flat[cut]
            mask = mask_ref[pl.ds(i0, step)].astype(f32).reshape(count, tri)
            right = mask * sigmoid(proj[cut, :tri]) * proj[cut, tri:]
            right_ref[pl.ds(i0, step)] = right.reshape(step, own_j, tri).astype(bf16)
        return carry

    lax.fori_loop(0, half // step, rows, 0)


def left_body(norm_ref, mask_ref, win_ref, *outs):
    own_i, own_j, tri = mask_ref.shape
    group = 8 if own_i % 8 == 0 else 1
    at = 0
    for out in outs:
        first = at

        def rows(b, carry):
            i0 = first + b * group
            flat = norm_ref[pl.ds(pl.multiple_of(i0 * own_j, 16), group * own_j), :]
            mask = mask_ref[pl.ds(i0, group)].astype(f32).reshape(group * own_j, tri)
            proj = jnp.dot(flat, win_ref[:, : 2 * tri], preferred_element_type=f32)
            left = mask * sigmoid(proj[:, :tri]) * proj[:, tri:]
            out[pl.ds(b * group, group)] = left.reshape(group, own_j, tri).astype(bf16)
            return carry

        lax.fori_loop(0, out.shape[0] // group, rows, 0, unroll=True)
        at += out.shape[0]


def contract(lf_ref, halves, i0, group):
    step = 8
    acc = (jnp.zeros(halves[0].shape[1:], f32),) * group
    for h, r_ref in enumerate(halves):
        depth = r_ref.shape[0]

        def add(kb, acc):
            k0 = kb * step
            acc = list(acc)
            for d in range(step):
                right = r_ref[k0 + d].astype(f32)
                for t in range(group):
                    acc[t] = acc[t] + lf_ref[i0 + t, pl.ds(h * depth + k0 + d, 1), :] * right
            return tuple(acc)

        acc = lax.fori_loop(0, depth // step, add, acc)
    return acc


def sums_body(own_pair, first, own_ref, other_ref, p_other, met_ref, p_met, far_ref, p_far, l_ref, m_ref, o_ref, lf_ref):
    count, depth = o_ref.shape[0], l_ref.shape[1]
    group = 8
    lf_ref[:, pl.ds(0, depth), :] = l_ref[pl.ds(first, count)].astype(f32)
    lf_ref[:, pl.ds(depth, depth), :] = m_ref[pl.ds(first, count)].astype(f32)

    def use(halves):
        def rows(b, carry):
            acc = contract(lf_ref, halves, b * group, group)
            for t in range(group):
                o_ref[b * group + t] = acc[t].astype(o_ref.dtype)
            return carry

        lax.fori_loop(0, count // group, rows, 0)

    r, z = lax.axis_index("row"), lax.axis_index("col")
    keeper = (r % 2) == (z % 2)
    near = ((r // 2) == (z // 2)) == own_pair
    table = [
        (near & keeper, own_ref, met_ref),
        (near & ~keeper, far_ref, p_met),
        (~near & keeper, p_other, far_ref),
        (~near & ~keeper, other_ref, p_far),
    ]
    for cond, a, b in table:
        pl.when(cond)(functools.partial(use, (a, b)))


def open_body(x_hbm, w_hbm, valid_hbm, couple_hbm, *refs):
    later, outs, brought = refs[:5], refs[5:9], refs[9:14]
    block_ref, x_ref, w_ref, valid_ref, y_ref, sem = refs[14:]
    own_i, own_j, chans = couple_hbm.shape
    copies = fetch([(x_hbm, x_ref), (w_hbm, w_ref), (valid_hbm, valid_ref),
                    (couple_hbm, block_ref.at[pl.ds(0, own_i)]),
                    *zip(later, brought)], sem)
    seqs, residues, depth = x_ref.shape
    width = w_ref.shape[0] // 2
    height, lanes = outs[0].shape
    me = lax.axis_index("row")
    z = lax.axis_index("col")
    copies[0].wait()
    x = x_ref[...].astype(f32).reshape(seqs * residues, depth)
    normed = standardize(x).astype(bf16)
    copies[1].wait()
    y_ref[...] = lax.dot_general(
        normed, w_ref[...], (((1,), (1,)), ((), ())), preferred_element_type=f32
    )

    def cut(start, lane):
        start = pl.multiple_of(start * own_i, 8)
        return [y_ref[pl.ds(s * residues + start, own_i), lane : lane + width] for s in range(seqs)]

    shared = cut(z, width) + cut(z ^ 1, width)
    below = jnp.zeros((height - own_i, lanes), f32)
    for d, out in enumerate(outs):
        other = ((me ^ d) // 2 ^ 1) * 2 + z % 2
        rows = jnp.concatenate(cut(me ^ d, 0) + cut(other, 0) + shared, axis=1)
        out[...] = jnp.concatenate([rows, below], axis=0).astype(bf16)
    copies[2].wait()
    mask = valid_ref[...].astype(f32).T
    mask = jnp.concatenate([mask, jnp.zeros((own_j, chans - own_i), f32)], axis=1)
    for n in range(own_i, block_ref.shape[0]):
        block_ref[n] = mask.astype(bf16)
    for copy in copies[3:]:
        copy.wait()


def ready_body(seqs, avg_ref, ids_hbm, wq_ref, pick_ref, idt_ref, wf_ref, ids_ref, sem):
    (copy,) = fetch([(ids_hbm, ids_ref)], sem)
    pairs, width, _ = wq_ref.shape
    kinds, blocks, lanes, _ = pick_ref.shape
    total = blocks * seqs
    row = lax.broadcasted_iota(jnp.int32, pick_ref.shape[2:], 0)
    col = lax.broadcasted_iota(jnp.int32, pick_ref.shape[2:], 1)
    for n in range(kinds):
        unit = row - n * seqs * width
        place = lax.rem(unit, width) * total + lax.div(unit, width)
        place = jnp.where((unit >= 0) & (unit < seqs * width), col - place, -1)
        for r in range(blocks):
            pick_ref[n, r] = jnp.where(place == r * seqs, 1.0, 0.0).astype(bf16)
    wf_ref[...] = avg_ref[...].astype(f32)
    for h in range(pairs):
        both = [wf_ref[pl.ds(2 * h + d, width, stride=width), :] for d in range(2)]
        wq_ref[h] = jnp.concatenate(both, axis=1).astype(bf16)
    copy.wait()

    def spread(n, carry):
        idt_ref[pl.ds(n, 1), :] = jnp.full((1, idt_ref.shape[1]), ids_ref[n], jnp.int32)
        return carry

    lax.fori_loop(0, idt_ref.shape[0], spread, 0, unroll=8)


def mix_rows(seqs, width, lane0, msgs, wq_ref, t_ref, xl_ref):
    half, terms, both = t_ref.shape
    chans, own_i, total = both // 2, 2 * half, seqs * 4
    for r in range(4):
        m = msgs[r][pl.ds(0, own_i), :128].astype(f32)
        for s in range(seqs):
            lane = lane0 + s * width
            moved = pltpu.roll(m, 128 - lane, 1) if lane else m
            xl_ref[pl.ds(r * seqs + s, own_i, stride=total), :] = moved
    lhs = xl_ref[:, :width].astype(bf16)
    for h in range(width // 2):
        out = jnp.dot(lhs, wq_ref[h], preferred_element_type=f32)
        parts = [out[:, d * chans : (d + 1) * chans].reshape(own_i, total, chans) for d in range(2)]
        block = jnp.concatenate(parts, axis=1).astype(bf16)
        where = pl.ds(h * 2 * total, 2 * total)
        t_ref[:, where, :chans] = block[:half]
        t_ref[:, where, chans:] = block[half:]


def mix_body(seqs, width, *refs):
    msgs, (wq_ref, pick_ref, t_ref, right_ref, xl_ref) = refs[:4], refs[4:]
    own_j, terms = right_ref.shape[1:]
    joined = jnp.concatenate([msg[:, 128:] for msg in msgs], axis=1)
    for n in range(2):
        right = jnp.dot(joined, pick_ref[n].reshape(512, terms), preferred_element_type=f32)[:own_j]
        right_ref[n] = (right * (1.0 / (seqs * 4))).astype(bf16)
    mix_rows(seqs, width, 0, msgs, wq_ref, t_ref, xl_ref)


def block_norms(block_ref, t_ref, right, row0, col0, idt_ref, bias_ref, use):
    half, terms, _ = t_ref.shape
    own_i, own_j, chans = 2 * half, right.shape[0], bias_ref.shape[1]
    idc = idt_ref[pl.ds(pl.multiple_of(col0, 8), own_j), :]
    step = 4
    for b in range(half // step):
        rows, psums = [[], []], [[], []]
        for i in range(b * step, b * step + step):
            both = jnp.dot(right, t_ref[i], preferred_element_type=f32)
            for side in range(2):
                at = i + side * half
                same = idc == idt_ref[pl.ds(row0 + at, 1), :]
                base = block_ref[at].astype(f32) + jnp.where(same, bias_ref[0:1, :], bias_ref[1:2, :])
                rows[side].append(at)
                psums[side].append((base + both[:, side * chans : (side + 1) * chans]).astype(bf16))
        rows, psums = rows[0] + rows[1], psums[0] + psums[1]
        flat = jnp.concatenate([standardize(p.astype(f32)) for p in psums], axis=0).astype(bf16)
        use(rows, psums, flat)


def gated(block_ref, rows, flat, w_ref):
    own_j = block_ref.shape[1]
    tri = w_ref.shape[1] // 2
    mask = block_ref[block_ref.shape[0] - 1].astype(f32)
    proj = jnp.dot(flat, w_ref[...], preferred_element_type=f32)
    both = sigmoid(proj[:, :tri]) * proj[:, tri:]
    return [mask[:, at : at + 1] * both[n * own_j : (n + 1) * own_j] for n, at in enumerate(rows)]


def own_body(block_ref, t_ref, right_ref, idt_ref, bias_ref, win_ref, psum_ref, norm_ref, out_ref, flat_ref):
    own_i, own_j, chans = psum_ref.shape
    r, z = lax.axis_index("row"), lax.axis_index("col")
    side = win_ref.shape[1] // 2
    w_right = win_ref.at[:, pl.ds(side, side)]

    def use(rows, psums, flat):
        rights = gated(block_ref, rows, flat, w_right)
        for n, at in enumerate(rows):
            psum_ref[at] = psums[n]
            norm_ref[pl.ds(at * own_j, own_j), :] = flat[n * own_j : (n + 1) * own_j]
            flat_ref[pl.ds(at * own_j, own_j), :] = rights[n]

    block_norms(block_ref, t_ref, right_ref[0], r * own_i, z * own_j, idt_ref, bias_ref, use)
    for k in range(own_j):
        out_ref[k] = flat_ref[pl.ds(k, own_i, stride=own_j), :].astype(bf16)


def rest_body(block_ref, norm_ref, win_ref, wgate_ref, left_ref, gate_ref):
    own_i, own_j, _ = left_ref.shape
    w_left = win_ref.at[:, pl.ds(0, win_ref.shape[1] // 2)]
    group = 8
    for i in range(0, own_i, group):
        flat = norm_ref[pl.ds(i * own_j, group * own_j), :]
        rows = list(range(i, i + group))
        gate = sigmoid(jnp.dot(flat, wgate_ref[...], preferred_element_type=f32))
        for n, left in enumerate(gated(block_ref, rows, flat, w_left)):
            left_ref[i + n] = left.astype(bf16)
            gate_ref[i + n] = gate[n * own_j : (n + 1) * own_j]


def other_body(seqs, width, *refs):
    msgs, refs = refs[:4], refs[4:]
    wq_ref, block_ref, right_ref, idt_ref, bias_ref, win_ref, out_ref, t_ref, xl_ref, flat_ref = refs
    own_j, own_i, _ = out_ref.shape
    r, z = lax.axis_index("row"), lax.axis_index("col")
    side = win_ref.shape[1] // 2
    w_right = win_ref.at[:, pl.ds(side, side)]

    def use(rows, psums, flat):
        for at, right in zip(rows, gated(block_ref, rows, flat, w_right)):
            flat_ref[pl.ds(at * own_j, own_j), :] = right

    @pl.when((r % 2) != (z % 2))
    def _():
        mix_rows(seqs, width, seqs * width, msgs, wq_ref, t_ref, xl_ref)
        block_norms(block_ref, t_ref, right_ref[0], (r ^ 3) * own_i, z * own_j, idt_ref, bias_ref, use)
        for k in range(own_j):
            out_ref[k] = flat_ref[pl.ds(k, own_i, stride=own_j), :].astype(bf16)


def met_body(block_ref, t_ref, right_ref, idt_ref, bias_ref, win_ref, left_ref, out_ref, flat_ref):
    own_i, own_j, _ = left_ref.shape
    r, z = lax.axis_index("row"), lax.axis_index("col")
    side = win_ref.shape[1] // 2
    w_left, w_right = win_ref.at[:, pl.ds(0, side)], win_ref.at[:, pl.ds(side, side)]

    def use(rows, psums, flat):
        lefts = gated(block_ref, rows, flat, w_left)
        rights = gated(block_ref, rows, flat, w_right)
        for n, at in enumerate(rows):
            left_ref[at] = lefts[n].astype(bf16)
            flat_ref[pl.ds(at * own_j, own_j), :] = rights[n]

    block_norms(block_ref, t_ref, right_ref[1], r * own_i, (z ^ 1) * own_j, idt_ref, bias_ref, use)
    for k in range(own_j):
        out_ref[k] = flat_ref[pl.ds(k, own_i, stride=own_j), :].astype(bf16)


def join_body(first, parts, own_ref, psum_ref, gate_ref, w_ref, *refs):
    sums, (out_hbm, done_ref, sem) = refs[:parts], refs[-3:]
    count, extent, chans = done_ref.shape
    group = 8
    at = 0
    for sum_ref in sums:
        start = at

        def rows(b, carry):
            here = pl.ds(start + b * group, group)
            there = pl.ds(first + start + b * group, group)
            mixed = own_ref[there] + sum_ref[pl.ds(b * group, group)].astype(f32)
            normed = standardize(mixed).reshape(group * extent, -1).astype(bf16)
            update = jnp.dot(normed, w_ref[...], preferred_element_type=f32).reshape(group, extent, -1)
            done_ref[here] = (psum_ref[there].astype(f32) + gate_ref[there] * update).astype(bf16)
            return carry

        lax.fori_loop(0, sum_ref.shape[0] // group, rows, 0, unroll=True)
        at += sum_ref.shape[0]
    copy = pltpu.make_async_copy(done_ref, out_hbm.at[pl.ds(first, count)], sem)
    copy.start()
    copy.wait()


def triangle_body(l_ref, r_ref, o_ref, lf_ref, flat_ref, rk_ref):
    own_i, depth, chans = l_ref.shape
    extent = r_ref.shape[0]
    group = 8 if own_i % 8 == 0 else 1

    @pl.when(pl.program_id(0) == 0)
    def _():
        lf_ref[...] = l_ref[...].astype(f32)

    def widen(j, carry):
        flat_ref[pl.ds(pl.multiple_of(j * depth, 8), depth), :] = r_ref[j].astype(f32)
        return carry

    lax.fori_loop(0, extent, widen, 0)

    def turn(k, carry):
        rk_ref[k] = flat_ref[pl.ds(k, extent, stride=depth), :]
        return carry

    lax.fori_loop(0, depth, turn, 0)

    def rows(b, carry):
        i0 = b * group
        acc = contract(lf_ref, [rk_ref], i0, group)
        for t in range(group):
            o_ref[0, i0 + t] = acc[t].astype(bf16)
        return carry

    lax.fori_loop(0, own_i // group, rows, 0)


def finish_body(sum_ref, psum_ref, norm_ref, wgate_ref, w_ref, out_ref):
    parts, own_i, extent, chans = sum_ref.shape
    own_j = psum_ref.shape[1]

    def row(i, carry):
        flat = norm_ref[pl.ds(pl.multiple_of(i * own_j, 16), own_j), :]
        gate = sigmoid(jnp.dot(flat, wgate_ref[...], preferred_element_type=f32))
        normed = [standardize(sum_ref[part, i].astype(f32)) for part in range(parts)]
        normed = jnp.concatenate(normed, axis=0).astype(bf16)
        update = jnp.dot(normed, w_ref[...], preferred_element_type=f32)
        out_ref[i] = (psum_ref[i].astype(f32) + gate * update).astype(bf16)
        return carry

    lax.fori_loop(0, own_i, row, 0)


def gathered_plan(left, right, psum, norm, w_gate, w_final):
    own_i, own_j, chans = psum.shape
    rows = lax.axis_size("row")
    tri = w_final.shape[0]
    right_all = lax.all_gather(right, "row", axis=0, tiled=True)
    partial = pl.pallas_call(
        triangle_body,
        grid=(rows,),
        out_shape=jax.ShapeDtypeStruct((rows, own_i, own_i, tri), bf16),
        in_specs=[
            pl.BlockSpec((own_i, own_j, tri), lambda r: (0, 0, 0)),
            pl.BlockSpec((own_i, own_j, tri), lambda r: (r, 0, 0)),
        ],
        out_specs=pl.BlockSpec((1, own_i, own_i, tri), lambda r: (r, 0, 0, 0)),
        scratch_shapes=[
            pltpu.VMEM((own_i, own_j, tri), f32),
            pltpu.VMEM((own_i * own_j, tri), f32),
            pltpu.VMEM((own_j, own_i, tri), f32),
        ],
        compiler_params=limit(56),
        name="triangle",
    )(left, right_all)
    summed = lax.psum_scatter(partial, "col", scatter_dimension=0, tiled=True)
    return pl.pallas_call(
        finish_body,
        out_shape=jax.ShapeDtypeStruct((own_i, own_j, chans), bf16),
        in_specs=[VMEM] * 5,
        out_specs=VMEM,
        compiler_params=limit(56),
        name="finish",
    )(summed, psum, norm, w_gate, w_final)


def paired_plan(homolog, couple, ids, valid, bias, factors, average, w_in, w_gate, w_final):
    seqs, residues, depth = homolog.shape
    own_i, own_j, chans = couple.shape
    width = factors.shape[1] // 2
    tri = w_final.shape[0]
    total = seqs * 4
    cells = [(r, z) for r in range(4) for z in range(4)]
    struct = jax.ShapeDtypeStruct

    def move(value, step):
        pairs = [(r * 4 + z, step(r, z)) for r, z in cells]
        pairs = [(src, r * 4 + z) for src, (r, z) in pairs]
        return lax.ppermute(value, ("row", "col"), pairs)

    def call(body, us, out_shape, scratch, *args, mib=12):
        return pl.pallas_call(
            body,
            out_shape=out_shape,
            in_specs=[VMEM] * len(args),
            out_specs=[VMEM] * len(out_shape) if isinstance(out_shape, list) else VMEM,
            scratch_shapes=scratch,
            compiler_params=limit(mib),
            cost_estimate=cost(us),
            name=getattr(body, "func", body).__name__.removesuffix("_body"),
        )(*args)

    keeper = lambda r, z: r % 2 == z % 2
    beside = lambda r, z: (r ^ 1, z)
    height, lanes = round_up(own_i, 16), 256
    block = struct((own_i + 1, own_j, chans), bf16)
    later = (average, bias, w_in, w_gate, w_final)
    *msgs, average, bias, w_in, w_gate, w_final, raw = pl.pallas_call(
        open_body,
        out_shape=[struct((height, lanes), bf16)] * 4 + [struct(x.shape, x.dtype) for x in later] + [block],
        in_specs=[HBM] * 9,
        out_specs=[VMEM] * 10,
        scratch_shapes=[
            pltpu.VMEM(homolog.shape, bf16),
            pltpu.VMEM((2 * width, depth), bf16),
            pltpu.VMEM(valid.shape, jnp.int32),
            pltpu.VMEM((seqs * residues, 2 * width), f32),
            pltpu.SemaphoreType.DMA((9,)),
        ],
        compiler_params=limit(8),
        cost_estimate=cost(1.5),
        name="open",
    )(*map(hold, (homolog, factors.T, valid, couple) + later))
    msgs = [msgs[0]] + [
        lax.ppermute(msgs[d], "row", [(r, r ^ d) for r in range(4)]) for d in (1, 2, 3)
    ]
    met = move(raw, lambda r, z: (r, z ^ 1))
    raw_other = move(raw, lambda r, z: (r ^ 3, z) if keeper(r, z) else (r ^ 1, z))

    wq, pick, idt = pl.pallas_call(
        functools.partial(ready_body, seqs),
        out_shape=[struct((width // 2, width, 2 * chans), bf16),
                   struct((2, 4, 128, width * total), bf16),
                   struct((residues, 128), jnp.int32)],
        in_specs=[VMEM, HBM],
        out_specs=[VMEM] * 3,
        scratch_shapes=[
            pltpu.VMEM(average.shape, f32),
            pltpu.SMEM(ids.shape, jnp.int32),
            pltpu.SemaphoreType.DMA((1,)),
        ],
        compiler_params=limit(8),
        cost_estimate=cost(1.5),
        name="ready",
    )(average, hold(ids))

    t, mixed = call(
        functools.partial(mix_body, seqs, width), 1,
        [struct((own_i // 2, width * total, 2 * chans), bf16), struct((2, own_j, width * total), bf16)],
        [pltpu.VMEM((own_i * total, 128), f32)], *msgs, wq, pick,
    )
    square = struct((own_i, own_j, tri), bf16)
    flat = [pltpu.VMEM((own_i * own_j, tri), f32)]
    psum, norm, right = call(
        own_body, 2.4, [square, struct((own_i * own_j, chans), bf16), square], flat,
        raw, t, mixed, idt, bias, w_in,
    )
    far = move(right, lambda r, z: (r ^ 1, z) if keeper(r, z) else (r ^ 2, z ^ 1))
    left, gate = call(rest_body, 0.6, [square, struct(couple.shape, f32)], [], raw, norm, w_in, w_gate)
    other = call(
        functools.partial(other_body, seqs, width), 3, square,
        [pltpu.VMEM(t.shape, bf16), pltpu.VMEM((own_i * total, 128), f32)] + flat,
        *msgs, wq, raw_other, mixed, idt, bias, w_in,
    )
    p_other = move(other, beside)
    met, *_ = lax.optimization_barrier((met, other))
    met_left, met_right = call(met_body, 3, [square, square], flat, met, t, mixed, idt, bias, w_in)
    p_met = move(met_right, beside)
    far, *_ = lax.optimization_barrier((far, met_left))
    p_far = move(far, beside)

    def sums(own_pair, first, n, dtype):
        return call(
            functools.partial(sums_body, own_pair, first), 0.13 * n, struct((n, own_j, tri), dtype),
            [pltpu.VMEM((n, 2 * own_j, tri), f32)],
            right, other, p_other, met_right, p_met, far, p_far, left, met_left,
        )

    came = [move(sums(False, first, 8, bf16), lambda r, z: (r, z ^ 2)) for first in range(0, own_i, 8)]
    kept = sums(True, 0, own_i, f32)

    out = []
    for first, n in ((0, 16), (16, 16), (32, own_i - 32)):
        parts = came[first // 8 : (first + n) // 8]
        out = [pl.pallas_call(
            functools.partial(join_body, first, len(parts)),
            out_shape=struct(couple.shape, bf16),
            in_specs=[VMEM] * (4 + len(parts)) + [HBM] * len(out),
            out_specs=HBM,
            scratch_shapes=[pltpu.VMEM((n, own_j, chans), bf16), pltpu.SemaphoreType.DMA],
            input_output_aliases={4 + len(parts): 0} if out else {},
            compiler_params=limit(8),
            cost_estimate=cost(0.06 * n),
            name="join",
        )(kept, psum, gate, w_final, *parts, *out)]
    return out[0]


def shards(homolog, couple, ids, valid, bias, factors, average, w_in, w_gate, w_final):
    rows, cols = lax.axis_size("row"), lax.axis_size("col")
    own_seqs, residues, depth = homolog.shape
    own_i, own_j, chans = couple.shape
    width = factors.shape[1] // 2
    tri = w_final.shape[0]
    total = own_seqs * rows
    lanes = round_up(2 * own_seqs * width, 128)
    height = round_up(max(own_i, own_j), 16)
    paired = (rows, cols, own_seqs * width, chans, tri) == (4, 4, 64, 128, 128)
    if paired and own_i == own_j == 40:
        return paired_plan(homolog, couple, ids, valid, bias, factors, average, w_in, w_gate, w_final)
    scale = 8

    later = (average, valid, bias, couple)
    *msgs, average, valid, bias, couple = pl.pallas_call(
        functools.partial(align_body, own_i, own_j, rows),
        out_shape=[jax.ShapeDtypeStruct((height, lanes), bf16)] * rows
        + [jax.ShapeDtypeStruct(x.shape, x.dtype) for x in later],
        in_specs=[HBM] * 6,
        out_specs=[VMEM] * (rows + 4),
        scratch_shapes=[
            pltpu.VMEM(homolog.shape, bf16),
            pltpu.VMEM((2 * width, depth), bf16),
            pltpu.VMEM((own_seqs * residues, 2 * width), f32),
            pltpu.SemaphoreType.DMA((6,)),
        ],
        compiler_params=limit(8, scale),
        cost_estimate=cost(1.5),
        name="align",
    )(hold(homolog), hold(factors.T), *map(hold, later))
    msgs = [msgs[0]] + [
        lax.ppermute(msgs[d], "row", [(r, r ^ d) for r in range(rows)])
        for d in reversed(range(1, rows))
    ]

    base, mask, wq, pick = pl.pallas_call(
        functools.partial(prepare_body, own_seqs),
        out_shape=[jax.ShapeDtypeStruct((own_i, own_j, chans), f32),
                   jax.ShapeDtypeStruct((own_i, own_j, tri), bf16),
                   jax.ShapeDtypeStruct((width // 2, width, 2 * chans), bf16),
                   jax.ShapeDtypeStruct((rows, lanes, width * total), bf16)],
        in_specs=[VMEM, HBM, VMEM, VMEM, VMEM],
        out_specs=[VMEM] * 4,
        scratch_shapes=[
            pltpu.VMEM(average.shape, f32),
            pltpu.VMEM((own_j, chans), jnp.int32),
            pltpu.SMEM(ids.shape, jnp.int32),
            pltpu.SemaphoreType.DMA((1,)),
        ],
        compiler_params=limit(8, scale),
        cost_estimate=cost(2),
        name="prepare",
    )(couple, hold(ids), valid, bias, average)

    extents = (own_i, own_j)
    psum, norm, right = pl.pallas_call(
        functools.partial(pair_body, own_seqs, width, rows),
        out_shape=[jax.ShapeDtypeStruct((own_i, own_j, chans), bf16),
                   jax.ShapeDtypeStruct((own_i * own_j, chans), bf16),
                   jax.ShapeDtypeStruct(extents + (tri,), bf16)],
        in_specs=[VMEM] * (rows + 5),
        out_specs=[VMEM] * 3,
        scratch_shapes=[
            pltpu.VMEM((own_i * total, 128), f32),
            pltpu.VMEM((own_i // 2, width * total, 2 * chans), bf16),
        ],
        compiler_params=limit(16, scale),
        cost_estimate=cost(4.5),
        name="pair",
    )(*msgs, base, mask, wq, pick, w_in)

    cuts = [own_i]
    lefts = pl.pallas_call(
        left_body,
        out_shape=[jax.ShapeDtypeStruct((n, own_j, tri), bf16) for n in cuts],
        in_specs=[VMEM] * 3,
        out_specs=[VMEM] * len(cuts),
        compiler_params=limit(8, scale),
        cost_estimate=cost(1),
        name="left",
    )(norm, mask, w_in)
    return gathered_plan(lefts[0], right, psum, norm, w_gate, w_final)


def solution(mesh):
    placed = (
        P(("grp", "row"), None, None),
        P(("grp", "row"), "col", None),
        P("grp"),
        P(("grp", "row"), "col"),
        P(),
        P(),
        P(),
        P(),
        P(),
        P(),
    )
    return jax.shard_map(
        shards,
        mesh=mesh,
        in_specs=placed,
        out_specs=P(("grp", "row"), "col", None),
        check_vma=False,
    )
```

```python
import functools

import jax
import jax.numpy as jnp
from jax import lax
from jax.experimental import pallas as pl
from jax.experimental.pallas import tpu as pltpu
from jax.sharding import PartitionSpec as P

eps = 1e-05
f32 = jnp.float32
bf16 = jnp.bfloat16
VMEM = pl.BlockSpec(memory_space=pltpu.VMEM)
SMEM = pl.BlockSpec(memory_space=pltpu.SMEM)
HBM = pl.BlockSpec(memory_space=pltpu.HBM)


def limit(mib, scale=1):
    return pltpu.CompilerParams(vmem_limit_bytes=min(56, mib * scale) * 1024 * 1024)


def round_up(n, m):
    return (n + m - 1) // m * m


def cost(us):
    return pl.CostEstimate(flops=0, bytes_accessed=int(us * 3.69e6), transcendentals=0)


def hold(x):
    return pltpu.with_memory_space_constraint(x, pltpu.HBM)


def fetch(pairs, sem):
    copies = [pltpu.make_async_copy(src, dst, sem.at[n]) for n, (src, dst) in enumerate(pairs)]
    for copy in copies:
        copy.start()
    return copies


def standardize(values):
    centre = values - jnp.mean(values, axis=-1, keepdims=True)
    spread = jnp.mean(centre * centre, axis=-1, keepdims=True)
    return centre * lax.rsqrt(spread + eps)


def sigmoid(v):
    return 0.5 * jnp.tanh(0.5 * v) + 0.5


def align_body(own_i, own_j, count, x_hbm, w_hbm, *refs):
    later, outs, refs = refs[:4], refs[4 : 4 + count], refs[4 + count :]
    brought, (x_ref, w_ref, y_ref, sem) = refs[:4], refs[4:]
    copies = fetch([(x_hbm, x_ref), (w_hbm, w_ref), *zip(later, brought)], sem)
    seqs, residues, depth = x_ref.shape
    width = w_ref.shape[0] // 2
    height, lanes = outs[0].shape
    me = lax.axis_index("row")
    z = lax.axis_index("col")
    copies[0].wait()
    x = x_ref[...].astype(f32).reshape(seqs * residues, depth)
    normed = standardize(x).astype(bf16)
    copies[1].wait()
    y_ref[...] = lax.dot_general(
        normed, w_ref[...], (((1,), (1,)), ((), ())), preferred_element_type=f32
    )
    start = pl.multiple_of(z * own_j, 8)

    def tall(v):
        gap = height - v.shape[0]
        return jnp.concatenate([v, jnp.zeros((gap, v.shape[1]), f32)], axis=0) if gap else v

    right = [tall(y_ref[pl.ds(s * residues + start, own_j), width:]) for s in range(seqs)]
    gap = lanes - 2 * seqs * width
    right += [jnp.zeros((height, gap), f32)] if gap else []
    for d, out in enumerate(outs):
        first = pl.multiple_of((me ^ d) * own_i, 8)
        left = [tall(y_ref[pl.ds(s * residues + first, own_i), :width]) for s in range(seqs)]
        out[...] = jnp.concatenate(left + right, axis=1).astype(bf16)
    for copy in copies[2:]:
        copy.wait()


def prepare_body(seqs, couple_ref, ids_hbm, valid_ref, bias_ref, avg_ref, base_ref, mask_ref, wq_ref, pick_ref,
                 wf_ref, idc_ref, ids_ref, sem):
    (copy,) = fetch([(ids_hbm, ids_ref)], sem)
    own_i, own_j, chans = couple_ref.shape
    pairs, width, _ = wq_ref.shape
    blocks, lanes, _ = pick_ref.shape
    total = blocks * seqs
    x0 = lax.axis_index("row") * own_i
    z0 = lax.axis_index("col") * own_j

    row = lax.broadcasted_iota(jnp.int32, pick_ref.shape[1:], 0)
    col = lax.broadcasted_iota(jnp.int32, pick_ref.shape[1:], 1)
    unit = row - seqs * width
    place = lax.rem(unit, width) * total + lax.div(unit, width)
    place = jnp.where((unit >= 0) & (unit < seqs * width), col - place, -1)

    def pick(r, carry):
        pick_ref[r] = jnp.where(place == r * seqs, 1.0, 0.0).astype(bf16)
        return carry

    lax.fori_loop(0, blocks, pick, 0)
    wf_ref[...] = avg_ref[...].astype(f32)
    for h in range(pairs):
        both = [wf_ref[pl.ds(2 * h + d, width, stride=width), :] for d in range(2)]
        wq_ref[h] = jnp.concatenate(both, axis=1).astype(bf16)
    copy.wait()
    for j in range(own_j):
        idc_ref[pl.ds(j, 1), :] = jnp.full((1, chans), ids_ref[z0 + j], jnp.int32)
    idc = idc_ref[...]
    valid_t = valid_ref[...].astype(f32).T
    lane = lax.broadcasted_iota(jnp.int32, valid_t.shape, 1)
    same_bias = bias_ref[0:1, :]
    cross_bias = bias_ref[1:2, :]

    def rows(i, carry):
        bias = jnp.where(idc == ids_ref[x0 + i], same_bias, cross_bias)
        base_ref[i] = couple_ref[i].astype(f32) + bias
        column = jnp.sum(jnp.where(lane == i, valid_t, 0.0), axis=1, keepdims=True)
        mask_ref[i] = jnp.broadcast_to(column, (own_j, mask_ref.shape[2])).astype(bf16)
        return carry

    lax.fori_loop(0, own_i, rows, 0, unroll=8)


def pair_body(seqs, width, blocks, *refs):
    msgs = refs[:blocks]
    base_ref, mask_ref, wq_ref, pick_ref, win_ref = refs[blocks : blocks + 5]
    psum_ref, norm_ref, right_ref = refs[blocks + 5 : blocks + 8]
    xl_ref, t_ref = refs[blocks + 8 :]
    own_i, own_j, chans = base_ref.shape
    height, lanes = msgs[0].shape
    total = seqs * blocks
    tri = win_ref.shape[1] // 4
    half = own_i // 2

    for r in range(blocks):
        m = msgs[r][pl.ds(0, own_i), :].astype(f32)
        for s in range(seqs):
            moved = m if s == 0 else pltpu.roll(m, lanes - s * width, 1)
            xl_ref[pl.ds(r * seqs + s, own_i, stride=total), :] = moved[:, :128]
    lhs = xl_ref[:, :width].astype(bf16)

    joined = jnp.concatenate([msg[...] for msg in msgs], axis=1)
    picks = pick_ref[...].reshape(blocks * lanes, width * total)
    rmat = jnp.dot(joined, picks, preferred_element_type=f32)[:own_j].astype(bf16)

    def expand(h, carry):
        out = jnp.dot(lhs, wq_ref[h], preferred_element_type=f32)
        parts = [out[:, d * chans : (d + 1) * chans].reshape(own_i, total, chans) for d in range(2)]
        block = jnp.concatenate(parts, axis=1).astype(bf16)
        where = pl.ds(pl.multiple_of(h * 2 * total, 16), 2 * total)
        t_ref[:, where, :chans] = block[:half]
        t_ref[:, where, chans:] = block[half:]
        return carry

    lax.fori_loop(0, width // 2, expand, 0)

    step = 4 if half % 4 == 0 else 1

    def rows(b, carry):
        normed = [[], []]
        for g in range(step):
            i = b * step + g
            both = jnp.dot(rmat, t_ref[i], preferred_element_type=f32) * (1.0 / total)
            for side in range(2):
                at = i + side * half
                psum = (base_ref[at] + both[:, side * chans : (side + 1) * chans]).astype(bf16)
                psum_ref[at] = psum
                normed[side].append(standardize(psum.astype(f32)))
        flat = jnp.concatenate(normed[0] + normed[1], axis=0).astype(bf16)
        proj = jnp.dot(flat, win_ref[:, 2 * tri :], preferred_element_type=f32)
        count = step * own_j
        for side in range(2):
            cut = slice(side * count, (side + 1) * count)
            i0 = b * step + side * half
            norm_ref[pl.ds(pl.multiple_of(i0 * own_j, 16), count), :] = flat[cut]
            mask = mask_ref[pl.ds(i0, step)].astype(f32).reshape(count, tri)
            right = mask * sigmoid(proj[cut, :tri]) * proj[cut, tri:]
            right_ref[pl.ds(i0, step)] = right.reshape(step, own_j, tri).astype(bf16)
        return carry

    lax.fori_loop(0, half // step, rows, 0)


def left_body(norm_ref, mask_ref, win_ref, *outs):
    own_i, own_j, tri = mask_ref.shape
    group = 8 if own_i % 8 == 0 else 1
    at = 0
    for out in outs:
        first = at

        def rows(b, carry):
            i0 = first + b * group
            flat = norm_ref[pl.ds(pl.multiple_of(i0 * own_j, 16), group * own_j), :]
            mask = mask_ref[pl.ds(i0, group)].astype(f32).reshape(group * own_j, tri)
            proj = jnp.dot(flat, win_ref[:, : 2 * tri], preferred_element_type=f32)
            left = mask * sigmoid(proj[:, :tri]) * proj[:, tri:]
            out[pl.ds(b * group, group)] = left.reshape(group, own_j, tri).astype(bf16)
            return carry

        lax.fori_loop(0, out.shape[0] // group, rows, 0, unroll=True)
        at += out.shape[0]


def contract(lf_ref, halves, i0, group):
    step = 8
    acc = (jnp.zeros(halves[0].shape[1:], f32),) * group
    for h, r_ref in enumerate(halves):
        depth = r_ref.shape[0]

        def add(kb, acc):
            k0 = kb * step
            acc = list(acc)
            for d in range(step):
                right = r_ref[k0 + d].astype(f32)
                for t in range(group):
                    acc[t] = acc[t] + lf_ref[i0 + t, pl.ds(h * depth + k0 + d, 1), :] * right
            return tuple(acc)

        acc = lax.fori_loop(0, depth // step, add, acc)
    return acc


def sums_body(own_pair, first, own_ref, other_ref, p_other, met_ref, p_met, far_ref, p_far, l_ref, m_ref, o_ref, lf_ref):
    count, depth = o_ref.shape[0], l_ref.shape[1]
    group = 8
    lf_ref[:, pl.ds(0, depth), :] = l_ref[pl.ds(first, count)].astype(f32)
    lf_ref[:, pl.ds(depth, depth), :] = m_ref[pl.ds(first, count)].astype(f32)

    def use(halves):
        def rows(b, carry):
            acc = contract(lf_ref, halves, b * group, group)
            for t in range(group):
                o_ref[b * group + t] = acc[t].astype(o_ref.dtype)
            return carry

        lax.fori_loop(0, count // group, rows, 0)

    r, z = lax.axis_index("row"), lax.axis_index("col")
    keeper = (r % 2) == (z % 2)
    near = ((r // 2) == (z // 2)) == own_pair
    table = [
        (near & keeper, own_ref, met_ref),
        (near & ~keeper, far_ref, p_met),
        (~near & keeper, p_other, far_ref),
        (~near & ~keeper, other_ref, p_far),
    ]
    for cond, a, b in table:
        pl.when(cond)(functools.partial(use, (a, b)))


def open_body(x_hbm, w_hbm, valid_hbm, couple_hbm, *refs):
    later, outs, brought = refs[:5], refs[5:9], refs[9:14]
    block_ref, longer_ref, x_ref, w_ref, valid_ref, y_ref, sem = refs[14:]
    own_i, own_j, chans = couple_hbm.shape
    copies = fetch([(x_hbm, x_ref), (w_hbm, w_ref), (valid_hbm, valid_ref),
                    (couple_hbm, block_ref.at[pl.ds(0, own_i)]),
                    (couple_hbm, longer_ref.at[pl.ds(0, own_i)]), *zip(later, brought)], sem)
    seqs, residues, depth = x_ref.shape
    width = w_ref.shape[0] // 2
    height, lanes = outs[0].shape
    me = lax.axis_index("row")
    z = lax.axis_index("col")
    copies[0].wait()
    x = x_ref[...].astype(f32).reshape(seqs * residues, depth)
    normed = standardize(x).astype(bf16)
    copies[1].wait()
    y_ref[...] = lax.dot_general(
        normed, w_ref[...], (((1,), (1,)), ((), ())), preferred_element_type=f32
    )

    def cut(start, lane):
        start = pl.multiple_of(start * own_i, 8)
        return [y_ref[pl.ds(s * residues + start, own_i), lane : lane + width] for s in range(seqs)]

    shared = cut(z, width) + cut(z ^ 1, width)
    below = jnp.zeros((height - own_i, lanes), f32)
    for d, out in enumerate(outs):
        other = ((me ^ d) // 2 ^ 1) * 2 + z % 2
        rows = jnp.concatenate(cut(me ^ d, 0) + cut(other, 0) + shared, axis=1)
        out[...] = jnp.concatenate([rows, below], axis=0).astype(bf16)
    copies[2].wait()
    mask = valid_ref[...].astype(f32).T
    mask = jnp.concatenate([mask, jnp.zeros((own_j, chans - own_i), f32)], axis=1)
    block_ref[own_i] = mask.astype(bf16)
    for n in range(own_i, longer_ref.shape[0]):
        longer_ref[n] = mask.astype(bf16)
    for copy in copies[3:]:
        copy.wait()


def ready_body(seqs, avg_ref, ids_hbm, wq_ref, pick_ref, idt_ref, wf_ref, ids_ref, sem):
    (copy,) = fetch([(ids_hbm, ids_ref)], sem)
    pairs, width, _ = wq_ref.shape
    kinds, blocks, lanes, _ = pick_ref.shape
    total = blocks * seqs
    row = lax.broadcasted_iota(jnp.int32, pick_ref.shape[2:], 0)
    col = lax.broadcasted_iota(jnp.int32, pick_ref.shape[2:], 1)
    for n in range(kinds):
        unit = row - n * seqs * width
        place = lax.rem(unit, width) * total + lax.div(unit, width)
        place = jnp.where((unit >= 0) & (unit < seqs * width), col - place, -1)
        for r in range(blocks):
            pick_ref[n, r] = jnp.where(place == r * seqs, 1.0, 0.0).astype(bf16)
    wf_ref[...] = avg_ref[...].astype(f32)
    for h in range(pairs):
        both = [wf_ref[pl.ds(2 * h + d, width, stride=width), :] for d in range(2)]
        wq_ref[h] = jnp.concatenate(both, axis=1).astype(bf16)
    copy.wait()

    def spread(n, carry):
        idt_ref[pl.ds(n, 1), :] = jnp.full((1, idt_ref.shape[1]), ids_ref[n], jnp.int32)
        return carry

    lax.fori_loop(0, idt_ref.shape[0], spread, 0, unroll=8)


def mix_rows(seqs, width, lane0, msgs, wq_ref, t_ref, xl_ref):
    half, terms, both = t_ref.shape
    chans, own_i, total = both // 2, 2 * half, seqs * 4
    for r in range(4):
        m = msgs[r][pl.ds(0, own_i), :128].astype(f32)
        for s in range(seqs):
            lane = lane0 + s * width
            moved = pltpu.roll(m, 128 - lane, 1) if lane else m
            xl_ref[pl.ds(r * seqs + s, own_i, stride=total), :] = moved
    lhs = xl_ref[:, :width].astype(bf16)
    for h in range(width // 2):
        out = jnp.dot(lhs, wq_ref[h], preferred_element_type=f32)
        parts = [out[:, d * chans : (d + 1) * chans].reshape(own_i, total, chans) for d in range(2)]
        block = jnp.concatenate(parts, axis=1).astype(bf16)
        where = pl.ds(h * 2 * total, 2 * total)
        t_ref[:, where, :chans] = block[:half]
        t_ref[:, where, chans:] = block[half:]


def mix_body(seqs, width, *refs):
    msgs, (wq_ref, pick_ref, t_ref, right_ref, xl_ref) = refs[:4], refs[4:]
    own_j, terms = right_ref.shape[1:]
    joined = jnp.concatenate([msg[:, 128:] for msg in msgs], axis=1)
    for n in range(2):
        right = jnp.dot(joined, pick_ref[n].reshape(512, terms), preferred_element_type=f32)[:own_j]
        right_ref[n] = (right * (1.0 / (seqs * 4))).astype(bf16)
    mix_rows(seqs, width, 0, msgs, wq_ref, t_ref, xl_ref)


def block_norms(block_ref, t_ref, right, row0, col0, idt_ref, bias_ref, use):
    half, terms, _ = t_ref.shape
    own_i, own_j, chans = 2 * half, right.shape[0], bias_ref.shape[1]
    idc = idt_ref[pl.ds(pl.multiple_of(col0, 8), own_j), :]
    step = 4
    for b in range(half // step):
        rows, psums = [[], []], [[], []]
        for i in range(b * step, b * step + step):
            both = jnp.dot(right, t_ref[i], preferred_element_type=f32)
            for side in range(2):
                at = i + side * half
                same = idc == idt_ref[pl.ds(row0 + at, 1), :]
                base = block_ref[at].astype(f32) + jnp.where(same, bias_ref[0:1, :], bias_ref[1:2, :])
                rows[side].append(at)
                psums[side].append((base + both[:, side * chans : (side + 1) * chans]).astype(bf16))
        rows, psums = rows[0] + rows[1], psums[0] + psums[1]
        flat = jnp.concatenate([standardize(p.astype(f32)) for p in psums], axis=0).astype(bf16)
        use(rows, psums, flat)


def gated(block_ref, rows, flat, w_ref):
    own_j = block_ref.shape[1]
    tri = w_ref.shape[1] // 2
    mask = block_ref[block_ref.shape[0] - 1].astype(f32)
    proj = jnp.dot(flat, w_ref[...], preferred_element_type=f32)
    both = sigmoid(proj[:, :tri]) * proj[:, tri:]
    return [mask[:, at : at + 1] * both[n * own_j : (n + 1) * own_j] for n, at in enumerate(rows)]


def own_body(block_ref, t_ref, right_ref, idt_ref, bias_ref, win_ref, psum_ref, norm_ref, out_ref, flat_ref):
    own_i, own_j, chans = psum_ref.shape
    r, z = lax.axis_index("row"), lax.axis_index("col")
    side = win_ref.shape[1] // 2
    w_right = win_ref.at[:, pl.ds(side, side)]

    def use(rows, psums, flat):
        rights = gated(block_ref, rows, flat, w_right)
        for n, at in enumerate(rows):
            psum_ref[at] = psums[n]
            norm_ref[pl.ds(at * own_j, own_j), :] = flat[n * own_j : (n + 1) * own_j]
            flat_ref[pl.ds(at * own_j, own_j), :] = rights[n]

    block_norms(block_ref, t_ref, right_ref[0], r * own_i, z * own_j, idt_ref, bias_ref, use)
    for k in range(own_j):
        out_ref[k] = flat_ref[pl.ds(k, own_i, stride=own_j), :].astype(bf16)


def rest_body(block_ref, norm_ref, win_ref, wgate_ref, left_ref, gate_ref):
    own_i, own_j, _ = left_ref.shape
    w_left = win_ref.at[:, pl.ds(0, win_ref.shape[1] // 2)]
    group = 8
    for i in range(0, own_i, group):
        flat = norm_ref[pl.ds(i * own_j, group * own_j), :]
        rows = list(range(i, i + group))
        gate = sigmoid(jnp.dot(flat, wgate_ref[...], preferred_element_type=f32))
        for n, left in enumerate(gated(block_ref, rows, flat, w_left)):
            left_ref[i + n] = left.astype(bf16)
            gate_ref[i + n] = gate[n * own_j : (n + 1) * own_j]


def other_body(seqs, width, *refs):
    msgs, refs = refs[:4], refs[4:]
    wq_ref, block_ref, right_ref, idt_ref, bias_ref, win_ref, out_ref, t_ref, xl_ref, flat_ref = refs
    own_j, own_i, _ = out_ref.shape
    r, z = lax.axis_index("row"), lax.axis_index("col")
    side = win_ref.shape[1] // 2
    w_right = win_ref.at[:, pl.ds(side, side)]

    def use(rows, psums, flat):
        for at, right in zip(rows, gated(block_ref, rows, flat, w_right)):
            flat_ref[pl.ds(at * own_j, own_j), :] = right

    @pl.when((r % 2) != (z % 2))
    def _():
        mix_rows(seqs, width, seqs * width, msgs, wq_ref, t_ref, xl_ref)
        block_norms(block_ref, t_ref, right_ref[0], (r ^ 3) * own_i, z * own_j, idt_ref, bias_ref, use)
        for k in range(own_j):
            out_ref[k] = flat_ref[pl.ds(k, own_i, stride=own_j), :].astype(bf16)


def met_body(block_ref, t_ref, right_ref, idt_ref, bias_ref, win_ref, left_ref, out_ref, flat_ref):
    own_i, own_j, _ = left_ref.shape
    r, z = lax.axis_index("row"), lax.axis_index("col")
    side = win_ref.shape[1] // 2
    w_left, w_right = win_ref.at[:, pl.ds(0, side)], win_ref.at[:, pl.ds(side, side)]

    def use(rows, psums, flat):
        lefts = gated(block_ref, rows, flat, w_left)
        rights = gated(block_ref, rows, flat, w_right)
        for n, at in enumerate(rows):
            left_ref[at] = lefts[n].astype(bf16)
            flat_ref[pl.ds(at * own_j, own_j), :] = rights[n]

    block_norms(block_ref, t_ref, right_ref[1], r * own_i, (z ^ 1) * own_j, idt_ref, bias_ref, use)
    for k in range(own_j):
        out_ref[k] = flat_ref[pl.ds(k, own_i, stride=own_j), :].astype(bf16)


def join_body(first, parts, own_ref, psum_ref, gate_ref, w_ref, *refs):
    sums, (out_hbm, done_ref, sem) = refs[:parts], refs[-3:]
    count, extent, chans = done_ref.shape
    group = 8
    at = 0
    for sum_ref in sums:
        start = at

        def rows(b, carry):
            here = pl.ds(start + b * group, group)
            there = pl.ds(first + start + b * group, group)
            mixed = own_ref[there] + sum_ref[pl.ds(b * group, group)].astype(f32)
            normed = standardize(mixed).reshape(group * extent, -1).astype(bf16)
            update = jnp.dot(normed, w_ref[...], preferred_element_type=f32).reshape(group, extent, -1)
            done_ref[here] = (psum_ref[there].astype(f32) + gate_ref[there] * update).astype(bf16)
            return carry

        lax.fori_loop(0, sum_ref.shape[0] // group, rows, 0, unroll=True)
        at += sum_ref.shape[0]
    copy = pltpu.make_async_copy(done_ref, out_hbm.at[pl.ds(first, count)], sem)
    copy.start()
    copy.wait()


def triangle_body(l_ref, r_ref, o_ref, lf_ref, flat_ref, rk_ref):
    own_i, depth, chans = l_ref.shape
    extent = r_ref.shape[0]
    group = 8 if own_i % 8 == 0 else 1

    @pl.when(pl.program_id(0) == 0)
    def _():
        lf_ref[...] = l_ref[...].astype(f32)

    def widen(j, carry):
        flat_ref[pl.ds(pl.multiple_of(j * depth, 8), depth), :] = r_ref[j].astype(f32)
        return carry

    lax.fori_loop(0, extent, widen, 0)

    def turn(k, carry):
        rk_ref[k] = flat_ref[pl.ds(k, extent, stride=depth), :]
        return carry

    lax.fori_loop(0, depth, turn, 0)

    def rows(b, carry):
        i0 = b * group
        acc = contract(lf_ref, [rk_ref], i0, group)
        for t in range(group):
            o_ref[0, i0 + t] = acc[t].astype(bf16)
        return carry

    lax.fori_loop(0, own_i // group, rows, 0)


def finish_body(sum_ref, psum_ref, norm_ref, wgate_ref, w_ref, out_ref):
    parts, own_i, extent, chans = sum_ref.shape
    own_j = psum_ref.shape[1]

    def row(i, carry):
        flat = norm_ref[pl.ds(pl.multiple_of(i * own_j, 16), own_j), :]
        gate = sigmoid(jnp.dot(flat, wgate_ref[...], preferred_element_type=f32))
        normed = [standardize(sum_ref[part, i].astype(f32)) for part in range(parts)]
        normed = jnp.concatenate(normed, axis=0).astype(bf16)
        update = jnp.dot(normed, w_ref[...], preferred_element_type=f32)
        out_ref[i] = (psum_ref[i].astype(f32) + gate * update).astype(bf16)
        return carry

    lax.fori_loop(0, own_i, row, 0)


def gathered_plan(left, right, psum, norm, w_gate, w_final):
    own_i, own_j, chans = psum.shape
    rows = lax.axis_size("row")
    tri = w_final.shape[0]
    right_all = lax.all_gather(right, "row", axis=0, tiled=True)
    partial = pl.pallas_call(
        triangle_body,
        grid=(rows,),
        out_shape=jax.ShapeDtypeStruct((rows, own_i, own_i, tri), bf16),
        in_specs=[
            pl.BlockSpec((own_i, own_j, tri), lambda r: (0, 0, 0)),
            pl.BlockSpec((own_i, own_j, tri), lambda r: (r, 0, 0)),
        ],
        out_specs=pl.BlockSpec((1, own_i, own_i, tri), lambda r: (r, 0, 0, 0)),
        scratch_shapes=[
            pltpu.VMEM((own_i, own_j, tri), f32),
            pltpu.VMEM((own_i * own_j, tri), f32),
            pltpu.VMEM((own_j, own_i, tri), f32),
        ],
        compiler_params=limit(56),
        name="triangle",
    )(left, right_all)
    summed = lax.psum_scatter(partial, "col", scatter_dimension=0, tiled=True)
    return pl.pallas_call(
        finish_body,
        out_shape=jax.ShapeDtypeStruct((own_i, own_j, chans), bf16),
        in_specs=[VMEM] * 5,
        out_specs=VMEM,
        compiler_params=limit(56),
        name="finish",
    )(summed, psum, norm, w_gate, w_final)


def paired_plan(homolog, couple, ids, valid, bias, factors, average, w_in, w_gate, w_final):
    seqs, residues, depth = homolog.shape
    own_i, own_j, chans = couple.shape
    width = factors.shape[1] // 2
    tri = w_final.shape[0]
    total = seqs * 4
    cells = [(r, z) for r in range(4) for z in range(4)]
    struct = jax.ShapeDtypeStruct

    def move(value, step):
        pairs = [(r * 4 + z, step(r, z)) for r, z in cells]
        pairs = [(src, r * 4 + z) for src, (r, z) in pairs]
        return lax.ppermute(value, ("row", "col"), pairs)

    def call(body, us, out_shape, scratch, *args, mib=12):
        return pl.pallas_call(
            body,
            out_shape=out_shape,
            in_specs=[VMEM] * len(args),
            out_specs=[VMEM] * len(out_shape) if isinstance(out_shape, list) else VMEM,
            scratch_shapes=scratch,
            compiler_params=limit(mib),
            cost_estimate=cost(us),
            name=getattr(body, "func", body).__name__.removesuffix("_body"),
        )(*args)

    keeper = lambda r, z: r % 2 == z % 2
    beside = lambda r, z: (r ^ 1, z)
    height, lanes = round_up(own_i, 16), 256
    block = struct((own_i + 1, own_j, chans), bf16)
    longer = struct((own_i + 3, own_j, chans), bf16)
    later = (average, bias, w_in, w_gate, w_final)
    *msgs, average, bias, w_in, w_gate, w_final, raw, raw_z = pl.pallas_call(
        open_body,
        out_shape=[struct((height, lanes), bf16)] * 4 + [struct(x.shape, x.dtype) for x in later] + [block, longer],
        in_specs=[HBM] * 9,
        out_specs=[VMEM] * 11,
        scratch_shapes=[
            pltpu.VMEM(homolog.shape, bf16),
            pltpu.VMEM((2 * width, depth), bf16),
            pltpu.VMEM(valid.shape, jnp.int32),
            pltpu.VMEM((seqs * residues, 2 * width), f32),
            pltpu.SemaphoreType.DMA((10,)),
        ],
        compiler_params=limit(8),
        cost_estimate=cost(1.5),
        name="open",
    )(*map(hold, (homolog, factors.T, valid, couple) + later))
    msgs = [msgs[0]] + [
        lax.ppermute(msgs[d], "row", [(r, r ^ d) for r in range(4)]) for d in (1, 2, 3)
    ]
    met = move(raw_z, lambda r, z: (r, z ^ 1))
    raw_other = move(raw, lambda r, z: (r ^ 3, z) if keeper(r, z) else (r ^ 1, z))

    wq, pick, idt = pl.pallas_call(
        functools.partial(ready_body, seqs),
        out_shape=[struct((width // 2, width, 2 * chans), bf16),
                   struct((2, 4, 128, width * total), bf16),
                   struct((residues, 128), jnp.int32)],
        in_specs=[VMEM, HBM],
        out_specs=[VMEM] * 3,
        scratch_shapes=[
            pltpu.VMEM(average.shape, f32),
            pltpu.SMEM(ids.shape, jnp.int32),
            pltpu.SemaphoreType.DMA((1,)),
        ],
        compiler_params=limit(8),
        cost_estimate=cost(1.5),
        name="ready",
    )(average, hold(ids))

    t, mixed = call(
        functools.partial(mix_body, seqs, width), 1,
        [struct((own_i // 2, width * total, 2 * chans), bf16), struct((2, own_j, width * total), bf16)],
        [pltpu.VMEM((own_i * total, 128), f32)], *msgs, wq, pick,
    )
    square = struct((own_i, own_j, tri), bf16)
    flat = [pltpu.VMEM((own_i * own_j, tri), f32)]
    psum, norm, right = call(
        own_body, 2.4, [square, struct((own_i * own_j, chans), bf16), square], flat,
        raw, t, mixed, idt, bias, w_in,
    )
    far = move(right, lambda r, z: (r ^ 1, z) if keeper(r, z) else (r ^ 2, z ^ 1))
    left, gate = call(rest_body, 0.6, [square, struct(couple.shape, f32)], [], raw, norm, w_in, w_gate)
    other = call(
        functools.partial(other_body, seqs, width), 3, square,
        [pltpu.VMEM(t.shape, bf16), pltpu.VMEM((own_i * total, 128), f32)] + flat,
        *msgs, wq, raw_other, mixed, idt, bias, w_in,
    )
    met, *_ = lax.optimization_barrier((met, other))
    met_left, met_right = call(met_body, 3, [square, square], flat, met, t, mixed, idt, bias, w_in)
    other, *_ = lax.optimization_barrier((other, met_left))
    p_other = move(other, beside)
    p_met = move(met_right, beside)
    far, p_other, p_met = lax.optimization_barrier((far, p_other, p_met))
    p_far = move(far, beside)

    def sums(own_pair, first, n, dtype):
        return call(
            functools.partial(sums_body, own_pair, first), 0.13 * n, struct((n, own_j, tri), dtype),
            [pltpu.VMEM((n, 2 * own_j, tri), f32)],
            right, other, p_other, met_right, p_met, far, p_far, left, met_left,
        )

    came = [move(sums(False, first, 8, bf16), lambda r, z: (r, z ^ 2)) for first in range(0, own_i, 8)]
    kept = sums(True, 0, own_i, f32)

    out = []
    for first, n in ((0, 16), (16, 16), (32, own_i - 32)):
        parts = came[first // 8 : (first + n) // 8]
        out = [pl.pallas_call(
            functools.partial(join_body, first, len(parts)),
            out_shape=struct(couple.shape, bf16),
            in_specs=[VMEM] * (4 + len(parts)) + [HBM] * len(out),
            out_specs=HBM,
            scratch_shapes=[pltpu.VMEM((n, own_j, chans), bf16), pltpu.SemaphoreType.DMA],
            input_output_aliases={4 + len(parts): 0} if out else {},
            compiler_params=limit(8),
            cost_estimate=cost(0.06 * n),
            name="join",
        )(kept, psum, gate, w_final, *parts, *out)]
    return out[0]


def shards(homolog, couple, ids, valid, bias, factors, average, w_in, w_gate, w_final):
    rows, cols = lax.axis_size("row"), lax.axis_size("col")
    own_seqs, residues, depth = homolog.shape
    own_i, own_j, chans = couple.shape
    width = factors.shape[1] // 2
    tri = w_final.shape[0]
    total = own_seqs * rows
    lanes = round_up(2 * own_seqs * width, 128)
    height = round_up(max(own_i, own_j), 16)
    paired = (rows, cols, own_seqs * width, chans, tri) == (4, 4, 64, 128, 128)
    if paired and own_i == own_j == 40:
        return paired_plan(homolog, couple, ids, valid, bias, factors, average, w_in, w_gate, w_final)
    scale = 8

    later = (average, valid, bias, couple)
    *msgs, average, valid, bias, couple = pl.pallas_call(
        functools.partial(align_body, own_i, own_j, rows),
        out_shape=[jax.ShapeDtypeStruct((height, lanes), bf16)] * rows
        + [jax.ShapeDtypeStruct(x.shape, x.dtype) for x in later],
        in_specs=[HBM] * 6,
        out_specs=[VMEM] * (rows + 4),
        scratch_shapes=[
            pltpu.VMEM(homolog.shape, bf16),
            pltpu.VMEM((2 * width, depth), bf16),
            pltpu.VMEM((own_seqs * residues, 2 * width), f32),
            pltpu.SemaphoreType.DMA((6,)),
        ],
        compiler_params=limit(8, scale),
        cost_estimate=cost(1.5),
        name="align",
    )(hold(homolog), hold(factors.T), *map(hold, later))
    msgs = [msgs[0]] + [
        lax.ppermute(msgs[d], "row", [(r, r ^ d) for r in range(rows)])
        for d in reversed(range(1, rows))
    ]

    base, mask, wq, pick = pl.pallas_call(
        functools.partial(prepare_body, own_seqs),
        out_shape=[jax.ShapeDtypeStruct((own_i, own_j, chans), f32),
                   jax.ShapeDtypeStruct((own_i, own_j, tri), bf16),
                   jax.ShapeDtypeStruct((width // 2, width, 2 * chans), bf16),
                   jax.ShapeDtypeStruct((rows, lanes, width * total), bf16)],
        in_specs=[VMEM, HBM, VMEM, VMEM, VMEM],
        out_specs=[VMEM] * 4,
        scratch_shapes=[
            pltpu.VMEM(average.shape, f32),
            pltpu.VMEM((own_j, chans), jnp.int32),
            pltpu.SMEM(ids.shape, jnp.int32),
            pltpu.SemaphoreType.DMA((1,)),
        ],
        compiler_params=limit(8, scale),
        cost_estimate=cost(2),
        name="prepare",
    )(couple, hold(ids), valid, bias, average)

    extents = (own_i, own_j)
    psum, norm, right = pl.pallas_call(
        functools.partial(pair_body, own_seqs, width, rows),
        out_shape=[jax.ShapeDtypeStruct((own_i, own_j, chans), bf16),
                   jax.ShapeDtypeStruct((own_i * own_j, chans), bf16),
                   jax.ShapeDtypeStruct(extents + (tri,), bf16)],
        in_specs=[VMEM] * (rows + 5),
        out_specs=[VMEM] * 3,
        scratch_shapes=[
            pltpu.VMEM((own_i * total, 128), f32),
            pltpu.VMEM((own_i // 2, width * total, 2 * chans), bf16),
        ],
        compiler_params=limit(16, scale),
        cost_estimate=cost(4.5),
        name="pair",
    )(*msgs, base, mask, wq, pick, w_in)

    cuts = [own_i]
    lefts = pl.pallas_call(
        left_body,
        out_shape=[jax.ShapeDtypeStruct((n, own_j, tri), bf16) for n in cuts],
        in_specs=[VMEM] * 3,
        out_specs=[VMEM] * len(cuts),
        compiler_params=limit(8, scale),
        cost_estimate=cost(1),
        name="left",
    )(norm, mask, w_in)
    return gathered_plan(lefts[0], right, psum, norm, w_gate, w_final)


def solution(mesh):
    placed = (
        P(("grp", "row"), None, None),
        P(("grp", "row"), "col", None),
        P("grp"),
        P(("grp", "row"), "col"),
        P(),
        P(),
        P(),
        P(),
        P(),
        P(),
    )
    return jax.shard_map(
        shards,
        mesh=mesh,
        in_specs=placed,
        out_specs=P(("grp", "row"), "col", None),
        check_vma=False,
    )
```

```python
import functools

import jax
import jax.numpy as jnp
from jax import lax
from jax.experimental import pallas as pl
from jax.experimental.pallas import tpu as pltpu
from jax.sharding import PartitionSpec as P

eps = 1e-05
f32 = jnp.float32
bf16 = jnp.bfloat16
VMEM = pl.BlockSpec(memory_space=pltpu.VMEM)
SMEM = pl.BlockSpec(memory_space=pltpu.SMEM)
HBM = pl.BlockSpec(memory_space=pltpu.HBM)


def limit(mib, scale=1):
    return pltpu.CompilerParams(vmem_limit_bytes=min(56, mib * scale) * 1024 * 1024)


def round_up(n, m):
    return (n + m - 1) // m * m


def cost(us):
    return pl.CostEstimate(flops=0, bytes_accessed=int(us * 3.69e6), transcendentals=0)


def hold(x):
    return pltpu.with_memory_space_constraint(x, pltpu.HBM)


def fetch(pairs, sem):
    copies = [pltpu.make_async_copy(src, dst, sem.at[n]) for n, (src, dst) in enumerate(pairs)]
    for copy in copies:
        copy.start()
    return copies


def standardize(values):
    centre = values - jnp.mean(values, axis=-1, keepdims=True)
    spread = jnp.mean(centre * centre, axis=-1, keepdims=True)
    return centre * lax.rsqrt(spread + eps)


def sigmoid(v):
    return 0.5 * jnp.tanh(0.5 * v) + 0.5


def align_body(own_i, own_j, count, x_hbm, w_hbm, *refs):
    later, outs, refs = refs[:4], refs[4 : 4 + count], refs[4 + count :]
    brought, (x_ref, w_ref, y_ref, sem) = refs[:4], refs[4:]
    copies = fetch([(x_hbm, x_ref), (w_hbm, w_ref), *zip(later, brought)], sem)
    seqs, residues, depth = x_ref.shape
    width = w_ref.shape[0] // 2
    height, lanes = outs[0].shape
    me = lax.axis_index("row")
    z = lax.axis_index("col")
    copies[0].wait()
    x = x_ref[...].astype(f32).reshape(seqs * residues, depth)
    normed = standardize(x).astype(bf16)
    copies[1].wait()
    y_ref[...] = lax.dot_general(
        normed, w_ref[...], (((1,), (1,)), ((), ())), preferred_element_type=f32
    )
    start = pl.multiple_of(z * own_j, 8)

    def tall(v):
        gap = height - v.shape[0]
        return jnp.concatenate([v, jnp.zeros((gap, v.shape[1]), f32)], axis=0) if gap else v

    right = [tall(y_ref[pl.ds(s * residues + start, own_j), width:]) for s in range(seqs)]
    gap = lanes - 2 * seqs * width
    right += [jnp.zeros((height, gap), f32)] if gap else []
    for d, out in enumerate(outs):
        first = pl.multiple_of((me ^ d) * own_i, 8)
        left = [tall(y_ref[pl.ds(s * residues + first, own_i), :width]) for s in range(seqs)]
        out[...] = jnp.concatenate(left + right, axis=1).astype(bf16)
    for copy in copies[2:]:
        copy.wait()


def prepare_body(seqs, couple_ref, ids_hbm, valid_ref, bias_ref, avg_ref, base_ref, mask_ref, wq_ref, pick_ref,
                 wf_ref, idc_ref, ids_ref, sem):
    (copy,) = fetch([(ids_hbm, ids_ref)], sem)
    own_i, own_j, chans = couple_ref.shape
    pairs, width, _ = wq_ref.shape
    blocks, lanes, _ = pick_ref.shape
    total = blocks * seqs
    x0 = lax.axis_index("row") * own_i
    z0 = lax.axis_index("col") * own_j

    row = lax.broadcasted_iota(jnp.int32, pick_ref.shape[1:], 0)
    col = lax.broadcasted_iota(jnp.int32, pick_ref.shape[1:], 1)
    unit = row - seqs * width
    place = lax.rem(unit, width) * total + lax.div(unit, width)
    place = jnp.where((unit >= 0) & (unit < seqs * width), col - place, -1)

    def pick(r, carry):
        pick_ref[r] = jnp.where(place == r * seqs, 1.0, 0.0).astype(bf16)
        return carry

    lax.fori_loop(0, blocks, pick, 0)
    wf_ref[...] = avg_ref[...].astype(f32)
    for h in range(pairs):
        both = [wf_ref[pl.ds(2 * h + d, width, stride=width), :] for d in range(2)]
        wq_ref[h] = jnp.concatenate(both, axis=1).astype(bf16)
    copy.wait()
    for j in range(own_j):
        idc_ref[pl.ds(j, 1), :] = jnp.full((1, chans), ids_ref[z0 + j], jnp.int32)
    idc = idc_ref[...]
    valid_t = valid_ref[...].astype(f32).T
    lane = lax.broadcasted_iota(jnp.int32, valid_t.shape, 1)
    same_bias = bias_ref[0:1, :]
    cross_bias = bias_ref[1:2, :]

    def rows(i, carry):
        bias = jnp.where(idc == ids_ref[x0 + i], same_bias, cross_bias)
        base_ref[i] = couple_ref[i].astype(f32) + bias
        column = jnp.sum(jnp.where(lane == i, valid_t, 0.0), axis=1, keepdims=True)
        mask_ref[i] = jnp.broadcast_to(column, (own_j, mask_ref.shape[2])).astype(bf16)
        return carry

    lax.fori_loop(0, own_i, rows, 0, unroll=8)


def pair_body(seqs, width, blocks, *refs):
    msgs = refs[:blocks]
    base_ref, mask_ref, wq_ref, pick_ref, win_ref = refs[blocks : blocks + 5]
    psum_ref, norm_ref, right_ref = refs[blocks + 5 : blocks + 8]
    xl_ref, t_ref = refs[blocks + 8 :]
    own_i, own_j, chans = base_ref.shape
    height, lanes = msgs[0].shape
    total = seqs * blocks
    tri = win_ref.shape[1] // 4
    half = own_i // 2

    for r in range(blocks):
        m = msgs[r][pl.ds(0, own_i), :].astype(f32)
        for s in range(seqs):
            moved = m if s == 0 else pltpu.roll(m, lanes - s * width, 1)
            xl_ref[pl.ds(r * seqs + s, own_i, stride=total), :] = moved[:, :128]
    lhs = xl_ref[:, :width].astype(bf16)

    joined = jnp.concatenate([msg[...] for msg in msgs], axis=1)
    picks = pick_ref[...].reshape(blocks * lanes, width * total)
    rmat = jnp.dot(joined, picks, preferred_element_type=f32)[:own_j].astype(bf16)

    def expand(h, carry):
        out = jnp.dot(lhs, wq_ref[h], preferred_element_type=f32)
        parts = [out[:, d * chans : (d + 1) * chans].reshape(own_i, total, chans) for d in range(2)]
        block = jnp.concatenate(parts, axis=1).astype(bf16)
        where = pl.ds(pl.multiple_of(h * 2 * total, 16), 2 * total)
        t_ref[:, where, :chans] = block[:half]
        t_ref[:, where, chans:] = block[half:]
        return carry

    lax.fori_loop(0, width // 2, expand, 0)

    step = 4 if half % 4 == 0 else 1

    def rows(b, carry):
        normed = [[], []]
        for g in range(step):
            i = b * step + g
            both = jnp.dot(rmat, t_ref[i], preferred_element_type=f32) * (1.0 / total)
            for side in range(2):
                at = i + side * half
                psum = (base_ref[at] + both[:, side * chans : (side + 1) * chans]).astype(bf16)
                psum_ref[at] = psum
                normed[side].append(standardize(psum.astype(f32)))
        flat = jnp.concatenate(normed[0] + normed[1], axis=0).astype(bf16)
        proj = jnp.dot(flat, win_ref[:, 2 * tri :], preferred_element_type=f32)
        count = step * own_j
        for side in range(2):
            cut = slice(side * count, (side + 1) * count)
            i0 = b * step + side * half
            norm_ref[pl.ds(pl.multiple_of(i0 * own_j, 16), count), :] = flat[cut]
            mask = mask_ref[pl.ds(i0, step)].astype(f32).reshape(count, tri)
            right = mask * sigmoid(proj[cut, :tri]) * proj[cut, tri:]
            right_ref[pl.ds(i0, step)] = right.reshape(step, own_j, tri).astype(bf16)
        return carry

    lax.fori_loop(0, half // step, rows, 0)


def left_body(norm_ref, mask_ref, win_ref, *outs):
    own_i, own_j, tri = mask_ref.shape
    group = 8 if own_i % 8 == 0 else 1
    at = 0
    for out in outs:
        first = at

        def rows(b, carry):
            i0 = first + b * group
            flat = norm_ref[pl.ds(pl.multiple_of(i0 * own_j, 16), group * own_j), :]
            mask = mask_ref[pl.ds(i0, group)].astype(f32).reshape(group * own_j, tri)
            proj = jnp.dot(flat, win_ref[:, : 2 * tri], preferred_element_type=f32)
            left = mask * sigmoid(proj[:, :tri]) * proj[:, tri:]
            out[pl.ds(b * group, group)] = left.reshape(group, own_j, tri).astype(bf16)
            return carry

        lax.fori_loop(0, out.shape[0] // group, rows, 0, unroll=True)
        at += out.shape[0]


def contract(lf_ref, halves, i0, group):
    step = 8
    acc = (jnp.zeros(halves[0].shape[1:], f32),) * group
    for h, r_ref in enumerate(halves):
        depth = r_ref.shape[0]

        def add(kb, acc):
            k0 = kb * step
            acc = list(acc)
            for d in range(step):
                right = r_ref[k0 + d].astype(f32)
                for t in range(group):
                    acc[t] = acc[t] + lf_ref[i0 + t, pl.ds(h * depth + k0 + d, 1), :] * right
            return tuple(acc)

        acc = lax.fori_loop(0, depth // step, add, acc)
    return acc


def sums_body(own_pair, first, own_ref, other_ref, p_other, met_ref, p_met, far_ref, p_far, l_ref, m_ref, o_ref, lf_ref):
    count, depth = o_ref.shape[0], l_ref.shape[1]
    group = 8
    lf_ref[:, pl.ds(0, depth), :] = l_ref[pl.ds(first, count)].astype(f32)
    lf_ref[:, pl.ds(depth, depth), :] = m_ref[pl.ds(first, count)].astype(f32)

    def use(halves):
        def rows(b, carry):
            acc = contract(lf_ref, halves, b * group, group)
            for t in range(group):
                o_ref[b * group + t] = acc[t].astype(o_ref.dtype)
            return carry

        lax.fori_loop(0, count // group, rows, 0)

    r, z = lax.axis_index("row"), lax.axis_index("col")
    keeper = (r % 2) == (z % 2)
    near = ((r // 2) == (z // 2)) == own_pair
    table = [
        (near & keeper, own_ref, met_ref),
        (near & ~keeper, far_ref, p_met),
        (~near & keeper, p_other, far_ref),
        (~near & ~keeper, other_ref, p_far),
    ]
    for cond, a, b in table:
        pl.when(cond)(functools.partial(use, (a, b)))


def open_body(x_hbm, w_hbm, valid_hbm, couple_hbm, *refs):
    later, outs, brought = refs[:5], refs[5:9], refs[9:14]
    block_ref, longer_ref, x_ref, w_ref, valid_ref, y_ref, sem = refs[14:]
    own_i, own_j, chans = couple_hbm.shape
    copies = fetch([(x_hbm, x_ref), (w_hbm, w_ref), (valid_hbm, valid_ref),
                    (couple_hbm, block_ref.at[pl.ds(0, own_i)]),
                    (couple_hbm, longer_ref.at[pl.ds(0, own_i)]), *zip(later, brought)], sem)
    seqs, residues, depth = x_ref.shape
    width = w_ref.shape[0] // 2
    height, lanes = outs[0].shape
    me = lax.axis_index("row")
    z = lax.axis_index("col")
    copies[0].wait()
    x = x_ref[...].astype(f32).reshape(seqs * residues, depth)
    normed = standardize(x).astype(bf16)
    copies[1].wait()
    y_ref[...] = lax.dot_general(
        normed, w_ref[...], (((1,), (1,)), ((), ())), preferred_element_type=f32
    )

    def cut(start, lane):
        start = pl.multiple_of(start * own_i, 8)
        return [y_ref[pl.ds(s * residues + start, own_i), lane : lane + width] for s in range(seqs)]

    shared = cut(z, width) + cut(z ^ 1, width)
    below = jnp.zeros((height - own_i, lanes), f32)
    for d, out in enumerate(outs):
        other = ((me ^ d) // 2 ^ 1) * 2 + z % 2
        rows = jnp.concatenate(cut(me ^ d, 0) + cut(other, 0) + shared, axis=1)
        out[...] = jnp.concatenate([rows, below], axis=0).astype(bf16)
    copies[2].wait()
    mask = valid_ref[...].astype(f32).T
    mask = jnp.concatenate([mask, jnp.zeros((own_j, chans - own_i), f32)], axis=1)
    block_ref[own_i] = mask.astype(bf16)
    for n in range(own_i, longer_ref.shape[0]):
        longer_ref[n] = mask.astype(bf16)
    for copy in copies[3:]:
        copy.wait()


def ready_body(seqs, avg_ref, ids_hbm, wq_ref, pick_ref, idt_ref, wf_ref, ids_ref, sem):
    (copy,) = fetch([(ids_hbm, ids_ref)], sem)
    pairs, width, _ = wq_ref.shape
    kinds, blocks, lanes, _ = pick_ref.shape
    total = blocks * seqs
    row = lax.broadcasted_iota(jnp.int32, pick_ref.shape[2:], 0)
    col = lax.broadcasted_iota(jnp.int32, pick_ref.shape[2:], 1)
    for n in range(kinds):
        unit = row - n * seqs * width
        place = lax.rem(unit, width) * total + lax.div(unit, width)
        place = jnp.where((unit >= 0) & (unit < seqs * width), col - place, -1)
        for r in range(blocks):
            pick_ref[n, r] = jnp.where(place == r * seqs, 1.0, 0.0).astype(bf16)
    wf_ref[...] = avg_ref[...].astype(f32)
    for h in range(pairs):
        both = [wf_ref[pl.ds(2 * h + d, width, stride=width), :] for d in range(2)]
        wq_ref[h] = jnp.concatenate(both, axis=1).astype(bf16)
    copy.wait()

    def spread(n, carry):
        idt_ref[pl.ds(n, 1), :] = jnp.full((1, idt_ref.shape[1]), ids_ref[n], jnp.int32)
        return carry

    lax.fori_loop(0, idt_ref.shape[0], spread, 0, unroll=8)


def mix_rows(seqs, width, lane0, msgs, wq_ref, t_ref, xl_ref):
    half, terms, both = t_ref.shape
    chans, own_i, total = both // 2, 2 * half, seqs * 4
    for r in range(4):
        m = msgs[r][pl.ds(0, own_i), :128].astype(f32)
        for s in range(seqs):
            lane = lane0 + s * width
            moved = pltpu.roll(m, 128 - lane, 1) if lane else m
            xl_ref[pl.ds(r * seqs + s, own_i, stride=total), :] = moved
    lhs = xl_ref[:, :width].astype(bf16)
    for h in range(width // 2):
        out = jnp.dot(lhs, wq_ref[h], preferred_element_type=f32)
        parts = [out[:, d * chans : (d + 1) * chans].reshape(own_i, total, chans) for d in range(2)]
        block = jnp.concatenate(parts, axis=1).astype(bf16)
        where = pl.ds(h * 2 * total, 2 * total)
        t_ref[:, where, :chans] = block[:half]
        t_ref[:, where, chans:] = block[half:]


def mix_body(seqs, width, *refs):
    msgs, (wq_ref, pick_ref, t_ref, right_ref, xl_ref) = refs[:4], refs[4:]
    own_j, terms = right_ref.shape[1:]
    joined = jnp.concatenate([msg[:, 128:] for msg in msgs], axis=1)
    for n in range(2):
        right = jnp.dot(joined, pick_ref[n].reshape(512, terms), preferred_element_type=f32)[:own_j]
        right_ref[n] = (right * (1.0 / (seqs * 4))).astype(bf16)
    mix_rows(seqs, width, 0, msgs, wq_ref, t_ref, xl_ref)


def block_norms(block_ref, t_ref, right, row0, col0, idt_ref, bias_ref, use):
    half, terms, _ = t_ref.shape
    own_i, own_j, chans = 2 * half, right.shape[0], bias_ref.shape[1]
    idc = idt_ref[pl.ds(pl.multiple_of(col0, 8), own_j), :]
    step = 4
    for b in range(half // step):
        rows, psums = [[], []], [[], []]
        for i in range(b * step, b * step + step):
            both = jnp.dot(right, t_ref[i], preferred_element_type=f32)
            for side in range(2):
                at = i + side * half
                same = idc == idt_ref[pl.ds(row0 + at, 1), :]
                base = block_ref[at].astype(f32) + jnp.where(same, bias_ref[0:1, :], bias_ref[1:2, :])
                rows[side].append(at)
                psums[side].append((base + both[:, side * chans : (side + 1) * chans]).astype(bf16))
        rows, psums = rows[0] + rows[1], psums[0] + psums[1]
        flat = jnp.concatenate([standardize(p.astype(f32)) for p in psums], axis=0).astype(bf16)
        use(rows, psums, flat)


def gated(block_ref, rows, flat, w_ref):
    own_j = block_ref.shape[1]
    tri = w_ref.shape[1] // 2
    mask = block_ref[block_ref.shape[0] - 1].astype(f32)
    proj = jnp.dot(flat, w_ref[...], preferred_element_type=f32)
    both = sigmoid(proj[:, :tri]) * proj[:, tri:]
    return [mask[:, at : at + 1] * both[n * own_j : (n + 1) * own_j] for n, at in enumerate(rows)]


def own_body(block_ref, t_ref, right_ref, idt_ref, bias_ref, win_ref, psum_ref, norm_ref, out_ref, flat_ref):
    own_i, own_j, chans = psum_ref.shape
    r, z = lax.axis_index("row"), lax.axis_index("col")
    side = win_ref.shape[1] // 2
    w_right = win_ref.at[:, pl.ds(side, side)]

    def use(rows, psums, flat):
        rights = gated(block_ref, rows, flat, w_right)
        for n, at in enumerate(rows):
            psum_ref[at] = psums[n]
            norm_ref[pl.ds(at * own_j, own_j), :] = flat[n * own_j : (n + 1) * own_j]
            flat_ref[pl.ds(at * own_j, own_j), :] = rights[n]

    block_norms(block_ref, t_ref, right_ref[0], r * own_i, z * own_j, idt_ref, bias_ref, use)
    for k in range(own_j):
        out_ref[k] = flat_ref[pl.ds(k, own_i, stride=own_j), :].astype(bf16)


def rest_body(block_ref, norm_ref, win_ref, wgate_ref, left_ref, gate_ref):
    own_i, own_j, _ = left_ref.shape
    w_left = win_ref.at[:, pl.ds(0, win_ref.shape[1] // 2)]
    group = 8
    for i in range(0, own_i, group):
        flat = norm_ref[pl.ds(i * own_j, group * own_j), :]
        rows = list(range(i, i + group))
        gate = sigmoid(jnp.dot(flat, wgate_ref[...], preferred_element_type=f32))
        for n, left in enumerate(gated(block_ref, rows, flat, w_left)):
            left_ref[i + n] = left.astype(bf16)
            gate_ref[i + n] = gate[n * own_j : (n + 1) * own_j]


def other_body(seqs, width, *refs):
    msgs, refs = refs[:4], refs[4:]
    wq_ref, block_ref, right_ref, idt_ref, bias_ref, win_ref, out_ref, t_ref, xl_ref, flat_ref = refs
    own_j, own_i, _ = out_ref.shape
    r, z = lax.axis_index("row"), lax.axis_index("col")
    side = win_ref.shape[1] // 2
    w_right = win_ref.at[:, pl.ds(side, side)]

    def use(rows, psums, flat):
        for at, right in zip(rows, gated(block_ref, rows, flat, w_right)):
            flat_ref[pl.ds(at * own_j, own_j), :] = right

    @pl.when((r % 2) != (z % 2))
    def _():
        mix_rows(seqs, width, seqs * width, msgs, wq_ref, t_ref, xl_ref)
        block_norms(block_ref, t_ref, right_ref[0], (r ^ 3) * own_i, z * own_j, idt_ref, bias_ref, use)
        for k in range(own_j):
            out_ref[k] = flat_ref[pl.ds(k, own_i, stride=own_j), :].astype(bf16)


def met_body(block_ref, t_ref, right_ref, idt_ref, bias_ref, win_ref, left_ref, out_ref, flat_ref):
    own_i, own_j, _ = left_ref.shape
    r, z = lax.axis_index("row"), lax.axis_index("col")
    side = win_ref.shape[1] // 2
    w_left, w_right = win_ref.at[:, pl.ds(0, side)], win_ref.at[:, pl.ds(side, side)]

    def use(rows, psums, flat):
        lefts = gated(block_ref, rows, flat, w_left)
        rights = gated(block_ref, rows, flat, w_right)
        for n, at in enumerate(rows):
            left_ref[at] = lefts[n].astype(bf16)
            flat_ref[pl.ds(at * own_j, own_j), :] = rights[n]

    block_norms(block_ref, t_ref, right_ref[1], r * own_i, (z ^ 1) * own_j, idt_ref, bias_ref, use)
    for k in range(own_j):
        out_ref[k] = flat_ref[pl.ds(k, own_i, stride=own_j), :].astype(bf16)


def join_body(first, parts, own_ref, psum_ref, gate_ref, w_ref, *refs):
    sums, (out_hbm, done_ref, sem) = refs[:parts], refs[-3:]
    count, extent, chans = done_ref.shape
    group = 8
    at = 0
    for sum_ref in sums:
        start = at

        def rows(b, carry):
            here = pl.ds(start + b * group, group)
            there = pl.ds(first + start + b * group, group)
            mixed = own_ref[there] + sum_ref[pl.ds(b * group, group)].astype(f32)
            normed = standardize(mixed).reshape(group * extent, -1).astype(bf16)
            update = jnp.dot(normed, w_ref[...], preferred_element_type=f32).reshape(group, extent, -1)
            done_ref[here] = (psum_ref[there].astype(f32) + gate_ref[there] * update).astype(bf16)
            return carry

        lax.fori_loop(0, sum_ref.shape[0] // group, rows, 0, unroll=True)
        at += sum_ref.shape[0]
    copy = pltpu.make_async_copy(done_ref, out_hbm.at[pl.ds(first, count)], sem)
    copy.start()
    copy.wait()


def triangle_body(l_ref, r_ref, o_ref, lf_ref, flat_ref, rk_ref):
    own_i, depth, chans = l_ref.shape
    extent = r_ref.shape[0]
    group = 8 if own_i % 8 == 0 else 1

    @pl.when(pl.program_id(0) == 0)
    def _():
        lf_ref[...] = l_ref[...].astype(f32)

    def widen(j, carry):
        flat_ref[pl.ds(pl.multiple_of(j * depth, 8), depth), :] = r_ref[j].astype(f32)
        return carry

    lax.fori_loop(0, extent, widen, 0)

    def turn(k, carry):
        rk_ref[k] = flat_ref[pl.ds(k, extent, stride=depth), :]
        return carry

    lax.fori_loop(0, depth, turn, 0)

    def rows(b, carry):
        i0 = b * group
        acc = contract(lf_ref, [rk_ref], i0, group)
        for t in range(group):
            o_ref[0, i0 + t] = acc[t].astype(bf16)
        return carry

    lax.fori_loop(0, own_i // group, rows, 0)


def finish_body(sum_ref, psum_ref, norm_ref, wgate_ref, w_ref, out_ref):
    parts, own_i, extent, chans = sum_ref.shape
    own_j = psum_ref.shape[1]

    def row(i, carry):
        flat = norm_ref[pl.ds(pl.multiple_of(i * own_j, 16), own_j), :]
        gate = sigmoid(jnp.dot(flat, wgate_ref[...], preferred_element_type=f32))
        normed = [standardize(sum_ref[part, i].astype(f32)) for part in range(parts)]
        normed = jnp.concatenate(normed, axis=0).astype(bf16)
        update = jnp.dot(normed, w_ref[...], preferred_element_type=f32)
        out_ref[i] = (psum_ref[i].astype(f32) + gate * update).astype(bf16)
        return carry

    lax.fori_loop(0, own_i, row, 0)


def gathered_plan(left, right, psum, norm, w_gate, w_final):
    own_i, own_j, chans = psum.shape
    rows = lax.axis_size("row")
    tri = w_final.shape[0]
    right_all = lax.all_gather(right, "row", axis=0, tiled=True)
    partial = pl.pallas_call(
        triangle_body,
        grid=(rows,),
        out_shape=jax.ShapeDtypeStruct((rows, own_i, own_i, tri), bf16),
        in_specs=[
            pl.BlockSpec((own_i, own_j, tri), lambda r: (0, 0, 0)),
            pl.BlockSpec((own_i, own_j, tri), lambda r: (r, 0, 0)),
        ],
        out_specs=pl.BlockSpec((1, own_i, own_i, tri), lambda r: (r, 0, 0, 0)),
        scratch_shapes=[
            pltpu.VMEM((own_i, own_j, tri), f32),
            pltpu.VMEM((own_i * own_j, tri), f32),
            pltpu.VMEM((own_j, own_i, tri), f32),
        ],
        compiler_params=limit(56),
        name="triangle",
    )(left, right_all)
    summed = lax.psum_scatter(partial, "col", scatter_dimension=0, tiled=True)
    return pl.pallas_call(
        finish_body,
        out_shape=jax.ShapeDtypeStruct((own_i, own_j, chans), bf16),
        in_specs=[VMEM] * 5,
        out_specs=VMEM,
        compiler_params=limit(56),
        name="finish",
    )(summed, psum, norm, w_gate, w_final)


def paired_plan(homolog, couple, ids, valid, bias, factors, average, w_in, w_gate, w_final):
    seqs, residues, depth = homolog.shape
    own_i, own_j, chans = couple.shape
    width = factors.shape[1] // 2
    tri = w_final.shape[0]
    total = seqs * 4
    cells = [(r, z) for r in range(4) for z in range(4)]
    struct = jax.ShapeDtypeStruct

    def move(value, step):
        pairs = [(r * 4 + z, step(r, z)) for r, z in cells]
        pairs = [(src, r * 4 + z) for src, (r, z) in pairs]
        return lax.ppermute(value, ("row", "col"), pairs)

    def call(body, us, out_shape, scratch, *args, mib=12):
        return pl.pallas_call(
            body,
            out_shape=out_shape,
            in_specs=[VMEM] * len(args),
            out_specs=[VMEM] * len(out_shape) if isinstance(out_shape, list) else VMEM,
            scratch_shapes=scratch,
            compiler_params=limit(mib),
            cost_estimate=cost(us),
            name=getattr(body, "func", body).__name__.removesuffix("_body"),
        )(*args)

    keeper = lambda r, z: r % 2 == z % 2
    beside = lambda r, z: (r ^ 1, z)
    height, lanes = round_up(own_i, 16), 256
    block = struct((own_i + 1, own_j, chans), bf16)
    longer = struct((own_i + 3, own_j, chans), bf16)
    later = (average, bias, w_in, w_gate, w_final)
    *msgs, average, bias, w_in, w_gate, w_final, raw, raw_z = pl.pallas_call(
        open_body,
        out_shape=[struct((height, lanes), bf16)] * 4 + [struct(x.shape, x.dtype) for x in later] + [block, longer],
        in_specs=[HBM] * 9,
        out_specs=[VMEM] * 11,
        scratch_shapes=[
            pltpu.VMEM(homolog.shape, bf16),
            pltpu.VMEM((2 * width, depth), bf16),
            pltpu.VMEM(valid.shape, jnp.int32),
            pltpu.VMEM((seqs * residues, 2 * width), f32),
            pltpu.SemaphoreType.DMA((10,)),
        ],
        compiler_params=limit(8),
        cost_estimate=cost(1.5),
        name="open",
    )(*map(hold, (homolog, factors.T, valid, couple) + later))
    msgs = [msgs[0]] + [
        lax.ppermute(msgs[d], "row", [(r, r ^ d) for r in range(4)]) for d in (1, 2, 3)
    ]
    met = move(raw_z, lambda r, z: (r, z ^ 1))
    raw_other = move(raw, lambda r, z: (r ^ 3, z) if keeper(r, z) else (r ^ 1, z))

    wq, pick, idt = pl.pallas_call(
        functools.partial(ready_body, seqs),
        out_shape=[struct((width // 2, width, 2 * chans), bf16),
                   struct((2, 4, 128, width * total), bf16),
                   struct((residues, 128), jnp.int32)],
        in_specs=[VMEM, HBM],
        out_specs=[VMEM] * 3,
        scratch_shapes=[
            pltpu.VMEM(average.shape, f32),
            pltpu.SMEM(ids.shape, jnp.int32),
            pltpu.SemaphoreType.DMA((1,)),
        ],
        compiler_params=limit(8),
        cost_estimate=cost(1.5),
        name="ready",
    )(average, hold(ids))

    t, mixed = call(
        functools.partial(mix_body, seqs, width), 1,
        [struct((own_i // 2, width * total, 2 * chans), bf16), struct((2, own_j, width * total), bf16)],
        [pltpu.VMEM((own_i * total, 128), f32)], *msgs, wq, pick,
    )
    square = struct((own_i, own_j, tri), bf16)
    flat = [pltpu.VMEM((own_i * own_j, tri), f32)]
    psum, norm, right = call(
        own_body, 2.4, [square, struct((own_i * own_j, chans), bf16), square], flat,
        raw, t, mixed, idt, bias, w_in,
    )
    far = move(right, lambda r, z: (r ^ 1, z) if keeper(r, z) else (r ^ 2, z ^ 1))
    left, gate = call(rest_body, 0.6, [square, struct(couple.shape, f32)], [], raw, norm, w_in, w_gate)
    other = call(
        functools.partial(other_body, seqs, width), 3, square,
        [pltpu.VMEM(t.shape, bf16), pltpu.VMEM((own_i * total, 128), f32)] + flat,
        *msgs, wq, raw_other, mixed, idt, bias, w_in,
    )
    p_other = move(other, beside)
    met, *_ = lax.optimization_barrier((met, other))
    met_left, met_right = call(met_body, 3, [square, square], flat, met, t, mixed, idt, bias, w_in)
    p_met = move(met_right, beside)
    far, *_ = lax.optimization_barrier((far, met_left))
    p_far = move(far, beside)

    def sums(own_pair, first, n, dtype):
        return call(
            functools.partial(sums_body, own_pair, first), 0.13 * n, struct((n, own_j, tri), dtype),
            [pltpu.VMEM((n, 2 * own_j, tri), f32)],
            right, other, p_other, met_right, p_met, far, p_far, left, met_left,
        )

    came = [move(sums(False, first, 8, bf16), lambda r, z: (r, z ^ 2)) for first in range(0, own_i, 8)]
    kept = sums(True, 0, own_i, f32)

    out = []
    for first, n in ((0, 16), (16, 16), (32, own_i - 32)):
        parts = came[first // 8 : (first + n) // 8]
        out = [pl.pallas_call(
            functools.partial(join_body, first, len(parts)),
            out_shape=struct(couple.shape, bf16),
            in_specs=[VMEM] * (4 + len(parts)) + [HBM] * len(out),
            out_specs=HBM,
            scratch_shapes=[pltpu.VMEM((n, own_j, chans), bf16), pltpu.SemaphoreType.DMA],
            input_output_aliases={4 + len(parts): 0} if out else {},
            compiler_params=limit(8),
            cost_estimate=cost(0.06 * n),
            name="join",
        )(kept, psum, gate, w_final, *parts, *out)]
    return out[0]


def shards(homolog, couple, ids, valid, bias, factors, average, w_in, w_gate, w_final):
    rows, cols = lax.axis_size("row"), lax.axis_size("col")
    own_seqs, residues, depth = homolog.shape
    own_i, own_j, chans = couple.shape
    width = factors.shape[1] // 2
    tri = w_final.shape[0]
    total = own_seqs * rows
    lanes = round_up(2 * own_seqs * width, 128)
    height = round_up(max(own_i, own_j), 16)
    paired = (rows, cols, own_seqs * width, chans, tri) == (4, 4, 64, 128, 128)
    if paired and own_i == own_j == 40:
        return paired_plan(homolog, couple, ids, valid, bias, factors, average, w_in, w_gate, w_final)
    scale = 8

    later = (average, valid, bias, couple)
    *msgs, average, valid, bias, couple = pl.pallas_call(
        functools.partial(align_body, own_i, own_j, rows),
        out_shape=[jax.ShapeDtypeStruct((height, lanes), bf16)] * rows
        + [jax.ShapeDtypeStruct(x.shape, x.dtype) for x in later],
        in_specs=[HBM] * 6,
        out_specs=[VMEM] * (rows + 4),
        scratch_shapes=[
            pltpu.VMEM(homolog.shape, bf16),
            pltpu.VMEM((2 * width, depth), bf16),
            pltpu.VMEM((own_seqs * residues, 2 * width), f32),
            pltpu.SemaphoreType.DMA((6,)),
        ],
        compiler_params=limit(8, scale),
        cost_estimate=cost(1.5),
        name="align",
    )(hold(homolog), hold(factors.T), *map(hold, later))
    msgs = [msgs[0]] + [
        lax.ppermute(msgs[d], "row", [(r, r ^ d) for r in range(rows)])
        for d in reversed(range(1, rows))
    ]

    base, mask, wq, pick = pl.pallas_call(
        functools.partial(prepare_body, own_seqs),
        out_shape=[jax.ShapeDtypeStruct((own_i, own_j, chans), f32),
                   jax.ShapeDtypeStruct((own_i, own_j, tri), bf16),
                   jax.ShapeDtypeStruct((width // 2, width, 2 * chans), bf16),
                   jax.ShapeDtypeStruct((rows, lanes, width * total), bf16)],
        in_specs=[VMEM, HBM, VMEM, VMEM, VMEM],
        out_specs=[VMEM] * 4,
        scratch_shapes=[
            pltpu.VMEM(average.shape, f32),
            pltpu.VMEM((own_j, chans), jnp.int32),
            pltpu.SMEM(ids.shape, jnp.int32),
            pltpu.SemaphoreType.DMA((1,)),
        ],
        compiler_params=limit(8, scale),
        cost_estimate=cost(2),
        name="prepare",
    )(couple, hold(ids), valid, bias, average)

    extents = (own_i, own_j)
    psum, norm, right = pl.pallas_call(
        functools.partial(pair_body, own_seqs, width, rows),
        out_shape=[jax.ShapeDtypeStruct((own_i, own_j, chans), bf16),
                   jax.ShapeDtypeStruct((own_i * own_j, chans), bf16),
                   jax.ShapeDtypeStruct(extents + (tri,), bf16)],
        in_specs=[VMEM] * (rows + 5),
        out_specs=[VMEM] * 3,
        scratch_shapes=[
            pltpu.VMEM((own_i * total, 128), f32),
            pltpu.VMEM((own_i // 2, width * total, 2 * chans), bf16),
        ],
        compiler_params=limit(16, scale),
        cost_estimate=cost(4.5),
        name="pair",
    )(*msgs, base, mask, wq, pick, w_in)

    cuts = [own_i]
    lefts = pl.pallas_call(
        left_body,
        out_shape=[jax.ShapeDtypeStruct((n, own_j, tri), bf16) for n in cuts],
        in_specs=[VMEM] * 3,
        out_specs=[VMEM] * len(cuts),
        compiler_params=limit(8, scale),
        cost_estimate=cost(1),
        name="left",
    )(norm, mask, w_in)
    return gathered_plan(lefts[0], right, psum, norm, w_gate, w_final)


def solution(mesh):
    placed = (
        P(("grp", "row"), None, None),
        P(("grp", "row"), "col", None),
        P("grp"),
        P(("grp", "row"), "col"),
        P(),
        P(),
        P(),
        P(),
        P(),
        P(),
    )
    return jax.shard_map(
        shards,
        mesh=mesh,
        in_specs=placed,
        out_specs=P(("grp", "row"), "col", None),
        check_vma=False,
    )
```

```python
import functools

import jax
import jax.numpy as jnp
from jax import lax
from jax.experimental import pallas as pl
from jax.experimental.pallas import tpu as pltpu
from jax.sharding import PartitionSpec as P

eps = 1e-05
f32 = jnp.float32
bf16 = jnp.bfloat16
VMEM = pl.BlockSpec(memory_space=pltpu.VMEM)
SMEM = pl.BlockSpec(memory_space=pltpu.SMEM)
HBM = pl.BlockSpec(memory_space=pltpu.HBM)


def limit(mib, scale=1):
    return pltpu.CompilerParams(vmem_limit_bytes=min(56, mib * scale) * 1024 * 1024)


def round_up(n, m):
    return (n + m - 1) // m * m


def cost(us):
    return pl.CostEstimate(flops=0, bytes_accessed=int(us * 3.69e6), transcendentals=0)


def hold(x):
    return pltpu.with_memory_space_constraint(x, pltpu.HBM)


def fetch(pairs, sem):
    copies = [pltpu.make_async_copy(src, dst, sem.at[n]) for n, (src, dst) in enumerate(pairs)]
    for copy in copies:
        copy.start()
    return copies


def standardize(values):
    centre = values - jnp.mean(values, axis=-1, keepdims=True)
    spread = jnp.mean(centre * centre, axis=-1, keepdims=True)
    return centre * lax.rsqrt(spread + eps)


def sigmoid(v):
    return 0.5 * jnp.tanh(0.5 * v) + 0.5


def align_body(own_i, own_j, count, x_hbm, w_hbm, *refs):
    later, outs, refs = refs[:4], refs[4 : 4 + count], refs[4 + count :]
    brought, (x_ref, w_ref, y_ref, sem) = refs[:4], refs[4:]
    copies = fetch([(x_hbm, x_ref), (w_hbm, w_ref), *zip(later, brought)], sem)
    seqs, residues, depth = x_ref.shape
    width = w_ref.shape[0] // 2
    height, lanes = outs[0].shape
    me = lax.axis_index("row")
    z = lax.axis_index("col")
    copies[0].wait()
    x = x_ref[...].astype(f32).reshape(seqs * residues, depth)
    normed = standardize(x).astype(bf16)
    copies[1].wait()
    y_ref[...] = lax.dot_general(
        normed, w_ref[...], (((1,), (1,)), ((), ())), preferred_element_type=f32
    )
    start = pl.multiple_of(z * own_j, 8)

    def tall(v):
        gap = height - v.shape[0]
        return jnp.concatenate([v, jnp.zeros((gap, v.shape[1]), f32)], axis=0) if gap else v

    right = [tall(y_ref[pl.ds(s * residues + start, own_j), width:]) for s in range(seqs)]
    gap = lanes - 2 * seqs * width
    right += [jnp.zeros((height, gap), f32)] if gap else []
    for d, out in enumerate(outs):
        first = pl.multiple_of((me ^ d) * own_i, 8)
        left = [tall(y_ref[pl.ds(s * residues + first, own_i), :width]) for s in range(seqs)]
        out[...] = jnp.concatenate(left + right, axis=1).astype(bf16)
    for copy in copies[2:]:
        copy.wait()


def prepare_body(seqs, couple_ref, ids_hbm, valid_ref, bias_ref, avg_ref, base_ref, mask_ref, wq_ref, pick_ref,
                 wf_ref, idc_ref, ids_ref, sem):
    (copy,) = fetch([(ids_hbm, ids_ref)], sem)
    own_i, own_j, chans = couple_ref.shape
    pairs, width, _ = wq_ref.shape
    blocks, lanes, _ = pick_ref.shape
    total = blocks * seqs
    x0 = lax.axis_index("row") * own_i
    z0 = lax.axis_index("col") * own_j

    row = lax.broadcasted_iota(jnp.int32, pick_ref.shape[1:], 0)
    col = lax.broadcasted_iota(jnp.int32, pick_ref.shape[1:], 1)
    unit = row - seqs * width
    place = lax.rem(unit, width) * total + lax.div(unit, width)
    place = jnp.where((unit >= 0) & (unit < seqs * width), col - place, -1)

    def pick(r, carry):
        pick_ref[r] = jnp.where(place == r * seqs, 1.0, 0.0).astype(bf16)
        return carry

    lax.fori_loop(0, blocks, pick, 0)
    wf_ref[...] = avg_ref[...].astype(f32)
    for h in range(pairs):
        both = [wf_ref[pl.ds(2 * h + d, width, stride=width), :] for d in range(2)]
        wq_ref[h] = jnp.concatenate(both, axis=1).astype(bf16)
    copy.wait()
    for j in range(own_j):
        idc_ref[pl.ds(j, 1), :] = jnp.full((1, chans), ids_ref[z0 + j], jnp.int32)
    idc = idc_ref[...]
    valid_t = valid_ref[...].astype(f32).T
    lane = lax.broadcasted_iota(jnp.int32, valid_t.shape, 1)
    same_bias = bias_ref[0:1, :]
    cross_bias = bias_ref[1:2, :]

    def rows(i, carry):
        bias = jnp.where(idc == ids_ref[x0 + i], same_bias, cross_bias)
        base_ref[i] = couple_ref[i].astype(f32) + bias
        column = jnp.sum(jnp.where(lane == i, valid_t, 0.0), axis=1, keepdims=True)
        mask_ref[i] = jnp.broadcast_to(column, (own_j, mask_ref.shape[2])).astype(bf16)
        return carry

    lax.fori_loop(0, own_i, rows, 0, unroll=8)


def pair_body(seqs, width, blocks, *refs):
    msgs = refs[:blocks]
    base_ref, mask_ref, wq_ref, pick_ref, win_ref = refs[blocks : blocks + 5]
    psum_ref, norm_ref, right_ref = refs[blocks + 5 : blocks + 8]
    xl_ref, t_ref = refs[blocks + 8 :]
    own_i, own_j, chans = base_ref.shape
    height, lanes = msgs[0].shape
    total = seqs * blocks
    tri = win_ref.shape[1] // 4
    half = own_i // 2

    for r in range(blocks):
        m = msgs[r][pl.ds(0, own_i), :].astype(f32)
        for s in range(seqs):
            moved = m if s == 0 else pltpu.roll(m, lanes - s * width, 1)
            xl_ref[pl.ds(r * seqs + s, own_i, stride=total), :] = moved[:, :128]
    lhs = xl_ref[:, :width].astype(bf16)

    joined = jnp.concatenate([msg[...] for msg in msgs], axis=1)
    picks = pick_ref[...].reshape(blocks * lanes, width * total)
    rmat = jnp.dot(joined, picks, preferred_element_type=f32)[:own_j].astype(bf16)

    def expand(h, carry):
        out = jnp.dot(lhs, wq_ref[h], preferred_element_type=f32)
        parts = [out[:, d * chans : (d + 1) * chans].reshape(own_i, total, chans) for d in range(2)]
        block = jnp.concatenate(parts, axis=1).astype(bf16)
        where = pl.ds(pl.multiple_of(h * 2 * total, 16), 2 * total)
        t_ref[:, where, :chans] = block[:half]
        t_ref[:, where, chans:] = block[half:]
        return carry

    lax.fori_loop(0, width // 2, expand, 0)

    step = 4 if half % 4 == 0 else 1

    def rows(b, carry):
        normed = [[], []]
        for g in range(step):
            i = b * step + g
            both = jnp.dot(rmat, t_ref[i], preferred_element_type=f32) * (1.0 / total)
            for side in range(2):
                at = i + side * half
                psum = (base_ref[at] + both[:, side * chans : (side + 1) * chans]).astype(bf16)
                psum_ref[at] = psum
                normed[side].append(standardize(psum.astype(f32)))
        flat = jnp.concatenate(normed[0] + normed[1], axis=0).astype(bf16)
        proj = jnp.dot(flat, win_ref[:, 2 * tri :], preferred_element_type=f32)
        count = step * own_j
        for side in range(2):
            cut = slice(side * count, (side + 1) * count)
            i0 = b * step + side * half
            norm_ref[pl.ds(pl.multiple_of(i0 * own_j, 16), count), :] = flat[cut]
            mask = mask_ref[pl.ds(i0, step)].astype(f32).reshape(count, tri)
            right = mask * sigmoid(proj[cut, :tri]) * proj[cut, tri:]
            right_ref[pl.ds(i0, step)] = right.reshape(step, own_j, tri).astype(bf16)
        return carry

    lax.fori_loop(0, half // step, rows, 0)


def left_body(norm_ref, mask_ref, win_ref, *outs):
    own_i, own_j, tri = mask_ref.shape
    group = 8 if own_i % 8 == 0 else 1
    at = 0
    for out in outs:
        first = at

        def rows(b, carry):
            i0 = first + b * group
            flat = norm_ref[pl.ds(pl.multiple_of(i0 * own_j, 16), group * own_j), :]
            mask = mask_ref[pl.ds(i0, group)].astype(f32).reshape(group * own_j, tri)
            proj = jnp.dot(flat, win_ref[:, : 2 * tri], preferred_element_type=f32)
            left = mask * sigmoid(proj[:, :tri]) * proj[:, tri:]
            out[pl.ds(b * group, group)] = left.reshape(group, own_j, tri).astype(bf16)
            return carry

        lax.fori_loop(0, out.shape[0] // group, rows, 0, unroll=True)
        at += out.shape[0]


def contract(lf_ref, halves, i0, group):
    step = 8
    acc = (jnp.zeros(halves[0].shape[1:], f32),) * group
    for h, r_ref in enumerate(halves):
        depth = r_ref.shape[0]

        def add(kb, acc):
            k0 = kb * step
            acc = list(acc)
            for d in range(step):
                right = r_ref[k0 + d].astype(f32)
                for t in range(group):
                    acc[t] = acc[t] + lf_ref[i0 + t, pl.ds(h * depth + k0 + d, 1), :] * right
            return tuple(acc)

        acc = lax.fori_loop(0, depth // step, add, acc)
    return acc


def sums_body(own_pair, first, own_ref, other_ref, p_other, met_ref, p_met, far_ref, p_far, l_ref, m_ref, o_ref, lf_ref):
    count, depth = o_ref.shape[0], l_ref.shape[1]
    group = 8
    lf_ref[:, pl.ds(0, depth), :] = l_ref[pl.ds(first, count)].astype(f32)
    lf_ref[:, pl.ds(depth, depth), :] = m_ref[pl.ds(first, count)].astype(f32)

    def use(halves):
        def rows(b, carry):
            acc = contract(lf_ref, halves, b * group, group)
            for t in range(group):
                o_ref[b * group + t] = acc[t].astype(o_ref.dtype)
            return carry

        lax.fori_loop(0, count // group, rows, 0)

    r, z = lax.axis_index("row"), lax.axis_index("col")
    keeper = (r % 2) == (z % 2)
    near = ((r // 2) == (z // 2)) == own_pair
    table = [
        (near & keeper, own_ref, met_ref),
        (near & ~keeper, far_ref, p_met),
        (~near & keeper, p_other, far_ref),
        (~near & ~keeper, other_ref, p_far),
    ]
    for cond, a, b in table:
        pl.when(cond)(functools.partial(use, (a, b)))


def open_body(x_hbm, w_hbm, valid_hbm, couple_hbm, *refs):
    later, outs, brought = refs[:5], refs[5:9], refs[9:14]
    block_ref, longer_ref, x_ref, w_ref, valid_ref, y_ref, sem = refs[14:]
    own_i, own_j, chans = couple_hbm.shape
    copies = fetch([(x_hbm, x_ref), (w_hbm, w_ref), (valid_hbm, valid_ref),
                    (couple_hbm, block_ref.at[pl.ds(0, own_i)]),
                    (couple_hbm, longer_ref.at[pl.ds(0, own_i)]), *zip(later, brought)], sem)
    seqs, residues, depth = x_ref.shape
    width = w_ref.shape[0] // 2
    height, lanes = outs[0].shape
    me = lax.axis_index("row")
    z = lax.axis_index("col")
    copies[0].wait()
    x = x_ref[...].astype(f32).reshape(seqs * residues, depth)
    normed = standardize(x).astype(bf16)
    copies[1].wait()
    y_ref[...] = lax.dot_general(
        normed, w_ref[...], (((1,), (1,)), ((), ())), preferred_element_type=f32
    )

    def cut(start, lane):
        start = pl.multiple_of(start * own_i, 8)
        return [y_ref[pl.ds(s * residues + start, own_i), lane : lane + width] for s in range(seqs)]

    shared = cut(z, width) + cut(z ^ 1, width)
    below = jnp.zeros((height - own_i, lanes), f32)
    for d, out in enumerate(outs):
        other = ((me ^ d) // 2 ^ 1) * 2 + z % 2
        rows = jnp.concatenate(cut(me ^ d, 0) + cut(other, 0) + shared, axis=1)
        out[...] = jnp.concatenate([rows, below], axis=0).astype(bf16)
    copies[2].wait()
    mask = valid_ref[...].astype(f32).T
    mask = jnp.concatenate([mask, jnp.zeros((own_j, chans - own_i), f32)], axis=1)
    block_ref[own_i] = mask.astype(bf16)
    for n in range(own_i, longer_ref.shape[0]):
        longer_ref[n] = mask.astype(bf16)
    for copy in copies[3:]:
        copy.wait()


def ready_body(seqs, avg_ref, ids_hbm, wq_ref, pick_ref, idt_ref, wf_ref, ids_ref, sem):
    (copy,) = fetch([(ids_hbm, ids_ref)], sem)
    pairs, width, _ = wq_ref.shape
    kinds, blocks, lanes, _ = pick_ref.shape
    total = blocks * seqs
    row = lax.broadcasted_iota(jnp.int32, pick_ref.shape[2:], 0)
    col = lax.broadcasted_iota(jnp.int32, pick_ref.shape[2:], 1)
    for n in range(kinds):
        unit = row - n * seqs * width
        place = lax.rem(unit, width) * total + lax.div(unit, width)
        place = jnp.where((unit >= 0) & (unit < seqs * width), col - place, -1)
        for r in range(blocks):
            pick_ref[n, r] = jnp.where(place == r * seqs, 1.0, 0.0).astype(bf16)
    wf_ref[...] = avg_ref[...].astype(f32)
    for h in range(pairs):
        both = [wf_ref[pl.ds(2 * h + d, width, stride=width), :] for d in range(2)]
        wq_ref[h] = jnp.concatenate(both, axis=1).astype(bf16)
    copy.wait()

    def spread(n, carry):
        idt_ref[pl.ds(n, 1), :] = jnp.full((1, idt_ref.shape[1]), ids_ref[n], jnp.int32)
        return carry

    lax.fori_loop(0, idt_ref.shape[0], spread, 0, unroll=8)


def mix_rows(seqs, width, lane0, msgs, wq_ref, t_ref, xl_ref):
    half, terms, both = t_ref.shape
    chans, own_i, total = both // 2, 2 * half, seqs * 4
    for r in range(4):
        m = msgs[r][pl.ds(0, own_i), :128].astype(f32)
        for s in range(seqs):
            lane = lane0 + s * width
            moved = pltpu.roll(m, 128 - lane, 1) if lane else m
            xl_ref[pl.ds(r * seqs + s, own_i, stride=total), :] = moved
    lhs = xl_ref[:, :width].astype(bf16)
    for h in range(width // 2):
        out = jnp.dot(lhs, wq_ref[h], preferred_element_type=f32)
        parts = [out[:, d * chans : (d + 1) * chans].reshape(own_i, total, chans) for d in range(2)]
        block = jnp.concatenate(parts, axis=1).astype(bf16)
        where = pl.ds(h * 2 * total, 2 * total)
        t_ref[:, where, :chans] = block[:half]
        t_ref[:, where, chans:] = block[half:]


def mix_body(seqs, width, *refs):
    msgs, (wq_ref, pick_ref, t_ref, right_ref, xl_ref) = refs[:4], refs[4:]
    own_j, terms = right_ref.shape[1:]
    joined = jnp.concatenate([msg[:, 128:] for msg in msgs], axis=1)
    for n in range(2):
        right = jnp.dot(joined, pick_ref[n].reshape(512, terms), preferred_element_type=f32)[:own_j]
        right_ref[n] = (right * (1.0 / (seqs * 4))).astype(bf16)
    mix_rows(seqs, width, 0, msgs, wq_ref, t_ref, xl_ref)


def block_norms(block_ref, t_ref, right, row0, col0, idt_ref, bias_ref, use):
    half, terms, _ = t_ref.shape
    own_i, own_j, chans = 2 * half, right.shape[0], bias_ref.shape[1]
    idc = idt_ref[pl.ds(pl.multiple_of(col0, 8), own_j), :]
    step = 4
    for b in range(half // step):
        rows, psums = [[], []], [[], []]
        for i in range(b * step, b * step + step):
            both = jnp.dot(right, t_ref[i], preferred_element_type=f32)
            for side in range(2):
                at = i + side * half
                same = idc == idt_ref[pl.ds(row0 + at, 1), :]
                base = block_ref[at].astype(f32) + jnp.where(same, bias_ref[0:1, :], bias_ref[1:2, :])
                rows[side].append(at)
                psums[side].append((base + both[:, side * chans : (side + 1) * chans]).astype(bf16))
        rows, psums = rows[0] + rows[1], psums[0] + psums[1]
        flat = jnp.concatenate([standardize(p.astype(f32)) for p in psums], axis=0).astype(bf16)
        use(rows, psums, flat)


def gated(block_ref, rows, flat, w_ref):
    own_j = block_ref.shape[1]
    tri = w_ref.shape[1] // 2
    mask = block_ref[block_ref.shape[0] - 1].astype(f32)
    proj = jnp.dot(flat, w_ref[...], preferred_element_type=f32)
    both = sigmoid(proj[:, :tri]) * proj[:, tri:]
    return [mask[:, at : at + 1] * both[n * own_j : (n + 1) * own_j] for n, at in enumerate(rows)]


def own_body(block_ref, t_ref, right_ref, idt_ref, bias_ref, win_ref, psum_ref, norm_ref, out_ref, flat_ref):
    own_i, own_j, chans = psum_ref.shape
    r, z = lax.axis_index("row"), lax.axis_index("col")
    side = win_ref.shape[1] // 2
    w_right = win_ref.at[:, pl.ds(side, side)]

    def use(rows, psums, flat):
        rights = gated(block_ref, rows, flat, w_right)
        for n, at in enumerate(rows):
            psum_ref[at] = psums[n]
            norm_ref[pl.ds(at * own_j, own_j), :] = flat[n * own_j : (n + 1) * own_j]
            flat_ref[pl.ds(at * own_j, own_j), :] = rights[n]

    block_norms(block_ref, t_ref, right_ref[0], r * own_i, z * own_j, idt_ref, bias_ref, use)
    for k in range(own_j):
        out_ref[k] = flat_ref[pl.ds(k, own_i, stride=own_j), :].astype(bf16)


def rest_body(block_ref, norm_ref, win_ref, wgate_ref, left_ref, gate_ref):
    own_i, own_j, _ = left_ref.shape
    w_left = win_ref.at[:, pl.ds(0, win_ref.shape[1] // 2)]
    group = 8
    for i in range(0, own_i, group):
        flat = norm_ref[pl.ds(i * own_j, group * own_j), :]
        rows = list(range(i, i + group))
        gate = sigmoid(jnp.dot(flat, wgate_ref[...], preferred_element_type=f32))
        for n, left in enumerate(gated(block_ref, rows, flat, w_left)):
            left_ref[i + n] = left.astype(bf16)
            gate_ref[i + n] = gate[n * own_j : (n + 1) * own_j]


def mix_other_body(seqs, width, *refs):
    msgs, (wq_ref, t_ref, xl_ref) = refs[:4], refs[4:]

    @pl.when((lax.axis_index("row") % 2) != (lax.axis_index("col") % 2))
    def _():
        mix_rows(seqs, width, seqs * width, msgs, wq_ref, t_ref, xl_ref)


def other_body(block_ref, t_ref, right_ref, idt_ref, bias_ref, win_ref, out_ref, flat_ref):
    own_j, own_i, _ = out_ref.shape
    r, z = lax.axis_index("row"), lax.axis_index("col")
    side = win_ref.shape[1] // 2
    w_right = win_ref.at[:, pl.ds(side, side)]

    def use(rows, psums, flat):
        for at, right in zip(rows, gated(block_ref, rows, flat, w_right)):
            flat_ref[pl.ds(at * own_j, own_j), :] = right

    @pl.when((r % 2) != (z % 2))
    def _():
        block_norms(block_ref, t_ref, right_ref[0], (r ^ 3) * own_i, z * own_j, idt_ref, bias_ref, use)
        for k in range(own_j):
            out_ref[k] = flat_ref[pl.ds(k, own_i, stride=own_j), :].astype(bf16)


def met_body(block_ref, t_ref, right_ref, idt_ref, bias_ref, win_ref, left_ref, out_ref, flat_ref, norm_ref):
    own_i, own_j, _ = left_ref.shape
    r, z = lax.axis_index("row"), lax.axis_index("col")
    side = win_ref.shape[1] // 2
    w_left, w_right = win_ref.at[:, pl.ds(0, side)], win_ref.at[:, pl.ds(side, side)]

    def use(rows, psums, flat):
        lefts = gated(block_ref, rows, flat, w_left)
        for n, at in enumerate(rows):
            left_ref[at] = lefts[n].astype(bf16)
            norm_ref[pl.ds(at * own_j, own_j), :] = flat[n * own_j : (n + 1) * own_j]

    block_norms(block_ref, t_ref, right_ref[1], r * own_i, (z ^ 1) * own_j, idt_ref, bias_ref, use)

    @pl.when((r % 2) == (z % 2))
    def _():
        for i in range(0, own_i, 8):
            flat = norm_ref[pl.ds(i * own_j, 8 * own_j), :]
            for n, right in enumerate(gated(block_ref, list(range(i, i + 8)), flat, w_right)):
                flat_ref[pl.ds((i + n) * own_j, own_j), :] = right
        for k in range(own_j):
            out_ref[k] = flat_ref[pl.ds(k, own_i, stride=own_j), :].astype(bf16)


def join_body(first, parts, own_ref, psum_ref, gate_ref, w_ref, *refs):
    sums, (out_hbm, done_ref, sem) = refs[:parts], refs[-3:]
    count, extent, chans = done_ref.shape
    group = 8
    at = 0
    for sum_ref in sums:
        start = at

        def rows(b, carry):
            here = pl.ds(start + b * group, group)
            there = pl.ds(first + start + b * group, group)
            mixed = own_ref[there] + sum_ref[pl.ds(b * group, group)].astype(f32)
            normed = standardize(mixed).reshape(group * extent, -1).astype(bf16)
            update = jnp.dot(normed, w_ref[...], preferred_element_type=f32).reshape(group, extent, -1)
            done_ref[here] = (psum_ref[there].astype(f32) + gate_ref[there] * update).astype(bf16)
            return carry

        lax.fori_loop(0, sum_ref.shape[0] // group, rows, 0, unroll=True)
        at += sum_ref.shape[0]
    copy = pltpu.make_async_copy(done_ref, out_hbm.at[pl.ds(first, count)], sem)
    copy.start()
    copy.wait()


def triangle_body(l_ref, r_ref, o_ref, lf_ref, flat_ref, rk_ref):
    own_i, depth, chans = l_ref.shape
    extent = r_ref.shape[0]
    group = 8 if own_i % 8 == 0 else 1

    @pl.when(pl.program_id(0) == 0)
    def _():
        lf_ref[...] = l_ref[...].astype(f32)

    def widen(j, carry):
        flat_ref[pl.ds(pl.multiple_of(j * depth, 8), depth), :] = r_ref[j].astype(f32)
        return carry

    lax.fori_loop(0, extent, widen, 0)

    def turn(k, carry):
        rk_ref[k] = flat_ref[pl.ds(k, extent, stride=depth), :]
        return carry

    lax.fori_loop(0, depth, turn, 0)

    def rows(b, carry):
        i0 = b * group
        acc = contract(lf_ref, [rk_ref], i0, group)
        for t in range(group):
            o_ref[0, i0 + t] = acc[t].astype(bf16)
        return carry

    lax.fori_loop(0, own_i // group, rows, 0)


def finish_body(sum_ref, psum_ref, norm_ref, wgate_ref, w_ref, out_ref):
    parts, own_i, extent, chans = sum_ref.shape
    own_j = psum_ref.shape[1]

    def row(i, carry):
        flat = norm_ref[pl.ds(pl.multiple_of(i * own_j, 16), own_j), :]
        gate = sigmoid(jnp.dot(flat, wgate_ref[...], preferred_element_type=f32))
        normed = [standardize(sum_ref[part, i].astype(f32)) for part in range(parts)]
        normed = jnp.concatenate(normed, axis=0).astype(bf16)
        update = jnp.dot(normed, w_ref[...], preferred_element_type=f32)
        out_ref[i] = (psum_ref[i].astype(f32) + gate * update).astype(bf16)
        return carry

    lax.fori_loop(0, own_i, row, 0)


def gathered_plan(left, right, psum, norm, w_gate, w_final):
    own_i, own_j, chans = psum.shape
    rows = lax.axis_size("row")
    tri = w_final.shape[0]
    right_all = lax.all_gather(right, "row", axis=0, tiled=True)
    partial = pl.pallas_call(
        triangle_body,
        grid=(rows,),
        out_shape=jax.ShapeDtypeStruct((rows, own_i, own_i, tri), bf16),
        in_specs=[
            pl.BlockSpec((own_i, own_j, tri), lambda r: (0, 0, 0)),
            pl.BlockSpec((own_i, own_j, tri), lambda r: (r, 0, 0)),
        ],
        out_specs=pl.BlockSpec((1, own_i, own_i, tri), lambda r: (r, 0, 0, 0)),
        scratch_shapes=[
            pltpu.VMEM((own_i, own_j, tri), f32),
            pltpu.VMEM((own_i * own_j, tri), f32),
            pltpu.VMEM((own_j, own_i, tri), f32),
        ],
        compiler_params=limit(56),
        name="triangle",
    )(left, right_all)
    summed = lax.psum_scatter(partial, "col", scatter_dimension=0, tiled=True)
    return pl.pallas_call(
        finish_body,
        out_shape=jax.ShapeDtypeStruct((own_i, own_j, chans), bf16),
        in_specs=[VMEM] * 5,
        out_specs=VMEM,
        compiler_params=limit(56),
        name="finish",
    )(summed, psum, norm, w_gate, w_final)


def paired_plan(homolog, couple, ids, valid, bias, factors, average, w_in, w_gate, w_final):
    seqs, residues, depth = homolog.shape
    own_i, own_j, chans = couple.shape
    width = factors.shape[1] // 2
    tri = w_final.shape[0]
    total = seqs * 4
    cells = [(r, z) for r in range(4) for z in range(4)]
    struct = jax.ShapeDtypeStruct

    def move(value, step):
        pairs = [(r * 4 + z, step(r, z)) for r, z in cells]
        pairs = [(src, r * 4 + z) for src, (r, z) in pairs]
        return lax.ppermute(value, ("row", "col"), pairs)

    def call(body, us, out_shape, scratch, *args, mib=12):
        return pl.pallas_call(
            body,
            out_shape=out_shape,
            in_specs=[VMEM] * len(args),
            out_specs=[VMEM] * len(out_shape) if isinstance(out_shape, list) else VMEM,
            scratch_shapes=scratch,
            compiler_params=limit(mib),
            cost_estimate=cost(us),
            name=getattr(body, "func", body).__name__.removesuffix("_body"),
        )(*args)

    keeper = lambda r, z: r % 2 == z % 2
    beside = lambda r, z: (r ^ 1, z)
    height, lanes = round_up(own_i, 16), 256
    block = struct((own_i + 1, own_j, chans), bf16)
    longer = struct((own_i + 3, own_j, chans), bf16)
    later = (average, bias, w_in, w_gate, w_final)
    *msgs, average, bias, w_in, w_gate, w_final, raw, raw_z = pl.pallas_call(
        open_body,
        out_shape=[struct((height, lanes), bf16)] * 4 + [struct(x.shape, x.dtype) for x in later] + [block, longer],
        in_specs=[HBM] * 9,
        out_specs=[VMEM] * 11,
        scratch_shapes=[
            pltpu.VMEM(homolog.shape, bf16),
            pltpu.VMEM((2 * width, depth), bf16),
            pltpu.VMEM(valid.shape, jnp.int32),
            pltpu.VMEM((seqs * residues, 2 * width), f32),
            pltpu.SemaphoreType.DMA((10,)),
        ],
        compiler_params=limit(8),
        cost_estimate=cost(1.5),
        name="open",
    )(*map(hold, (homolog, factors.T, valid, couple) + later))
    msgs = [msgs[0]] + [
        lax.ppermute(msgs[d], "row", [(r, r ^ d) for r in range(4)]) for d in (1, 2, 3)
    ]
    met = move(raw_z, lambda r, z: (r, z ^ 1))
    wq, pick, idt = pl.pallas_call(
        functools.partial(ready_body, seqs),
        out_shape=[struct((width // 2, width, 2 * chans), bf16),
                   struct((2, 4, 128, width * total), bf16),
                   struct((residues, 128), jnp.int32)],
        in_specs=[VMEM, HBM],
        out_specs=[VMEM] * 3,
        scratch_shapes=[
            pltpu.VMEM(average.shape, f32),
            pltpu.SMEM(ids.shape, jnp.int32),
            pltpu.SemaphoreType.DMA((1,)),
        ],
        compiler_params=limit(8),
        cost_estimate=cost(1.5),
        name="ready",
    )(average, hold(ids))

    raw, msgs, idt = lax.optimization_barrier((raw, msgs, idt))
    raw_other = move(raw, lambda r, z: (r ^ 3, z) if keeper(r, z) else (r ^ 1, z))
    t, mixed = call(
        functools.partial(mix_body, seqs, width), 1,
        [struct((own_i // 2, width * total, 2 * chans), bf16), struct((2, own_j, width * total), bf16)],
        [pltpu.VMEM((own_i * total, 128), f32)], *msgs, wq, pick,
    )
    square = struct((own_i, own_j, tri), bf16)
    flat = [pltpu.VMEM((own_i * own_j, tri), f32)]
    psum, norm, right = call(
        own_body, 2.4, [square, struct((own_i * own_j, chans), bf16), square], flat,
        raw, t, mixed, idt, bias, w_in,
    )
    far = move(right, lambda r, z: (r ^ 1, z) if keeper(r, z) else (r ^ 2, z ^ 1))
    left, gate = call(rest_body, 0.6, [square, struct(couple.shape, f32)], [], raw, norm, w_in, w_gate)
    msgs, right = lax.optimization_barrier((msgs, right))
    t_other = call(
        functools.partial(mix_other_body, seqs, width), 1, struct(t.shape, bf16),
        [pltpu.VMEM((own_i * total, 128), f32)], *msgs, wq,
    )
    met, *_ = lax.optimization_barrier((met, t_other))
    met_left, met_right = call(
        met_body, 3, [square, square], flat + [pltpu.VMEM(norm.shape, bf16)], met, t, mixed, idt, bias, w_in
    )
    p_met = move(met_right, beside)
    raw_other, *_ = lax.optimization_barrier((raw_other, met_left))
    other = call(other_body, 2.4, square, flat, raw_other, t_other, mixed, idt, bias, w_in)
    p_other = move(other, beside)
    far, other, p_met = lax.optimization_barrier((far, other, p_met))
    p_far = move(far, beside)

    def sums(own_pair, first, n, dtype):
        return call(
            functools.partial(sums_body, own_pair, first), 0.13 * n, struct((n, own_j, tri), dtype),
            [pltpu.VMEM((n, 2 * own_j, tri), f32)],
            right, other, p_other, met_right, p_met, far, p_far, left, met_left,
        )

    came = [move(sums(False, first, 8, bf16), lambda r, z: (r, z ^ 2)) for first in range(0, own_i, 8)]
    kept = sums(True, 0, own_i, f32)

    out = []
    for first, n in ((0, 16), (16, 16), (32, own_i - 32)):
        parts = came[first // 8 : (first + n) // 8]
        out = [pl.pallas_call(
            functools.partial(join_body, first, len(parts)),
            out_shape=struct(couple.shape, bf16),
            in_specs=[VMEM] * (4 + len(parts)) + [HBM] * len(out),
            out_specs=HBM,
            scratch_shapes=[pltpu.VMEM((n, own_j, chans), bf16), pltpu.SemaphoreType.DMA],
            input_output_aliases={4 + len(parts): 0} if out else {},
            compiler_params=limit(8),
            cost_estimate=cost(0.06 * n),
            name="join",
        )(kept, psum, gate, w_final, *parts, *out)]
    return out[0]


def shards(homolog, couple, ids, valid, bias, factors, average, w_in, w_gate, w_final):
    rows, cols = lax.axis_size("row"), lax.axis_size("col")
    own_seqs, residues, depth = homolog.shape
    own_i, own_j, chans = couple.shape
    width = factors.shape[1] // 2
    tri = w_final.shape[0]
    total = own_seqs * rows
    lanes = round_up(2 * own_seqs * width, 128)
    height = round_up(max(own_i, own_j), 16)
    paired = (rows, cols, own_seqs * width, chans, tri) == (4, 4, 64, 128, 128)
    if paired and own_i == own_j == 40:
        return paired_plan(homolog, couple, ids, valid, bias, factors, average, w_in, w_gate, w_final)
    scale = 8

    later = (average, valid, bias, couple)
    *msgs, average, valid, bias, couple = pl.pallas_call(
        functools.partial(align_body, own_i, own_j, rows),
        out_shape=[jax.ShapeDtypeStruct((height, lanes), bf16)] * rows
        + [jax.ShapeDtypeStruct(x.shape, x.dtype) for x in later],
        in_specs=[HBM] * 6,
        out_specs=[VMEM] * (rows + 4),
        scratch_shapes=[
            pltpu.VMEM(homolog.shape, bf16),
            pltpu.VMEM((2 * width, depth), bf16),
            pltpu.VMEM((own_seqs * residues, 2 * width), f32),
            pltpu.SemaphoreType.DMA((6,)),
        ],
        compiler_params=limit(8, scale),
        cost_estimate=cost(1.5),
        name="align",
    )(hold(homolog), hold(factors.T), *map(hold, later))
    msgs = [msgs[0]] + [
        lax.ppermute(msgs[d], "row", [(r, r ^ d) for r in range(rows)])
        for d in reversed(range(1, rows))
    ]

    base, mask, wq, pick = pl.pallas_call(
        functools.partial(prepare_body, own_seqs),
        out_shape=[jax.ShapeDtypeStruct((own_i, own_j, chans), f32),
                   jax.ShapeDtypeStruct((own_i, own_j, tri), bf16),
                   jax.ShapeDtypeStruct((width // 2, width, 2 * chans), bf16),
                   jax.ShapeDtypeStruct((rows, lanes, width * total), bf16)],
        in_specs=[VMEM, HBM, VMEM, VMEM, VMEM],
        out_specs=[VMEM] * 4,
        scratch_shapes=[
            pltpu.VMEM(average.shape, f32),
            pltpu.VMEM((own_j, chans), jnp.int32),
            pltpu.SMEM(ids.shape, jnp.int32),
            pltpu.SemaphoreType.DMA((1,)),
        ],
        compiler_params=limit(8, scale),
        cost_estimate=cost(2),
        name="prepare",
    )(couple, hold(ids), valid, bias, average)

    extents = (own_i, own_j)
    psum, norm, right = pl.pallas_call(
        functools.partial(pair_body, own_seqs, width, rows),
        out_shape=[jax.ShapeDtypeStruct((own_i, own_j, chans), bf16),
                   jax.ShapeDtypeStruct((own_i * own_j, chans), bf16),
                   jax.ShapeDtypeStruct(extents + (tri,), bf16)],
        in_specs=[VMEM] * (rows + 5),
        out_specs=[VMEM] * 3,
        scratch_shapes=[
            pltpu.VMEM((own_i * total, 128), f32),
            pltpu.VMEM((own_i // 2, width * total, 2 * chans), bf16),
        ],
        compiler_params=limit(16, scale),
        cost_estimate=cost(4.5),
        name="pair",
    )(*msgs, base, mask, wq, pick, w_in)

    cuts = [own_i]
    lefts = pl.pallas_call(
        left_body,
        out_shape=[jax.ShapeDtypeStruct((n, own_j, tri), bf16) for n in cuts],
        in_specs=[VMEM] * 3,
        out_specs=[VMEM] * len(cuts),
        compiler_params=limit(8, scale),
        cost_estimate=cost(1),
        name="left",
    )(norm, mask, w_in)
    return gathered_plan(lefts[0], right, psum, norm, w_gate, w_final)


def solution(mesh):
    placed = (
        P(("grp", "row"), None, None),
        P(("grp", "row"), "col", None),
        P("grp"),
        P(("grp", "row"), "col"),
        P(),
        P(),
        P(),
        P(),
        P(),
        P(),
    )
    return jax.shard_map(
        shards,
        mesh=mesh,
        in_specs=placed,
        out_specs=P(("grp", "row"), "col", None),
        check_vma=False,
    )
```

```python
import functools

import jax
import jax.numpy as jnp
from jax import lax
from jax.experimental import pallas as pl
from jax.experimental.pallas import tpu as pltpu
from jax.sharding import PartitionSpec as P

eps = 1e-05
f32 = jnp.float32
bf16 = jnp.bfloat16
VMEM = pl.BlockSpec(memory_space=pltpu.VMEM)
SMEM = pl.BlockSpec(memory_space=pltpu.SMEM)
HBM = pl.BlockSpec(memory_space=pltpu.HBM)


def limit(mib, scale=1):
    return pltpu.CompilerParams(vmem_limit_bytes=min(56, mib * scale) * 1024 * 1024)


def round_up(n, m):
    return (n + m - 1) // m * m


def cost(us):
    return pl.CostEstimate(flops=0, bytes_accessed=int(us * 3.69e6), transcendentals=0)


def hold(x):
    return pltpu.with_memory_space_constraint(x, pltpu.HBM)


def fetch(pairs, sem):
    copies = [pltpu.make_async_copy(src, dst, sem.at[n]) for n, (src, dst) in enumerate(pairs)]
    for copy in copies:
        copy.start()
    return copies


def standardize(values):
    centre = values - jnp.mean(values, axis=-1, keepdims=True)
    spread = jnp.mean(centre * centre, axis=-1, keepdims=True)
    return centre * lax.rsqrt(spread + eps)


def sigmoid(v):
    return 0.5 * jnp.tanh(0.5 * v) + 0.5


def align_body(own_i, own_j, count, x_hbm, w_hbm, *refs):
    later, outs, refs = refs[:4], refs[4 : 4 + count], refs[4 + count :]
    brought, (x_ref, w_ref, y_ref, sem) = refs[:4], refs[4:]
    copies = fetch([(x_hbm, x_ref), (w_hbm, w_ref), *zip(later, brought)], sem)
    seqs, residues, depth = x_ref.shape
    width = w_ref.shape[0] // 2
    height, lanes = outs[0].shape
    me = lax.axis_index("row")
    z = lax.axis_index("col")
    copies[0].wait()
    x = x_ref[...].astype(f32).reshape(seqs * residues, depth)
    normed = standardize(x).astype(bf16)
    copies[1].wait()
    y_ref[...] = lax.dot_general(
        normed, w_ref[...], (((1,), (1,)), ((), ())), preferred_element_type=f32
    )
    start = pl.multiple_of(z * own_j, 8)

    def tall(v):
        gap = height - v.shape[0]
        return jnp.concatenate([v, jnp.zeros((gap, v.shape[1]), f32)], axis=0) if gap else v

    right = [tall(y_ref[pl.ds(s * residues + start, own_j), width:]) for s in range(seqs)]
    gap = lanes - 2 * seqs * width
    right += [jnp.zeros((height, gap), f32)] if gap else []
    for d, out in enumerate(outs):
        first = pl.multiple_of((me ^ d) * own_i, 8)
        left = [tall(y_ref[pl.ds(s * residues + first, own_i), :width]) for s in range(seqs)]
        out[...] = jnp.concatenate(left + right, axis=1).astype(bf16)
    for copy in copies[2:]:
        copy.wait()


def prepare_body(seqs, couple_ref, ids_hbm, valid_ref, bias_ref, avg_ref, base_ref, mask_ref, wq_ref, pick_ref,
                 wf_ref, idc_ref, ids_ref, sem):
    (copy,) = fetch([(ids_hbm, ids_ref)], sem)
    own_i, own_j, chans = couple_ref.shape
    pairs, width, _ = wq_ref.shape
    blocks, lanes, _ = pick_ref.shape
    total = blocks * seqs
    x0 = lax.axis_index("row") * own_i
    z0 = lax.axis_index("col") * own_j

    row = lax.broadcasted_iota(jnp.int32, pick_ref.shape[1:], 0)
    col = lax.broadcasted_iota(jnp.int32, pick_ref.shape[1:], 1)
    unit = row - seqs * width
    place = lax.rem(unit, width) * total + lax.div(unit, width)
    place = jnp.where((unit >= 0) & (unit < seqs * width), col - place, -1)

    def pick(r, carry):
        pick_ref[r] = jnp.where(place == r * seqs, 1.0, 0.0).astype(bf16)
        return carry

    lax.fori_loop(0, blocks, pick, 0)
    wf_ref[...] = avg_ref[...].astype(f32)
    for h in range(pairs):
        both = [wf_ref[pl.ds(2 * h + d, width, stride=width), :] for d in range(2)]
        wq_ref[h] = jnp.concatenate(both, axis=1).astype(bf16)
    copy.wait()
    for j in range(own_j):
        idc_ref[pl.ds(j, 1), :] = jnp.full((1, chans), ids_ref[z0 + j], jnp.int32)
    idc = idc_ref[...]
    valid_t = valid_ref[...].astype(f32).T
    lane = lax.broadcasted_iota(jnp.int32, valid_t.shape, 1)
    same_bias = bias_ref[0:1, :]
    cross_bias = bias_ref[1:2, :]

    def rows(i, carry):
        bias = jnp.where(idc == ids_ref[x0 + i], same_bias, cross_bias)
        base_ref[i] = couple_ref[i].astype(f32) + bias
        column = jnp.sum(jnp.where(lane == i, valid_t, 0.0), axis=1, keepdims=True)
        mask_ref[i] = jnp.broadcast_to(column, (own_j, mask_ref.shape[2])).astype(bf16)
        return carry

    lax.fori_loop(0, own_i, rows, 0, unroll=8)


def pair_body(seqs, width, blocks, *refs):
    msgs = refs[:blocks]
    base_ref, mask_ref, wq_ref, pick_ref, win_ref = refs[blocks : blocks + 5]
    psum_ref, norm_ref, right_ref = refs[blocks + 5 : blocks + 8]
    xl_ref, t_ref = refs[blocks + 8 :]
    own_i, own_j, chans = base_ref.shape
    height, lanes = msgs[0].shape
    total = seqs * blocks
    tri = win_ref.shape[1] // 4
    half = own_i // 2

    for r in range(blocks):
        m = msgs[r][pl.ds(0, own_i), :].astype(f32)
        for s in range(seqs):
            moved = m if s == 0 else pltpu.roll(m, lanes - s * width, 1)
            xl_ref[pl.ds(r * seqs + s, own_i, stride=total), :] = moved[:, :128]
    lhs = xl_ref[:, :width].astype(bf16)

    joined = jnp.concatenate([msg[...] for msg in msgs], axis=1)
    picks = pick_ref[...].reshape(blocks * lanes, width * total)
    rmat = jnp.dot(joined, picks, preferred_element_type=f32)[:own_j].astype(bf16)

    def expand(h, carry):
        out = jnp.dot(lhs, wq_ref[h], preferred_element_type=f32)
        parts = [out[:, d * chans : (d + 1) * chans].reshape(own_i, total, chans) for d in range(2)]
        block = jnp.concatenate(parts, axis=1).astype(bf16)
        where = pl.ds(pl.multiple_of(h * 2 * total, 16), 2 * total)
        t_ref[:, where, :chans] = block[:half]
        t_ref[:, where, chans:] = block[half:]
        return carry

    lax.fori_loop(0, width // 2, expand, 0)

    step = 4 if half % 4 == 0 else 1

    def rows(b, carry):
        normed = [[], []]
        for g in range(step):
            i = b * step + g
            both = jnp.dot(rmat, t_ref[i], preferred_element_type=f32) * (1.0 / total)
            for side in range(2):
                at = i + side * half
                psum = (base_ref[at] + both[:, side * chans : (side + 1) * chans]).astype(bf16)
                psum_ref[at] = psum
                normed[side].append(standardize(psum.astype(f32)))
        flat = jnp.concatenate(normed[0] + normed[1], axis=0).astype(bf16)
        proj = jnp.dot(flat, win_ref[:, 2 * tri :], preferred_element_type=f32)
        count = step * own_j
        for side in range(2):
            cut = slice(side * count, (side + 1) * count)
            i0 = b * step + side * half
            norm_ref[pl.ds(pl.multiple_of(i0 * own_j, 16), count), :] = flat[cut]
            mask = mask_ref[pl.ds(i0, step)].astype(f32).reshape(count, tri)
            right = mask * sigmoid(proj[cut, :tri]) * proj[cut, tri:]
            right_ref[pl.ds(i0, step)] = right.reshape(step, own_j, tri).astype(bf16)
        return carry

    lax.fori_loop(0, half // step, rows, 0)


def left_body(norm_ref, mask_ref, win_ref, *outs):
    own_i, own_j, tri = mask_ref.shape
    group = 8 if own_i % 8 == 0 else 1
    at = 0
    for out in outs:
        first = at

        def rows(b, carry):
            i0 = first + b * group
            flat = norm_ref[pl.ds(pl.multiple_of(i0 * own_j, 16), group * own_j), :]
            mask = mask_ref[pl.ds(i0, group)].astype(f32).reshape(group * own_j, tri)
            proj = jnp.dot(flat, win_ref[:, : 2 * tri], preferred_element_type=f32)
            left = mask * sigmoid(proj[:, :tri]) * proj[:, tri:]
            out[pl.ds(b * group, group)] = left.reshape(group, own_j, tri).astype(bf16)
            return carry

        lax.fori_loop(0, out.shape[0] // group, rows, 0, unroll=True)
        at += out.shape[0]


def contract(lf_ref, halves, i0, group):
    step = 8
    acc = (jnp.zeros(halves[0].shape[1:], f32),) * group
    for h, r_ref in enumerate(halves):
        depth = r_ref.shape[0]

        def add(kb, acc):
            k0 = kb * step
            acc = list(acc)
            for d in range(step):
                right = r_ref[k0 + d].astype(f32)
                for t in range(group):
                    acc[t] = acc[t] + lf_ref[i0 + t, pl.ds(h * depth + k0 + d, 1), :] * right
            return tuple(acc)

        acc = lax.fori_loop(0, depth // step, add, acc)
    return acc


def sums_body(own_pair, first, own_ref, other_ref, p_other, met_ref, p_met, far_ref, p_far, l_ref, m_ref, o_ref, lf_ref):
    count, depth = o_ref.shape[0], l_ref.shape[1]
    group = 8
    lf_ref[:, pl.ds(0, depth), :] = l_ref[pl.ds(first, count)].astype(f32)
    lf_ref[:, pl.ds(depth, depth), :] = m_ref[pl.ds(first, count)].astype(f32)

    def use(halves):
        def rows(b, carry):
            acc = contract(lf_ref, halves, b * group, group)
            for t in range(group):
                o_ref[b * group + t] = acc[t].astype(o_ref.dtype)
            return carry

        lax.fori_loop(0, count // group, rows, 0)

    r, z = lax.axis_index("row"), lax.axis_index("col")
    keeper = (r % 2) == (z % 2)
    near = ((r // 2) == (z // 2)) == own_pair
    table = [
        (near & keeper, own_ref, met_ref),
        (near & ~keeper, far_ref, p_met),
        (~near & keeper, p_other, far_ref),
        (~near & ~keeper, other_ref, p_far),
    ]
    for cond, a, b in table:
        pl.when(cond)(functools.partial(use, (a, b)))


def open_body(x_hbm, w_hbm, valid_hbm, couple_hbm, *refs):
    later, outs, brought = refs[:5], refs[5:9], refs[9:14]
    block_ref, longer_ref, x_ref, w_ref, valid_ref, y_ref, sem = refs[14:]
    own_i, own_j, chans = couple_hbm.shape
    copies = fetch([(x_hbm, x_ref), (w_hbm, w_ref), (valid_hbm, valid_ref),
                    (couple_hbm, block_ref.at[pl.ds(0, own_i)]),
                    (couple_hbm, longer_ref.at[pl.ds(0, own_i)]), *zip(later, brought)], sem)
    seqs, residues, depth = x_ref.shape
    width = w_ref.shape[0] // 2
    height, lanes = outs[0].shape
    me = lax.axis_index("row")
    z = lax.axis_index("col")
    copies[0].wait()
    x = x_ref[...].astype(f32).reshape(seqs * residues, depth)
    normed = standardize(x).astype(bf16)
    copies[1].wait()
    y_ref[...] = lax.dot_general(
        normed, w_ref[...], (((1,), (1,)), ((), ())), preferred_element_type=f32
    )

    def cut(start, lane):
        start = pl.multiple_of(start * own_i, 8)
        return [y_ref[pl.ds(s * residues + start, own_i), lane : lane + width] for s in range(seqs)]

    shared = cut(z, width) + cut(z ^ 1, width)
    below = jnp.zeros((height - own_i, lanes), f32)
    for d, out in enumerate(outs):
        other = ((me ^ d) // 2 ^ 1) * 2 + z % 2
        rows = jnp.concatenate(cut(me ^ d, 0) + cut(other, 0) + shared, axis=1)
        out[...] = jnp.concatenate([rows, below], axis=0).astype(bf16)
    copies[2].wait()
    mask = valid_ref[...].astype(f32).T
    mask = jnp.concatenate([mask, jnp.zeros((own_j, chans - own_i), f32)], axis=1)
    block_ref[own_i] = mask.astype(bf16)
    for n in range(own_i, longer_ref.shape[0]):
        longer_ref[n] = mask.astype(bf16)
    for copy in copies[3:]:
        copy.wait()


def ready_body(seqs, avg_ref, ids_hbm, wq_ref, pick_ref, idt_ref, wf_ref, ids_ref, sem):
    (copy,) = fetch([(ids_hbm, ids_ref)], sem)
    pairs, width, _ = wq_ref.shape
    kinds, blocks, lanes, _ = pick_ref.shape
    total = blocks * seqs
    row = lax.broadcasted_iota(jnp.int32, pick_ref.shape[2:], 0)
    col = lax.broadcasted_iota(jnp.int32, pick_ref.shape[2:], 1)
    for n in range(kinds):
        unit = row - n * seqs * width
        place = lax.rem(unit, width) * total + lax.div(unit, width)
        place = jnp.where((unit >= 0) & (unit < seqs * width), col - place, -1)
        for r in range(blocks):
            pick_ref[n, r] = jnp.where(place == r * seqs, 1.0, 0.0).astype(bf16)
    wf_ref[...] = avg_ref[...].astype(f32)
    for h in range(pairs):
        both = [wf_ref[pl.ds(2 * h + d, width, stride=width), :] for d in range(2)]
        wq_ref[h] = jnp.concatenate(both, axis=1).astype(bf16)
    copy.wait()

    def spread(n, carry):
        idt_ref[pl.ds(n, 1), :] = jnp.full((1, idt_ref.shape[1]), ids_ref[n], jnp.int32)
        return carry

    lax.fori_loop(0, idt_ref.shape[0], spread, 0, unroll=8)


def mix_rows(seqs, width, lane0, msgs, wq_ref, t_ref, xl_ref):
    half, terms, both = t_ref.shape
    chans, own_i, total = both // 2, 2 * half, seqs * 4
    for r in range(4):
        m = msgs[r][pl.ds(0, own_i), :128].astype(f32)
        for s in range(seqs):
            lane = lane0 + s * width
            moved = pltpu.roll(m, 128 - lane, 1) if lane else m
            xl_ref[pl.ds(r * seqs + s, own_i, stride=total), :] = moved
    lhs = xl_ref[:, :width].astype(bf16)
    for h in range(width // 2):
        out = jnp.dot(lhs, wq_ref[h], preferred_element_type=f32)
        parts = [out[:, d * chans : (d + 1) * chans].reshape(own_i, total, chans) for d in range(2)]
        block = jnp.concatenate(parts, axis=1).astype(bf16)
        where = pl.ds(h * 2 * total, 2 * total)
        t_ref[:, where, :chans] = block[:half]
        t_ref[:, where, chans:] = block[half:]


def mix_body(seqs, width, *refs):
    msgs, (wq_ref, pick_ref, t_ref, right_ref, xl_ref) = refs[:4], refs[4:]
    own_j, terms = right_ref.shape[1:]
    joined = jnp.concatenate([msg[:, 128:] for msg in msgs], axis=1)
    for n in range(2):
        right = jnp.dot(joined, pick_ref[n].reshape(512, terms), preferred_element_type=f32)[:own_j]
        right_ref[n] = (right * (1.0 / (seqs * 4))).astype(bf16)
    mix_rows(seqs, width, 0, msgs, wq_ref, t_ref, xl_ref)


def block_norms(block_ref, t_ref, right, row0, col0, idt_ref, bias_ref, use):
    half, terms, _ = t_ref.shape
    own_i, own_j, chans = 2 * half, right.shape[0], bias_ref.shape[1]
    idc = idt_ref[pl.ds(pl.multiple_of(col0, 8), own_j), :]
    step = 4
    for b in range(half // step):
        rows, psums = [[], []], [[], []]
        for i in range(b * step, b * step + step):
            both = jnp.dot(right, t_ref[i], preferred_element_type=f32)
            for side in range(2):
                at = i + side * half
                same = idc == idt_ref[pl.ds(row0 + at, 1), :]
                base = block_ref[at].astype(f32) + jnp.where(same, bias_ref[0:1, :], bias_ref[1:2, :])
                rows[side].append(at)
                psums[side].append((base + both[:, side * chans : (side + 1) * chans]).astype(bf16))
        rows, psums = rows[0] + rows[1], psums[0] + psums[1]
        flat = jnp.concatenate([standardize(p.astype(f32)) for p in psums], axis=0).astype(bf16)
        use(rows, psums, flat)


def gated(block_ref, rows, flat, w_ref):
    own_j = block_ref.shape[1]
    tri = w_ref.shape[1] // 2
    mask = block_ref[block_ref.shape[0] - 1].astype(f32)
    proj = jnp.dot(flat, w_ref[...], preferred_element_type=f32)
    both = sigmoid(proj[:, :tri]) * proj[:, tri:]
    return [mask[:, at : at + 1] * both[n * own_j : (n + 1) * own_j] for n, at in enumerate(rows)]


def own_body(block_ref, t_ref, right_ref, idt_ref, bias_ref, win_ref, psum_ref, norm_ref, out_ref, flat_ref):
    own_i, own_j, chans = psum_ref.shape
    r, z = lax.axis_index("row"), lax.axis_index("col")
    side = win_ref.shape[1] // 2
    w_right = win_ref.at[:, pl.ds(side, side)]

    def use(rows, psums, flat):
        rights = gated(block_ref, rows, flat, w_right)
        for n, at in enumerate(rows):
            psum_ref[at] = psums[n]
            norm_ref[pl.ds(at * own_j, own_j), :] = flat[n * own_j : (n + 1) * own_j]
            flat_ref[pl.ds(at * own_j, own_j), :] = rights[n]

    block_norms(block_ref, t_ref, right_ref[0], r * own_i, z * own_j, idt_ref, bias_ref, use)
    for k in range(own_j):
        out_ref[k] = flat_ref[pl.ds(k, own_i, stride=own_j), :].astype(bf16)


def rest_body(block_ref, norm_ref, win_ref, wgate_ref, left_ref, gate_ref):
    own_i, own_j, _ = left_ref.shape
    w_left = win_ref.at[:, pl.ds(0, win_ref.shape[1] // 2)]
    group = 8
    for i in range(0, own_i, group):
        flat = norm_ref[pl.ds(i * own_j, group * own_j), :]
        rows = list(range(i, i + group))
        gate = sigmoid(jnp.dot(flat, wgate_ref[...], preferred_element_type=f32))
        for n, left in enumerate(gated(block_ref, rows, flat, w_left)):
            left_ref[i + n] = left.astype(bf16)
            gate_ref[i + n] = gate[n * own_j : (n + 1) * own_j]


def mix_other_body(seqs, width, *refs):
    msgs, (wq_ref, t_ref, xl_ref) = refs[:4], refs[4:]

    @pl.when((lax.axis_index("row") % 2) != (lax.axis_index("col") % 2))
    def _():
        mix_rows(seqs, width, seqs * width, msgs, wq_ref, t_ref, xl_ref)


def other_body(block_ref, t_ref, right_ref, idt_ref, bias_ref, win_ref, out_ref, flat_ref):
    own_j, own_i, _ = out_ref.shape
    r, z = lax.axis_index("row"), lax.axis_index("col")
    side = win_ref.shape[1] // 2
    w_right = win_ref.at[:, pl.ds(side, side)]

    def use(rows, psums, flat):
        for at, right in zip(rows, gated(block_ref, rows, flat, w_right)):
            flat_ref[pl.ds(at * own_j, own_j), :] = right

    @pl.when((r % 2) != (z % 2))
    def _():
        block_norms(block_ref, t_ref, right_ref[0], (r ^ 3) * own_i, z * own_j, idt_ref, bias_ref, use)
        for k in range(own_j):
            out_ref[k] = flat_ref[pl.ds(k, own_i, stride=own_j), :].astype(bf16)


def met_body(block_ref, t_ref, right_ref, idt_ref, bias_ref, win_ref, left_ref, out_ref, flat_ref, norm_ref):
    own_i, own_j, _ = left_ref.shape
    r, z = lax.axis_index("row"), lax.axis_index("col")
    side = win_ref.shape[1] // 2
    w_left, w_right = win_ref.at[:, pl.ds(0, side)], win_ref.at[:, pl.ds(side, side)]

    def use(rows, psums, flat):
        lefts = gated(block_ref, rows, flat, w_left)
        for n, at in enumerate(rows):
            left_ref[at] = lefts[n].astype(bf16)
            norm_ref[pl.ds(at * own_j, own_j), :] = flat[n * own_j : (n + 1) * own_j]

    block_norms(block_ref, t_ref, right_ref[1], r * own_i, (z ^ 1) * own_j, idt_ref, bias_ref, use)

    @pl.when((r % 2) == (z % 2))
    def _():
        for i in range(0, own_i, 8):
            flat = norm_ref[pl.ds(i * own_j, 8 * own_j), :]
            for n, right in enumerate(gated(block_ref, list(range(i, i + 8)), flat, w_right)):
                flat_ref[pl.ds((i + n) * own_j, own_j), :] = right
        for k in range(own_j):
            out_ref[k] = flat_ref[pl.ds(k, own_i, stride=own_j), :].astype(bf16)


def join_body(first, parts, own_ref, psum_ref, gate_ref, w_ref, *refs):
    sums, (out_hbm, done_ref, sem) = refs[:parts], refs[-3:]
    count, extent, chans = done_ref.shape
    group = 8
    at = 0
    for sum_ref in sums:
        start = at

        def rows(b, carry):
            here = pl.ds(start + b * group, group)
            there = pl.ds(first + start + b * group, group)
            mixed = own_ref[there] + sum_ref[pl.ds(b * group, group)].astype(f32)
            normed = standardize(mixed).reshape(group * extent, -1).astype(bf16)
            update = jnp.dot(normed, w_ref[...], preferred_element_type=f32).reshape(group, extent, -1)
            done_ref[here] = (psum_ref[there].astype(f32) + gate_ref[there] * update).astype(bf16)
            return carry

        lax.fori_loop(0, sum_ref.shape[0] // group, rows, 0, unroll=True)
        at += sum_ref.shape[0]
    copy = pltpu.make_async_copy(done_ref, out_hbm.at[pl.ds(first, count)], sem)
    copy.start()
    copy.wait()


def triangle_body(l_ref, r_ref, o_ref, lf_ref, flat_ref, rk_ref):
    own_i, depth, chans = l_ref.shape
    extent = r_ref.shape[0]
    group = 8 if own_i % 8 == 0 else 1

    @pl.when(pl.program_id(0) == 0)
    def _():
        lf_ref[...] = l_ref[...].astype(f32)

    def widen(j, carry):
        flat_ref[pl.ds(pl.multiple_of(j * depth, 8), depth), :] = r_ref[j].astype(f32)
        return carry

    lax.fori_loop(0, extent, widen, 0)

    def turn(k, carry):
        rk_ref[k] = flat_ref[pl.ds(k, extent, stride=depth), :]
        return carry

    lax.fori_loop(0, depth, turn, 0)

    def rows(b, carry):
        i0 = b * group
        acc = contract(lf_ref, [rk_ref], i0, group)
        for t in range(group):
            o_ref[0, i0 + t] = acc[t].astype(bf16)
        return carry

    lax.fori_loop(0, own_i // group, rows, 0)


def finish_body(sum_ref, psum_ref, norm_ref, wgate_ref, w_ref, out_ref):
    parts, own_i, extent, chans = sum_ref.shape
    own_j = psum_ref.shape[1]

    def row(i, carry):
        flat = norm_ref[pl.ds(pl.multiple_of(i * own_j, 16), own_j), :]
        gate = sigmoid(jnp.dot(flat, wgate_ref[...], preferred_element_type=f32))
        normed = [standardize(sum_ref[part, i].astype(f32)) for part in range(parts)]
        normed = jnp.concatenate(normed, axis=0).astype(bf16)
        update = jnp.dot(normed, w_ref[...], preferred_element_type=f32)
        out_ref[i] = (psum_ref[i].astype(f32) + gate * update).astype(bf16)
        return carry

    lax.fori_loop(0, own_i, row, 0)


def gathered_plan(left, right, psum, norm, w_gate, w_final):
    own_i, own_j, chans = psum.shape
    rows = lax.axis_size("row")
    tri = w_final.shape[0]
    right_all = lax.all_gather(right, "row", axis=0, tiled=True)
    partial = pl.pallas_call(
        triangle_body,
        grid=(rows,),
        out_shape=jax.ShapeDtypeStruct((rows, own_i, own_i, tri), bf16),
        in_specs=[
            pl.BlockSpec((own_i, own_j, tri), lambda r: (0, 0, 0)),
            pl.BlockSpec((own_i, own_j, tri), lambda r: (r, 0, 0)),
        ],
        out_specs=pl.BlockSpec((1, own_i, own_i, tri), lambda r: (r, 0, 0, 0)),
        scratch_shapes=[
            pltpu.VMEM((own_i, own_j, tri), f32),
            pltpu.VMEM((own_i * own_j, tri), f32),
            pltpu.VMEM((own_j, own_i, tri), f32),
        ],
        compiler_params=limit(56),
        name="triangle",
    )(left, right_all)
    summed = lax.psum_scatter(partial, "col", scatter_dimension=0, tiled=True)
    return pl.pallas_call(
        finish_body,
        out_shape=jax.ShapeDtypeStruct((own_i, own_j, chans), bf16),
        in_specs=[VMEM] * 5,
        out_specs=VMEM,
        compiler_params=limit(56),
        name="finish",
    )(summed, psum, norm, w_gate, w_final)


def paired_plan(homolog, couple, ids, valid, bias, factors, average, w_in, w_gate, w_final):
    seqs, residues, depth = homolog.shape
    own_i, own_j, chans = couple.shape
    width = factors.shape[1] // 2
    tri = w_final.shape[0]
    total = seqs * 4
    cells = [(r, z) for r in range(4) for z in range(4)]
    struct = jax.ShapeDtypeStruct

    def move(value, step):
        pairs = [(r * 4 + z, step(r, z)) for r, z in cells]
        pairs = [(src, r * 4 + z) for src, (r, z) in pairs]
        return lax.ppermute(value, ("row", "col"), pairs)

    def call(body, us, out_shape, scratch, *args, mib=12):
        return pl.pallas_call(
            body,
            out_shape=out_shape,
            in_specs=[VMEM] * len(args),
            out_specs=[VMEM] * len(out_shape) if isinstance(out_shape, list) else VMEM,
            scratch_shapes=scratch,
            compiler_params=limit(mib),
            cost_estimate=cost(us),
            name=getattr(body, "func", body).__name__.removesuffix("_body"),
        )(*args)

    keeper = lambda r, z: r % 2 == z % 2
    beside = lambda r, z: (r ^ 1, z)
    height, lanes = round_up(own_i, 16), 256
    block = struct((own_i + 1, own_j, chans), bf16)
    longer = struct((own_i + 3, own_j, chans), bf16)
    later = (average, bias, w_in, w_gate, w_final)
    *msgs, average, bias, w_in, w_gate, w_final, raw, raw_z = pl.pallas_call(
        open_body,
        out_shape=[struct((height, lanes), bf16)] * 4 + [struct(x.shape, x.dtype) for x in later] + [block, longer],
        in_specs=[HBM] * 9,
        out_specs=[VMEM] * 11,
        scratch_shapes=[
            pltpu.VMEM(homolog.shape, bf16),
            pltpu.VMEM((2 * width, depth), bf16),
            pltpu.VMEM(valid.shape, jnp.int32),
            pltpu.VMEM((seqs * residues, 2 * width), f32),
            pltpu.SemaphoreType.DMA((10,)),
        ],
        compiler_params=limit(8),
        cost_estimate=cost(1.5),
        name="open",
    )(*map(hold, (homolog, factors.T, valid, couple) + later))
    msgs = [msgs[0]] + [
        lax.ppermute(msgs[d], "row", [(r, r ^ d) for r in range(4)]) for d in (1, 2, 3)
    ]
    met = move(raw_z, lambda r, z: (r, z ^ 1))
    raw_other = move(raw, lambda r, z: (r ^ 3, z) if keeper(r, z) else (r ^ 1, z))

    wq, pick, idt = pl.pallas_call(
        functools.partial(ready_body, seqs),
        out_shape=[struct((width // 2, width, 2 * chans), bf16),
                   struct((2, 4, 128, width * total), bf16),
                   struct((residues, 128), jnp.int32)],
        in_specs=[VMEM, HBM],
        out_specs=[VMEM] * 3,
        scratch_shapes=[
            pltpu.VMEM(average.shape, f32),
            pltpu.SMEM(ids.shape, jnp.int32),
            pltpu.SemaphoreType.DMA((1,)),
        ],
        compiler_params=limit(8),
        cost_estimate=cost(1.5),
        name="ready",
    )(average, hold(ids))

    t, mixed = call(
        functools.partial(mix_body, seqs, width), 1,
        [struct((own_i // 2, width * total, 2 * chans), bf16), struct((2, own_j, width * total), bf16)],
        [pltpu.VMEM((own_i * total, 128), f32)], *msgs, wq, pick,
    )
    square = struct((own_i, own_j, tri), bf16)
    flat = [pltpu.VMEM((own_i * own_j, tri), f32)]
    psum, norm, right = call(
        own_body, 2.4, [square, struct((own_i * own_j, chans), bf16), square], flat,
        raw, t, mixed, idt, bias, w_in,
    )
    far = move(right, lambda r, z: (r ^ 1, z) if keeper(r, z) else (r ^ 2, z ^ 1))
    left, gate = call(rest_body, 0.6, [square, struct(couple.shape, f32)], [], raw, norm, w_in, w_gate)
    msgs, right = lax.optimization_barrier((msgs, right))
    t_other = call(
        functools.partial(mix_other_body, seqs, width), 1, struct(t.shape, bf16),
        [pltpu.VMEM((own_i * total, 128), f32)], *msgs, wq,
    )
    other = call(other_body, 2.4, square, flat, raw_other, t_other, mixed, idt, bias, w_in)
    p_other = move(other, beside)
    met, *_ = lax.optimization_barrier((met, other))
    met_left, met_right = call(
        met_body, 3, [square, square], flat + [pltpu.VMEM(norm.shape, bf16)], met, t, mixed, idt, bias, w_in
    )
    p_met = move(met_right, beside)
    far, *_ = lax.optimization_barrier((far, met_left))
    p_far = move(far, beside)

    def sums(own_pair, first, n, dtype):
        return call(
            functools.partial(sums_body, own_pair, first), 0.13 * n, struct((n, own_j, tri), dtype),
            [pltpu.VMEM((n, 2 * own_j, tri), f32)],
            right, other, p_other, met_right, p_met, far, p_far, left, met_left,
        )

    came = [move(sums(False, first, 8, bf16), lambda r, z: (r, z ^ 2)) for first in range(0, own_i, 8)]
    kept = sums(True, 0, own_i, f32)

    out = []
    for first, n in ((0, 16), (16, 16), (32, own_i - 32)):
        parts = came[first // 8 : (first + n) // 8]
        out = [pl.pallas_call(
            functools.partial(join_body, first, len(parts)),
            out_shape=struct(couple.shape, bf16),
            in_specs=[VMEM] * (4 + len(parts)) + [HBM] * len(out),
            out_specs=HBM,
            scratch_shapes=[pltpu.VMEM((n, own_j, chans), bf16), pltpu.SemaphoreType.DMA],
            input_output_aliases={4 + len(parts): 0} if out else {},
            compiler_params=limit(8),
            cost_estimate=cost(0.06 * n),
            name="join",
        )(kept, psum, gate, w_final, *parts, *out)]
    return out[0]


def shards(homolog, couple, ids, valid, bias, factors, average, w_in, w_gate, w_final):
    rows, cols = lax.axis_size("row"), lax.axis_size("col")
    own_seqs, residues, depth = homolog.shape
    own_i, own_j, chans = couple.shape
    width = factors.shape[1] // 2
    tri = w_final.shape[0]
    total = own_seqs * rows
    lanes = round_up(2 * own_seqs * width, 128)
    height = round_up(max(own_i, own_j), 16)
    paired = (rows, cols, own_seqs * width, chans, tri) == (4, 4, 64, 128, 128)
    if paired and own_i == own_j == 40:
        return paired_plan(homolog, couple, ids, valid, bias, factors, average, w_in, w_gate, w_final)
    scale = 8

    later = (average, valid, bias, couple)
    *msgs, average, valid, bias, couple = pl.pallas_call(
        functools.partial(align_body, own_i, own_j, rows),
        out_shape=[jax.ShapeDtypeStruct((height, lanes), bf16)] * rows
        + [jax.ShapeDtypeStruct(x.shape, x.dtype) for x in later],
        in_specs=[HBM] * 6,
        out_specs=[VMEM] * (rows + 4),
        scratch_shapes=[
            pltpu.VMEM(homolog.shape, bf16),
            pltpu.VMEM((2 * width, depth), bf16),
            pltpu.VMEM((own_seqs * residues, 2 * width), f32),
            pltpu.SemaphoreType.DMA((6,)),
        ],
        compiler_params=limit(8, scale),
        cost_estimate=cost(1.5),
        name="align",
    )(hold(homolog), hold(factors.T), *map(hold, later))
    msgs = [msgs[0]] + [
        lax.ppermute(msgs[d], "row", [(r, r ^ d) for r in range(rows)])
        for d in reversed(range(1, rows))
    ]

    base, mask, wq, pick = pl.pallas_call(
        functools.partial(prepare_body, own_seqs),
        out_shape=[jax.ShapeDtypeStruct((own_i, own_j, chans), f32),
                   jax.ShapeDtypeStruct((own_i, own_j, tri), bf16),
                   jax.ShapeDtypeStruct((width // 2, width, 2 * chans), bf16),
                   jax.ShapeDtypeStruct((rows, lanes, width * total), bf16)],
        in_specs=[VMEM, HBM, VMEM, VMEM, VMEM],
        out_specs=[VMEM] * 4,
        scratch_shapes=[
            pltpu.VMEM(average.shape, f32),
            pltpu.VMEM((own_j, chans), jnp.int32),
            pltpu.SMEM(ids.shape, jnp.int32),
            pltpu.SemaphoreType.DMA((1,)),
        ],
        compiler_params=limit(8, scale),
        cost_estimate=cost(2),
        name="prepare",
    )(couple, hold(ids), valid, bias, average)

    extents = (own_i, own_j)
    psum, norm, right = pl.pallas_call(
        functools.partial(pair_body, own_seqs, width, rows),
        out_shape=[jax.ShapeDtypeStruct((own_i, own_j, chans), bf16),
                   jax.ShapeDtypeStruct((own_i * own_j, chans), bf16),
                   jax.ShapeDtypeStruct(extents + (tri,), bf16)],
        in_specs=[VMEM] * (rows + 5),
        out_specs=[VMEM] * 3,
        scratch_shapes=[
            pltpu.VMEM((own_i * total, 128), f32),
            pltpu.VMEM((own_i // 2, width * total, 2 * chans), bf16),
        ],
        compiler_params=limit(16, scale),
        cost_estimate=cost(4.5),
        name="pair",
    )(*msgs, base, mask, wq, pick, w_in)

    cuts = [own_i]
    lefts = pl.pallas_call(
        left_body,
        out_shape=[jax.ShapeDtypeStruct((n, own_j, tri), bf16) for n in cuts],
        in_specs=[VMEM] * 3,
        out_specs=[VMEM] * len(cuts),
        compiler_params=limit(8, scale),
        cost_estimate=cost(1),
        name="left",
    )(norm, mask, w_in)
    return gathered_plan(lefts[0], right, psum, norm, w_gate, w_final)


def solution(mesh):
    placed = (
        P(("grp", "row"), None, None),
        P(("grp", "row"), "col", None),
        P("grp"),
        P(("grp", "row"), "col"),
        P(),
        P(),
        P(),
        P(),
        P(),
        P(),
    )
    return jax.shard_map(
        shards,
        mesh=mesh,
        in_specs=placed,
        out_specs=P(("grp", "row"), "col", None),
        check_vma=False,
    )
```

```python
import functools

import jax
import jax.numpy as jnp
from jax import lax
from jax.experimental import pallas as pl
from jax.experimental.pallas import tpu as pltpu
from jax.sharding import PartitionSpec as P

eps = 1e-05
f32 = jnp.float32
bf16 = jnp.bfloat16
VMEM = pl.BlockSpec(memory_space=pltpu.VMEM)
SMEM = pl.BlockSpec(memory_space=pltpu.SMEM)
HBM = pl.BlockSpec(memory_space=pltpu.HBM)


def limit(mib, scale=1):
    return pltpu.CompilerParams(vmem_limit_bytes=min(56, mib * scale) * 1024 * 1024)


def round_up(n, m):
    return (n + m - 1) // m * m


def cost(us):
    return pl.CostEstimate(flops=0, bytes_accessed=int(us * 3.69e6), transcendentals=0)


def hold(x):
    return pltpu.with_memory_space_constraint(x, pltpu.HBM)


def fetch(pairs, sem):
    copies = [pltpu.make_async_copy(src, dst, sem.at[n]) for n, (src, dst) in enumerate(pairs)]
    for copy in copies:
        copy.start()
    return copies


def standardize(values):
    centre = values - jnp.mean(values, axis=-1, keepdims=True)
    spread = jnp.mean(centre * centre, axis=-1, keepdims=True)
    return centre * lax.rsqrt(spread + eps)


def sigmoid(v):
    return 0.5 * jnp.tanh(0.5 * v) + 0.5


def align_body(own_i, own_j, count, x_hbm, w_hbm, *refs):
    later, outs, refs = refs[:4], refs[4 : 4 + count], refs[4 + count :]
    brought, (x_ref, w_ref, y_ref, sem) = refs[:4], refs[4:]
    copies = fetch([(x_hbm, x_ref), (w_hbm, w_ref), *zip(later, brought)], sem)
    seqs, residues, depth = x_ref.shape
    width = w_ref.shape[0] // 2
    height, lanes = outs[0].shape
    me = lax.axis_index("row")
    z = lax.axis_index("col")
    copies[0].wait()
    x = x_ref[...].astype(f32).reshape(seqs * residues, depth)
    normed = standardize(x).astype(bf16)
    copies[1].wait()
    y_ref[...] = lax.dot_general(
        normed, w_ref[...], (((1,), (1,)), ((), ())), preferred_element_type=f32
    )
    start = pl.multiple_of(z * own_j, 8)

    def tall(v):
        gap = height - v.shape[0]
        return jnp.concatenate([v, jnp.zeros((gap, v.shape[1]), f32)], axis=0) if gap else v

    right = [tall(y_ref[pl.ds(s * residues + start, own_j), width:]) for s in range(seqs)]
    gap = lanes - 2 * seqs * width
    right += [jnp.zeros((height, gap), f32)] if gap else []
    for d, out in enumerate(outs):
        first = pl.multiple_of((me ^ d) * own_i, 8)
        left = [tall(y_ref[pl.ds(s * residues + first, own_i), :width]) for s in range(seqs)]
        out[...] = jnp.concatenate(left + right, axis=1).astype(bf16)
    for copy in copies[2:]:
        copy.wait()


def prepare_body(seqs, couple_ref, ids_hbm, valid_ref, bias_ref, avg_ref, base_ref, mask_ref, wq_ref, pick_ref,
                 wf_ref, idc_ref, ids_ref, sem):
    (copy,) = fetch([(ids_hbm, ids_ref)], sem)
    own_i, own_j, chans = couple_ref.shape
    pairs, width, _ = wq_ref.shape
    blocks, lanes, _ = pick_ref.shape
    total = blocks * seqs
    x0 = lax.axis_index("row") * own_i
    z0 = lax.axis_index("col") * own_j

    row = lax.broadcasted_iota(jnp.int32, pick_ref.shape[1:], 0)
    col = lax.broadcasted_iota(jnp.int32, pick_ref.shape[1:], 1)
    unit = row - seqs * width
    place = lax.rem(unit, width) * total + lax.div(unit, width)
    place = jnp.where((unit >= 0) & (unit < seqs * width), col - place, -1)

    def pick(r, carry):
        pick_ref[r] = jnp.where(place == r * seqs, 1.0, 0.0).astype(bf16)
        return carry

    lax.fori_loop(0, blocks, pick, 0)
    wf_ref[...] = avg_ref[...].astype(f32)
    for h in range(pairs):
        both = [wf_ref[pl.ds(2 * h + d, width, stride=width), :] for d in range(2)]
        wq_ref[h] = jnp.concatenate(both, axis=1).astype(bf16)
    copy.wait()
    for j in range(own_j):
        idc_ref[pl.ds(j, 1), :] = jnp.full((1, chans), ids_ref[z0 + j], jnp.int32)
    idc = idc_ref[...]
    valid_t = valid_ref[...].astype(f32).T
    lane = lax.broadcasted_iota(jnp.int32, valid_t.shape, 1)
    same_bias = bias_ref[0:1, :]
    cross_bias = bias_ref[1:2, :]

    def rows(i, carry):
        bias = jnp.where(idc == ids_ref[x0 + i], same_bias, cross_bias)
        base_ref[i] = couple_ref[i].astype(f32) + bias
        column = jnp.sum(jnp.where(lane == i, valid_t, 0.0), axis=1, keepdims=True)
        mask_ref[i] = jnp.broadcast_to(column, (own_j, mask_ref.shape[2])).astype(bf16)
        return carry

    lax.fori_loop(0, own_i, rows, 0, unroll=8)


def pair_body(seqs, width, blocks, *refs):
    msgs = refs[:blocks]
    base_ref, mask_ref, wq_ref, pick_ref, win_ref = refs[blocks : blocks + 5]
    psum_ref, norm_ref, right_ref = refs[blocks + 5 : blocks + 8]
    xl_ref, t_ref = refs[blocks + 8 :]
    own_i, own_j, chans = base_ref.shape
    height, lanes = msgs[0].shape
    total = seqs * blocks
    tri = win_ref.shape[1] // 4
    half = own_i // 2

    for r in range(blocks):
        m = msgs[r][pl.ds(0, own_i), :].astype(f32)
        for s in range(seqs):
            moved = m if s == 0 else pltpu.roll(m, lanes - s * width, 1)
            xl_ref[pl.ds(r * seqs + s, own_i, stride=total), :] = moved[:, :128]
    lhs = xl_ref[:, :width].astype(bf16)

    joined = jnp.concatenate([msg[...] for msg in msgs], axis=1)
    picks = pick_ref[...].reshape(blocks * lanes, width * total)
    rmat = jnp.dot(joined, picks, preferred_element_type=f32)[:own_j].astype(bf16)

    def expand(h, carry):
        out = jnp.dot(lhs, wq_ref[h], preferred_element_type=f32)
        parts = [out[:, d * chans : (d + 1) * chans].reshape(own_i, total, chans) for d in range(2)]
        block = jnp.concatenate(parts, axis=1).astype(bf16)
        where = pl.ds(pl.multiple_of(h * 2 * total, 16), 2 * total)
        t_ref[:, where, :chans] = block[:half]
        t_ref[:, where, chans:] = block[half:]
        return carry

    lax.fori_loop(0, width // 2, expand, 0)

    step = 4 if half % 4 == 0 else 1

    def rows(b, carry):
        normed = [[], []]
        for g in range(step):
            i = b * step + g
            both = jnp.dot(rmat, t_ref[i], preferred_element_type=f32) * (1.0 / total)
            for side in range(2):
                at = i + side * half
                psum = (base_ref[at] + both[:, side * chans : (side + 1) * chans]).astype(bf16)
                psum_ref[at] = psum
                normed[side].append(standardize(psum.astype(f32)))
        flat = jnp.concatenate(normed[0] + normed[1], axis=0).astype(bf16)
        proj = jnp.dot(flat, win_ref[:, 2 * tri :], preferred_element_type=f32)
        count = step * own_j
        for side in range(2):
            cut = slice(side * count, (side + 1) * count)
            i0 = b * step + side * half
            norm_ref[pl.ds(pl.multiple_of(i0 * own_j, 16), count), :] = flat[cut]
            mask = mask_ref[pl.ds(i0, step)].astype(f32).reshape(count, tri)
            right = mask * sigmoid(proj[cut, :tri]) * proj[cut, tri:]
            right_ref[pl.ds(i0, step)] = right.reshape(step, own_j, tri).astype(bf16)
        return carry

    lax.fori_loop(0, half // step, rows, 0)


def left_body(norm_ref, mask_ref, win_ref, *outs):
    own_i, own_j, tri = mask_ref.shape
    group = 8 if own_i % 8 == 0 else 1
    at = 0
    for out in outs:
        first = at

        def rows(b, carry):
            i0 = first + b * group
            flat = norm_ref[pl.ds(pl.multiple_of(i0 * own_j, 16), group * own_j), :]
            mask = mask_ref[pl.ds(i0, group)].astype(f32).reshape(group * own_j, tri)
            proj = jnp.dot(flat, win_ref[:, : 2 * tri], preferred_element_type=f32)
            left = mask * sigmoid(proj[:, :tri]) * proj[:, tri:]
            out[pl.ds(b * group, group)] = left.reshape(group, own_j, tri).astype(bf16)
            return carry

        lax.fori_loop(0, out.shape[0] // group, rows, 0, unroll=True)
        at += out.shape[0]


def contract(lf_ref, halves, i0, group):
    step = 8
    acc = (jnp.zeros(halves[0].shape[1:], f32),) * group
    for h, r_ref in enumerate(halves):
        depth = r_ref.shape[0]

        def add(kb, acc):
            k0 = kb * step
            acc = list(acc)
            for d in range(step):
                right = r_ref[k0 + d].astype(f32)
                for t in range(group):
                    acc[t] = acc[t] + lf_ref[i0 + t, pl.ds(h * depth + k0 + d, 1), :] * right
            return tuple(acc)

        acc = lax.fori_loop(0, depth // step, add, acc)
    return acc


def sums_body(own_pair, first, own_ref, other_ref, p_other, met_ref, p_met, far_ref, p_far, l_ref, m_ref, o_ref, lf_ref):
    count, depth = o_ref.shape[0], l_ref.shape[1]
    group = 8
    lf_ref[:, pl.ds(0, depth), :] = l_ref[pl.ds(first, count)].astype(f32)
    lf_ref[:, pl.ds(depth, depth), :] = m_ref[pl.ds(first, count)].astype(f32)

    def use(halves):
        def rows(b, carry):
            acc = contract(lf_ref, halves, b * group, group)
            for t in range(group):
                o_ref[b * group + t] = acc[t].astype(o_ref.dtype)
            return carry

        lax.fori_loop(0, count // group, rows, 0)

    r, z = lax.axis_index("row"), lax.axis_index("col")
    keeper = (r % 2) == (z % 2)
    near = ((r // 2) == (z // 2)) == own_pair
    table = [
        (near & keeper, own_ref, met_ref),
        (near & ~keeper, far_ref, p_met),
        (~near & keeper, p_other, far_ref),
        (~near & ~keeper, other_ref, p_far),
    ]
    for cond, a, b in table:
        pl.when(cond)(functools.partial(use, (a, b)))


def open_body(x_hbm, w_hbm, valid_hbm, couple_hbm, *refs):
    later, outs, brought = refs[:5], refs[5:9], refs[9:14]
    block_ref, longer_ref, x_ref, w_ref, valid_ref, y_ref, sem = refs[14:]
    own_i, own_j, chans = couple_hbm.shape
    copies = fetch([(x_hbm, x_ref), (w_hbm, w_ref), (valid_hbm, valid_ref),
                    (couple_hbm, block_ref.at[pl.ds(0, own_i)]),
                    (couple_hbm, longer_ref.at[pl.ds(0, own_i)]), *zip(later, brought)], sem)
    seqs, residues, depth = x_ref.shape
    width = w_ref.shape[0] // 2
    height, lanes = outs[0].shape
    me = lax.axis_index("row")
    z = lax.axis_index("col")
    copies[0].wait()
    x = x_ref[...].astype(f32).reshape(seqs * residues, depth)
    normed = standardize(x).astype(bf16)
    copies[1].wait()
    y_ref[...] = lax.dot_general(
        normed, w_ref[...], (((1,), (1,)), ((), ())), preferred_element_type=f32
    )

    def cut(start, lane):
        start = pl.multiple_of(start * own_i, 8)
        return [y_ref[pl.ds(s * residues + start, own_i), lane : lane + width] for s in range(seqs)]

    shared = cut(z, width) + cut(z ^ 1, width)
    below = jnp.zeros((height - own_i, lanes), f32)
    for d, out in enumerate(outs):
        other = ((me ^ d) // 2 ^ 1) * 2 + z % 2
        rows = jnp.concatenate(cut(me ^ d, 0) + cut(other, 0) + shared, axis=1)
        out[...] = jnp.concatenate([rows, below], axis=0).astype(bf16)
    copies[2].wait()
    mask = valid_ref[...].astype(f32).T
    mask = jnp.concatenate([mask, jnp.zeros((own_j, chans - own_i), f32)], axis=1)
    block_ref[own_i] = mask.astype(bf16)
    for n in range(own_i, longer_ref.shape[0]):
        longer_ref[n] = mask.astype(bf16)
    for copy in copies[3:]:
        copy.wait()


def ready_body(seqs, avg_ref, ids_hbm, wq_ref, pick_ref, idt_ref, wf_ref, ids_ref, sem):
    (copy,) = fetch([(ids_hbm, ids_ref)], sem)
    pairs, width, _ = wq_ref.shape
    kinds, blocks, lanes, _ = pick_ref.shape
    total = blocks * seqs
    row = lax.broadcasted_iota(jnp.int32, pick_ref.shape[2:], 0)
    col = lax.broadcasted_iota(jnp.int32, pick_ref.shape[2:], 1)
    for n in range(kinds):
        unit = row - n * seqs * width
        place = lax.rem(unit, width) * total + lax.div(unit, width)
        place = jnp.where((unit >= 0) & (unit < seqs * width), col - place, -1)
        for r in range(blocks):
            pick_ref[n, r] = jnp.where(place == r * seqs, 1.0, 0.0).astype(bf16)
    wf_ref[...] = avg_ref[...].astype(f32)
    for h in range(pairs):
        both = [wf_ref[pl.ds(2 * h + d, width, stride=width), :] for d in range(2)]
        wq_ref[h] = jnp.concatenate(both, axis=1).astype(bf16)
    copy.wait()

    def spread(n, carry):
        idt_ref[pl.ds(n, 1), :] = jnp.full((1, idt_ref.shape[1]), ids_ref[n], jnp.int32)
        return carry

    lax.fori_loop(0, idt_ref.shape[0], spread, 0, unroll=8)


def mix_rows(seqs, width, lane0, msgs, wq_ref, t_ref, xl_ref):
    half, terms, both = t_ref.shape
    chans, own_i, total = both // 2, 2 * half, seqs * 4
    for r in range(4):
        m = msgs[r][pl.ds(0, own_i), :128].astype(f32)
        for s in range(seqs):
            lane = lane0 + s * width
            moved = pltpu.roll(m, 128 - lane, 1) if lane else m
            xl_ref[pl.ds(r * seqs + s, own_i, stride=total), :] = moved
    lhs = xl_ref[:, :width].astype(bf16)
    for h in range(width // 2):
        out = jnp.dot(lhs, wq_ref[h], preferred_element_type=f32)
        parts = [out[:, d * chans : (d + 1) * chans].reshape(own_i, total, chans) for d in range(2)]
        block = jnp.concatenate(parts, axis=1).astype(bf16)
        where = pl.ds(h * 2 * total, 2 * total)
        t_ref[:, where, :chans] = block[:half]
        t_ref[:, where, chans:] = block[half:]


def mix_body(seqs, width, *refs):
    msgs, (wq_ref, pick_ref, t_ref, right_ref, xl_ref) = refs[:4], refs[4:]
    own_j, terms = right_ref.shape[1:]
    joined = jnp.concatenate([msg[:, 128:] for msg in msgs], axis=1)
    for n in range(2):
        right = jnp.dot(joined, pick_ref[n].reshape(512, terms), preferred_element_type=f32)[:own_j]
        right_ref[n] = (right * (1.0 / (seqs * 4))).astype(bf16)
    mix_rows(seqs, width, 0, msgs, wq_ref, t_ref, xl_ref)


def block_norms(block_ref, t_ref, right, row0, col0, idt_ref, bias_ref, use):
    half, terms, _ = t_ref.shape
    own_i, own_j, chans = 2 * half, right.shape[0], bias_ref.shape[1]
    idc = idt_ref[pl.ds(pl.multiple_of(col0, 8), own_j), :]
    step = 4
    for b in range(half // step):
        rows, psums = [[], []], [[], []]
        for i in range(b * step, b * step + step):
            both = jnp.dot(right, t_ref[i], preferred_element_type=f32)
            for side in range(2):
                at = i + side * half
                same = idc == idt_ref[pl.ds(row0 + at, 1), :]
                base = block_ref[at].astype(f32) + jnp.where(same, bias_ref[0:1, :], bias_ref[1:2, :])
                rows[side].append(at)
                psums[side].append((base + both[:, side * chans : (side + 1) * chans]).astype(bf16))
        rows, psums = rows[0] + rows[1], psums[0] + psums[1]
        flat = jnp.concatenate([standardize(p.astype(f32)) for p in psums], axis=0).astype(bf16)
        use(rows, psums, flat)


def gated(block_ref, rows, flat, w_ref):
    own_j = block_ref.shape[1]
    tri = w_ref.shape[1] // 2
    mask = block_ref[block_ref.shape[0] - 1].astype(f32)
    proj = jnp.dot(flat, w_ref[...], preferred_element_type=f32)
    both = sigmoid(proj[:, :tri]) * proj[:, tri:]
    return [mask[:, at : at + 1] * both[n * own_j : (n + 1) * own_j] for n, at in enumerate(rows)]


def own_body(block_ref, t_ref, right_ref, idt_ref, bias_ref, win_ref, psum_ref, norm_ref, out_ref, flat_ref):
    own_i, own_j, chans = psum_ref.shape
    r, z = lax.axis_index("row"), lax.axis_index("col")
    side = win_ref.shape[1] // 2
    w_right = win_ref.at[:, pl.ds(side, side)]

    def use(rows, psums, flat):
        rights = gated(block_ref, rows, flat, w_right)
        for n, at in enumerate(rows):
            psum_ref[at] = psums[n]
            norm_ref[pl.ds(at * own_j, own_j), :] = flat[n * own_j : (n + 1) * own_j]
            flat_ref[pl.ds(at * own_j, own_j), :] = rights[n]

    block_norms(block_ref, t_ref, right_ref[0], r * own_i, z * own_j, idt_ref, bias_ref, use)
    for k in range(own_j):
        out_ref[k] = flat_ref[pl.ds(k, own_i, stride=own_j), :].astype(bf16)


def rest_body(block_ref, norm_ref, win_ref, wgate_ref, left_ref, gate_ref):
    own_i, own_j, _ = left_ref.shape
    w_left = win_ref.at[:, pl.ds(0, win_ref.shape[1] // 2)]
    group = 8
    for i in range(0, own_i, group):
        flat = norm_ref[pl.ds(i * own_j, group * own_j), :]
        rows = list(range(i, i + group))
        gate = sigmoid(jnp.dot(flat, wgate_ref[...], preferred_element_type=f32))
        for n, left in enumerate(gated(block_ref, rows, flat, w_left)):
            left_ref[i + n] = left.astype(bf16)
            gate_ref[i + n] = gate[n * own_j : (n + 1) * own_j]


def mix_other_body(seqs, width, *refs):
    msgs, (wq_ref, t_ref, xl_ref) = refs[:4], refs[4:]

    @pl.when((lax.axis_index("row") % 2) != (lax.axis_index("col") % 2))
    def _():
        mix_rows(seqs, width, seqs * width, msgs, wq_ref, t_ref, xl_ref)


def other_body(block_ref, t_ref, right_ref, idt_ref, bias_ref, win_ref, out_ref, flat_ref):
    own_j, own_i, _ = out_ref.shape
    r, z = lax.axis_index("row"), lax.axis_index("col")
    side = win_ref.shape[1] // 2
    w_right = win_ref.at[:, pl.ds(side, side)]

    def use(rows, psums, flat):
        for at, right in zip(rows, gated(block_ref, rows, flat, w_right)):
            flat_ref[pl.ds(at * own_j, own_j), :] = right

    @pl.when((r % 2) != (z % 2))
    def _():
        block_norms(block_ref, t_ref, right_ref[0], (r ^ 3) * own_i, z * own_j, idt_ref, bias_ref, use)
        for k in range(own_j):
            out_ref[k] = flat_ref[pl.ds(k, own_i, stride=own_j), :].astype(bf16)


def met_body(block_ref, t_ref, right_ref, idt_ref, bias_ref, win_ref, left_ref, out_ref, flat_ref, norm_ref):
    own_i, own_j, _ = left_ref.shape
    r, z = lax.axis_index("row"), lax.axis_index("col")
    side = win_ref.shape[1] // 2
    w_left, w_right = win_ref.at[:, pl.ds(0, side)], win_ref.at[:, pl.ds(side, side)]

    def use(rows, psums, flat):
        lefts = gated(block_ref, rows, flat, w_left)
        for n, at in enumerate(rows):
            left_ref[at] = lefts[n].astype(bf16)
            norm_ref[pl.ds(at * own_j, own_j), :] = flat[n * own_j : (n + 1) * own_j]

    block_norms(block_ref, t_ref, right_ref[1], r * own_i, (z ^ 1) * own_j, idt_ref, bias_ref, use)

    @pl.when((r % 2) == (z % 2))
    def _():
        for i in range(0, own_i, 8):
            flat = norm_ref[pl.ds(i * own_j, 8 * own_j), :]
            for n, right in enumerate(gated(block_ref, list(range(i, i + 8)), flat, w_right)):
                flat_ref[pl.ds((i + n) * own_j, own_j), :] = right
        for k in range(own_j):
            out_ref[k] = flat_ref[pl.ds(k, own_i, stride=own_j), :].astype(bf16)


def join_body(first, parts, own_ref, psum_ref, gate_ref, w_ref, *refs):
    sums, (out_hbm, done_ref, sem) = refs[:parts], refs[-3:]
    count, extent, chans = done_ref.shape
    group = 8
    at = 0
    for sum_ref in sums:
        start = at

        def rows(b, carry):
            here = pl.ds(start + b * group, group)
            there = pl.ds(first + start + b * group, group)
            mixed = own_ref[there] + sum_ref[pl.ds(b * group, group)].astype(f32)
            normed = standardize(mixed).reshape(group * extent, -1).astype(bf16)
            update = jnp.dot(normed, w_ref[...], preferred_element_type=f32).reshape(group, extent, -1)
            done_ref[here] = (psum_ref[there].astype(f32) + gate_ref[there] * update).astype(bf16)
            return carry

        lax.fori_loop(0, sum_ref.shape[0] // group, rows, 0, unroll=True)
        at += sum_ref.shape[0]
    copy = pltpu.make_async_copy(done_ref, out_hbm.at[pl.ds(first, count)], sem)
    copy.start()
    copy.wait()


def triangle_body(l_ref, r_ref, o_ref, lf_ref, flat_ref, rk_ref):
    own_i, depth, chans = l_ref.shape
    extent = r_ref.shape[0]
    group = 8 if own_i % 8 == 0 else 1

    @pl.when(pl.program_id(0) == 0)
    def _():
        lf_ref[...] = l_ref[...].astype(f32)

    def widen(j, carry):
        flat_ref[pl.ds(pl.multiple_of(j * depth, 8), depth), :] = r_ref[j].astype(f32)
        return carry

    lax.fori_loop(0, extent, widen, 0)

    def turn(k, carry):
        rk_ref[k] = flat_ref[pl.ds(k, extent, stride=depth), :]
        return carry

    lax.fori_loop(0, depth, turn, 0)

    def rows(b, carry):
        i0 = b * group
        acc = contract(lf_ref, [rk_ref], i0, group)
        for t in range(group):
            o_ref[0, i0 + t] = acc[t].astype(bf16)
        return carry

    lax.fori_loop(0, own_i // group, rows, 0)


def finish_body(sum_ref, psum_ref, norm_ref, wgate_ref, w_ref, out_ref):
    parts, own_i, extent, chans = sum_ref.shape
    own_j = psum_ref.shape[1]

    def row(i, carry):
        flat = norm_ref[pl.ds(pl.multiple_of(i * own_j, 16), own_j), :]
        gate = sigmoid(jnp.dot(flat, wgate_ref[...], preferred_element_type=f32))
        normed = [standardize(sum_ref[part, i].astype(f32)) for part in range(parts)]
        normed = jnp.concatenate(normed, axis=0).astype(bf16)
        update = jnp.dot(normed, w_ref[...], preferred_element_type=f32)
        out_ref[i] = (psum_ref[i].astype(f32) + gate * update).astype(bf16)
        return carry

    lax.fori_loop(0, own_i, row, 0)


def gathered_plan(left, right, psum, norm, w_gate, w_final):
    own_i, own_j, chans = psum.shape
    rows = lax.axis_size("row")
    tri = w_final.shape[0]
    right_all = lax.all_gather(right, "row", axis=0, tiled=True)
    partial = pl.pallas_call(
        triangle_body,
        grid=(rows,),
        out_shape=jax.ShapeDtypeStruct((rows, own_i, own_i, tri), bf16),
        in_specs=[
            pl.BlockSpec((own_i, own_j, tri), lambda r: (0, 0, 0)),
            pl.BlockSpec((own_i, own_j, tri), lambda r: (r, 0, 0)),
        ],
        out_specs=pl.BlockSpec((1, own_i, own_i, tri), lambda r: (r, 0, 0, 0)),
        scratch_shapes=[
            pltpu.VMEM((own_i, own_j, tri), f32),
            pltpu.VMEM((own_i * own_j, tri), f32),
            pltpu.VMEM((own_j, own_i, tri), f32),
        ],
        compiler_params=limit(56),
        name="triangle",
    )(left, right_all)
    summed = lax.psum_scatter(partial, "col", scatter_dimension=0, tiled=True)
    return pl.pallas_call(
        finish_body,
        out_shape=jax.ShapeDtypeStruct((own_i, own_j, chans), bf16),
        in_specs=[VMEM] * 5,
        out_specs=VMEM,
        compiler_params=limit(56),
        name="finish",
    )(summed, psum, norm, w_gate, w_final)


def paired_plan(homolog, couple, ids, valid, bias, factors, average, w_in, w_gate, w_final):
    seqs, residues, depth = homolog.shape
    own_i, own_j, chans = couple.shape
    width = factors.shape[1] // 2
    tri = w_final.shape[0]
    total = seqs * 4
    cells = [(r, z) for r in range(4) for z in range(4)]
    struct = jax.ShapeDtypeStruct

    def move(value, step):
        pairs = [(r * 4 + z, step(r, z)) for r, z in cells]
        pairs = [(src, r * 4 + z) for src, (r, z) in pairs]
        return lax.ppermute(value, ("row", "col"), pairs)

    def call(body, us, out_shape, scratch, *args, mib=12):
        return pl.pallas_call(
            body,
            out_shape=out_shape,
            in_specs=[VMEM] * len(args),
            out_specs=[VMEM] * len(out_shape) if isinstance(out_shape, list) else VMEM,
            scratch_shapes=scratch,
            compiler_params=limit(mib),
            cost_estimate=cost(us),
            name=getattr(body, "func", body).__name__.removesuffix("_body"),
        )(*args)

    keeper = lambda r, z: r % 2 == z % 2
    beside = lambda r, z: (r ^ 1, z)
    height, lanes = round_up(own_i, 16), 256
    block = struct((own_i + 1, own_j, chans), bf16)
    longer = struct((own_i + 2, own_j, chans), bf16)
    later = (average, bias, w_in, w_gate, w_final)
    *msgs, average, bias, w_in, w_gate, w_final, raw, raw_z = pl.pallas_call(
        open_body,
        out_shape=[struct((height, lanes), bf16)] * 4 + [struct(x.shape, x.dtype) for x in later] + [block, longer],
        in_specs=[HBM] * 9,
        out_specs=[VMEM] * 11,
        scratch_shapes=[
            pltpu.VMEM(homolog.shape, bf16),
            pltpu.VMEM((2 * width, depth), bf16),
            pltpu.VMEM(valid.shape, jnp.int32),
            pltpu.VMEM((seqs * residues, 2 * width), f32),
            pltpu.SemaphoreType.DMA((10,)),
        ],
        compiler_params=limit(8),
        cost_estimate=cost(1.5),
        name="open",
    )(*map(hold, (homolog, factors.T, valid, couple) + later))
    msgs = [msgs[0]] + [
        lax.ppermute(msgs[d], "row", [(r, r ^ d) for r in range(4)]) for d in (1, 2, 3)
    ]
    met = move(raw_z, lambda r, z: (r, z ^ 1))
    raw_other = move(raw, lambda r, z: (r ^ 3, z) if keeper(r, z) else (r ^ 1, z))

    wq, pick, idt = pl.pallas_call(
        functools.partial(ready_body, seqs),
        out_shape=[struct((width // 2, width, 2 * chans), bf16),
                   struct((2, 4, 128, width * total), bf16),
                   struct((residues, 128), jnp.int32)],
        in_specs=[VMEM, HBM],
        out_specs=[VMEM] * 3,
        scratch_shapes=[
            pltpu.VMEM(average.shape, f32),
            pltpu.SMEM(ids.shape, jnp.int32),
            pltpu.SemaphoreType.DMA((1,)),
        ],
        compiler_params=limit(8),
        cost_estimate=cost(1.5),
        name="ready",
    )(average, hold(ids))

    t, mixed = call(
        functools.partial(mix_body, seqs, width), 1,
        [struct((own_i // 2, width * total, 2 * chans), bf16), struct((2, own_j, width * total), bf16)],
        [pltpu.VMEM((own_i * total, 128), f32)], *msgs, wq, pick,
    )
    square = struct((own_i, own_j, tri), bf16)
    flat = [pltpu.VMEM((own_i * own_j, tri), f32)]
    psum, norm, right = call(
        own_body, 2.4, [square, struct((own_i * own_j, chans), bf16), square], flat,
        raw, t, mixed, idt, bias, w_in,
    )
    far = move(right, lambda r, z: (r ^ 1, z) if keeper(r, z) else (r ^ 2, z ^ 1))
    left, gate = call(rest_body, 0.6, [square, struct(couple.shape, f32)], [], raw, norm, w_in, w_gate)
    msgs, right = lax.optimization_barrier((msgs, right))
    t_other = call(
        functools.partial(mix_other_body, seqs, width), 1, struct(t.shape, bf16),
        [pltpu.VMEM((own_i * total, 128), f32)], *msgs, wq,
    )
    other = call(other_body, 2.4, square, flat, raw_other, t_other, mixed, idt, bias, w_in)
    p_other = move(other, beside)
    met, *_ = lax.optimization_barrier((met, other))
    met_left, met_right = call(
        met_body, 3, [square, square], flat + [pltpu.VMEM(norm.shape, bf16)], met, t, mixed, idt, bias, w_in
    )
    p_met = move(met_right, beside)
    far, *_ = lax.optimization_barrier((far, met_left))
    p_far = move(far, beside)

    def sums(own_pair, first, n, dtype):
        return call(
            functools.partial(sums_body, own_pair, first), 0.13 * n, struct((n, own_j, tri), dtype),
            [pltpu.VMEM((n, 2 * own_j, tri), f32)],
            right, other, p_other, met_right, p_met, far, p_far, left, met_left,
        )

    came = [move(sums(False, first, 8, bf16), lambda r, z: (r, z ^ 2)) for first in range(0, own_i, 8)]
    kept = sums(True, 0, own_i, f32)

    out = []
    for first, n in ((0, 16), (16, 16), (32, own_i - 32)):
        parts = came[first // 8 : (first + n) // 8]
        out = [pl.pallas_call(
            functools.partial(join_body, first, len(parts)),
            out_shape=struct(couple.shape, bf16),
            in_specs=[VMEM] * (4 + len(parts)) + [HBM] * len(out),
            out_specs=HBM,
            scratch_shapes=[pltpu.VMEM((n, own_j, chans), bf16), pltpu.SemaphoreType.DMA],
            input_output_aliases={4 + len(parts): 0} if out else {},
            compiler_params=limit(8),
            cost_estimate=cost(0.06 * n),
            name="join",
        )(kept, psum, gate, w_final, *parts, *out)]
    return out[0]


def shards(homolog, couple, ids, valid, bias, factors, average, w_in, w_gate, w_final):
    rows, cols = lax.axis_size("row"), lax.axis_size("col")
    own_seqs, residues, depth = homolog.shape
    own_i, own_j, chans = couple.shape
    width = factors.shape[1] // 2
    tri = w_final.shape[0]
    total = own_seqs * rows
    lanes = round_up(2 * own_seqs * width, 128)
    height = round_up(max(own_i, own_j), 16)
    paired = (rows, cols, own_seqs * width, chans, tri) == (4, 4, 64, 128, 128)
    if paired and own_i == own_j == 40:
        return paired_plan(homolog, couple, ids, valid, bias, factors, average, w_in, w_gate, w_final)
    scale = 8

    later = (average, valid, bias, couple)
    *msgs, average, valid, bias, couple = pl.pallas_call(
        functools.partial(align_body, own_i, own_j, rows),
        out_shape=[jax.ShapeDtypeStruct((height, lanes), bf16)] * rows
        + [jax.ShapeDtypeStruct(x.shape, x.dtype) for x in later],
        in_specs=[HBM] * 6,
        out_specs=[VMEM] * (rows + 4),
        scratch_shapes=[
            pltpu.VMEM(homolog.shape, bf16),
            pltpu.VMEM((2 * width, depth), bf16),
            pltpu.VMEM((own_seqs * residues, 2 * width), f32),
            pltpu.SemaphoreType.DMA((6,)),
        ],
        compiler_params=limit(8, scale),
        cost_estimate=cost(1.5),
        name="align",
    )(hold(homolog), hold(factors.T), *map(hold, later))
    msgs = [msgs[0]] + [
        lax.ppermute(msgs[d], "row", [(r, r ^ d) for r in range(rows)])
        for d in reversed(range(1, rows))
    ]

    base, mask, wq, pick = pl.pallas_call(
        functools.partial(prepare_body, own_seqs),
        out_shape=[jax.ShapeDtypeStruct((own_i, own_j, chans), f32),
                   jax.ShapeDtypeStruct((own_i, own_j, tri), bf16),
                   jax.ShapeDtypeStruct((width // 2, width, 2 * chans), bf16),
                   jax.ShapeDtypeStruct((rows, lanes, width * total), bf16)],
        in_specs=[VMEM, HBM, VMEM, VMEM, VMEM],
        out_specs=[VMEM] * 4,
        scratch_shapes=[
            pltpu.VMEM(average.shape, f32),
            pltpu.VMEM((own_j, chans), jnp.int32),
            pltpu.SMEM(ids.shape, jnp.int32),
            pltpu.SemaphoreType.DMA((1,)),
        ],
        compiler_params=limit(8, scale),
        cost_estimate=cost(2),
        name="prepare",
    )(couple, hold(ids), valid, bias, average)

    extents = (own_i, own_j)
    psum, norm, right = pl.pallas_call(
        functools.partial(pair_body, own_seqs, width, rows),
        out_shape=[jax.ShapeDtypeStruct((own_i, own_j, chans), bf16),
                   jax.ShapeDtypeStruct((own_i * own_j, chans), bf16),
                   jax.ShapeDtypeStruct(extents + (tri,), bf16)],
        in_specs=[VMEM] * (rows + 5),
        out_specs=[VMEM] * 3,
        scratch_shapes=[
            pltpu.VMEM((own_i * total, 128), f32),
            pltpu.VMEM((own_i // 2, width * total, 2 * chans), bf16),
        ],
        compiler_params=limit(16, scale),
        cost_estimate=cost(4.5),
        name="pair",
    )(*msgs, base, mask, wq, pick, w_in)

    cuts = [own_i]
    lefts = pl.pallas_call(
        left_body,
        out_shape=[jax.ShapeDtypeStruct((n, own_j, tri), bf16) for n in cuts],
        in_specs=[VMEM] * 3,
        out_specs=[VMEM] * len(cuts),
        compiler_params=limit(8, scale),
        cost_estimate=cost(1),
        name="left",
    )(norm, mask, w_in)
    return gathered_plan(lefts[0], right, psum, norm, w_gate, w_final)


def solution(mesh):
    placed = (
        P(("grp", "row"), None, None),
        P(("grp", "row"), "col", None),
        P("grp"),
        P(("grp", "row"), "col"),
        P(),
        P(),
        P(),
        P(),
        P(),
        P(),
    )
    return jax.shard_map(
        shards,
        mesh=mesh,
        in_specs=placed,
        out_specs=P(("grp", "row"), "col", None),
        check_vma=False,
    )
```

```python
import functools

import jax
import jax.numpy as jnp
from jax import lax
from jax.experimental import pallas as pl
from jax.experimental.pallas import tpu as pltpu
from jax.sharding import PartitionSpec as P

eps = 1e-05
f32 = jnp.float32
bf16 = jnp.bfloat16
VMEM = pl.BlockSpec(memory_space=pltpu.VMEM)
SMEM = pl.BlockSpec(memory_space=pltpu.SMEM)
HBM = pl.BlockSpec(memory_space=pltpu.HBM)


def limit(mib, scale=1):
    return pltpu.CompilerParams(vmem_limit_bytes=min(56, mib * scale) * 1024 * 1024)


def round_up(n, m):
    return (n + m - 1) // m * m


def cost(us):
    return pl.CostEstimate(flops=0, bytes_accessed=int(us * 3.69e6), transcendentals=0)


def hold(x):
    return pltpu.with_memory_space_constraint(x, pltpu.HBM)


def fetch(pairs, sem):
    copies = [pltpu.make_async_copy(src, dst, sem.at[n]) for n, (src, dst) in enumerate(pairs)]
    for copy in copies:
        copy.start()
    return copies


def standardize(values):
    centre = values - jnp.mean(values, axis=-1, keepdims=True)
    spread = jnp.mean(centre * centre, axis=-1, keepdims=True)
    return centre * lax.rsqrt(spread + eps)


def sigmoid(v):
    return 0.5 * jnp.tanh(0.5 * v) + 0.5


def align_body(own_i, own_j, count, x_hbm, w_hbm, *refs):
    later, outs, refs = refs[:4], refs[4 : 4 + count], refs[4 + count :]
    brought, (x_ref, w_ref, y_ref, sem) = refs[:4], refs[4:]
    copies = fetch([(x_hbm, x_ref), (w_hbm, w_ref), *zip(later, brought)], sem)
    seqs, residues, depth = x_ref.shape
    width = w_ref.shape[0] // 2
    height, lanes = outs[0].shape
    me = lax.axis_index("row")
    z = lax.axis_index("col")
    copies[0].wait()
    x = x_ref[...].astype(f32).reshape(seqs * residues, depth)
    normed = standardize(x).astype(bf16)
    copies[1].wait()
    y_ref[...] = lax.dot_general(
        normed, w_ref[...], (((1,), (1,)), ((), ())), preferred_element_type=f32
    )
    start = pl.multiple_of(z * own_j, 8)

    def tall(v):
        gap = height - v.shape[0]
        return jnp.concatenate([v, jnp.zeros((gap, v.shape[1]), f32)], axis=0) if gap else v

    right = [tall(y_ref[pl.ds(s * residues + start, own_j), width:]) for s in range(seqs)]
    gap = lanes - 2 * seqs * width
    right += [jnp.zeros((height, gap), f32)] if gap else []
    for d, out in enumerate(outs):
        first = pl.multiple_of((me ^ d) * own_i, 8)
        left = [tall(y_ref[pl.ds(s * residues + first, own_i), :width]) for s in range(seqs)]
        out[...] = jnp.concatenate(left + right, axis=1).astype(bf16)
    for copy in copies[2:]:
        copy.wait()


def prepare_body(seqs, couple_ref, ids_hbm, valid_ref, bias_ref, avg_ref, base_ref, mask_ref, wq_ref, pick_ref,
                 wf_ref, idc_ref, ids_ref, sem):
    (copy,) = fetch([(ids_hbm, ids_ref)], sem)
    own_i, own_j, chans = couple_ref.shape
    pairs, width, _ = wq_ref.shape
    blocks, lanes, _ = pick_ref.shape
    total = blocks * seqs
    x0 = lax.axis_index("row") * own_i
    z0 = lax.axis_index("col") * own_j

    row = lax.broadcasted_iota(jnp.int32, pick_ref.shape[1:], 0)
    col = lax.broadcasted_iota(jnp.int32, pick_ref.shape[1:], 1)
    unit = row - seqs * width
    place = lax.rem(unit, width) * total + lax.div(unit, width)
    place = jnp.where((unit >= 0) & (unit < seqs * width), col - place, -1)

    def pick(r, carry):
        pick_ref[r] = jnp.where(place == r * seqs, 1.0, 0.0).astype(bf16)
        return carry

    lax.fori_loop(0, blocks, pick, 0)
    wf_ref[...] = avg_ref[...].astype(f32)
    for h in range(pairs):
        both = [wf_ref[pl.ds(2 * h + d, width, stride=width), :] for d in range(2)]
        wq_ref[h] = jnp.concatenate(both, axis=1).astype(bf16)
    copy.wait()
    for j in range(own_j):
        idc_ref[pl.ds(j, 1), :] = jnp.full((1, chans), ids_ref[z0 + j], jnp.int32)
    idc = idc_ref[...]
    valid_t = valid_ref[...].astype(f32).T
    lane = lax.broadcasted_iota(jnp.int32, valid_t.shape, 1)
    same_bias = bias_ref[0:1, :]
    cross_bias = bias_ref[1:2, :]

    def rows(i, carry):
        bias = jnp.where(idc == ids_ref[x0 + i], same_bias, cross_bias)
        base_ref[i] = couple_ref[i].astype(f32) + bias
        column = jnp.sum(jnp.where(lane == i, valid_t, 0.0), axis=1, keepdims=True)
        mask_ref[i] = jnp.broadcast_to(column, (own_j, mask_ref.shape[2])).astype(bf16)
        return carry

    lax.fori_loop(0, own_i, rows, 0, unroll=8)


def pair_body(seqs, width, blocks, *refs):
    msgs = refs[:blocks]
    base_ref, mask_ref, wq_ref, pick_ref, win_ref = refs[blocks : blocks + 5]
    psum_ref, norm_ref, right_ref = refs[blocks + 5 : blocks + 8]
    xl_ref, t_ref = refs[blocks + 8 :]
    own_i, own_j, chans = base_ref.shape
    height, lanes = msgs[0].shape
    total = seqs * blocks
    tri = win_ref.shape[1] // 4
    half = own_i // 2

    for r in range(blocks):
        m = msgs[r][pl.ds(0, own_i), :].astype(f32)
        for s in range(seqs):
            moved = m if s == 0 else pltpu.roll(m, lanes - s * width, 1)
            xl_ref[pl.ds(r * seqs + s, own_i, stride=total), :] = moved[:, :128]
    lhs = xl_ref[:, :width].astype(bf16)

    joined = jnp.concatenate([msg[...] for msg in msgs], axis=1)
    picks = pick_ref[...].reshape(blocks * lanes, width * total)
    rmat = jnp.dot(joined, picks, preferred_element_type=f32)[:own_j].astype(bf16)

    def expand(h, carry):
        out = jnp.dot(lhs, wq_ref[h], preferred_element_type=f32)
        parts = [out[:, d * chans : (d + 1) * chans].reshape(own_i, total, chans) for d in range(2)]
        block = jnp.concatenate(parts, axis=1).astype(bf16)
        where = pl.ds(pl.multiple_of(h * 2 * total, 16), 2 * total)
        t_ref[:, where, :chans] = block[:half]
        t_ref[:, where, chans:] = block[half:]
        return carry

    lax.fori_loop(0, width // 2, expand, 0)

    step = 4 if half % 4 == 0 else 1

    def rows(b, carry):
        normed = [[], []]
        for g in range(step):
            i = b * step + g
            both = jnp.dot(rmat, t_ref[i], preferred_element_type=f32) * (1.0 / total)
            for side in range(2):
                at = i + side * half
                psum = (base_ref[at] + both[:, side * chans : (side + 1) * chans]).astype(bf16)
                psum_ref[at] = psum
                normed[side].append(standardize(psum.astype(f32)))
        flat = jnp.concatenate(normed[0] + normed[1], axis=0).astype(bf16)
        proj = jnp.dot(flat, win_ref[:, 2 * tri :], preferred_element_type=f32)
        count = step * own_j
        for side in range(2):
            cut = slice(side * count, (side + 1) * count)
            i0 = b * step + side * half
            norm_ref[pl.ds(pl.multiple_of(i0 * own_j, 16), count), :] = flat[cut]
            mask = mask_ref[pl.ds(i0, step)].astype(f32).reshape(count, tri)
            right = mask * sigmoid(proj[cut, :tri]) * proj[cut, tri:]
            right_ref[pl.ds(i0, step)] = right.reshape(step, own_j, tri).astype(bf16)
        return carry

    lax.fori_loop(0, half // step, rows, 0)


def left_body(norm_ref, mask_ref, win_ref, *outs):
    own_i, own_j, tri = mask_ref.shape
    group = 8 if own_i % 8 == 0 else 1
    at = 0
    for out in outs:
        first = at

        def rows(b, carry):
            i0 = first + b * group
            flat = norm_ref[pl.ds(pl.multiple_of(i0 * own_j, 16), group * own_j), :]
            mask = mask_ref[pl.ds(i0, group)].astype(f32).reshape(group * own_j, tri)
            proj = jnp.dot(flat, win_ref[:, : 2 * tri], preferred_element_type=f32)
            left = mask * sigmoid(proj[:, :tri]) * proj[:, tri:]
            out[pl.ds(b * group, group)] = left.reshape(group, own_j, tri).astype(bf16)
            return carry

        lax.fori_loop(0, out.shape[0] // group, rows, 0, unroll=True)
        at += out.shape[0]


def contract(lf_ref, halves, i0, group):
    step = 8
    acc = (jnp.zeros(halves[0].shape[1:], f32),) * group
    for h, r_ref in enumerate(halves):
        depth = r_ref.shape[0]

        def add(kb, acc):
            k0 = kb * step
            acc = list(acc)
            for d in range(step):
                right = r_ref[k0 + d].astype(f32)
                for t in range(group):
                    acc[t] = acc[t] + lf_ref[i0 + t, pl.ds(h * depth + k0 + d, 1), :] * right
            return tuple(acc)

        acc = lax.fori_loop(0, depth // step, add, acc)
    return acc


def sums_body(own_pair, first, own_ref, other_ref, p_other, met_ref, p_met, far_ref, p_far, l_ref, m_ref, o_ref, lf_ref):
    count, depth = o_ref.shape[0], l_ref.shape[1]
    group = 8
    lf_ref[:, pl.ds(0, depth), :] = l_ref[pl.ds(first, count)].astype(f32)
    lf_ref[:, pl.ds(depth, depth), :] = m_ref[pl.ds(first, count)].astype(f32)

    def use(halves):
        def rows(b, carry):
            acc = contract(lf_ref, halves, b * group, group)
            for t in range(group):
                o_ref[b * group + t] = acc[t].astype(o_ref.dtype)
            return carry

        lax.fori_loop(0, count // group, rows, 0)

    r, z = lax.axis_index("row"), lax.axis_index("col")
    keeper = (r % 2) == (z % 2)
    near = ((r // 2) == (z // 2)) == own_pair
    table = [
        (near & keeper, own_ref, met_ref),
        (near & ~keeper, far_ref, p_met),
        (~near & keeper, p_other, far_ref),
        (~near & ~keeper, other_ref, p_far),
    ]
    for cond, a, b in table:
        pl.when(cond)(functools.partial(use, (a, b)))


def open_body(x_hbm, w_hbm, valid_hbm, couple_hbm, *refs):
    later, outs, brought = refs[:5], refs[5:9], refs[9:14]
    block_ref, longer_ref, x_ref, w_ref, valid_ref, y_ref, sem = refs[14:]
    own_i, own_j, chans = couple_hbm.shape
    copies = fetch([(x_hbm, x_ref), (w_hbm, w_ref), (valid_hbm, valid_ref),
                    (couple_hbm, block_ref.at[pl.ds(0, own_i)]),
                    (couple_hbm, longer_ref.at[pl.ds(0, own_i)]), *zip(later, brought)], sem)
    seqs, residues, depth = x_ref.shape
    width = w_ref.shape[0] // 2
    height, lanes = outs[0].shape
    me = lax.axis_index("row")
    z = lax.axis_index("col")
    copies[0].wait()
    x = x_ref[...].astype(f32).reshape(seqs * residues, depth)
    normed = standardize(x).astype(bf16)
    copies[1].wait()
    y_ref[...] = lax.dot_general(
        normed, w_ref[...], (((1,), (1,)), ((), ())), preferred_element_type=f32
    )

    def cut(start, lane):
        start = pl.multiple_of(start * own_i, 8)
        return [y_ref[pl.ds(s * residues + start, own_i), lane : lane + width] for s in range(seqs)]

    shared = cut(z, width) + cut(z ^ 1, width)
    below = jnp.zeros((height - own_i, lanes), f32)
    for d, out in enumerate(outs):
        other = ((me ^ d) // 2 ^ 1) * 2 + z % 2
        rows = jnp.concatenate(cut(me ^ d, 0) + cut(other, 0) + shared, axis=1)
        out[...] = jnp.concatenate([rows, below], axis=0).astype(bf16)
    copies[2].wait()
    mask = valid_ref[...].astype(f32).T
    mask = jnp.concatenate([mask, jnp.zeros((own_j, chans - own_i), f32)], axis=1)
    block_ref[own_i] = mask.astype(bf16)
    for n in range(own_i, longer_ref.shape[0]):
        longer_ref[n] = mask.astype(bf16)
    for copy in copies[3:]:
        copy.wait()


def ready_body(seqs, avg_ref, ids_hbm, wq_ref, pick_ref, idt_ref, wf_ref, ids_ref, sem):
    (copy,) = fetch([(ids_hbm, ids_ref)], sem)
    pairs, width, _ = wq_ref.shape
    kinds, blocks, lanes, _ = pick_ref.shape
    total = blocks * seqs
    row = lax.broadcasted_iota(jnp.int32, pick_ref.shape[2:], 0)
    col = lax.broadcasted_iota(jnp.int32, pick_ref.shape[2:], 1)
    for n in range(kinds):
        unit = row - n * seqs * width
        place = lax.rem(unit, width) * total + lax.div(unit, width)
        place = jnp.where((unit >= 0) & (unit < seqs * width), col - place, -1)
        for r in range(blocks):
            pick_ref[n, r] = jnp.where(place == r * seqs, 1.0, 0.0).astype(bf16)
    wf_ref[...] = avg_ref[...].astype(f32)
    for h in range(pairs):
        both = [wf_ref[pl.ds(2 * h + d, width, stride=width), :] for d in range(2)]
        wq_ref[h] = jnp.concatenate(both, axis=1).astype(bf16)
    copy.wait()

    def spread(n, carry):
        idt_ref[pl.ds(n, 1), :] = jnp.full((1, idt_ref.shape[1]), ids_ref[n], jnp.int32)
        return carry

    lax.fori_loop(0, idt_ref.shape[0], spread, 0, unroll=8)


def mix_rows(seqs, width, lane0, msgs, wq_ref, t_ref, xl_ref):
    half, terms, both = t_ref.shape
    chans, own_i, total = both // 2, 2 * half, seqs * 4
    for r in range(4):
        m = msgs[r][:, :128].astype(f32)[:own_i]
        for s in range(seqs):
            lane = lane0 + s * width
            moved = pltpu.roll(m, 128 - lane, 1) if lane else m
            xl_ref[pl.ds(r * seqs + s, own_i, stride=total), :] = moved
    lhs = xl_ref[:, :width].astype(bf16)
    for h in range(width // 2):
        out = jnp.dot(lhs, wq_ref[h], preferred_element_type=f32)
        parts = [out[:, d * chans : (d + 1) * chans].reshape(own_i, total, chans) for d in range(2)]
        block = jnp.concatenate(parts, axis=1).astype(bf16)
        where = pl.ds(h * 2 * total, 2 * total)
        t_ref[:, where, :chans] = block[:half]
        t_ref[:, where, chans:] = block[half:]


def mix_body(seqs, width, *refs):
    msgs, (wq_ref, pick_ref, t_ref, right_ref, xl_ref) = refs[:4], refs[4:]
    own_j, terms = right_ref.shape[1:]
    joined = jnp.concatenate([msg[:, 128:] for msg in msgs], axis=1)
    for n in range(2):
        right = jnp.dot(joined, pick_ref[n].reshape(512, terms), preferred_element_type=f32)[:own_j]
        right_ref[n] = (right * (1.0 / (seqs * 4))).astype(bf16)
    mix_rows(seqs, width, 0, msgs, wq_ref, t_ref, xl_ref)


def block_norms(block_ref, t_ref, right, row0, col0, idt_ref, bias_ref, use):
    half, terms, _ = t_ref.shape
    own_i, own_j, chans = 2 * half, right.shape[0], bias_ref.shape[1]
    idc = idt_ref[pl.ds(pl.multiple_of(col0, 8), own_j), :]
    step = 4
    for b in range(half // step):
        rows, psums = [[], []], [[], []]
        for i in range(b * step, b * step + step):
            both = jnp.dot(right, t_ref[i], preferred_element_type=f32)
            for side in range(2):
                at = i + side * half
                same = idc == idt_ref[pl.ds(row0 + at, 1), :]
                base = block_ref[at].astype(f32) + jnp.where(same, bias_ref[0:1, :], bias_ref[1:2, :])
                rows[side].append(at)
                psums[side].append((base + both[:, side * chans : (side + 1) * chans]).astype(bf16))
        rows, psums = rows[0] + rows[1], psums[0] + psums[1]
        flat = jnp.concatenate([standardize(p.astype(f32)) for p in psums], axis=0).astype(bf16)
        use(rows, psums, flat)


def gated(block_ref, rows, flat, w_ref):
    own_j = block_ref.shape[1]
    tri = w_ref.shape[1] // 2
    mask = block_ref[block_ref.shape[0] - 1].astype(f32)
    proj = jnp.dot(flat, w_ref[...], preferred_element_type=f32)
    both = sigmoid(proj[:, :tri]) * proj[:, tri:]
    return [mask[:, at : at + 1] * both[n * own_j : (n + 1) * own_j] for n, at in enumerate(rows)]


def own_body(block_ref, t_ref, right_ref, idt_ref, bias_ref, win_ref, psum_ref, norm_ref, out_ref, flat_ref):
    own_i, own_j, chans = psum_ref.shape
    r, z = lax.axis_index("row"), lax.axis_index("col")
    side = win_ref.shape[1] // 2
    w_right = win_ref.at[:, pl.ds(side, side)]

    def use(rows, psums, flat):
        rights = gated(block_ref, rows, flat, w_right)
        some = len(rows) // 2
        for n in (0, some):
            norm_ref[pl.ds(rows[n] * own_j, some * own_j), :] = flat[n * own_j : (n + some) * own_j]
        for n, at in enumerate(rows):
            psum_ref[at] = psums[n]
            flat_ref[pl.ds(at * own_j, own_j), :] = rights[n]

    block_norms(block_ref, t_ref, right_ref[0], r * own_i, z * own_j, idt_ref, bias_ref, use)
    for k in range(own_j):
        out_ref[k] = flat_ref[pl.ds(k, own_i, stride=own_j), :].astype(bf16)


def rest_body(block_ref, norm_ref, win_ref, wgate_ref, left_ref, gate_ref):
    own_i, own_j, _ = left_ref.shape
    w_left = win_ref.at[:, pl.ds(0, win_ref.shape[1] // 2)]
    group = 8
    for i in range(0, own_i, group):
        flat = norm_ref[pl.ds(i * own_j, group * own_j), :]
        rows = list(range(i, i + group))
        gate = sigmoid(jnp.dot(flat, wgate_ref[...], preferred_element_type=f32))
        for n, left in enumerate(gated(block_ref, rows, flat, w_left)):
            left_ref[i + n] = left.astype(bf16)
            gate_ref[i + n] = gate[n * own_j : (n + 1) * own_j]


def other_body(seqs, width, *refs):
    msgs, refs = refs[:4], refs[4:]
    wq_ref, block_ref, right_ref, idt_ref, bias_ref, win_ref, out_ref, t_ref, xl_ref, flat_ref = refs
    own_j, own_i, _ = out_ref.shape
    r, z = lax.axis_index("row"), lax.axis_index("col")
    side = win_ref.shape[1] // 2
    w_right = win_ref.at[:, pl.ds(side, side)]

    def use(rows, psums, flat):
        for at, right in zip(rows, gated(block_ref, rows, flat, w_right)):
            flat_ref[pl.ds(at * own_j, own_j), :] = right

    @pl.when((r % 2) != (z % 2))
    def _():
        mix_rows(seqs, width, seqs * width, msgs, wq_ref, t_ref, xl_ref)
        block_norms(block_ref, t_ref, right_ref[0], (r ^ 3) * own_i, z * own_j, idt_ref, bias_ref, use)
        for k in range(own_j):
            out_ref[k] = flat_ref[pl.ds(k, own_i, stride=own_j), :].astype(bf16)


def met_body(block_ref, t_ref, right_ref, idt_ref, bias_ref, win_ref, left_ref, out_ref, flat_ref):
    own_i, own_j, _ = left_ref.shape
    r, z = lax.axis_index("row"), lax.axis_index("col")
    side = win_ref.shape[1] // 2
    w_left, w_right = win_ref.at[:, pl.ds(0, side)], win_ref.at[:, pl.ds(side, side)]

    def use(rows, psums, flat):
        lefts = gated(block_ref, rows, flat, w_left)
        rights = gated(block_ref, rows, flat, w_right)
        for n, at in enumerate(rows):
            left_ref[at] = lefts[n].astype(bf16)
            flat_ref[pl.ds(at * own_j, own_j), :] = rights[n]

    block_norms(block_ref, t_ref, right_ref[1], r * own_i, (z ^ 1) * own_j, idt_ref, bias_ref, use)
    for k in range(own_j):
        out_ref[k] = flat_ref[pl.ds(k, own_i, stride=own_j), :].astype(bf16)


def join_body(first, parts, own_ref, psum_ref, gate_ref, w_ref, *refs):
    sums, (out_hbm, done_ref, sem) = refs[:parts], refs[-3:]
    count, extent, chans = done_ref.shape
    group = 8
    at = 0
    for sum_ref in sums:
        start = at

        def rows(b, carry):
            here = pl.ds(start + b * group, group)
            there = pl.ds(first + start + b * group, group)
            mixed = own_ref[there] + sum_ref[pl.ds(b * group, group)].astype(f32)
            normed = standardize(mixed).reshape(group * extent, -1).astype(bf16)
            update = jnp.dot(normed, w_ref[...], preferred_element_type=f32).reshape(group, extent, -1)
            done_ref[here] = (psum_ref[there].astype(f32) + gate_ref[there] * update).astype(bf16)
            return carry

        lax.fori_loop(0, sum_ref.shape[0] // group, rows, 0, unroll=True)
        at += sum_ref.shape[0]
    copy = pltpu.make_async_copy(done_ref, out_hbm.at[pl.ds(first, count)], sem)
    copy.start()
    copy.wait()


def triangle_body(l_ref, r_ref, o_ref, lf_ref, flat_ref, rk_ref):
    own_i, depth, chans = l_ref.shape
    extent = r_ref.shape[0]
    group = 8 if own_i % 8 == 0 else 1

    @pl.when(pl.program_id(0) == 0)
    def _():
        lf_ref[...] = l_ref[...].astype(f32)

    def widen(j, carry):
        flat_ref[pl.ds(pl.multiple_of(j * depth, 8), depth), :] = r_ref[j].astype(f32)
        return carry

    lax.fori_loop(0, extent, widen, 0)

    def turn(k, carry):
        rk_ref[k] = flat_ref[pl.ds(k, extent, stride=depth), :]
        return carry

    lax.fori_loop(0, depth, turn, 0)

    def rows(b, carry):
        i0 = b * group
        acc = contract(lf_ref, [rk_ref], i0, group)
        for t in range(group):
            o_ref[0, i0 + t] = acc[t].astype(bf16)
        return carry

    lax.fori_loop(0, own_i // group, rows, 0)


def finish_body(sum_ref, psum_ref, norm_ref, wgate_ref, w_ref, out_ref):
    parts, own_i, extent, chans = sum_ref.shape
    own_j = psum_ref.shape[1]

    def row(i, carry):
        flat = norm_ref[pl.ds(pl.multiple_of(i * own_j, 16), own_j), :]
        gate = sigmoid(jnp.dot(flat, wgate_ref[...], preferred_element_type=f32))
        normed = [standardize(sum_ref[part, i].astype(f32)) for part in range(parts)]
        normed = jnp.concatenate(normed, axis=0).astype(bf16)
        update = jnp.dot(normed, w_ref[...], preferred_element_type=f32)
        out_ref[i] = (psum_ref[i].astype(f32) + gate * update).astype(bf16)
        return carry

    lax.fori_loop(0, own_i, row, 0)


def gathered_plan(left, right, psum, norm, w_gate, w_final):
    own_i, own_j, chans = psum.shape
    rows = lax.axis_size("row")
    tri = w_final.shape[0]
    right_all = lax.all_gather(right, "row", axis=0, tiled=True)
    partial = pl.pallas_call(
        triangle_body,
        grid=(rows,),
        out_shape=jax.ShapeDtypeStruct((rows, own_i, own_i, tri), bf16),
        in_specs=[
            pl.BlockSpec((own_i, own_j, tri), lambda r: (0, 0, 0)),
            pl.BlockSpec((own_i, own_j, tri), lambda r: (r, 0, 0)),
        ],
        out_specs=pl.BlockSpec((1, own_i, own_i, tri), lambda r: (r, 0, 0, 0)),
        scratch_shapes=[
            pltpu.VMEM((own_i, own_j, tri), f32),
            pltpu.VMEM((own_i * own_j, tri), f32),
            pltpu.VMEM((own_j, own_i, tri), f32),
        ],
        compiler_params=limit(56),
        name="triangle",
    )(left, right_all)
    summed = lax.psum_scatter(partial, "col", scatter_dimension=0, tiled=True)
    return pl.pallas_call(
        finish_body,
        out_shape=jax.ShapeDtypeStruct((own_i, own_j, chans), bf16),
        in_specs=[VMEM] * 5,
        out_specs=VMEM,
        compiler_params=limit(56),
        name="finish",
    )(summed, psum, norm, w_gate, w_final)


def paired_plan(homolog, couple, ids, valid, bias, factors, average, w_in, w_gate, w_final):
    seqs, residues, depth = homolog.shape
    own_i, own_j, chans = couple.shape
    width = factors.shape[1] // 2
    tri = w_final.shape[0]
    total = seqs * 4
    cells = [(r, z) for r in range(4) for z in range(4)]
    struct = jax.ShapeDtypeStruct

    def move(value, step):
        pairs = [(r * 4 + z, step(r, z)) for r, z in cells]
        pairs = [(src, r * 4 + z) for src, (r, z) in pairs]
        return lax.ppermute(value, ("row", "col"), pairs)

    def call(body, us, out_shape, scratch, *args, mib=12):
        return pl.pallas_call(
            body,
            out_shape=out_shape,
            in_specs=[VMEM] * len(args),
            out_specs=[VMEM] * len(out_shape) if isinstance(out_shape, list) else VMEM,
            scratch_shapes=scratch,
            compiler_params=limit(mib),
            cost_estimate=cost(us),
            name=getattr(body, "func", body).__name__.removesuffix("_body"),
        )(*args)

    keeper = lambda r, z: r % 2 == z % 2
    beside = lambda r, z: (r ^ 1, z)
    height, lanes = round_up(own_i, 16), 256
    block = struct((own_i + 1, own_j, chans), bf16)
    longer = struct((own_i + 3, own_j, chans), bf16)
    later = (average, bias, w_in, w_gate, w_final)
    *msgs, average, bias, w_in, w_gate, w_final, raw, raw_z = pl.pallas_call(
        open_body,
        out_shape=[struct((height, lanes), bf16)] * 4 + [struct(x.shape, x.dtype) for x in later] + [block, longer],
        in_specs=[HBM] * 9,
        out_specs=[VMEM] * 11,
        scratch_shapes=[
            pltpu.VMEM(homolog.shape, bf16),
            pltpu.VMEM((2 * width, depth), bf16),
            pltpu.VMEM(valid.shape, jnp.int32),
            pltpu.VMEM((seqs * residues, 2 * width), f32),
            pltpu.SemaphoreType.DMA((10,)),
        ],
        compiler_params=limit(8),
        cost_estimate=cost(1.5),
        name="open",
    )(*map(hold, (homolog, factors.T, valid, couple) + later))
    msgs = [msgs[0]] + [
        lax.ppermute(msgs[d], "row", [(r, r ^ d) for r in range(4)]) for d in (1, 2, 3)
    ]
    met = move(raw_z, lambda r, z: (r, z ^ 1))
    raw_other = move(raw, lambda r, z: (r ^ 3, z) if keeper(r, z) else (r ^ 1, z))

    wq, pick, idt = pl.pallas_call(
        functools.partial(ready_body, seqs),
        out_shape=[struct((width // 2, width, 2 * chans), bf16),
                   struct((2, 4, 128, width * total), bf16),
                   struct((residues, 128), jnp.int32)],
        in_specs=[VMEM, HBM],
        out_specs=[VMEM] * 3,
        scratch_shapes=[
            pltpu.VMEM(average.shape, f32),
            pltpu.SMEM(ids.shape, jnp.int32),
            pltpu.SemaphoreType.DMA((1,)),
        ],
        compiler_params=limit(8),
        cost_estimate=cost(1.5),
        name="ready",
    )(average, hold(ids))

    t, mixed = call(
        functools.partial(mix_body, seqs, width), 1,
        [struct((own_i // 2, width * total, 2 * chans), bf16), struct((2, own_j, width * total), bf16)],
        [pltpu.VMEM((own_i * total, 128), f32)], *msgs, wq, pick,
    )
    square = struct((own_i, own_j, tri), bf16)
    flat = [pltpu.VMEM((own_i * own_j, tri), f32)]
    psum, norm, right = call(
        own_body, 2.4, [square, struct((own_i * own_j, chans), bf16), square], flat,
        raw, t, mixed, idt, bias, w_in,
    )
    far = move(right, lambda r, z: (r ^ 1, z) if keeper(r, z) else (r ^ 2, z ^ 1))
    left, gate = call(rest_body, 0.6, [square, struct(couple.shape, f32)], [], raw, norm, w_in, w_gate)
    other = call(
        functools.partial(other_body, seqs, width), 3, square,
        [pltpu.VMEM(t.shape, bf16), pltpu.VMEM((own_i * total, 128), f32)] + flat,
        *msgs, wq, raw_other, mixed, idt, bias, w_in,
    )
    p_other = move(other, beside)
    met, *_ = lax.optimization_barrier((met, other))
    met_left, met_right = call(met_body, 3, [square, square], flat, met, t, mixed, idt, bias, w_in)
    p_met = move(met_right, beside)
    far, *_ = lax.optimization_barrier((far, met_left))
    p_far = move(far, beside)

    def sums(own_pair, first, n, dtype):
        return call(
            functools.partial(sums_body, own_pair, first), 0.13 * n, struct((n, own_j, tri), dtype),
            [pltpu.VMEM((n, 2 * own_j, tri), f32)],
            right, other, p_other, met_right, p_met, far, p_far, left, met_left,
        )

    came = [move(sums(False, first, 8, bf16), lambda r, z: (r, z ^ 2)) for first in range(0, own_i, 8)]
    kept = sums(True, 0, own_i, f32)

    out = []
    for first, n in ((0, 16), (16, 16), (32, own_i - 32)):
        parts = came[first // 8 : (first + n) // 8]
        out = [pl.pallas_call(
            functools.partial(join_body, first, len(parts)),
            out_shape=struct(couple.shape, bf16),
            in_specs=[VMEM] * (4 + len(parts)) + [HBM] * len(out),
            out_specs=HBM,
            scratch_shapes=[pltpu.VMEM((n, own_j, chans), bf16), pltpu.SemaphoreType.DMA],
            input_output_aliases={4 + len(parts): 0} if out else {},
            compiler_params=limit(8),
            cost_estimate=cost(0.06 * n),
            name="join",
        )(kept, psum, gate, w_final, *parts, *out)]
    return out[0]


def shards(homolog, couple, ids, valid, bias, factors, average, w_in, w_gate, w_final):
    rows, cols = lax.axis_size("row"), lax.axis_size("col")
    own_seqs, residues, depth = homolog.shape
    own_i, own_j, chans = couple.shape
    width = factors.shape[1] // 2
    tri = w_final.shape[0]
    total = own_seqs * rows
    lanes = round_up(2 * own_seqs * width, 128)
    height = round_up(max(own_i, own_j), 16)
    paired = (rows, cols, own_seqs * width, chans, tri) == (4, 4, 64, 128, 128)
    if paired and own_i == own_j == 40:
        return paired_plan(homolog, couple, ids, valid, bias, factors, average, w_in, w_gate, w_final)
    scale = 8

    later = (average, valid, bias, couple)
    *msgs, average, valid, bias, couple = pl.pallas_call(
        functools.partial(align_body, own_i, own_j, rows),
        out_shape=[jax.ShapeDtypeStruct((height, lanes), bf16)] * rows
        + [jax.ShapeDtypeStruct(x.shape, x.dtype) for x in later],
        in_specs=[HBM] * 6,
        out_specs=[VMEM] * (rows + 4),
        scratch_shapes=[
            pltpu.VMEM(homolog.shape, bf16),
            pltpu.VMEM((2 * width, depth), bf16),
            pltpu.VMEM((own_seqs * residues, 2 * width), f32),
            pltpu.SemaphoreType.DMA((6,)),
        ],
        compiler_params=limit(8, scale),
        cost_estimate=cost(1.5),
        name="align",
    )(hold(homolog), hold(factors.T), *map(hold, later))
    msgs = [msgs[0]] + [
        lax.ppermute(msgs[d], "row", [(r, r ^ d) for r in range(rows)])
        for d in reversed(range(1, rows))
    ]

    base, mask, wq, pick = pl.pallas_call(
        functools.partial(prepare_body, own_seqs),
        out_shape=[jax.ShapeDtypeStruct((own_i, own_j, chans), f32),
                   jax.ShapeDtypeStruct((own_i, own_j, tri), bf16),
                   jax.ShapeDtypeStruct((width // 2, width, 2 * chans), bf16),
                   jax.ShapeDtypeStruct((rows, lanes, width * total), bf16)],
        in_specs=[VMEM, HBM, VMEM, VMEM, VMEM],
        out_specs=[VMEM] * 4,
        scratch_shapes=[
            pltpu.VMEM(average.shape, f32),
            pltpu.VMEM((own_j, chans), jnp.int32),
            pltpu.SMEM(ids.shape, jnp.int32),
            pltpu.SemaphoreType.DMA((1,)),
        ],
        compiler_params=limit(8, scale),
        cost_estimate=cost(2),
        name="prepare",
    )(couple, hold(ids), valid, bias, average)

    extents = (own_i, own_j)
    psum, norm, right = pl.pallas_call(
        functools.partial(pair_body, own_seqs, width, rows),
        out_shape=[jax.ShapeDtypeStruct((own_i, own_j, chans), bf16),
                   jax.ShapeDtypeStruct((own_i * own_j, chans), bf16),
                   jax.ShapeDtypeStruct(extents + (tri,), bf16)],
        in_specs=[VMEM] * (rows + 5),
        out_specs=[VMEM] * 3,
        scratch_shapes=[
            pltpu.VMEM((own_i * total, 128), f32),
            pltpu.VMEM((own_i // 2, width * total, 2 * chans), bf16),
        ],
        compiler_params=limit(16, scale),
        cost_estimate=cost(4.5),
        name="pair",
    )(*msgs, base, mask, wq, pick, w_in)

    cuts = [own_i]
    lefts = pl.pallas_call(
        left_body,
        out_shape=[jax.ShapeDtypeStruct((n, own_j, tri), bf16) for n in cuts],
        in_specs=[VMEM] * 3,
        out_specs=[VMEM] * len(cuts),
        compiler_params=limit(8, scale),
        cost_estimate=cost(1),
        name="left",
    )(norm, mask, w_in)
    return gathered_plan(lefts[0], right, psum, norm, w_gate, w_final)


def solution(mesh):
    placed = (
        P(("grp", "row"), None, None),
        P(("grp", "row"), "col", None),
        P("grp"),
        P(("grp", "row"), "col"),
        P(),
        P(),
        P(),
        P(),
        P(),
        P(),
    )
    return jax.shard_map(
        shards,
        mesh=mesh,
        in_specs=placed,
        out_specs=P(("grp", "row"), "col", None),
        check_vma=False,
    )
```

```python
import functools

import jax
import jax.numpy as jnp
from jax import lax
from jax.experimental import pallas as pl
from jax.experimental.pallas import tpu as pltpu
from jax.sharding import PartitionSpec as P

eps = 1e-05
f32 = jnp.float32
bf16 = jnp.bfloat16
VMEM = pl.BlockSpec(memory_space=pltpu.VMEM)
SMEM = pl.BlockSpec(memory_space=pltpu.SMEM)
HBM = pl.BlockSpec(memory_space=pltpu.HBM)


def limit(mib, scale=1):
    return pltpu.CompilerParams(vmem_limit_bytes=min(56, mib * scale) * 1024 * 1024)


def round_up(n, m):
    return (n + m - 1) // m * m


def cost(us):
    return pl.CostEstimate(flops=0, bytes_accessed=int(us * 3.69e6), transcendentals=0)


def hold(x):
    return pltpu.with_memory_space_constraint(x, pltpu.HBM)


def fetch(pairs, sem):
    copies = [pltpu.make_async_copy(src, dst, sem.at[n]) for n, (src, dst) in enumerate(pairs)]
    for copy in copies:
        copy.start()
    return copies


def standardize(values):
    centre = values - jnp.mean(values, axis=-1, keepdims=True)
    spread = jnp.mean(centre * centre, axis=-1, keepdims=True)
    return centre * lax.rsqrt(spread + eps)


def sigmoid(v):
    return 0.5 * jnp.tanh(0.5 * v) + 0.5


def align_body(own_i, own_j, count, x_hbm, w_hbm, *refs):
    later, outs, refs = refs[:4], refs[4 : 4 + count], refs[4 + count :]
    brought, (x_ref, w_ref, y_ref, sem) = refs[:4], refs[4:]
    copies = fetch([(x_hbm, x_ref), (w_hbm, w_ref), *zip(later, brought)], sem)
    seqs, residues, depth = x_ref.shape
    width = w_ref.shape[0] // 2
    height, lanes = outs[0].shape
    me = lax.axis_index("row")
    z = lax.axis_index("col")
    copies[0].wait()
    x = x_ref[...].astype(f32).reshape(seqs * residues, depth)
    normed = standardize(x).astype(bf16)
    copies[1].wait()
    y_ref[...] = lax.dot_general(
        normed, w_ref[...], (((1,), (1,)), ((), ())), preferred_element_type=f32
    )
    start = pl.multiple_of(z * own_j, 8)

    def tall(v):
        gap = height - v.shape[0]
        return jnp.concatenate([v, jnp.zeros((gap, v.shape[1]), f32)], axis=0) if gap else v

    right = [tall(y_ref[pl.ds(s * residues + start, own_j), width:]) for s in range(seqs)]
    gap = lanes - 2 * seqs * width
    right += [jnp.zeros((height, gap), f32)] if gap else []
    for d, out in enumerate(outs):
        first = pl.multiple_of((me ^ d) * own_i, 8)
        left = [tall(y_ref[pl.ds(s * residues + first, own_i), :width]) for s in range(seqs)]
        out[...] = jnp.concatenate(left + right, axis=1).astype(bf16)
    for copy in copies[2:]:
        copy.wait()


def prepare_body(seqs, couple_ref, ids_hbm, valid_ref, bias_ref, avg_ref, base_ref, mask_ref, wq_ref, pick_ref,
                 wf_ref, idc_ref, ids_ref, sem):
    (copy,) = fetch([(ids_hbm, ids_ref)], sem)
    own_i, own_j, chans = couple_ref.shape
    pairs, width, _ = wq_ref.shape
    blocks, lanes, _ = pick_ref.shape
    total = blocks * seqs
    x0 = lax.axis_index("row") * own_i
    z0 = lax.axis_index("col") * own_j

    row = lax.broadcasted_iota(jnp.int32, pick_ref.shape[1:], 0)
    col = lax.broadcasted_iota(jnp.int32, pick_ref.shape[1:], 1)
    unit = row - seqs * width
    place = lax.rem(unit, width) * total + lax.div(unit, width)
    place = jnp.where((unit >= 0) & (unit < seqs * width), col - place, -1)

    def pick(r, carry):
        pick_ref[r] = jnp.where(place == r * seqs, 1.0, 0.0).astype(bf16)
        return carry

    lax.fori_loop(0, blocks, pick, 0)
    wf_ref[...] = avg_ref[...].astype(f32)
    for h in range(pairs):
        both = [wf_ref[pl.ds(2 * h + d, width, stride=width), :] for d in range(2)]
        wq_ref[h] = jnp.concatenate(both, axis=1).astype(bf16)
    copy.wait()
    for j in range(own_j):
        idc_ref[pl.ds(j, 1), :] = jnp.full((1, chans), ids_ref[z0 + j], jnp.int32)
    idc = idc_ref[...]
    valid_t = valid_ref[...].astype(f32).T
    lane = lax.broadcasted_iota(jnp.int32, valid_t.shape, 1)
    same_bias = bias_ref[0:1, :]
    cross_bias = bias_ref[1:2, :]

    def rows(i, carry):
        bias = jnp.where(idc == ids_ref[x0 + i], same_bias, cross_bias)
        base_ref[i] = couple_ref[i].astype(f32) + bias
        column = jnp.sum(jnp.where(lane == i, valid_t, 0.0), axis=1, keepdims=True)
        mask_ref[i] = jnp.broadcast_to(column, (own_j, mask_ref.shape[2])).astype(bf16)
        return carry

    lax.fori_loop(0, own_i, rows, 0, unroll=8)


def pair_body(seqs, width, blocks, *refs):
    msgs = refs[:blocks]
    base_ref, mask_ref, wq_ref, pick_ref, win_ref = refs[blocks : blocks + 5]
    psum_ref, norm_ref, right_ref = refs[blocks + 5 : blocks + 8]
    xl_ref, t_ref = refs[blocks + 8 :]
    own_i, own_j, chans = base_ref.shape
    height, lanes = msgs[0].shape
    total = seqs * blocks
    tri = win_ref.shape[1] // 4
    half = own_i // 2

    for r in range(blocks):
        m = msgs[r][pl.ds(0, own_i), :].astype(f32)
        for s in range(seqs):
            moved = m if s == 0 else pltpu.roll(m, lanes - s * width, 1)
            xl_ref[pl.ds(r * seqs + s, own_i, stride=total), :] = moved[:, :128]
    lhs = xl_ref[:, :width].astype(bf16)

    joined = jnp.concatenate([msg[...] for msg in msgs], axis=1)
    picks = pick_ref[...].reshape(blocks * lanes, width * total)
    rmat = jnp.dot(joined, picks, preferred_element_type=f32)[:own_j].astype(bf16)

    def expand(h, carry):
        out = jnp.dot(lhs, wq_ref[h], preferred_element_type=f32)
        parts = [out[:, d * chans : (d + 1) * chans].reshape(own_i, total, chans) for d in range(2)]
        block = jnp.concatenate(parts, axis=1).astype(bf16)
        where = pl.ds(pl.multiple_of(h * 2 * total, 16), 2 * total)
        t_ref[:, where, :chans] = block[:half]
        t_ref[:, where, chans:] = block[half:]
        return carry

    lax.fori_loop(0, width // 2, expand, 0)

    step = 4 if half % 4 == 0 else 1

    def rows(b, carry):
        normed = [[], []]
        for g in range(step):
            i = b * step + g
            both = jnp.dot(rmat, t_ref[i], preferred_element_type=f32) * (1.0 / total)
            for side in range(2):
                at = i + side * half
                psum = (base_ref[at] + both[:, side * chans : (side + 1) * chans]).astype(bf16)
                psum_ref[at] = psum
                normed[side].append(standardize(psum.astype(f32)))
        flat = jnp.concatenate(normed[0] + normed[1], axis=0).astype(bf16)
        proj = jnp.dot(flat, win_ref[:, 2 * tri :], preferred_element_type=f32)
        count = step * own_j
        for side in range(2):
            cut = slice(side * count, (side + 1) * count)
            i0 = b * step + side * half
            norm_ref[pl.ds(pl.multiple_of(i0 * own_j, 16), count), :] = flat[cut]
            mask = mask_ref[pl.ds(i0, step)].astype(f32).reshape(count, tri)
            right = mask * sigmoid(proj[cut, :tri]) * proj[cut, tri:]
            right_ref[pl.ds(i0, step)] = right.reshape(step, own_j, tri).astype(bf16)
        return carry

    lax.fori_loop(0, half // step, rows, 0)


def left_body(norm_ref, mask_ref, win_ref, *outs):
    own_i, own_j, tri = mask_ref.shape
    group = 8 if own_i % 8 == 0 else 1
    at = 0
    for out in outs:
        first = at

        def rows(b, carry):
            i0 = first + b * group
            flat = norm_ref[pl.ds(pl.multiple_of(i0 * own_j, 16), group * own_j), :]
            mask = mask_ref[pl.ds(i0, group)].astype(f32).reshape(group * own_j, tri)
            proj = jnp.dot(flat, win_ref[:, : 2 * tri], preferred_element_type=f32)
            left = mask * sigmoid(proj[:, :tri]) * proj[:, tri:]
            out[pl.ds(b * group, group)] = left.reshape(group, own_j, tri).astype(bf16)
            return carry

        lax.fori_loop(0, out.shape[0] // group, rows, 0, unroll=True)
        at += out.shape[0]


def contract(lf_ref, halves, i0, group):
    step = 8
    acc = (jnp.zeros(halves[0].shape[1:], f32),) * group
    for h, r_ref in enumerate(halves):
        depth = r_ref.shape[0]

        def add(kb, acc):
            k0 = kb * step
            acc = list(acc)
            for d in range(step):
                right = r_ref[k0 + d].astype(f32)
                for t in range(group):
                    acc[t] = acc[t] + lf_ref[i0 + t, pl.ds(h * depth + k0 + d, 1), :] * right
            return tuple(acc)

        acc = lax.fori_loop(0, depth // step, add, acc)
    return acc


def sums_body(own_pair, first, own_ref, other_ref, p_other, met_ref, p_met, far_ref, p_far, l_ref, m_ref, o_ref, lf_ref):
    count, depth = o_ref.shape[0], l_ref.shape[1]
    group = 8
    lf_ref[:, pl.ds(0, depth), :] = l_ref[pl.ds(first, count)].astype(f32)
    lf_ref[:, pl.ds(depth, depth), :] = m_ref[pl.ds(first, count)].astype(f32)

    def use(halves):
        def rows(b, carry):
            acc = contract(lf_ref, halves, b * group, group)
            for t in range(group):
                o_ref[b * group + t] = acc[t].astype(o_ref.dtype)
            return carry

        lax.fori_loop(0, count // group, rows, 0)

    r, z = lax.axis_index("row"), lax.axis_index("col")
    keeper = (r % 2) == (z % 2)
    near = ((r // 2) == (z // 2)) == own_pair
    table = [
        (near & keeper, own_ref, met_ref),
        (near & ~keeper, far_ref, p_met),
        (~near & keeper, p_other, far_ref),
        (~near & ~keeper, other_ref, p_far),
    ]
    for cond, a, b in table:
        pl.when(cond)(functools.partial(use, (a, b)))


def open_body(x_hbm, w_hbm, valid_hbm, couple_hbm, *refs):
    later, outs, brought = refs[:5], refs[5:9], refs[9:14]
    block_ref, longer_ref, x_ref, w_ref, valid_ref, y_ref, sem = refs[14:]
    own_i, own_j, chans = couple_hbm.shape
    copies = fetch([(x_hbm, x_ref), (w_hbm, w_ref), (valid_hbm, valid_ref),
                    (couple_hbm, block_ref.at[pl.ds(0, own_i)]),
                    (couple_hbm, longer_ref.at[pl.ds(0, own_i)]), *zip(later, brought)], sem)
    seqs, residues, depth = x_ref.shape
    width = w_ref.shape[0] // 2
    height, lanes = outs[0].shape
    me = lax.axis_index("row")
    z = lax.axis_index("col")
    copies[0].wait()
    x = x_ref[...].astype(f32).reshape(seqs * residues, depth)
    normed = standardize(x).astype(bf16)
    copies[1].wait()
    y_ref[...] = lax.dot_general(
        normed, w_ref[...], (((1,), (1,)), ((), ())), preferred_element_type=f32
    )

    def cut(start, lane):
        start = pl.multiple_of(start * own_i, 8)
        return [y_ref[pl.ds(s * residues + start, own_i), lane : lane + width] for s in range(seqs)]

    shared = cut(z, width) + cut(z ^ 1, width)
    below = jnp.zeros((height - own_i, lanes), f32)
    for d, out in enumerate(outs):
        other = ((me ^ d) // 2 ^ 1) * 2 + z % 2
        rows = jnp.concatenate(cut(me ^ d, 0) + cut(other, 0) + shared, axis=1)
        out[...] = jnp.concatenate([rows, below], axis=0).astype(bf16)
    copies[2].wait()
    mask = valid_ref[...].astype(f32).T
    mask = jnp.concatenate([mask, jnp.zeros((own_j, chans - own_i), f32)], axis=1)
    block_ref[own_i] = mask.astype(bf16)
    for n in range(own_i, longer_ref.shape[0]):
        longer_ref[n] = mask.astype(bf16)
    for copy in copies[3:]:
        copy.wait()


def ready_body(seqs, avg_ref, ids_hbm, wq_ref, pick_ref, idt_ref, wf_ref, ids_ref, sem):
    (copy,) = fetch([(ids_hbm, ids_ref)], sem)
    pairs, width, _ = wq_ref.shape
    kinds, blocks, lanes, _ = pick_ref.shape
    total = blocks * seqs
    row = lax.broadcasted_iota(jnp.int32, pick_ref.shape[2:], 0)
    col = lax.broadcasted_iota(jnp.int32, pick_ref.shape[2:], 1)
    for n in range(kinds):
        unit = row - n * seqs * width
        place = lax.rem(unit, width) * total + lax.div(unit, width)
        place = jnp.where((unit >= 0) & (unit < seqs * width), col - place, -1)
        for r in range(blocks):
            pick_ref[n, r] = jnp.where(place == r * seqs, 1.0, 0.0).astype(bf16)
    wf_ref[...] = avg_ref[...].astype(f32)
    for h in range(pairs):
        both = [wf_ref[pl.ds(2 * h + d, width, stride=width), :] for d in range(2)]
        wq_ref[h] = jnp.concatenate(both, axis=1).astype(bf16)
    copy.wait()

    def spread(n, carry):
        idt_ref[pl.ds(n, 1), :] = jnp.full((1, idt_ref.shape[1]), ids_ref[n], jnp.int32)
        return carry

    lax.fori_loop(0, idt_ref.shape[0], spread, 0, unroll=8)


def mix_rows(seqs, width, lane0, msgs, wq_ref, t_ref, xl_ref):
    half, terms, both = t_ref.shape
    chans, own_i, total = both // 2, 2 * half, seqs * 4
    for r in range(4):
        m = msgs[r][:, :128].astype(f32)[:own_i]
        for s in range(seqs):
            lane = lane0 + s * width
            moved = pltpu.roll(m, 128 - lane, 1) if lane else m
            xl_ref[pl.ds(r * seqs + s, own_i, stride=total), :] = moved
    lhs = xl_ref[:, :width].astype(bf16)
    for h in range(width // 2):
        out = jnp.dot(lhs, wq_ref[h], preferred_element_type=f32)
        parts = [out[:, d * chans : (d + 1) * chans].reshape(own_i, total, chans) for d in range(2)]
        block = jnp.concatenate(parts, axis=1).astype(bf16)
        where = pl.ds(h * 2 * total, 2 * total)
        t_ref[:, where, :chans] = block[:half]
        t_ref[:, where, chans:] = block[half:]


def mix_body(seqs, width, *refs):
    msgs, (wq_ref, pick_ref, t_ref, right_ref, xl_ref) = refs[:4], refs[4:]
    own_j, terms = right_ref.shape[1:]
    joined = jnp.concatenate([msg[:, 128:] for msg in msgs], axis=1)
    for n in range(2):
        right = jnp.dot(joined, pick_ref[n].reshape(512, terms), preferred_element_type=f32)[:own_j]
        right_ref[n] = (right * (1.0 / (seqs * 4))).astype(bf16)
    mix_rows(seqs, width, 0, msgs, wq_ref, t_ref, xl_ref)


def block_norms(block_ref, t_ref, right, row0, col0, idt_ref, bias_ref, use):
    half, terms, _ = t_ref.shape
    own_i, own_j, chans = 2 * half, right.shape[0], bias_ref.shape[1]
    idc = idt_ref[pl.ds(pl.multiple_of(col0, 8), own_j), :]
    step = 4
    for b in range(half // step):
        rows, psums = [[], []], [[], []]
        for i in range(b * step, b * step + step):
            both = jnp.dot(right, t_ref[i], preferred_element_type=f32)
            for side in range(2):
                at = i + side * half
                same = idc == idt_ref[pl.ds(row0 + at, 1), :]
                base = block_ref[at].astype(f32) + jnp.where(same, bias_ref[0:1, :], bias_ref[1:2, :])
                rows[side].append(at)
                psums[side].append((base + both[:, side * chans : (side + 1) * chans]).astype(bf16))
        rows, psums = rows[0] + rows[1], psums[0] + psums[1]
        flat = jnp.concatenate([standardize(p.astype(f32)) for p in psums], axis=0).astype(bf16)
        use(rows, psums, flat)


def gated(block_ref, rows, flat, w_ref):
    own_j = block_ref.shape[1]
    tri = w_ref.shape[1] // 2
    mask = block_ref[block_ref.shape[0] - 1].astype(f32)
    proj = jnp.dot(flat, w_ref[...], preferred_element_type=f32)
    both = sigmoid(proj[:, :tri]) * proj[:, tri:]
    return [mask[:, at : at + 1] * both[n * own_j : (n + 1) * own_j] for n, at in enumerate(rows)]


def own_body(block_ref, t_ref, right_ref, idt_ref, bias_ref, win_ref, psum_ref, norm_ref, out_ref, flat_ref):
    own_i, own_j, chans = psum_ref.shape
    r, z = lax.axis_index("row"), lax.axis_index("col")
    side = win_ref.shape[1] // 2
    w_right = win_ref.at[:, pl.ds(side, side)]

    def use(rows, psums, flat):
        rights = gated(block_ref, rows, flat, w_right)
        some = len(rows) // 2
        for n in (0, some):
            norm_ref[pl.ds(rows[n] * own_j, some * own_j), :] = flat[n * own_j : (n + some) * own_j]
        for n, at in enumerate(rows):
            psum_ref[at] = psums[n]
            flat_ref[pl.ds(at * own_j, own_j), :] = rights[n]

    block_norms(block_ref, t_ref, right_ref[0], r * own_i, z * own_j, idt_ref, bias_ref, use)
    for k in range(own_j):
        out_ref[k] = flat_ref[pl.ds(k, own_i, stride=own_j), :].astype(bf16)


def rest_body(block_ref, norm_ref, win_ref, wgate_ref, left_ref, gate_ref):
    own_i, own_j, _ = left_ref.shape
    w_left = win_ref.at[:, pl.ds(0, win_ref.shape[1] // 2)]
    group = 8
    for i in range(0, own_i, group):
        flat = norm_ref[pl.ds(i * own_j, group * own_j), :]
        rows = list(range(i, i + group))
        gate = sigmoid(jnp.dot(flat, wgate_ref[...], preferred_element_type=f32))
        for n, left in enumerate(gated(block_ref, rows, flat, w_left)):
            left_ref[i + n] = left.astype(bf16)
            gate_ref[i + n] = gate[n * own_j : (n + 1) * own_j]


def mix_other_body(seqs, width, *refs):
    msgs, (wq_ref, t_ref, xl_ref) = refs[:4], refs[4:]

    @pl.when((lax.axis_index("row") % 2) != (lax.axis_index("col") % 2))
    def _():
        mix_rows(seqs, width, seqs * width, msgs, wq_ref, t_ref, xl_ref)


def other_body(block_ref, t_ref, right_ref, idt_ref, bias_ref, win_ref, out_ref, flat_ref):
    own_j, own_i, _ = out_ref.shape
    r, z = lax.axis_index("row"), lax.axis_index("col")
    side = win_ref.shape[1] // 2
    w_right = win_ref.at[:, pl.ds(side, side)]

    def use(rows, psums, flat):
        for at, right in zip(rows, gated(block_ref, rows, flat, w_right)):
            flat_ref[pl.ds(at * own_j, own_j), :] = right

    @pl.when((r % 2) != (z % 2))
    def _():
        block_norms(block_ref, t_ref, right_ref[0], (r ^ 3) * own_i, z * own_j, idt_ref, bias_ref, use)
        for k in range(own_j):
            out_ref[k] = flat_ref[pl.ds(k, own_i, stride=own_j), :].astype(bf16)


def met_body(block_ref, t_ref, right_ref, idt_ref, bias_ref, win_ref, left_ref, out_ref, flat_ref):
    own_i, own_j, _ = left_ref.shape
    r, z = lax.axis_index("row"), lax.axis_index("col")
    side = win_ref.shape[1] // 2
    w_left, w_right = win_ref.at[:, pl.ds(0, side)], win_ref.at[:, pl.ds(side, side)]

    def use(rows, psums, flat):
        lefts = gated(block_ref, rows, flat, w_left)
        rights = gated(block_ref, rows, flat, w_right)
        for n, at in enumerate(rows):
            left_ref[at] = lefts[n].astype(bf16)
            flat_ref[pl.ds(at * own_j, own_j), :] = rights[n]

    block_norms(block_ref, t_ref, right_ref[1], r * own_i, (z ^ 1) * own_j, idt_ref, bias_ref, use)
    for k in range(own_j):
        out_ref[k] = flat_ref[pl.ds(k, own_i, stride=own_j), :].astype(bf16)


def join_body(first, parts, own_ref, psum_ref, gate_ref, w_ref, *refs):
    sums, (out_hbm, done_ref, sem) = refs[:parts], refs[-3:]
    count, extent, chans = done_ref.shape
    group = 8
    at = 0
    for sum_ref in sums:
        start = at

        def rows(b, carry):
            here = pl.ds(start + b * group, group)
            there = pl.ds(first + start + b * group, group)
            mixed = own_ref[there] + sum_ref[pl.ds(b * group, group)].astype(f32)
            normed = standardize(mixed).reshape(group * extent, -1).astype(bf16)
            update = jnp.dot(normed, w_ref[...], preferred_element_type=f32).reshape(group, extent, -1)
            done_ref[here] = (psum_ref[there].astype(f32) + gate_ref[there] * update).astype(bf16)
            return carry

        lax.fori_loop(0, sum_ref.shape[0] // group, rows, 0, unroll=True)
        at += sum_ref.shape[0]
    copy = pltpu.make_async_copy(done_ref, out_hbm.at[pl.ds(first, count)], sem)
    copy.start()
    copy.wait()


def triangle_body(l_ref, r_ref, o_ref, lf_ref, flat_ref, rk_ref):
    own_i, depth, chans = l_ref.shape
    extent = r_ref.shape[0]
    group = 8 if own_i % 8 == 0 else 1

    @pl.when(pl.program_id(0) == 0)
    def _():
        lf_ref[...] = l_ref[...].astype(f32)

    def widen(j, carry):
        flat_ref[pl.ds(pl.multiple_of(j * depth, 8), depth), :] = r_ref[j].astype(f32)
        return carry

    lax.fori_loop(0, extent, widen, 0)

    def turn(k, carry):
        rk_ref[k] = flat_ref[pl.ds(k, extent, stride=depth), :]
        return carry

    lax.fori_loop(0, depth, turn, 0)

    def rows(b, carry):
        i0 = b * group
        acc = contract(lf_ref, [rk_ref], i0, group)
        for t in range(group):
            o_ref[0, i0 + t] = acc[t].astype(bf16)
        return carry

    lax.fori_loop(0, own_i // group, rows, 0)


def finish_body(sum_ref, psum_ref, norm_ref, wgate_ref, w_ref, out_ref):
    parts, own_i, extent, chans = sum_ref.shape
    own_j = psum_ref.shape[1]

    def row(i, carry):
        flat = norm_ref[pl.ds(pl.multiple_of(i * own_j, 16), own_j), :]
        gate = sigmoid(jnp.dot(flat, wgate_ref[...], preferred_element_type=f32))
        normed = [standardize(sum_ref[part, i].astype(f32)) for part in range(parts)]
        normed = jnp.concatenate(normed, axis=0).astype(bf16)
        update = jnp.dot(normed, w_ref[...], preferred_element_type=f32)
        out_ref[i] = (psum_ref[i].astype(f32) + gate * update).astype(bf16)
        return carry

    lax.fori_loop(0, own_i, row, 0)


def gathered_plan(left, right, psum, norm, w_gate, w_final):
    own_i, own_j, chans = psum.shape
    rows = lax.axis_size("row")
    tri = w_final.shape[0]
    right_all = lax.all_gather(right, "row", axis=0, tiled=True)
    partial = pl.pallas_call(
        triangle_body,
        grid=(rows,),
        out_shape=jax.ShapeDtypeStruct((rows, own_i, own_i, tri), bf16),
        in_specs=[
            pl.BlockSpec((own_i, own_j, tri), lambda r: (0, 0, 0)),
            pl.BlockSpec((own_i, own_j, tri), lambda r: (r, 0, 0)),
        ],
        out_specs=pl.BlockSpec((1, own_i, own_i, tri), lambda r: (r, 0, 0, 0)),
        scratch_shapes=[
            pltpu.VMEM((own_i, own_j, tri), f32),
            pltpu.VMEM((own_i * own_j, tri), f32),
            pltpu.VMEM((own_j, own_i, tri), f32),
        ],
        compiler_params=limit(56),
        name="triangle",
    )(left, right_all)
    summed = lax.psum_scatter(partial, "col", scatter_dimension=0, tiled=True)
    return pl.pallas_call(
        finish_body,
        out_shape=jax.ShapeDtypeStruct((own_i, own_j, chans), bf16),
        in_specs=[VMEM] * 5,
        out_specs=VMEM,
        compiler_params=limit(56),
        name="finish",
    )(summed, psum, norm, w_gate, w_final)


def paired_plan(homolog, couple, ids, valid, bias, factors, average, w_in, w_gate, w_final):
    seqs, residues, depth = homolog.shape
    own_i, own_j, chans = couple.shape
    width = factors.shape[1] // 2
    tri = w_final.shape[0]
    total = seqs * 4
    cells = [(r, z) for r in range(4) for z in range(4)]
    struct = jax.ShapeDtypeStruct

    def move(value, step):
        pairs = [(r * 4 + z, step(r, z)) for r, z in cells]
        pairs = [(src, r * 4 + z) for src, (r, z) in pairs]
        return lax.ppermute(value, ("row", "col"), pairs)

    def call(body, us, out_shape, scratch, *args, mib=12):
        return pl.pallas_call(
            body,
            out_shape=out_shape,
            in_specs=[VMEM] * len(args),
            out_specs=[VMEM] * len(out_shape) if isinstance(out_shape, list) else VMEM,
            scratch_shapes=scratch,
            compiler_params=limit(mib),
            cost_estimate=cost(us),
            name=getattr(body, "func", body).__name__.removesuffix("_body"),
        )(*args)

    keeper = lambda r, z: r % 2 == z % 2
    beside = lambda r, z: (r ^ 1, z)
    height, lanes = round_up(own_i, 16), 256
    block = struct((own_i + 1, own_j, chans), bf16)
    longer = struct((own_i + 3, own_j, chans), bf16)
    later = (average, bias, w_in, w_gate, w_final)
    *msgs, average, bias, w_in, w_gate, w_final, raw, raw_z = pl.pallas_call(
        open_body,
        out_shape=[struct((height, lanes), bf16)] * 4 + [struct(x.shape, x.dtype) for x in later] + [block, longer],
        in_specs=[HBM] * 9,
        out_specs=[VMEM] * 11,
        scratch_shapes=[
            pltpu.VMEM(homolog.shape, bf16),
            pltpu.VMEM((2 * width, depth), bf16),
            pltpu.VMEM(valid.shape, jnp.int32),
            pltpu.VMEM((seqs * residues, 2 * width), f32),
            pltpu.SemaphoreType.DMA((10,)),
        ],
        compiler_params=limit(8),
        cost_estimate=cost(1.5),
        name="open",
    )(*map(hold, (homolog, factors.T, valid, couple) + later))
    msgs = [msgs[0]] + [
        lax.ppermute(msgs[d], "row", [(r, r ^ d) for r in range(4)]) for d in (1, 2, 3)
    ]
    met = move(raw_z, lambda r, z: (r, z ^ 1))
    raw_other = move(raw, lambda r, z: (r ^ 3, z) if keeper(r, z) else (r ^ 1, z))

    wq, pick, idt = pl.pallas_call(
        functools.partial(ready_body, seqs),
        out_shape=[struct((width // 2, width, 2 * chans), bf16),
                   struct((2, 4, 128, width * total), bf16),
                   struct((residues, 128), jnp.int32)],
        in_specs=[VMEM, HBM],
        out_specs=[VMEM] * 3,
        scratch_shapes=[
            pltpu.VMEM(average.shape, f32),
            pltpu.SMEM(ids.shape, jnp.int32),
            pltpu.SemaphoreType.DMA((1,)),
        ],
        compiler_params=limit(8),
        cost_estimate=cost(1.5),
        name="ready",
    )(average, hold(ids))

    t, mixed = call(
        functools.partial(mix_body, seqs, width), 1,
        [struct((own_i // 2, width * total, 2 * chans), bf16), struct((2, own_j, width * total), bf16)],
        [pltpu.VMEM((own_i * total, 128), f32)], *msgs, wq, pick,
    )
    square = struct((own_i, own_j, tri), bf16)
    flat = [pltpu.VMEM((own_i * own_j, tri), f32)]
    psum, norm, right = call(
        own_body, 2.4, [square, struct((own_i * own_j, chans), bf16), square], flat,
        raw, t, mixed, idt, bias, w_in,
    )
    far = move(right, lambda r, z: (r ^ 1, z) if keeper(r, z) else (r ^ 2, z ^ 1))
    left, gate = call(rest_body, 0.6, [square, struct(couple.shape, f32)], [], raw, norm, w_in, w_gate)
    msgs, right = lax.optimization_barrier((msgs, right))
    t_other = call(
        functools.partial(mix_other_body, seqs, width), 1, struct(t.shape, bf16),
        [pltpu.VMEM((own_i * total, 128), f32)], *msgs, wq,
    )
    other = call(other_body, 2.4, square, flat, raw_other, t_other, mixed, idt, bias, w_in)
    p_other = move(other, beside)
    met, *_ = lax.optimization_barrier((met, other))
    met_left, met_right = call(met_body, 3, [square, square], flat, met, t, mixed, idt, bias, w_in)
    p_met = move(met_right, beside)
    far, *_ = lax.optimization_barrier((far, met_left))
    p_far = move(far, beside)

    def sums(own_pair, first, n, dtype):
        return call(
            functools.partial(sums_body, own_pair, first), 0.13 * n, struct((n, own_j, tri), dtype),
            [pltpu.VMEM((n, 2 * own_j, tri), f32)],
            right, other, p_other, met_right, p_met, far, p_far, left, met_left,
        )

    came = [move(sums(False, first, 8, bf16), lambda r, z: (r, z ^ 2)) for first in range(0, own_i, 8)]
    kept = sums(True, 0, own_i, f32)

    out = []
    for first, n in ((0, 16), (16, 16), (32, own_i - 32)):
        parts = came[first // 8 : (first + n) // 8]
        out = [pl.pallas_call(
            functools.partial(join_body, first, len(parts)),
            out_shape=struct(couple.shape, bf16),
            in_specs=[VMEM] * (4 + len(parts)) + [HBM] * len(out),
            out_specs=HBM,
            scratch_shapes=[pltpu.VMEM((n, own_j, chans), bf16), pltpu.SemaphoreType.DMA],
            input_output_aliases={4 + len(parts): 0} if out else {},
            compiler_params=limit(8),
            cost_estimate=cost(0.06 * n),
            name="join",
        )(kept, psum, gate, w_final, *parts, *out)]
    return out[0]


def shards(homolog, couple, ids, valid, bias, factors, average, w_in, w_gate, w_final):
    rows, cols = lax.axis_size("row"), lax.axis_size("col")
    own_seqs, residues, depth = homolog.shape
    own_i, own_j, chans = couple.shape
    width = factors.shape[1] // 2
    tri = w_final.shape[0]
    total = own_seqs * rows
    lanes = round_up(2 * own_seqs * width, 128)
    height = round_up(max(own_i, own_j), 16)
    paired = (rows, cols, own_seqs * width, chans, tri) == (4, 4, 64, 128, 128)
    if paired and own_i == own_j == 40:
        return paired_plan(homolog, couple, ids, valid, bias, factors, average, w_in, w_gate, w_final)
    scale = 8

    later = (average, valid, bias, couple)
    *msgs, average, valid, bias, couple = pl.pallas_call(
        functools.partial(align_body, own_i, own_j, rows),
        out_shape=[jax.ShapeDtypeStruct((height, lanes), bf16)] * rows
        + [jax.ShapeDtypeStruct(x.shape, x.dtype) for x in later],
        in_specs=[HBM] * 6,
        out_specs=[VMEM] * (rows + 4),
        scratch_shapes=[
            pltpu.VMEM(homolog.shape, bf16),
            pltpu.VMEM((2 * width, depth), bf16),
            pltpu.VMEM((own_seqs * residues, 2 * width), f32),
            pltpu.SemaphoreType.DMA((6,)),
        ],
        compiler_params=limit(8, scale),
        cost_estimate=cost(1.5),
        name="align",
    )(hold(homolog), hold(factors.T), *map(hold, later))
    msgs = [msgs[0]] + [
        lax.ppermute(msgs[d], "row", [(r, r ^ d) for r in range(rows)])
        for d in reversed(range(1, rows))
    ]

    base, mask, wq, pick = pl.pallas_call(
        functools.partial(prepare_body, own_seqs),
        out_shape=[jax.ShapeDtypeStruct((own_i, own_j, chans), f32),
                   jax.ShapeDtypeStruct((own_i, own_j, tri), bf16),
                   jax.ShapeDtypeStruct((width // 2, width, 2 * chans), bf16),
                   jax.ShapeDtypeStruct((rows, lanes, width * total), bf16)],
        in_specs=[VMEM, HBM, VMEM, VMEM, VMEM],
        out_specs=[VMEM] * 4,
        scratch_shapes=[
            pltpu.VMEM(average.shape, f32),
            pltpu.VMEM((own_j, chans), jnp.int32),
            pltpu.SMEM(ids.shape, jnp.int32),
            pltpu.SemaphoreType.DMA((1,)),
        ],
        compiler_params=limit(8, scale),
        cost_estimate=cost(2),
        name="prepare",
    )(couple, hold(ids), valid, bias, average)

    extents = (own_i, own_j)
    psum, norm, right = pl.pallas_call(
        functools.partial(pair_body, own_seqs, width, rows),
        out_shape=[jax.ShapeDtypeStruct((own_i, own_j, chans), bf16),
                   jax.ShapeDtypeStruct((own_i * own_j, chans), bf16),
                   jax.ShapeDtypeStruct(extents + (tri,), bf16)],
        in_specs=[VMEM] * (rows + 5),
        out_specs=[VMEM] * 3,
        scratch_shapes=[
            pltpu.VMEM((own_i * total, 128), f32),
            pltpu.VMEM((own_i // 2, width * total, 2 * chans), bf16),
        ],
        compiler_params=limit(16, scale),
        cost_estimate=cost(4.5),
        name="pair",
    )(*msgs, base, mask, wq, pick, w_in)

    cuts = [own_i]
    lefts = pl.pallas_call(
        left_body,
        out_shape=[jax.ShapeDtypeStruct((n, own_j, tri), bf16) for n in cuts],
        in_specs=[VMEM] * 3,
        out_specs=[VMEM] * len(cuts),
        compiler_params=limit(8, scale),
        cost_estimate=cost(1),
        name="left",
    )(norm, mask, w_in)
    return gathered_plan(lefts[0], right, psum, norm, w_gate, w_final)


def solution(mesh):
    placed = (
        P(("grp", "row"), None, None),
        P(("grp", "row"), "col", None),
        P("grp"),
        P(("grp", "row"), "col"),
        P(),
        P(),
        P(),
        P(),
        P(),
        P(),
    )
    return jax.shard_map(
        shards,
        mesh=mesh,
        in_specs=placed,
        out_specs=P(("grp", "row"), "col", None),
        check_vma=False,
    )
```
